32 devices in a mesh: seq: 4 (over x, core), chan: 8 (over z, y).
Axes of the slice: x: 2, y: 2, z: 4, core: 2. Of those that a mesh axis runs over, the one named last changes fastest.
Arguments:
- projections: bfloat16 [3, 2048, 8192], P(None, 'chan', 'seq'), may hold values from -6 to 6
- filter_taps: float32 [2048, 8192], P('chan', 'seq'), may hold values from -1.3 to 1.3
- skip_gain: float32 [2048], P('chan'), may hold values from -1 to 1
- head_weight: bfloat16 [2048, 3840], P('chan'), may hold values from -0.75 to 0.75
- head_bias: float32 [3840], replicated, may hold values from -1 to 1
- counts: int32 [256, 3840], P('seq'), may hold values from 0 to 11
Outputs:
- mean_loss: float32 [], replicated
- feature_grads: float32 [3, 2048, 8192], P(None, 'chan', 'seq')
The draws below stay inside these ranges and needn't reach their ends.
All inputs are finite; a program needn't handle non-finite values.
Results may differ from the reference program's by a relative error of at most 0.007.
Values may be sent and summed in bfloat16 or wider, within the bound.
No kernel may reach another device: no remote copies, remote signals or barrier semaphores. Data moves between devices by JAX's collectives and lax.ppermute only.
A program may use at most 128 MiB of HBM per device.

```python
import jax
import jax.numpy as jnp
from jax import lax

CH = 2048
TRACKS = 3840
POOL = 32
SEQ = 8192
BINS = 256


def draw_filter_taps(key, part):
    key_tau, key_noise = jax.random.split(key)
    low = jnp.log(jnp.float32(30.0))
    noise = jnp.clip(jax.random.normal(key_noise, (CH, SEQ), jnp.float32), -5.0, 5.0)
    high = jnp.log(jnp.float32(64.0 * SEQ))
    tau = jnp.exp(jax.random.uniform(key_tau, (CH, 1), jnp.float32, 0.0, 1.0) * (high - low) + low)
    steps = jnp.arange(SEQ, dtype=jnp.float32)[None, :]
    envelope = jnp.exp(-steps / tau)
    scale = jnp.sqrt((1.0 - jnp.exp(-2.0 / tau)) / (1.0 - jnp.exp(-2.0 * SEQ / tau)))
    return (noise * envelope * scale).astype(jnp.float32)


def draw_counts(key, part):
    bins = jnp.arange(BINS, dtype=jnp.int32)
    upper = 4 + 9 * bins // BINS
    upper = jnp.broadcast_to(upper[:, None], (BINS, TRACKS))
    return jax.random.randint(key, (BINS, TRACKS), 0, upper, dtype=jnp.int32)


def levels(own_key, dims, shards, least, largest):
    level, own = 1.0, jax.random.fold_in(own_key, 6)
    for position, parts in shards:
        heights = jnp.exp(jax.random.uniform(jax.random.fold_in(own, position), (parts,), jnp.float32, least / len(shards), largest / len(shards)))
        level = level * jnp.repeat(heights, dims[position] // parts).reshape([-1 if axis == position else 1 for axis in range(len(dims))])
    return level


def normal_values(stream_key, shape, deviation, most, cuts=(), held_as=jnp.bfloat16):
    factor_of = levels(stream_key, shape, cuts, -0.22, 0.18) if cuts else 1.0
    result = jax.random.normal(stream_key, shape, jnp.float32) * deviation * factor_of
    return jnp.minimum(jnp.maximum(result, -most), most).astype(held_as)


def setup_inputs(seed: int = 0) -> dict:
    key_list = jax.random.split(jax.random.key(seed), 7)
    projections = normal_values(key_list[0], (3, CH, SEQ), 1.0, 6.0, ((1, 8), (2, 4)))
    filter_taps = draw_filter_taps(jax.random.fold_in(key_list[6], 71), 0)
    skip_gain = jnp.clip(jax.random.uniform(key_list[2], (CH,), jnp.float32, -1.0, 1.0) * levels(key_list[2], (CH,), ((0, 8),), -0.4, 0.0), -1.0, 1.0)
    head_weight = normal_values(key_list[3], (CH, TRACKS), (CH // POOL) ** -0.5, 0.75, ((0, 8),))
    head_bias = jnp.clip(jax.random.uniform(key_list[4], (TRACKS,), jnp.float32, -1.0, 1.0), -1.0, 1.0)
    counts = draw_counts(jax.random.fold_in(key_list[6], 71), 0)
    return dict(projections=projections, filter_taps=filter_taps, skip_gain=skip_gain, head_weight=head_weight, head_bias=head_bias, counts=counts)


total_weight = 0.2
rate_floor = 0.5


def causal_block(pair):
    signal, taps = pair
    length = signal.shape[-1]
    padded_len = 2 * length
    spectrum = jnp.fft.rfft(signal, padded_len, axis=-1) * jnp.fft.rfft(taps, padded_len, axis=-1)
    return jnp.fft.irfft(spectrum, padded_len, axis=-1)[..., :length]


def anti_block(pair):
    signal, taps = pair
    length = signal.shape[-1]
    padded_len = 2 * length
    spectrum = jnp.fft.rfft(signal, padded_len, axis=-1) * jnp.conj(jnp.fft.rfft(taps, padded_len, axis=-1))
    return jnp.fft.irfft(spectrum, padded_len, axis=-1)[..., :length]


def blockwise(block_fn, signal, taps):
    groups = 16
    shaped = (signal.reshape(groups, -1, signal.shape[-1]), taps.reshape(groups, -1, taps.shape[-1]))
    return lax.map(block_fn, shaped).reshape(signal.shape)


def reference(projections, filter_taps, skip_gain, head_weight, head_bias, counts):
    query = projections[0].astype(jnp.float32)
    keyed = projections[1].astype(jnp.float32)
    valued = projections[2].astype(jnp.float32)
    key_value = keyed * valued
    conv = blockwise(causal_block, key_value, filter_taps)
    mixed = conv + skip_gain[:, None] * key_value
    output = query * mixed
    pooled = output.reshape(CH, BINS, POOL).mean(axis=2).astype(jnp.bfloat16)
    logits = jnp.dot(pooled.T, head_weight, preferred_element_type=jnp.float32) + head_bias[None, :]
    rates = jax.nn.softplus(logits) + rate_floor
    observed = counts.astype(jnp.float32)
    pred_total = jnp.sum(rates, axis=0)
    obs_total = jnp.sum(observed, axis=0)
    log_pred = jnp.log(pred_total)
    log_sum = jnp.sum(observed * jnp.log(rates))
    loss_sum = jnp.sum(total_weight * (pred_total - obs_total * log_pred) + obs_total * log_pred) - log_sum
    mean_loss = loss_sum / (BINS * TRACKS)
    ratio = obs_total / pred_total
    grad_rates = total_weight * (1.0 - ratio)[None, :] + ratio[None, :] - observed / rates
    grad_logits = (grad_rates * jax.nn.sigmoid(logits)).astype(jnp.bfloat16)
    grad_pooled = jnp.dot(head_weight, grad_logits.T, preferred_element_type=jnp.float32)
    grad_output = jnp.broadcast_to(grad_pooled[:, :, None] / POOL, (CH, BINS, POOL)).reshape(CH, SEQ)
    grad_query = grad_output * mixed
    gated = grad_output * query
    grad_kv = blockwise(anti_block, gated, filter_taps) + skip_gain[:, None] * gated
    return mean_loss, jnp.stack([grad_query, grad_kv * valued, grad_kv * keyed], axis=0)
```

```python
import math

import jax
import jax.numpy as jnp
import ml_dtypes
import numpy as np
from jax import lax
from jax.experimental import pallas as pl
from jax.experimental.pallas import tpu as pltpu
from jax.sharding import PartitionSpec as P

POOL = 32
LANES = 128
ROWS = 16
SHIFT = 0.25

total_weight = 0.2
rate_floor = 0.5

VMEM_LIMIT = 48 * 1024 * 1024


def split_bf16(table):
    high = table.astype(ml_dtypes.bfloat16)
    low = (table - high.astype(np.float64)).astype(ml_dtypes.bfloat16)
    return high, low


def radices(outer):
    first = 1
    while first * first < outer:
        first *= 2
    return first, outer // first


def transform_tables(length):
    outer = length // LANES
    idx = np.arange(LANES)
    angle = 2.0 * np.pi * (np.outer(idx, idx) % LANES) / LANES
    wr, wi = np.cos(angle), -np.sin(angle)
    forward = np.block([[wr, wi], [-wi, wr]])
    backward = np.block([[wr, -wi], [wi, wr]]) / length
    k1 = np.arange(outer)[:, None]
    twist = 2.0 * np.pi * (k1 - SHIFT) * idx[None, :] / length
    f_hi, f_lo = split_bf16(forward)
    b_hi, b_lo = split_bf16(backward)
    return dict(
        fwd=np.stack([f_hi, f_lo]),
        bwd=np.stack([b_hi, b_lo]),
        twist=np.stack([np.cos(twist), -np.sin(twist)]).astype(np.float32),
    )


def pool_tables():
    per = LANES // POOL
    lane = np.arange(LANES)
    hit = (lane[:, None] // POOL) == (lane[None, :] % per)
    gather = np.concatenate([hit, hit], axis=0) / POOL
    spread = np.concatenate([hit.T, hit.T], axis=0) / POOL
    return gather.astype(ml_dtypes.bfloat16), spread.astype(ml_dtypes.bfloat16)


def times(value, angle):
    re, im = value
    c, s = math.cos(angle), math.sin(angle)
    tiny = 1e-12
    if im is None:
        if abs(s) < tiny and c > 0:
            return (re, None)
        return (re * c, re * s)
    if abs(s) < tiny:
        return (re, im) if c > 0 else (-re, -im)
    if abs(c) < tiny:
        return (-im, re) if s > 0 else (im, -re)
    return (re * c - im * s, re * s + im * c)


def add(a, b):
    if a[1] is None and b[1] is None:
        return (a[0] + b[0], None)
    if a[1] is None:
        return (a[0] + b[0], b[1])
    if b[1] is None:
        return (a[0] + b[0], a[1])
    return (a[0] + b[0], a[1] + b[1])


def sub(a, b):
    if a[1] is None and b[1] is None:
        return (a[0] - b[0], None)
    if a[1] is None:
        return (a[0] - b[0], -b[1])
    if b[1] is None:
        return (a[0] - b[0], a[1])
    return (a[0] - b[0], a[1] - b[1])


def small_dft(values, sign):
    count = len(values)
    if count == 1:
        return values
    even = small_dft(values[0::2], sign)
    odd = small_dft(values[1::2], sign)
    out = [None] * count
    half = count // 2
    for k in range(half):
        turned = times(odd[k], sign * 2.0 * math.pi * k / count)
        out[k] = add(even[k], turned)
        out[k + half] = sub(even[k], turned)
    return out


def dot(a, b):
    return jnp.dot(a, b, preferred_element_type=jnp.float32)


def split(value):
    high = value.astype(jnp.bfloat16)
    return high, (value - high.astype(jnp.float32)).astype(jnp.bfloat16)


def lane_transform(re_parts, im_parts, lhs, table_ref):
    for i, (re, im) in enumerate(zip(re_parts, im_parts)):
        rows = pl.ds(i * ROWS, ROWS)
        re_hi, re_lo = split(re)
        im_hi, im_lo = split(im)
        lhs[0, rows, :LANES] = re_hi
        lhs[0, rows, LANES:] = im_hi
        lhs[1, rows, :LANES] = re_lo
        lhs[1, rows, LANES:] = im_lo
    high = lhs[0]
    return dot(high, table_ref[0]) + (dot(lhs[1], table_ref[0]) + dot(high, table_ref[1]))


def first_pass(load, store, outer):
    ra, rb = radices(outer)
    for b in range(rb):
        values = [times((load(rb * a + b), None), 2.0 * math.pi * a * SHIFT / ra) for a in range(ra)]
        out = small_dft(values, -1)
        for alpha in range(ra):
            re, im = times(out[alpha], -2.0 * math.pi * b * (alpha - SHIFT) / outer)
            store(b, alpha, re, im)


def second_pass(parts, alpha, outer, twist_ref):
    ra, rb = radices(outer)
    values = [(parts[0, b, alpha], parts[1, b, alpha]) for b in range(rb)]
    out = small_dft(values, -1)
    res, ims = [], []
    for beta in range(rb):
        k1 = alpha + ra * beta
        tr = twist_ref[0, k1 : k1 + 1, :]
        ti = twist_ref[1, k1 : k1 + 1, :]
        re, im = out[beta]
        res.append(re * tr - im * ti)
        ims.append(re * ti + im * tr)
    return res, ims


def back_second_pass(spectrum, alpha, outer, twist_ref, store):
    ra, rb = radices(outer)
    values = []
    for beta in range(rb):
        k1 = alpha + ra * beta
        tr = twist_ref[0, k1 : k1 + 1, :]
        ti = twist_ref[1, k1 : k1 + 1, :]
        re = spectrum[beta * ROWS : (beta + 1) * ROWS, :LANES]
        im = spectrum[beta * ROWS : (beta + 1) * ROWS, LANES:]
        values.append((re * tr + im * ti, im * tr - re * ti))
    out = small_dft(values, +1)
    for b in range(rb):
        re, im = times(out[b], 2.0 * math.pi * b * (alpha - SHIFT) / outer)
        store(b, alpha, re, im)


def back_first_pass(parts, outer, emit):
    ra, rb = radices(outer)
    for b in range(rb):
        values = [(parts[0, b, alpha], parts[1, b, alpha]) for alpha in range(ra)]
        out = small_dft(values, +1)
        for a in range(ra):
            angle = -2.0 * math.pi * a * SHIFT / ra
            re, im = out[a]
            c, s = math.cos(angle), math.sin(angle)
            emit(rb * a + b, re if a == 0 else re * c - im * s)


def keep(parts):
    def store(b, alpha, re, im):
        parts[0, b, alpha] = re
        parts[1, b, alpha] = im

    return store


def conv_kernel(peers, outer, me_ref, *refs):
    pieces = refs[:peers]
    skip_ref, fwd_ref, bwd_ref, twist_ref = refs[peers : peers + 4]
    outs = refs[peers + 4 : 2 * peers + 4]
    mixed_ref, spec_ref = refs[2 * peers + 4 : 2 * peers + 6]
    rows_in, parts_x, parts_h, parts_y, lhs, rows_out = refs[2 * peers + 6 :]
    me = me_ref[0]
    ra, rb = radices(outer)
    per = outer // peers
    width = per * LANES
    for k in range(peers):
        rows_in[me ^ k] = pieces[k][...]

    def loader(which):
        def load(n1):
            lanes = slice((n1 % per) * LANES, (n1 % per + 1) * LANES)
            return rows_in[n1 // per, which, :, lanes].astype(jnp.float32)

        return load

    load_x = loader(0)
    first_pass(load_x, keep(parts_x), outer)
    first_pass(loader(1), keep(parts_h), outer)
    chunk = rb * ROWS
    for alpha in range(ra):
        x = lane_transform(*second_pass(parts_x, alpha, outer, twist_ref), lhs.at[3 * alpha], fwd_ref)
        h = lane_transform(*second_pass(parts_h, alpha, outer, twist_ref), lhs.at[3 * alpha + 1], fwd_ref)
        spec_ref[0, alpha * chunk : (alpha + 1) * chunk, :] = h
        xr, xi, hr, hi = x[:, :LANES], x[:, LANES:], h[:, :LANES], h[:, LANES:]
        pr = xr * hr - xi * hi
        pi = xr * hi + xi * hr
        rows = [slice(i * ROWS, (i + 1) * ROWS) for i in range(rb)]
        y = lane_transform([pr[r] for r in rows], [pi[r] for r in rows], lhs.at[3 * alpha + 2], bwd_ref)
        back_second_pass(y, alpha, outer, twist_ref, keep(parts_y))
    skip = jnp.broadcast_to(skip_ref[...], (ROWS, LANES))

    def emit(n1, value):
        mixed = value + skip * load_x(n1)
        lanes = slice((n1 % per) * LANES, (n1 % per + 1) * LANES)
        mixed_ref[:, n1 * LANES : (n1 + 1) * LANES] = mixed
        rows_out[n1 // per, :, lanes] = mixed.astype(jnp.bfloat16)

    back_first_pass(parts_y, outer, emit)
    for k in range(peers):
        outs[k][...] = rows_out[me ^ k]


def pool_kernel(peers, outer, me_ref, *refs):
    queries = refs[:peers]
    mixed_ref, gather_ref, pooled_ref, rows_in, lhs = refs[peers:]
    me = me_ref[0]
    per = outer // peers
    for k in range(peers):
        rows_in[me ^ k] = queries[k][...]
    for n1 in range(outer):
        lanes = slice((n1 % per) * LANES, (n1 % per + 1) * LANES)
        query = rows_in[n1 // per, :, lanes].astype(jnp.float32)
        high, low = split(query * mixed_ref[:, n1 * LANES : (n1 + 1) * LANES])
        lhs[n1 * ROWS : (n1 + 1) * ROWS, :LANES] = high
        lhs[n1 * ROWS : (n1 + 1) * ROWS, LANES:] = low
    sums = dot(lhs[...], gather_ref[...])
    each = LANES // POOL
    held = LANES // each
    place = lax.broadcasted_iota(jnp.int32, (ROWS, LANES), 1) // each
    for tile in range(-(-outer // held)):
        total = jnp.zeros((ROWS, LANES), jnp.float32)
        count = min(held, outer - tile * held)
        for j in range(count):
            n1 = tile * held + j
            total = jnp.where(place == j, sums[n1 * ROWS : (n1 + 1) * ROWS], total)
        used = count * each
        pooled_ref[:, tile * LANES : tile * LANES + used] = total[:, :used].astype(jnp.bfloat16)


def corr_kernel(peers, outer, me_ref, *refs):
    queries = refs[:peers]
    grad_ref, spec_ref, skip_ref, fwd_ref, bwd_ref, twist_ref, spread_ref = refs[peers : peers + 7]
    outs = refs[peers + 7 : 2 * peers + 7]
    rows_in, lhs_g, gated, parts_g, parts_y, lhs, rows_out = refs[2 * peers + 7 :]
    me = me_ref[0]
    ra, rb = radices(outer)
    per = outer // peers
    for k in range(peers):
        rows_in[me ^ k] = queries[k][...]
    each = LANES // POOL
    held = LANES // each
    place = lax.broadcasted_iota(jnp.int32, (ROWS, LANES), 1) // each
    zero = jnp.zeros((ROWS, LANES), jnp.float32)
    for tile in range(-(-outer // held)):
        count = min(held, outer - tile * held)
        used = count * each
        part = grad_ref[:, tile * LANES : tile * LANES + used]
        if used < LANES:
            part = jnp.concatenate([part, jnp.zeros((ROWS, LANES - used), jnp.float32)], axis=1)
        high = part.astype(jnp.bfloat16).astype(jnp.float32)
        low = part - high
        for j in range(count):
            rows = pl.ds((tile * held + j) * ROWS, ROWS)
            lhs_g[rows, :LANES] = jnp.where(place == j, high, zero).astype(jnp.bfloat16)
            lhs_g[rows, LANES:] = jnp.where(place == j, low, zero).astype(jnp.bfloat16)
    gated[...] = dot(lhs_g[...], spread_ref[...])
    for n1 in range(outer):
        lanes = slice((n1 % per) * LANES, (n1 % per + 1) * LANES)
        rows = pl.ds(n1 * ROWS, ROWS)
        gated[rows, :] = gated[rows, :] * rows_in[n1 // per, :, lanes].astype(jnp.float32)

    def load_g(n1):
        return gated[n1 * ROWS : (n1 + 1) * ROWS, :]

    first_pass(load_g, keep(parts_g), outer)
    chunk = rb * ROWS
    for alpha in range(ra):
        g = lane_transform(*second_pass(parts_g, alpha, outer, twist_ref), lhs.at[2 * alpha], fwd_ref)
        h = spec_ref[0, alpha * chunk : (alpha + 1) * chunk, :]
        gr, gi, hr, hi = g[:, :LANES], g[:, LANES:], h[:, :LANES], h[:, LANES:]
        pr = gr * hr + gi * hi
        pi = gi * hr - gr * hi
        rows = [slice(i * ROWS, (i + 1) * ROWS) for i in range(rb)]
        y = lane_transform([pr[r] for r in rows], [pi[r] for r in rows], lhs.at[2 * alpha + 1], bwd_ref)
        back_second_pass(y, alpha, outer, twist_ref, keep(parts_y))
    skip = jnp.broadcast_to(skip_ref[...], (ROWS, LANES))

    def emit(n1, value):
        lanes = slice((n1 % per) * LANES, (n1 % per + 1) * LANES)
        rows_out[n1 // per, :, lanes] = (value + skip * load_g(n1)).astype(jnp.bfloat16)

    back_first_pass(parts_y, outer, emit)
    for k in range(peers):
        outs[k][...] = rows_out[me ^ k]


def whole(array):
    rank = array.ndim
    return pl.BlockSpec(array.shape, lambda i, me: (0,) * rank)


def by_rows(width):
    return pl.BlockSpec((ROWS, width), lambda i, me: (i, 0))


def call(kernel, name, me, steps, inputs, in_specs, out_shapes, out_specs, scratch, flops):
    moved = sum(x.size * x.dtype.itemsize for x in inputs)
    moved += sum(math.prod(o.shape) * o.dtype.itemsize for o in out_shapes)
    return pl.pallas_call(
        kernel,
        name=name,
        grid_spec=pltpu.PrefetchScalarGridSpec(
            num_scalar_prefetch=1,
            grid=(steps,),
            in_specs=in_specs,
            out_specs=out_specs,
            scratch_shapes=scratch,
        ),
        out_shape=out_shapes,
        compiler_params=pltpu.CompilerParams(
            dimension_semantics=("arbitrary",), vmem_limit_bytes=VMEM_LIMIT
        ),
        cost_estimate=pl.CostEstimate(flops=flops, bytes_accessed=moved, transcendentals=0),
    )(me, *inputs)


def convolve(me, pieces, skip, tables):
    peers = len(pieces)
    rows, width = pieces[0].shape[1:]
    length = width * peers
    outer = length // LANES
    ra, rb = radices(outer)
    chunk = rb * ROWS
    steps = rows // ROWS
    f32, bf16 = jnp.float32, jnp.bfloat16
    fwd, bwd, twist = tables["fwd"], tables["bwd"], tables["twist"]
    out_shapes = [jax.ShapeDtypeStruct((rows, width), bf16)] * peers + [
        jax.ShapeDtypeStruct((rows, length), f32),
        jax.ShapeDtypeStruct((steps, outer * ROWS, 2 * LANES), f32),
    ]
    out_specs = [by_rows(width)] * peers + [
        by_rows(length),
        pl.BlockSpec((1, outer * ROWS, 2 * LANES), lambda i, me: (i, 0, 0)),
    ]
    in_specs = [pl.BlockSpec((2, ROWS, width), lambda i, me: (0, i, 0))] * peers + [
        pl.BlockSpec((ROWS, 1), lambda i, me: (i, 0)),
        whole(fwd),
        whole(bwd),
        whole(twist),
    ]
    parts = pltpu.VMEM((2, rb, ra, ROWS, LANES), f32)
    scratch = [
        pltpu.VMEM((peers, 2, ROWS, width), bf16),
        parts,
        parts,
        parts,
        pltpu.VMEM((3 * ra, 2, chunk, 2 * LANES), bf16),
        pltpu.VMEM((peers, ROWS, width), bf16),
    ]

    def kernel(*refs):
        conv_kernel(peers, outer, *refs)

    out = call(
        kernel, "long_convolution", me, steps, [*pieces, skip, fwd, bwd, twist], in_specs, out_shapes, out_specs,
        scratch, 2 * 9 * rows * outer * (2 * LANES) ** 2,
    )
    return out[:peers], out[peers], out[peers + 1]


def pool(me, queries, mixed, gather):
    peers = len(queries)
    rows, width = queries[0].shape
    length = width * peers
    outer = length // LANES
    bins = length // POOL
    bf16 = jnp.bfloat16

    def kernel(*refs):
        pool_kernel(peers, outer, *refs)

    return call(
        kernel, "pool_bins", me, rows // ROWS, [*queries, mixed, gather],
        [by_rows(width)] * peers + [by_rows(length), whole(gather)],
        [jax.ShapeDtypeStruct((rows, bins), bf16)], [by_rows(bins)],
        [pltpu.VMEM((peers, ROWS, width), bf16), pltpu.VMEM((outer * ROWS, 2 * LANES), bf16)],
        2 * rows * outer * 2 * LANES * LANES,
    )[0]


def correlate(me, queries, grad_pooled, spec, skip, tables, spread):
    peers = len(queries)
    rows, width = queries[0].shape
    length = width * peers
    outer = length // LANES
    bins = length // POOL
    ra, rb = radices(outer)
    chunk = rb * ROWS
    f32, bf16 = jnp.float32, jnp.bfloat16
    fwd, bwd, twist = tables["fwd"], tables["bwd"], tables["twist"]
    in_specs = [by_rows(width)] * peers + [
        by_rows(bins),
        pl.BlockSpec((1, outer * ROWS, 2 * LANES), lambda i, me: (i, 0, 0)),
        pl.BlockSpec((ROWS, 1), lambda i, me: (i, 0)),
        whole(fwd),
        whole(bwd),
        whole(twist),
        whole(spread),
    ]
    parts = pltpu.VMEM((2, rb, ra, ROWS, LANES), f32)
    scratch = [
        pltpu.VMEM((peers, ROWS, width), bf16),
        pltpu.VMEM((outer * ROWS, 2 * LANES), bf16),
        pltpu.VMEM((outer * ROWS, LANES), f32),
        parts,
        parts,
        pltpu.VMEM((2 * ra, 2, chunk, 2 * LANES), bf16),
        pltpu.VMEM((peers, ROWS, width), bf16),
    ]

    def kernel(*refs):
        corr_kernel(peers, outer, *refs)

    return call(
        kernel, "long_correlation", me, rows // ROWS,
        [*queries, grad_pooled, spec, skip, fwd, bwd, twist, spread], in_specs,
        [jax.ShapeDtypeStruct((rows, width), bf16)] * peers, [by_rows(width)] * peers,
        scratch, 2 * 7 * rows * outer * (2 * LANES) ** 2,
    )


def swap(value, k, count):
    if k == 0:
        return value
    return lax.ppermute(value, "seq", [(i, i ^ k) for i in range(count)])


def pad_rows(value, rows):
    short = rows - value.shape[-2]
    if short == 0:
        return value
    widths = [(0, 0)] * value.ndim
    widths[-2] = (0, short)
    return jnp.pad(value, widths)


def per_device(projections, filter_taps, skip_gain, head_weight, head_bias, counts):
    f32, bf16 = jnp.float32, jnp.bfloat16
    _, channels, width = projections.shape
    peers = lax.axis_size("seq")
    groups = lax.axis_size("chan")
    seat = lax.axis_index("seq")
    group = lax.axis_index("chan")
    bins = width // POOL
    length = width * peers
    tracks = head_weight.shape[1]
    own_tracks = tracks // groups
    pencil = channels // peers
    rows = -(-pencil // ROWS) * ROWS
    me = jnp.asarray(seat, jnp.int32).reshape(1)
    tables = transform_tables(length)
    gather, spread = pool_tables()

    def block(array, k):
        return lax.dynamic_index_in_dim(array, seat ^ k, axis=-3, keepdims=False)

    query = projections[0]
    key_value = projections[1].astype(f32) * projections[2].astype(f32)
    stacked = jnp.stack([key_value.astype(bf16), filter_taps.astype(bf16)])
    stacked = stacked.reshape(2, peers, pencil, width)
    pieces = [pad_rows(swap(block(stacked, k), k, peers), rows) for k in range(peers)]
    query_blocks = query.reshape(peers, pencil, width)
    queries = [pad_rows(swap(block(query_blocks, k), k, peers), rows) for k in range(peers)]
    skip = pad_rows(block(skip_gain.reshape(peers, pencil, 1), 0), rows)

    half = channels // 2
    by_track = head_weight.reshape(2, half, groups, own_tracks).transpose(0, 2, 1, 3)
    mine = lax.dynamic_index_in_dim(by_track, seat & 1, axis=0, keepdims=False)
    mine = lax.all_to_all(mine, "chan", split_axis=0, concat_axis=0, tiled=True)
    other = swap(mine, 1, peers)
    mine = mine.reshape(groups * half, own_tracks)
    other = other.reshape(groups * half, own_tracks)

    mixed_out, mixed, spec = convolve(me, pieces, skip, tables)
    mixed_home = [swap(mixed_out[k][:pencil], k, peers) for k in range(peers)]
    pooled = pool(me, queries, mixed, gather)[:pencil]

    sent = pooled.reshape(pencil, peers, bins).transpose(1, 0, 2)
    sent = jnp.broadcast_to(sent[None], (groups, peers, pencil, bins))
    got = lax.all_to_all(
        sent.reshape(groups * peers, pencil, bins), ("chan", "seq"), split_axis=0, concat_axis=0, tiled=True
    )
    got = got.reshape(groups, 2, half, bins)
    low_half = got[:, 0].reshape(groups * half, bins)
    high_half = got[:, 1].reshape(groups * half, bins)
    odd = (seat & 1) == 1
    pooled_mine = jnp.where(odd, high_half, low_half)
    pooled_other = jnp.where(odd, low_half, high_half)

    def project(x, w):
        return lax.dot_general(x, w, (((0,), (0,)), ((), ())), preferred_element_type=f32)

    own_bias = lax.dynamic_slice_in_dim(head_bias, group * own_tracks, own_tracks)
    own_counts = lax.dynamic_slice_in_dim(counts, group * own_tracks, own_tracks, axis=1)
    logits = project(pooled_mine, mine) + project(pooled_other, other) + own_bias[None, :]
    rates = jax.nn.softplus(logits) + rate_floor
    observed = own_counts.astype(f32)
    partial_sums = jnp.stack(
        [jnp.sum(rates, axis=0), jnp.sum(observed, axis=0), jnp.sum(observed * jnp.log(rates), axis=0)]
    )
    pred_total, obs_total, log_sum = jnp.sum(lax.all_gather(partial_sums, "seq"), axis=0)
    log_pred = jnp.log(pred_total)
    loss_part = jnp.sum(
        total_weight * (pred_total - obs_total * log_pred) + obs_total * log_pred - log_sum
    )
    mean_loss = lax.psum(loss_part, "chan") / (bins * peers * tracks)
    ratio = obs_total / pred_total
    grad_rates = total_weight * (1.0 - ratio)[None, :] + ratio[None, :] - observed / rates
    grad_logits = (grad_rates * jax.nn.sigmoid(logits)).astype(bf16)

    def spread_back(w):
        return lax.dot_general(w, grad_logits, (((1,), (1,)), ((), ())), preferred_element_type=f32)

    part_mine = spread_back(mine).astype(bf16).reshape(groups, 1, half, bins)
    part_other = spread_back(other).astype(bf16).reshape(groups, 1, half, bins)
    part = jnp.concatenate(
        [jnp.where(odd, part_other, part_mine), jnp.where(odd, part_mine, part_other)], axis=1
    )
    back = lax.all_to_all(
        part.reshape(groups * peers, pencil, bins), ("chan", "seq"), split_axis=0, concat_axis=0, tiled=True
    )
    grad_pooled = jnp.sum(back.reshape(groups, peers, pencil, bins).astype(f32), axis=0)
    grad_home = [swap(block(grad_pooled, k), k, peers) for k in range(peers)]
    grad_rows = pad_rows(grad_pooled.transpose(1, 0, 2).reshape(pencil, peers * bins), rows)

    corr_out = correlate(me, queries, grad_rows, spec, skip, tables, spread)
    corr_home = [swap(corr_out[k][:pencil], k, peers) for k in range(peers)]

    def assemble(parts):
        out = jnp.zeros((peers,) + parts[0].shape, parts[0].dtype)
        for k, part in enumerate(parts):
            out = lax.dynamic_update_index_in_dim(out, part, seat ^ k, axis=0)
        return out.reshape((channels,) + parts[0].shape[1:])

    grad_output = jnp.repeat(assemble(grad_home) / POOL, POOL, axis=1)
    grad_kv = assemble(corr_home).astype(f32)
    grad_query = grad_output * assemble(mixed_home).astype(f32)
    grads = jnp.stack(
        [grad_query, grad_kv * projections[2].astype(f32), grad_kv * projections[1].astype(f32)], axis=0
    )
    return mean_loss, grads


def solution(mesh):
    placed = (
        P(None, "chan", "seq"),
        P("chan", "seq"),
        P("chan"),
        P("chan", None),
        P(),
        P("seq", None),
    )
    return jax.shard_map(
        per_device,
        mesh=mesh,
        in_specs=placed,
        out_specs=(P(), P(None, "chan", "seq")),
        check_vma=False,
    )
```

```python
import math

import jax
import jax.numpy as jnp
import ml_dtypes
import numpy as np
from jax import lax
from jax.experimental import pallas as pl
from jax.experimental.pallas import tpu as pltpu
from jax.sharding import PartitionSpec as P

POOL = 32
LANES = 128
ROWS = 16
SHIFT = 0.25

total_weight = 0.2
rate_floor = 0.5

VMEM_LIMIT = 48 * 1024 * 1024
CHUNKS = 2
MOST_GROUPS = 16


def split_bf16(table):
    high = table.astype(ml_dtypes.bfloat16)
    low = (table - high.astype(np.float64)).astype(ml_dtypes.bfloat16)
    return high, low


def radices(outer):
    first = 1
    while first * first < outer:
        first *= 2
    return first, outer // first


def transform_tables(length):
    outer = length // LANES
    idx = np.arange(LANES)
    angle = 2.0 * np.pi * (np.outer(idx, idx) % LANES) / LANES
    wr, wi = np.cos(angle), -np.sin(angle)
    forward = np.block([[wr, wi], [-wi, wr]])
    backward = np.block([[wr, -wi], [wi, wr]]) / length
    k1 = np.arange(outer)[:, None]
    twist = 2.0 * np.pi * (k1 - SHIFT) * idx[None, :] / length
    f_hi, f_lo = split_bf16(forward)
    b_hi, b_lo = split_bf16(backward)
    return dict(
        fwd=np.stack([f_hi, f_lo]),
        bwd=np.stack([b_hi, b_lo]),
        twist=np.stack([np.cos(twist), -np.sin(twist)]).astype(np.float32),
    )


def pool_tables():
    per = LANES // POOL
    lane = np.arange(LANES)
    hit = (lane[:, None] // POOL) == (lane[None, :] % per)
    gather = np.concatenate([hit, hit], axis=0) / POOL
    spread = np.concatenate([hit.T, hit.T], axis=0) / POOL
    return gather.astype(ml_dtypes.bfloat16), spread.astype(ml_dtypes.bfloat16)


def times(value, angle):
    re, im = value
    c, s = math.cos(angle), math.sin(angle)
    tiny = 1e-12
    if im is None:
        if abs(s) < tiny and c > 0:
            return (re, None)
        return (re * c, re * s)
    if abs(s) < tiny:
        return (re, im) if c > 0 else (-re, -im)
    if abs(c) < tiny:
        return (-im, re) if s > 0 else (im, -re)
    return (re * c - im * s, re * s + im * c)


def add(a, b):
    if a[1] is None and b[1] is None:
        return (a[0] + b[0], None)
    if a[1] is None:
        return (a[0] + b[0], b[1])
    if b[1] is None:
        return (a[0] + b[0], a[1])
    return (a[0] + b[0], a[1] + b[1])


def sub(a, b):
    if a[1] is None and b[1] is None:
        return (a[0] - b[0], None)
    if a[1] is None:
        return (a[0] - b[0], -b[1])
    if b[1] is None:
        return (a[0] - b[0], a[1])
    return (a[0] - b[0], a[1] - b[1])


def small_dft(values, sign):
    count = len(values)
    if count == 1:
        return values
    even = small_dft(values[0::2], sign)
    odd = small_dft(values[1::2], sign)
    out = [None] * count
    half = count // 2
    for k in range(half):
        turned = times(odd[k], sign * 2.0 * math.pi * k / count)
        out[k] = add(even[k], turned)
        out[k + half] = sub(even[k], turned)
    return out


def dot(a, b):
    return jnp.dot(a, b, preferred_element_type=jnp.float32)


def split(value):
    high = value.astype(jnp.bfloat16)
    return high, (value - high.astype(jnp.float32)).astype(jnp.bfloat16)


def lane_transform(re_parts, im_parts, lhs, table_ref):
    for i, (re, im) in enumerate(zip(re_parts, im_parts)):
        rows = pl.ds(i * ROWS, ROWS)
        re_hi, re_lo = split(re)
        im_hi, im_lo = split(im)
        lhs[0, rows, :LANES] = re_hi
        lhs[0, rows, LANES:] = im_hi
        lhs[1, rows, :LANES] = re_lo
        lhs[1, rows, LANES:] = im_lo
    high = lhs[0]
    return dot(high, table_ref[0]) + (dot(lhs[1], table_ref[0]) + dot(high, table_ref[1]))


def first_pass(load, store, outer):
    ra, rb = radices(outer)
    for b in range(rb):
        values = [times((load(rb * a + b), None), 2.0 * math.pi * a * SHIFT / ra) for a in range(ra)]
        out = small_dft(values, -1)
        for alpha in range(ra):
            re, im = times(out[alpha], -2.0 * math.pi * b * (alpha - SHIFT) / outer)
            store(b, alpha, re, im)


def second_pass(parts, alpha, outer, twist_ref):
    ra, rb = radices(outer)
    values = [(parts[0, b, alpha], parts[1, b, alpha]) for b in range(rb)]
    out = small_dft(values, -1)
    res, ims = [], []
    for beta in range(rb):
        k1 = alpha + ra * beta
        tr = twist_ref[0, k1 : k1 + 1, :]
        ti = twist_ref[1, k1 : k1 + 1, :]
        re, im = out[beta]
        res.append(re * tr - im * ti)
        ims.append(re * ti + im * tr)
    return res, ims


def back_second_pass(spectrum, alpha, outer, twist_ref, store):
    ra, rb = radices(outer)
    values = []
    for beta in range(rb):
        k1 = alpha + ra * beta
        tr = twist_ref[0, k1 : k1 + 1, :]
        ti = twist_ref[1, k1 : k1 + 1, :]
        re = spectrum[beta * ROWS : (beta + 1) * ROWS, :LANES]
        im = spectrum[beta * ROWS : (beta + 1) * ROWS, LANES:]
        values.append((re * tr + im * ti, im * tr - re * ti))
    out = small_dft(values, +1)
    for b in range(rb):
        re, im = times(out[b], 2.0 * math.pi * b * (alpha - SHIFT) / outer)
        store(b, alpha, re, im)


def back_first_pass(parts, outer, emit):
    ra, rb = radices(outer)
    for b in range(rb):
        values = [(parts[0, b, alpha], parts[1, b, alpha]) for alpha in range(ra)]
        out = small_dft(values, +1)
        for a in range(ra):
            angle = -2.0 * math.pi * a * SHIFT / ra
            re, im = out[a]
            c, s = math.cos(angle), math.sin(angle)
            emit(rb * a + b, re if a == 0 else re * c - im * s)


def keep(parts):
    def store(b, alpha, re, im):
        parts[0, b, alpha] = re
        parts[1, b, alpha] = im

    return store


def conv_kernel(peers, outer, me_ref, *refs):
    pieces = refs[:peers]
    skip_ref, fwd_ref, bwd_ref, twist_ref = refs[peers : peers + 4]
    mixed_ref, spec_ref, rows_in, parts_x, parts_h, parts_y, lhs = refs[-7:]
    me = me_ref[0]
    ra, rb = radices(outer)
    per = outer // peers
    for k in range(peers):
        rows_in[me ^ k] = pieces[k][...]

    def loader(which):
        def load(n1):
            lanes = slice((n1 % per) * LANES, (n1 % per + 1) * LANES)
            return rows_in[n1 // per, which, :, lanes].astype(jnp.float32)

        return load

    load_x = loader(0)
    first_pass(load_x, keep(parts_x), outer)
    first_pass(loader(1), keep(parts_h), outer)
    chunk = rb * ROWS
    for alpha in range(ra):
        x = lane_transform(*second_pass(parts_x, alpha, outer, twist_ref), lhs.at[3 * alpha], fwd_ref)
        h = lane_transform(*second_pass(parts_h, alpha, outer, twist_ref), lhs.at[3 * alpha + 1], fwd_ref)
        spec_ref[0, alpha * chunk : (alpha + 1) * chunk, :] = h
        xr, xi, hr, hi = x[:, :LANES], x[:, LANES:], h[:, :LANES], h[:, LANES:]
        pr = xr * hr - xi * hi
        pi = xr * hi + xi * hr
        rows = [slice(i * ROWS, (i + 1) * ROWS) for i in range(rb)]
        y = lane_transform([pr[r] for r in rows], [pi[r] for r in rows], lhs.at[3 * alpha + 2], bwd_ref)
        back_second_pass(y, alpha, outer, twist_ref, keep(parts_y))
    skip = jnp.broadcast_to(skip_ref[...], (ROWS, LANES))

    def emit(n1, value):
        mixed_ref[:, n1 * LANES : (n1 + 1) * LANES] = value + skip * load_x(n1)

    back_first_pass(parts_y, outer, emit)


def pool_rows(rows_in, mixed_ref, rows_out, row, gather_ref, lhs, per, outer):
    for n1 in range(outer):
        lanes = slice((n1 % per) * LANES, (n1 % per + 1) * LANES)
        query = rows_in[n1 // per, row : row + ROWS, lanes].astype(jnp.float32)
        mixed = mixed_ref[row : row + ROWS, n1 * LANES : (n1 + 1) * LANES]
        rows_out[n1 // per, row : row + ROWS, lanes] = mixed.astype(jnp.bfloat16)
        high, low = split(query * mixed)
        lhs[n1 * ROWS : (n1 + 1) * ROWS, :LANES] = high
        lhs[n1 * ROWS : (n1 + 1) * ROWS, LANES:] = low
    sums = dot(lhs[...], gather_ref[...])
    each = LANES // POOL
    held = LANES // each
    place = lax.broadcasted_iota(jnp.int32, (ROWS, LANES), 1) // each
    tiles = []
    for tile in range(-(-outer // held)):
        total = jnp.zeros((ROWS, LANES), jnp.float32)
        for j in range(min(held, outer - tile * held)):
            n1 = tile * held + j
            total = jnp.where(place == j, sums[n1 * ROWS : (n1 + 1) * ROWS], total)
        tiles.append(total)
    return jnp.concatenate(tiles, axis=1)


def pool_kernel(peers, outer, me_ref, *refs):
    queries = refs[:peers]
    mixed_ref, gather_ref = refs[peers : peers + 2]
    outs = refs[peers + 2 : 2 * peers + 2]
    pooled_ref, rows_in, rows_out, lhs = refs[2 * peers + 2 :]
    me = me_ref[0]
    per = outer // peers
    for k in range(peers):
        rows_in[me ^ k] = queries[k][...]
    rows = mixed_ref.shape[0]
    bins = outer * LANES // POOL
    if rows == ROWS:
        pooled = pool_rows(rows_in, mixed_ref, rows_out, 0, gather_ref, lhs.at[0], per, outer)
        pooled_ref[...] = pooled[:, :bins].astype(jnp.bfloat16)
    else:
        left = pool_rows(rows_in, mixed_ref, rows_out, 0, gather_ref, lhs.at[0], per, outer)
        right = pool_rows(rows_in, mixed_ref, rows_out, ROWS, gather_ref, lhs.at[1], per, outer)
        each = bins // peers
        for seat in range(peers):
            mine = slice(seat * each, (seat + 1) * each)
            pair = jnp.concatenate([left[:, mine], right[:, mine]], axis=1).astype(jnp.bfloat16)
            for group in range(pooled_ref.shape[0]):
                pooled_ref[group, seat] = pair
    for k in range(peers):
        outs[k][...] = rows_out[me ^ k]


def corr_kernel(peers, outer, me_ref, *refs):
    queries = refs[:peers]
    grad_ref, spec_ref, skip_ref, fwd_ref, bwd_ref, twist_ref, spread_ref = refs[peers : peers + 7]
    outs = refs[peers + 7 : 2 * peers + 7]
    rows_in, lhs_g, gated, parts_g, parts_y, lhs, rows_out = refs[2 * peers + 7 :]
    me = me_ref[0]
    ra, rb = radices(outer)
    per = outer // peers
    for k in range(peers):
        rows_in[me ^ k] = queries[k][...]
    each = LANES // POOL
    held = LANES // each
    place = lax.broadcasted_iota(jnp.int32, (ROWS, LANES), 1) // each
    zero = jnp.zeros((ROWS, LANES), jnp.float32)
    for tile in range(-(-outer // held)):
        count = min(held, outer - tile * held)
        used = count * each
        part = grad_ref[:, tile * LANES : tile * LANES + used]
        if used < LANES:
            part = jnp.concatenate([part, jnp.zeros((ROWS, LANES - used), jnp.float32)], axis=1)
        high = part.astype(jnp.bfloat16).astype(jnp.float32)
        low = part - high
        for j in range(count):
            rows = pl.ds((tile * held + j) * ROWS, ROWS)
            lhs_g[rows, :LANES] = jnp.where(place == j, high, zero).astype(jnp.bfloat16)
            lhs_g[rows, LANES:] = jnp.where(place == j, low, zero).astype(jnp.bfloat16)
    gated[...] = dot(lhs_g[...], spread_ref[...])
    for n1 in range(outer):
        lanes = slice((n1 % per) * LANES, (n1 % per + 1) * LANES)
        rows = pl.ds(n1 * ROWS, ROWS)
        gated[rows, :] = gated[rows, :] * rows_in[n1 // per, :, lanes].astype(jnp.float32)

    def load_g(n1):
        return gated[n1 * ROWS : (n1 + 1) * ROWS, :]

    first_pass(load_g, keep(parts_g), outer)
    chunk = rb * ROWS
    for alpha in range(ra):
        g = lane_transform(*second_pass(parts_g, alpha, outer, twist_ref), lhs.at[2 * alpha], fwd_ref)
        h = spec_ref[0, alpha * chunk : (alpha + 1) * chunk, :]
        gr, gi, hr, hi = g[:, :LANES], g[:, LANES:], h[:, :LANES], h[:, LANES:]
        pr = gr * hr + gi * hi
        pi = gi * hr - gr * hi
        rows = [slice(i * ROWS, (i + 1) * ROWS) for i in range(rb)]
        y = lane_transform([pr[r] for r in rows], [pi[r] for r in rows], lhs.at[2 * alpha + 1], bwd_ref)
        back_second_pass(y, alpha, outer, twist_ref, keep(parts_y))
    skip = jnp.broadcast_to(skip_ref[...], (ROWS, LANES))

    def emit(n1, value):
        lanes = slice((n1 % per) * LANES, (n1 % per + 1) * LANES)
        rows_out[n1 // per, :, lanes] = (value + skip * load_g(n1)).astype(jnp.bfloat16)

    back_first_pass(parts_y, outer, emit)
    for k in range(peers):
        outs[k][...] = rows_out[me ^ k]


def whole(array):
    rank = array.ndim
    return pl.BlockSpec(array.shape, lambda i, me: (0,) * rank)


def by_rows(width, rows=ROWS, start=0):
    return pl.BlockSpec((rows, width), lambda i, me: (start + i, 0))


def call(kernel, name, me, steps, inputs, in_specs, out_shapes, out_specs, scratch, flops, aliases=None):
    moved = sum(x.size * x.dtype.itemsize for x in inputs)
    moved += sum(math.prod(o.shape) * o.dtype.itemsize for o in out_shapes)
    return pl.pallas_call(
        kernel,
        name=name,
        grid_spec=pltpu.PrefetchScalarGridSpec(
            num_scalar_prefetch=1,
            grid=(steps,),
            in_specs=in_specs,
            out_specs=out_specs,
            scratch_shapes=scratch,
        ),
        out_shape=out_shapes,
        input_output_aliases=aliases or {},
        compiler_params=pltpu.CompilerParams(
            dimension_semantics=("arbitrary",), vmem_limit_bytes=VMEM_LIMIT
        ),
        cost_estimate=pl.CostEstimate(flops=flops, bytes_accessed=moved, transcendentals=0),
    )(me, *inputs)


def shape(dims, dtype):
    return jax.ShapeDtypeStruct(dims, dtype)


def convolve(me, pieces, skip, tables, total_rows, start, before):
    peers = len(pieces)
    rows, width = pieces[0].shape[1:]
    length = width * peers
    outer = length // LANES
    ra, rb = radices(outer)
    chunk = rb * ROWS
    steps = rows // ROWS
    first = start // ROWS
    f32, bf16 = jnp.float32, jnp.bfloat16
    fwd, bwd, twist = tables["fwd"], tables["bwd"], tables["twist"]
    inputs = [*pieces, skip, fwd, bwd, twist]
    in_specs = [pl.BlockSpec((2, ROWS, width), lambda i, me: (0, i, 0))] * peers + [
        by_rows(1, start=first),
        whole(fwd),
        whole(bwd),
        whole(twist),
    ]
    aliases = {}
    if before is not None:
        aliases = {1 + len(inputs): 0}
        inputs.append(before)
        in_specs.append(pl.BlockSpec(memory_space=pl.ANY))
    parts = pltpu.VMEM((2, rb, ra, ROWS, LANES), f32)

    def kernel(*refs):
        conv_kernel(peers, outer, *refs)

    return call(
        kernel, "long_convolution", me, steps, inputs, in_specs,
        [shape((total_rows, length), f32), shape((steps, outer * ROWS, 2 * LANES), f32)],
        [by_rows(length, start=first), pl.BlockSpec((1, outer * ROWS, 2 * LANES), lambda i, me: (i, 0, 0))],
        [
            pltpu.VMEM((peers, 2, ROWS, width), bf16),
            parts,
            parts,
            parts,
            pltpu.VMEM((3 * ra, 2, chunk, 2 * LANES), bf16),
        ],
        2 * 9 * rows * outer * (2 * LANES) ** 2, aliases,
    )


def pool(me, queries, mixed, gather, groups):
    peers = len(queries)
    rows, width = queries[0].shape
    length = width * peers
    outer = length // LANES
    bins = length // POOL
    bf16 = jnp.bfloat16
    if groups:
        step = 2 * ROWS
        pooled_shape = shape((groups, peers, rows // 2, LANES), bf16)
        pooled_spec = pl.BlockSpec((groups, peers, ROWS, LANES), lambda i, me: (0, 0, i, 0))
    else:
        step = ROWS
        pooled_shape = shape((rows, bins), bf16)
        pooled_spec = by_rows(bins)

    def kernel(*refs):
        pool_kernel(peers, outer, *refs)

    out = call(
        kernel, "pool_bins", me, rows // step, [*queries, mixed, gather],
        [by_rows(width, step)] * peers + [by_rows(length, step), whole(gather)],
        [shape((rows, width), bf16)] * peers + [pooled_shape],
        [by_rows(width, step)] * peers + [pooled_spec],
        [
            pltpu.VMEM((peers, step, width), bf16),
            pltpu.VMEM((peers, step, width), bf16),
            pltpu.VMEM((step // ROWS, outer * ROWS, 2 * LANES), bf16),
        ],
        2 * rows * outer * 2 * LANES * LANES,
    )
    return out[:peers], out[peers]


def correlate(me, queries, grad_pooled, spec, skip, tables, spread, start):
    peers = len(queries)
    width = queries[0].shape[1]
    rows = spec.shape[0] * ROWS
    length = width * peers
    outer = length // LANES
    bins = length // POOL
    ra, rb = radices(outer)
    chunk = rb * ROWS
    first = start // ROWS
    f32, bf16 = jnp.float32, jnp.bfloat16
    fwd, bwd, twist = tables["fwd"], tables["bwd"], tables["twist"]
    in_specs = [by_rows(width, start=first)] * peers + [
        by_rows(bins, start=first),
        pl.BlockSpec((1, outer * ROWS, 2 * LANES), lambda i, me: (i, 0, 0)),
        by_rows(1, start=first),
        whole(fwd),
        whole(bwd),
        whole(twist),
        whole(spread),
    ]
    parts = pltpu.VMEM((2, rb, ra, ROWS, LANES), f32)
    scratch = [
        pltpu.VMEM((peers, ROWS, width), bf16),
        pltpu.VMEM((outer * ROWS, 2 * LANES), bf16),
        pltpu.VMEM((outer * ROWS, LANES), f32),
        parts,
        parts,
        pltpu.VMEM((2 * ra, 2, chunk, 2 * LANES), bf16),
        pltpu.VMEM((peers, ROWS, width), bf16),
    ]

    def kernel(*refs):
        corr_kernel(peers, outer, *refs)

    return call(
        kernel, "long_correlation", me, rows // ROWS,
        [*queries, grad_pooled, spec, skip, fwd, bwd, twist, spread], in_specs,
        [shape((rows, width), bf16)] * peers, [by_rows(width)] * peers,
        scratch, 2 * 7 * rows * outer * (2 * LANES) ** 2,
    )


def lay_out(me, projections, filter_taps, peers, chunks):
    _, channels, width = projections.shape
    pencil = channels // peers
    rows = pencil // chunks
    bf16 = jnp.bfloat16

    def kernel(me_ref, keyed_ref, valued_ref, taps_ref, *outs):
        for k in range(peers):

            @pl.when(pl.program_id(0) == k)
            def _():
                for j in range(chunks):
                    part = slice(j * rows, (j + 1) * rows)
                    keyed = keyed_ref[0, part, :].astype(jnp.float32)
                    valued = valued_ref[0, part, :].astype(jnp.float32)
                    outs[j * peers + k][0] = (keyed * valued).astype(bf16)
                    outs[j * peers + k][1] = taps_ref[part, :].astype(bf16)

    piece = shape((2, rows, width), bf16)
    out = call(
        kernel, "lay_out", me, peers, [projections, projections, filter_taps],
        [
            pl.BlockSpec((1, pencil, width), lambda i, me: (1, me[0] ^ i, 0)),
            pl.BlockSpec((1, pencil, width), lambda i, me: (2, me[0] ^ i, 0)),
            pl.BlockSpec((pencil, width), lambda i, me: (me[0] ^ i, 0)),
        ],
        [piece] * (peers * chunks),
        [pl.BlockSpec(piece.shape, lambda i, me: (0, 0, 0))] * (peers * chunks),
        [], channels * width,
    )
    return [out[j * peers : (j + 1) * peers] for j in range(chunks)]


def by_track(me, head_weight, groups):
    channels, tracks = head_weight.shape
    half, own = channels // 2, tracks // groups

    def kernel(me_ref, weight_ref, out_ref):
        for group in range(groups):
            out_ref[group] = weight_ref[:, group * own : (group + 1) * own]

    out = shape((groups, half, own), head_weight.dtype)
    return call(
        kernel, "by_track", me, 1, [head_weight],
        [pl.BlockSpec((half, tracks), lambda i, me: (me[0] & 1, 0))],
        [out], [pl.BlockSpec(out.shape, lambda i, me: (0, 0, 0))], [], half * tracks,
    )[0]


def weight_pair(weight_ref, seats, pencil):
    groups, _, own = weight_ref.shape
    rows = weight_ref[...].reshape(groups, seats, pencil // (2 * ROWS), 2, ROWS, own)
    count = groups * seats * pencil // 2
    return rows[:, :, :, 0].reshape(count, own), rows[:, :, :, 1].reshape(count, own)


def head_rates(me, got, mine, other, bias, counts):
    groups, peers, half_rows, _ = got.shape
    own = mine.shape[2]
    seats = peers // 2
    pencil = 2 * half_rows
    bins = LANES // 2
    f32 = jnp.float32

    def kernel(me_ref, got_ref, mine_ref, other_ref, bias_ref, counts_ref, logits_ref, sums_ref):
        odd = me_ref[0] & 1
        total = jnp.broadcast_to(bias_ref[...], (bins, own))
        for weight_ref, place in ((mine_ref, odd), (other_ref, 1 - odd)):
            block = got_ref[:, pl.ds(place * seats, seats)].reshape(groups * seats * half_rows, LANES)
            turned = block.astype(f32).T.astype(jnp.bfloat16)
            left, right = weight_pair(weight_ref, seats, pencil)
            total = total + dot(turned[:bins], left) + dot(turned[bins:], right)
        logits_ref[...] = total
        rates = jax.nn.softplus(total) + rate_floor
        observed = counts_ref[...].astype(f32)
        sums_ref[0:1, :] = jnp.sum(rates, axis=0, keepdims=True)
        sums_ref[1:2, :] = jnp.sum(observed, axis=0, keepdims=True)
        sums_ref[2:3, :] = jnp.sum(observed * jnp.log(rates), axis=0, keepdims=True)
        sums_ref[3:8, :] = jnp.zeros((5, own), f32)

    inputs = [got, mine, other, bias, counts]
    return call(
        kernel, "head_rates", me, 1, inputs, [whole(x) for x in inputs],
        [shape((bins, own), f32), shape((8, own), f32)],
        [pl.BlockSpec((bins, own), lambda i, me: (0, 0)), pl.BlockSpec((8, own), lambda i, me: (0, 0))],
        [], 2 * bins * groups * peers * pencil * own,
    )


def head_grads(me, logits, sums, mine, other, counts, peers):
    groups, half, own = mine.shape
    seats = peers // 2
    pencil = half // seats
    bins = LANES // 2
    f32, bf16 = jnp.float32, jnp.bfloat16

    def kernel(me_ref, logits_ref, sums_ref, mine_ref, other_ref, counts_ref, out_ref, loss_ref):
        odd = me_ref[0] & 1
        totals = sums_ref[0]
        for seat in range(1, peers):
            totals = totals + sums_ref[seat]
        pred_total, obs_total, log_sum = totals[0:1], totals[1:2], totals[2:3]
        log_pred = jnp.log(pred_total)
        terms = total_weight * (pred_total - obs_total * log_pred) + obs_total * log_pred - log_sum
        loss_ref[...] = jnp.broadcast_to(jnp.sum(terms, axis=1, keepdims=True), loss_ref.shape)
        ratio = obs_total / pred_total
        logits_here = logits_ref[...]
        rates = jax.nn.softplus(logits_here) + rate_floor
        observed = counts_ref[...].astype(f32)
        grad_rates = total_weight * (1.0 - ratio) + ratio - observed / rates
        grads = (grad_rates * jax.nn.sigmoid(logits_here)).astype(bf16)
        none = jnp.zeros_like(grads)
        in_left = jnp.concatenate([grads, none], axis=0)
        in_right = jnp.concatenate([none, grads], axis=0)
        across = (((1,), (1,)), ((), ()))
        for weight_ref, place in ((mine_ref, odd), (other_ref, 1 - odd)):
            left, right = weight_pair(weight_ref, seats, pencil)
            part = lax.dot_general(left, in_left, across, preferred_element_type=f32)
            part = part + lax.dot_general(right, in_right, across, preferred_element_type=f32)
            out_ref[:, pl.ds(place * seats, seats)] = part.astype(bf16).reshape(groups, seats, pencil // 2, LANES)

    inputs = [logits, sums, mine, other, counts]
    out = shape((groups, peers, pencil // 2, LANES), bf16)
    return call(
        kernel, "head_grads", me, 1, inputs, [whole(x) for x in inputs],
        [out, shape((8, LANES), f32)],
        [pl.BlockSpec(out.shape, lambda i, me: (0, 0, 0, 0)), pl.BlockSpec((8, LANES), lambda i, me: (0, 0))],
        [], 4 * bins * groups * peers * pencil * own,
    )


def sum_grads(me, back):
    groups, peers, half_rows, _ = back.shape
    bins = LANES // 2
    f32 = jnp.float32

    def kernel(me_ref, back_ref, rows_ref, *refs):
        outs, total_ref = refs[:peers], refs[peers]
        for seat in range(peers):
            total = back_ref[0, seat].astype(f32)
            for group in range(1, groups):
                total = total + back_ref[group, seat].astype(f32)
            total_ref[seat] = total
            for i in range(half_rows // ROWS):
                pair = total[i * ROWS : (i + 1) * ROWS]
                lanes = slice(seat * bins, (seat + 1) * bins)
                rows_ref[2 * i * ROWS : (2 * i + 1) * ROWS, lanes] = pair[:, :bins]
                rows_ref[(2 * i + 1) * ROWS : (2 * i + 2) * ROWS, lanes] = pair[:, bins:]
        for k in range(peers):
            outs[k][...] = total_ref[me_ref[0] ^ k]

    packed = shape((half_rows, LANES), f32)
    out = call(
        kernel, "sum_grads", me, 1, [back], [whole(back)],
        [shape((2 * half_rows, peers * bins), f32)] + [packed] * peers,
        [pl.BlockSpec((2 * half_rows, peers * bins), lambda i, me: (0, 0))]
        + [pl.BlockSpec(packed.shape, lambda i, me: (0, 0))] * peers,
        [pltpu.VMEM((peers, half_rows, LANES), f32)], back.size,
    )
    return out[0], out[1:]


def finish(me, projections, mixed_home, grad_home, corr_home, spread, chunk, chunks, before):
    peers = len(mixed_home)
    _, channels, width = projections.shape
    pencil = channels // peers
    rows = pencil // chunks
    bins = width // POOL
    tiles = width // LANES
    each = LANES // POOL
    f32, bf16 = jnp.float32, jnp.bfloat16

    def kernel(me_ref, keyed_ref, valued_ref, spread_ref, *refs):
        mixed_refs, grad_refs, corr_refs = refs[:peers], refs[peers : 2 * peers], refs[2 * peers : 3 * peers]
        out_ref, lhs = refs[-2:]
        place = lax.broadcasted_iota(jnp.int32, (ROWS, LANES), 1) // each
        zero = jnp.zeros((ROWS, LANES), f32)
        for k in range(peers):

            @pl.when(pl.program_id(0) == k)
            def _():
                for i in range(rows // ROWS):
                    part = slice(i * ROWS, (i + 1) * ROWS)
                    source = (chunk * rows + i * ROWS) // (2 * ROWS) * ROWS
                    side = (chunk * rows // ROWS + i) % 2
                    pair = grad_refs[k][source : source + ROWS, :]
                    high = pair.astype(bf16).astype(f32)
                    low = pair - high
                    for t in range(tiles):
                        here = place == t + side * tiles
                        lhs[t * ROWS : (t + 1) * ROWS, :LANES] = jnp.where(here, high, zero).astype(bf16)
                        lhs[t * ROWS : (t + 1) * ROWS, LANES:] = jnp.where(here, low, zero).astype(bf16)
                    grad = dot(lhs[...], spread_ref[...])
                    for t in range(tiles):
                        lanes = slice(t * LANES, (t + 1) * LANES)
                        mixed = mixed_refs[k][part, lanes].astype(f32)
                        out_ref[0, part, lanes] = grad[t * ROWS : (t + 1) * ROWS] * mixed
                    corr = corr_refs[k][part, :].astype(f32)
                    out_ref[1, part, :] = corr * valued_ref[0, part, :].astype(f32)
                    out_ref[2, part, :] = corr * keyed_ref[0, part, :].astype(f32)

    inputs = [projections, projections, spread, *mixed_home, *grad_home, *corr_home]
    in_specs = [
        pl.BlockSpec((1, rows, width), lambda i, me: (1, (me[0] ^ i) * chunks + chunk, 0)),
        pl.BlockSpec((1, rows, width), lambda i, me: (2, (me[0] ^ i) * chunks + chunk, 0)),
        whole(spread),
    ]
    in_specs += [pl.BlockSpec((rows, width), lambda i, me: (chunk, 0))] * peers
    in_specs += [whole(x) for x in [*grad_home, *corr_home]]
    aliases = {}
    if before is not None:
        aliases = {1 + len(inputs): 0}
        inputs.append(before)
        in_specs.append(pl.BlockSpec(memory_space=pl.ANY))
    return call(
        kernel, "finish", me, peers, inputs, in_specs,
        [shape((3, channels, width), f32)],
        [pl.BlockSpec((3, rows, width), lambda i, me: (0, (me[0] ^ i) * chunks + chunk, 0))],
        [pltpu.VMEM((tiles * ROWS, 2 * LANES), bf16)], 4 * channels * width, aliases,
    )[0]


def swap(value, k, count):
    if k == 0:
        return value
    return lax.ppermute(value, "seq", [(i, i ^ k) for i in range(count)])


def pad_rows(value, rows):
    short = rows - value.shape[-2]
    if short == 0:
        return value
    widths = [(0, 0)] * value.ndim
    widths[-2] = (0, short)
    return jnp.pad(value, widths)


def aligned(projections, filter_taps, skip_gain, head_weight, head_bias, counts):
    f32 = jnp.float32
    _, channels, width = projections.shape
    peers = lax.axis_size("seq")
    groups = lax.axis_size("chan")
    seat = lax.axis_index("seq")
    group = lax.axis_index("chan")
    bins = width // POOL
    length = width * peers
    tracks = head_weight.shape[1]
    own_tracks = tracks // groups
    pencil = channels // peers
    chunks = CHUNKS
    rows = pencil // chunks
    me = jnp.asarray(seat, jnp.int32).reshape(1)
    tables = transform_tables(length)
    gather, spread = pool_tables()

    laid = lay_out(me, projections, filter_taps, peers, chunks)
    pieces = [[swap(laid[j][k], k, peers) for k in range(peers)] for j in range(chunks)]
    skip = lax.dynamic_index_in_dim(skip_gain.reshape(peers, pencil, 1), seat, axis=0, keepdims=False)

    me_late, _ = lax.optimization_barrier((me, laid[chunks - 1][0]))
    mine = by_track(me_late, head_weight, groups)
    mine = lax.all_to_all(mine, "chan", split_axis=0, concat_axis=0, tiled=True)
    other = swap(mine, 1, peers)

    mixed, specs = None, []
    for j in range(chunks):
        mixed, spec = convolve(me, pieces[j], skip, tables, pencil, j * rows, mixed)
        specs.append(spec)
        if j == 0:
            seat_late, _ = lax.optimization_barrier((seat, spec))
            query_blocks = projections[0].reshape(peers, pencil, width)
            queries = [
                swap(lax.dynamic_index_in_dim(query_blocks, seat_late ^ k, axis=0, keepdims=False), k, peers)
                for k in range(peers)
            ]
    mixed_out, sent = pool(me, queries, mixed, gather, groups)
    mixed_home = [swap(mixed_out[k], k, peers) for k in range(peers)]

    def exchange(blocks):
        flat = blocks.reshape(groups * peers, pencil // 2, LANES)
        flat = lax.all_to_all(flat, ("chan", "seq"), split_axis=0, concat_axis=0, tiled=True)
        return flat.reshape(blocks.shape)

    got = exchange(sent)
    own_bias = lax.dynamic_slice_in_dim(head_bias, group * own_tracks, own_tracks).reshape(1, own_tracks)
    own_counts = lax.dynamic_slice_in_dim(counts, group * own_tracks, own_tracks, axis=1)
    logits, sums = head_rates(me, got, mine, other, own_bias, own_counts)
    all_sums = lax.all_gather(sums, "seq")
    part, loss = head_grads(me, logits, all_sums, mine, other, own_counts, peers)
    back = exchange(part)
    step = 1
    while step < groups:
        loss = loss + lax.ppermute(loss, "chan", [(i, i ^ step) for i in range(groups)])
        step *= 2
    mean_loss = loss[0, 0] / (bins * peers * tracks)

    grad_rows, grad_out = sum_grads(me, back)
    grad_home = [swap(grad_out[k], k, peers) for k in range(peers)]
    grads = None
    corr_home = []
    for j in range(chunks):
        corr = correlate(me, queries, grad_rows, specs[j], skip, tables, spread, j * rows)
        corr_home.append([swap(corr[k], k, peers) for k in range(peers)])
    for j in range(chunks):
        grads = finish(me, projections, mixed_home, grad_home, corr_home[j], spread, j, chunks, grads)
    return mean_loss, grads


def power_of_two(value):
    return value & (value - 1) == 0


def per_device(projections, filter_taps, skip_gain, head_weight, head_bias, counts):
    channels, width = projections.shape[1:]
    peers, groups = lax.axis_size("seq"), lax.axis_size("chan")
    pencil = channels // peers
    fits = (
        pencil % (2 * ROWS * CHUNKS) == 0
        and 2 * (width // POOL) == LANES
        and power_of_two(peers)
        and peers > 1
        and power_of_two(groups)
        and groups <= MOST_GROUPS
    )
    run = aligned if fits else general
    return run(projections, filter_taps, skip_gain, head_weight, head_bias, counts)


def general(projections, filter_taps, skip_gain, head_weight, head_bias, counts):
    f32, bf16 = jnp.float32, jnp.bfloat16
    _, channels, width = projections.shape
    peers = lax.axis_size("seq")
    groups = lax.axis_size("chan")
    seat = lax.axis_index("seq")
    group = lax.axis_index("chan")
    bins = width // POOL
    length = width * peers
    tracks = head_weight.shape[1]
    own_tracks = tracks // groups
    pencil = channels // peers
    rows = -(-pencil // ROWS) * ROWS
    me = jnp.asarray(seat, jnp.int32).reshape(1)
    tables = transform_tables(length)
    gather, spread = pool_tables()

    def block(array, k):
        return lax.dynamic_index_in_dim(array, seat ^ k, axis=-3, keepdims=False)

    query = projections[0]
    key_value = projections[1].astype(f32) * projections[2].astype(f32)
    stacked = jnp.stack([key_value.astype(bf16), filter_taps.astype(bf16)])
    stacked = stacked.reshape(2, peers, pencil, width)
    pieces = [pad_rows(swap(block(stacked, k), k, peers), rows) for k in range(peers)]
    query_blocks = query.reshape(peers, pencil, width)
    queries = [pad_rows(swap(block(query_blocks, k), k, peers), rows) for k in range(peers)]
    skip = pad_rows(block(skip_gain.reshape(peers, pencil, 1), 0), rows)

    half = channels // 2
    by_track = head_weight.reshape(2, half, groups, own_tracks).transpose(0, 2, 1, 3)
    mine = lax.dynamic_index_in_dim(by_track, seat & 1, axis=0, keepdims=False)
    mine = lax.all_to_all(mine, "chan", split_axis=0, concat_axis=0, tiled=True)
    other = swap(mine, 1, peers)
    mine = mine.reshape(groups * half, own_tracks)
    other = other.reshape(groups * half, own_tracks)

    mixed, spec = convolve(me, pieces, skip, tables, rows, 0, None)
    mixed_out, pooled = pool(me, queries, mixed, gather, 0)
    pooled = pooled[:pencil]
    mixed_home = [swap(mixed_out[k][:pencil], k, peers) for k in range(peers)]

    sent = pooled.reshape(pencil, peers, bins).transpose(1, 0, 2)
    sent = jnp.broadcast_to(sent[None], (groups, peers, pencil, bins))
    got = lax.all_to_all(
        sent.reshape(groups * peers, pencil, bins), ("chan", "seq"), split_axis=0, concat_axis=0, tiled=True
    )
    got = got.reshape(groups, 2, half, bins)
    low_half = got[:, 0].reshape(groups * half, bins)
    high_half = got[:, 1].reshape(groups * half, bins)
    odd = (seat & 1) == 1
    pooled_mine = jnp.where(odd, high_half, low_half)
    pooled_other = jnp.where(odd, low_half, high_half)

    def project(x, w):
        return lax.dot_general(x, w, (((0,), (0,)), ((), ())), preferred_element_type=f32)

    own_bias = lax.dynamic_slice_in_dim(head_bias, group * own_tracks, own_tracks)
    own_counts = lax.dynamic_slice_in_dim(counts, group * own_tracks, own_tracks, axis=1)
    logits = project(pooled_mine, mine) + project(pooled_other, other) + own_bias[None, :]
    rates = jax.nn.softplus(logits) + rate_floor
    observed = own_counts.astype(f32)
    partial_sums = jnp.stack(
        [jnp.sum(rates, axis=0), jnp.sum(observed, axis=0), jnp.sum(observed * jnp.log(rates), axis=0)]
    )
    pred_total, obs_total, log_sum = jnp.sum(lax.all_gather(partial_sums, "seq"), axis=0)
    log_pred = jnp.log(pred_total)
    loss_part = jnp.sum(
        total_weight * (pred_total - obs_total * log_pred) + obs_total * log_pred - log_sum
    )
    mean_loss = lax.psum(loss_part, "chan") / (bins * peers * tracks)
    ratio = obs_total / pred_total
    grad_rates = total_weight * (1.0 - ratio)[None, :] + ratio[None, :] - observed / rates
    grad_logits = (grad_rates * jax.nn.sigmoid(logits)).astype(bf16)

    def spread_back(w):
        return lax.dot_general(w, grad_logits, (((1,), (1,)), ((), ())), preferred_element_type=f32)

    part_mine = spread_back(mine).astype(bf16).reshape(groups, 1, half, bins)
    part_other = spread_back(other).astype(bf16).reshape(groups, 1, half, bins)
    part = jnp.concatenate(
        [jnp.where(odd, part_other, part_mine), jnp.where(odd, part_mine, part_other)], axis=1
    )
    back = lax.all_to_all(
        part.reshape(groups * peers, pencil, bins), ("chan", "seq"), split_axis=0, concat_axis=0, tiled=True
    )
    grad_pooled = jnp.sum(back.reshape(groups, peers, pencil, bins).astype(f32), axis=0)
    grad_home = [swap(block(grad_pooled, k), k, peers) for k in range(peers)]
    grad_rows = pad_rows(grad_pooled.transpose(1, 0, 2).reshape(pencil, peers * bins), rows)

    corr_out = correlate(me, queries, grad_rows, spec, skip, tables, spread, 0)
    corr_home = [swap(corr_out[k][:pencil], k, peers) for k in range(peers)]

    def assemble(parts):
        out = jnp.zeros((peers,) + parts[0].shape, parts[0].dtype)
        for k, part in enumerate(parts):
            out = lax.dynamic_update_index_in_dim(out, part, seat ^ k, axis=0)
        return out.reshape((channels,) + parts[0].shape[1:])

    grad_output = jnp.repeat(assemble(grad_home) / POOL, POOL, axis=1)
    grad_kv = assemble(corr_home).astype(f32)
    grad_query = grad_output * assemble(mixed_home).astype(f32)
    grads = jnp.stack(
        [grad_query, grad_kv * projections[2].astype(f32), grad_kv * projections[1].astype(f32)], axis=0
    )
    return mean_loss, grads


def solution(mesh):
    placed = (
        P(None, "chan", "seq"),
        P("chan", "seq"),
        P("chan"),
        P("chan", None),
        P(),
        P("seq", None),
    )
    return jax.shard_map(
        per_device,
        mesh=mesh,
        in_specs=placed,
        out_specs=(P(), P(None, "chan", "seq")),
        check_vma=False,
    )
```

```python
import math

import jax
import jax.numpy as jnp
import ml_dtypes
import numpy as np
from jax import lax
from jax.experimental import pallas as pl
from jax.experimental.pallas import tpu as pltpu
from jax.sharding import PartitionSpec as P

POOL = 32
LANES = 128
ROWS = 16
SHIFT = 0.25

total_weight = 0.2
rate_floor = 0.5

MICROSECOND = 1.0e9

VMEM_LIMIT = 20 * 1024 * 1024
CHUNKS = 2
MOST_GROUPS = 16


def split_bf16(table):
    high = table.astype(ml_dtypes.bfloat16)
    low = (table - high.astype(np.float64)).astype(ml_dtypes.bfloat16)
    return high, low


def radices(outer):
    first = 1
    while first * first < outer:
        first *= 2
    return first, outer // first


def transform_tables(length):
    outer = length // LANES
    idx = np.arange(LANES)
    angle = 2.0 * np.pi * (np.outer(idx, idx) % LANES) / LANES
    wr, wi = np.cos(angle), -np.sin(angle)
    forward = np.block([[wr, wi], [-wi, wr]])
    backward = np.block([[wr, -wi], [wi, wr]]) / length
    k1 = np.arange(outer)[:, None]
    twist = 2.0 * np.pi * (k1 - SHIFT) * idx[None, :] / length
    f_hi, f_lo = split_bf16(forward)
    b_hi, b_lo = split_bf16(backward)
    return dict(
        fwd=np.stack([f_hi, f_lo]),
        bwd=np.stack([b_hi, b_lo]),
        twist=np.stack([np.cos(twist), -np.sin(twist)]).astype(np.float32),
    )


def pool_tables():
    per = LANES // POOL
    lane = np.arange(LANES)
    hit = (lane[:, None] // POOL) == (lane[None, :] % per)
    gather = np.concatenate([hit, hit], axis=0) / POOL
    spread = np.concatenate([hit.T, hit.T], axis=0) / POOL
    return gather.astype(ml_dtypes.bfloat16), spread.astype(ml_dtypes.bfloat16)


def times(value, angle):
    re, im = value
    c, s = math.cos(angle), math.sin(angle)
    tiny = 1e-12
    if im is None:
        if abs(s) < tiny and c > 0:
            return (re, None)
        return (re * c, re * s)
    if abs(s) < tiny:
        return (re, im) if c > 0 else (-re, -im)
    if abs(c) < tiny:
        return (-im, re) if s > 0 else (im, -re)
    return (re * c - im * s, re * s + im * c)


def add(a, b):
    if a[1] is None and b[1] is None:
        return (a[0] + b[0], None)
    if a[1] is None:
        return (a[0] + b[0], b[1])
    if b[1] is None:
        return (a[0] + b[0], a[1])
    return (a[0] + b[0], a[1] + b[1])


def sub(a, b):
    if a[1] is None and b[1] is None:
        return (a[0] - b[0], None)
    if a[1] is None:
        return (a[0] - b[0], -b[1])
    if b[1] is None:
        return (a[0] - b[0], a[1])
    return (a[0] - b[0], a[1] - b[1])


def small_dft(values, sign):
    count = len(values)
    if count == 1:
        return values
    even = small_dft(values[0::2], sign)
    odd = small_dft(values[1::2], sign)
    out = [None] * count
    half = count // 2
    for k in range(half):
        turned = times(odd[k], sign * 2.0 * math.pi * k / count)
        out[k] = add(even[k], turned)
        out[k + half] = sub(even[k], turned)
    return out


def dot(a, b):
    return jnp.dot(a, b, preferred_element_type=jnp.float32)


def split(value):
    high = value.astype(jnp.bfloat16)
    return high, (value - high.astype(jnp.float32)).astype(jnp.bfloat16)


def lane_transform(re_parts, im_parts, lhs, table_ref):
    for i, (re, im) in enumerate(zip(re_parts, im_parts)):
        rows = pl.ds(i * ROWS, ROWS)
        re_hi, re_lo = split(re)
        im_hi, im_lo = split(im)
        lhs[0, rows, :LANES] = re_hi
        lhs[0, rows, LANES:] = im_hi
        lhs[1, rows, :LANES] = re_lo
        lhs[1, rows, LANES:] = im_lo
    high = lhs[0]
    return dot(high, table_ref[0]) + (dot(lhs[1], table_ref[0]) + dot(high, table_ref[1]))


def first_pass(load, store, outer):
    ra, rb = radices(outer)
    for b in range(rb):
        values = [times((load(rb * a + b), None), 2.0 * math.pi * a * SHIFT / ra) for a in range(ra)]
        out = small_dft(values, -1)
        for alpha in range(ra):
            re, im = times(out[alpha], -2.0 * math.pi * b * (alpha - SHIFT) / outer)
            store(b, alpha, re, im)


def second_pass(parts, alpha, outer, twist_ref):
    ra, rb = radices(outer)
    values = [(parts[0, b, alpha], parts[1, b, alpha]) for b in range(rb)]
    out = small_dft(values, -1)
    res, ims = [], []
    for beta in range(rb):
        k1 = alpha + ra * beta
        tr = twist_ref[0, k1 : k1 + 1, :]
        ti = twist_ref[1, k1 : k1 + 1, :]
        re, im = out[beta]
        res.append(re * tr - im * ti)
        ims.append(re * ti + im * tr)
    return res, ims


def back_second_pass(spectrum, alpha, outer, twist_ref, store):
    ra, rb = radices(outer)
    values = []
    for beta in range(rb):
        k1 = alpha + ra * beta
        tr = twist_ref[0, k1 : k1 + 1, :]
        ti = twist_ref[1, k1 : k1 + 1, :]
        re = spectrum[beta * ROWS : (beta + 1) * ROWS, :LANES]
        im = spectrum[beta * ROWS : (beta + 1) * ROWS, LANES:]
        values.append((re * tr + im * ti, im * tr - re * ti))
    out = small_dft(values, +1)
    for b in range(rb):
        re, im = times(out[b], 2.0 * math.pi * b * (alpha - SHIFT) / outer)
        store(b, alpha, re, im)


def back_first_pass(parts, outer, emit):
    ra, rb = radices(outer)
    for b in range(rb):
        values = [(parts[0, b, alpha], parts[1, b, alpha]) for alpha in range(ra)]
        out = small_dft(values, +1)
        for a in range(ra):
            angle = -2.0 * math.pi * a * SHIFT / ra
            re, im = out[a]
            c, s = math.cos(angle), math.sin(angle)
            emit(rb * a + b, re if a == 0 else re * c - im * s)


def keep(parts):
    def store(b, alpha, re, im):
        parts[0, b, alpha] = re
        parts[1, b, alpha] = im

    return store


def conv_kernel(peers, outer, me_ref, *refs):
    pieces = refs[:peers]
    skip_ref, fwd_ref, bwd_ref, twist_ref = refs[peers : peers + 4]
    mixed_ref, spec_ref, rows_in, parts_x, parts_h, parts_y, lhs = refs[-7:]
    me = me_ref[0]
    ra, rb = radices(outer)
    per = outer // peers
    for k in range(peers):
        rows_in[me ^ k] = pieces[k][...]

    def loader(which):
        def load(n1):
            lanes = slice((n1 % per) * LANES, (n1 % per + 1) * LANES)
            return rows_in[n1 // per, which, :, lanes].astype(jnp.float32)

        return load

    load_x = loader(0)
    first_pass(load_x, keep(parts_x), outer)
    first_pass(loader(1), keep(parts_h), outer)
    chunk = rb * ROWS
    for alpha in range(ra):
        x = lane_transform(*second_pass(parts_x, alpha, outer, twist_ref), lhs.at[3 * alpha], fwd_ref)
        h = lane_transform(*second_pass(parts_h, alpha, outer, twist_ref), lhs.at[3 * alpha + 1], fwd_ref)
        spec_ref[0, alpha * chunk : (alpha + 1) * chunk, :] = h
        xr, xi, hr, hi = x[:, :LANES], x[:, LANES:], h[:, :LANES], h[:, LANES:]
        pr = xr * hr - xi * hi
        pi = xr * hi + xi * hr
        rows = [slice(i * ROWS, (i + 1) * ROWS) for i in range(rb)]
        y = lane_transform([pr[r] for r in rows], [pi[r] for r in rows], lhs.at[3 * alpha + 2], bwd_ref)
        back_second_pass(y, alpha, outer, twist_ref, keep(parts_y))
    skip = jnp.broadcast_to(skip_ref[...], (ROWS, LANES))

    def emit(n1, value):
        mixed_ref[:, n1 * LANES : (n1 + 1) * LANES] = value + skip * load_x(n1)

    back_first_pass(parts_y, outer, emit)


def pool_rows(rows_in, mixed_ref, rows_out, row, gather_ref, lhs, per, outer):
    for n1 in range(outer):
        lanes = slice((n1 % per) * LANES, (n1 % per + 1) * LANES)
        query = rows_in[n1 // per, row : row + ROWS, lanes].astype(jnp.float32)
        mixed = mixed_ref[row : row + ROWS, n1 * LANES : (n1 + 1) * LANES]
        rows_out[n1 // per, row : row + ROWS, lanes] = mixed.astype(jnp.bfloat16)
        high, low = split(query * mixed)
        lhs[n1 * ROWS : (n1 + 1) * ROWS, :LANES] = high
        lhs[n1 * ROWS : (n1 + 1) * ROWS, LANES:] = low
    sums = dot(lhs[...], gather_ref[...])
    each = LANES // POOL
    held = LANES // each
    place = lax.broadcasted_iota(jnp.int32, (ROWS, LANES), 1) // each
    tiles = []
    for tile in range(-(-outer // held)):
        total = jnp.zeros((ROWS, LANES), jnp.float32)
        for j in range(min(held, outer - tile * held)):
            n1 = tile * held + j
            total = jnp.where(place == j, sums[n1 * ROWS : (n1 + 1) * ROWS], total)
        tiles.append(total)
    return jnp.concatenate(tiles, axis=1)


def pool_kernel(peers, outer, me_ref, *refs):
    queries = refs[:peers]
    mixed_ref, gather_ref = refs[peers : peers + 2]
    outs = refs[peers + 2 : 2 * peers + 2]
    pooled_ref, rows_in, rows_out, lhs = refs[2 * peers + 2 :]
    me = me_ref[0]
    per = outer // peers
    for k in range(peers):
        rows_in[me ^ k] = queries[k][...]
    rows = mixed_ref.shape[0]
    bins = outer * LANES // POOL
    if rows == ROWS:
        pooled = pool_rows(rows_in, mixed_ref, rows_out, 0, gather_ref, lhs.at[0], per, outer)
        pooled_ref[...] = pooled[:, :bins].astype(jnp.bfloat16)
    else:
        left = pool_rows(rows_in, mixed_ref, rows_out, 0, gather_ref, lhs.at[0], per, outer)
        right = pool_rows(rows_in, mixed_ref, rows_out, ROWS, gather_ref, lhs.at[1], per, outer)
        each = bins // peers
        for seat in range(peers):
            mine = slice(seat * each, (seat + 1) * each)
            pair = jnp.concatenate([left[:, mine], right[:, mine]], axis=1).astype(jnp.bfloat16)
            for group in range(pooled_ref.shape[0]):
                pooled_ref[group, seat] = pair
    for k in range(peers):
        outs[k][...] = rows_out[me ^ k]


def corr_kernel(peers, outer, me_ref, *refs):
    queries = refs[:peers]
    grad_ref, spec_ref, skip_ref, fwd_ref, bwd_ref, twist_ref, spread_ref = refs[peers : peers + 7]
    outs = refs[peers + 7 : 2 * peers + 7]
    rows_in, lhs_g, gated, parts_g, parts_y, lhs, rows_out = refs[2 * peers + 7 :]
    me = me_ref[0]
    ra, rb = radices(outer)
    per = outer // peers
    for k in range(peers):
        rows_in[me ^ k] = queries[k][...]
    each = LANES // POOL
    held = LANES // each
    place = lax.broadcasted_iota(jnp.int32, (ROWS, LANES), 1) // each
    zero = jnp.zeros((ROWS, LANES), jnp.float32)
    for tile in range(-(-outer // held)):
        count = min(held, outer - tile * held)
        used = count * each
        part = grad_ref[:, tile * LANES : tile * LANES + used]
        if used < LANES:
            part = jnp.concatenate([part, jnp.zeros((ROWS, LANES - used), jnp.float32)], axis=1)
        high = part.astype(jnp.bfloat16).astype(jnp.float32)
        low = part - high
        for j in range(count):
            rows = pl.ds((tile * held + j) * ROWS, ROWS)
            lhs_g[rows, :LANES] = jnp.where(place == j, high, zero).astype(jnp.bfloat16)
            lhs_g[rows, LANES:] = jnp.where(place == j, low, zero).astype(jnp.bfloat16)
    gated[...] = dot(lhs_g[...], spread_ref[...])
    for n1 in range(outer):
        lanes = slice((n1 % per) * LANES, (n1 % per + 1) * LANES)
        rows = pl.ds(n1 * ROWS, ROWS)
        gated[rows, :] = gated[rows, :] * rows_in[n1 // per, :, lanes].astype(jnp.float32)

    def load_g(n1):
        return gated[n1 * ROWS : (n1 + 1) * ROWS, :]

    first_pass(load_g, keep(parts_g), outer)
    chunk = rb * ROWS
    for alpha in range(ra):
        g = lane_transform(*second_pass(parts_g, alpha, outer, twist_ref), lhs.at[2 * alpha], fwd_ref)
        h = spec_ref[0, alpha * chunk : (alpha + 1) * chunk, :]
        gr, gi, hr, hi = g[:, :LANES], g[:, LANES:], h[:, :LANES], h[:, LANES:]
        pr = gr * hr + gi * hi
        pi = gi * hr - gr * hi
        rows = [slice(i * ROWS, (i + 1) * ROWS) for i in range(rb)]
        y = lane_transform([pr[r] for r in rows], [pi[r] for r in rows], lhs.at[2 * alpha + 1], bwd_ref)
        back_second_pass(y, alpha, outer, twist_ref, keep(parts_y))
    skip = jnp.broadcast_to(skip_ref[...], (ROWS, LANES))

    def emit(n1, value):
        lanes = slice((n1 % per) * LANES, (n1 % per + 1) * LANES)
        rows_out[n1 // per, :, lanes] = (value + skip * load_g(n1)).astype(jnp.bfloat16)

    back_first_pass(parts_y, outer, emit)
    for k in range(peers):
        outs[k][...] = rows_out[me ^ k]


def whole(array):
    rank = array.ndim
    return pl.BlockSpec(array.shape, lambda i, me: (0,) * rank)


def by_rows(width, rows=ROWS, start=0):
    return pl.BlockSpec((rows, width), lambda i, me: (start + i, 0))


def call(kernel, name, me, steps, inputs, in_specs, out_shapes, out_specs, scratch, flops, aliases=None, near=(), vmem=()):
    moved = sum(x.size * x.dtype.itemsize for x in inputs)
    moved += sum(math.prod(o.shape) * o.dtype.itemsize for o in out_shapes)
    def space(i):
        return pltpu.VMEM if i in vmem else pltpu.HBM

    count = len(inputs)
    inputs = [x if i in near else pltpu.with_memory_space_constraint(x, space(i)) for i, x in enumerate(inputs)]
    out_shapes = [
        o if count + i in near else space(count + i)(o.shape, o.dtype) for i, o in enumerate(out_shapes)
    ]
    return pl.pallas_call(
        kernel,
        name=name,
        grid_spec=pltpu.PrefetchScalarGridSpec(
            num_scalar_prefetch=1,
            grid=(steps,),
            in_specs=in_specs,
            out_specs=out_specs,
            scratch_shapes=scratch,
        ),
        out_shape=out_shapes,
        input_output_aliases=aliases or {},
        compiler_params=pltpu.CompilerParams(
            dimension_semantics=("arbitrary",), vmem_limit_bytes=VMEM_LIMIT
        ),
        cost_estimate=pl.CostEstimate(flops=int(flops), bytes_accessed=moved, transcendentals=0),
    )(me, *inputs)


def shape(dims, dtype):
    return jax.ShapeDtypeStruct(dims, dtype)


def convolve(me, pieces, skip, tables, total_rows, start, before):
    peers = len(pieces)
    rows, width = pieces[0].shape[1:]
    length = width * peers
    outer = length // LANES
    ra, rb = radices(outer)
    chunk = rb * ROWS
    steps = rows // ROWS
    first = start // ROWS
    f32, bf16 = jnp.float32, jnp.bfloat16
    fwd, bwd, twist = tables["fwd"], tables["bwd"], tables["twist"]
    inputs = [*pieces, skip, fwd, bwd, twist]
    in_specs = [pl.BlockSpec((2, ROWS, width), lambda i, me: (0, i, 0))] * peers + [
        by_rows(1, start=first),
        whole(fwd),
        whole(bwd),
        whole(twist),
    ]
    aliases = {}
    if before is not None:
        aliases = {1 + len(inputs): 0}
        inputs.append(before)
        in_specs.append(pl.BlockSpec(memory_space=pl.ANY))
    parts = pltpu.VMEM((2, rb, ra, ROWS, LANES), f32)

    def kernel(*refs):
        conv_kernel(peers, outer, *refs)

    return call(
        kernel, "long_convolution", me, steps, inputs, in_specs,
        [shape((total_rows, length), f32), shape((steps, outer * ROWS, 2 * LANES), f32)],
        [by_rows(length, start=first), pl.BlockSpec((1, outer * ROWS, 2 * LANES), lambda i, me: (i, 0, 0))],
        [
            pltpu.VMEM((peers, 2, ROWS, width), bf16),
            parts,
            parts,
            parts,
            pltpu.VMEM((3 * ra, 2, chunk, 2 * LANES), bf16),
        ],
        rows * outer * 0.004 * MICROSECOND, aliases, (peers,), range(peers + 4, len(inputs) + 1),
    )


def pool(me, queries, mixed, gather, groups):
    peers = len(queries)
    rows, width = queries[0].shape
    length = width * peers
    outer = length // LANES
    bins = length // POOL
    bf16 = jnp.bfloat16
    if groups:
        step = 2 * ROWS
        pooled_shape = shape((groups, peers, rows // 2, LANES), bf16)
        pooled_spec = pl.BlockSpec((groups, peers, ROWS, LANES), lambda i, me: (0, 0, i, 0))
    else:
        step = ROWS
        pooled_shape = shape((rows, bins), bf16)
        pooled_spec = by_rows(bins)

    def kernel(*refs):
        pool_kernel(peers, outer, *refs)

    out = call(
        kernel, "pool_bins", me, rows // step, [*queries, mixed, gather],
        [by_rows(width, step)] * peers + [by_rows(length, step), whole(gather)],
        [shape((rows, width), bf16)] * peers + [pooled_shape],
        [by_rows(width, step)] * peers + [pooled_spec],
        [
            pltpu.VMEM((peers, step, width), bf16),
            pltpu.VMEM((peers, step, width), bf16),
            pltpu.VMEM((step // ROWS, outer * ROWS, 2 * LANES), bf16),
        ],
        rows * outer * 0.001 * MICROSECOND, vmem=(peers,),
    )
    return out[:peers], out[peers]


def correlate(me, queries, grad_pooled, spec, skip, tables, spread, start):
    peers = len(queries)
    width = queries[0].shape[1]
    rows = spec.shape[0] * ROWS
    length = width * peers
    outer = length // LANES
    bins = length // POOL
    ra, rb = radices(outer)
    chunk = rb * ROWS
    first = start // ROWS
    f32, bf16 = jnp.float32, jnp.bfloat16
    fwd, bwd, twist = tables["fwd"], tables["bwd"], tables["twist"]
    in_specs = [by_rows(width, start=first)] * peers + [
        by_rows(bins, start=first),
        pl.BlockSpec((1, outer * ROWS, 2 * LANES), lambda i, me: (i, 0, 0)),
        by_rows(1, start=first),
        whole(fwd),
        whole(bwd),
        whole(twist),
        whole(spread),
    ]
    parts = pltpu.VMEM((2, rb, ra, ROWS, LANES), f32)
    scratch = [
        pltpu.VMEM((peers, ROWS, width), bf16),
        pltpu.VMEM((outer * ROWS, 2 * LANES), bf16),
        pltpu.VMEM((outer * ROWS, LANES), f32),
        parts,
        parts,
        pltpu.VMEM((2 * ra, 2, chunk, 2 * LANES), bf16),
        pltpu.VMEM((peers, ROWS, width), bf16),
    ]

    def kernel(*refs):
        corr_kernel(peers, outer, *refs)

    return call(
        kernel, "long_correlation", me, rows // ROWS,
        [*queries, grad_pooled, spec, skip, fwd, bwd, twist, spread], in_specs,
        [shape((rows, width), bf16)] * peers, [by_rows(width)] * peers,
        scratch, rows * outer * 0.004 * MICROSECOND, near=(peers, peers + 2),
    )


def lay_out(me, projections, filter_taps, peers, chunk, chunks):
    last = chunk == chunks - 1
    _, channels, width = projections.shape
    pencil = channels // peers
    rows = pencil // chunks
    f32, bf16 = jnp.float32, jnp.bfloat16
    order = list(range(peers))[::-1]

    def kernel(me_ref, proj_ref, taps_ref, *refs):
        outs = refs[:peers]
        queries = refs[peers:-7]
        pair, taps, laid, passing, sems, out_sems, query_sems = refs[-7:]

        def take(k):
            block = pl.ds(pl.multiple_of((me_ref[0] ^ k) * pencil, pencil), pencil)
            return pltpu.make_async_copy(proj_ref.at[0, block], passing.at[k], query_sems.at[k, 0])

        def hand_on(k):
            return pltpu.make_async_copy(passing.at[k], queries[k], query_sems.at[k, 1])


        def fetch(k):
            here = pl.ds(pl.multiple_of((me_ref[0] ^ k) * pencil + chunk * rows, rows), rows)
            return (
                pltpu.make_async_copy(proj_ref.at[1, here], pair.at[k, 0], sems.at[k, 0]),
                pltpu.make_async_copy(proj_ref.at[2, here], pair.at[k, 1], sems.at[k, 1]),
                pltpu.make_async_copy(taps_ref.at[here], taps.at[k], sems.at[k, 2]),
            )

        def leave(k):
            return pltpu.make_async_copy(laid.at[k], outs[k], out_sems.at[k])

        for k in order:
            for copy in fetch(k):
                copy.start()
        for k in range(len(queries)):
            take(k).start()
        for k in order:
            keyed, valued, lags = fetch(k)
            keyed.wait()
            valued.wait()
            laid[k, 0] = (pair[k, 0].astype(f32) * pair[k, 1].astype(f32)).astype(bf16)
            lags.wait()
            laid[k, 1] = taps[k].astype(bf16)
            leave(k).start()
        for k in range(len(queries)):
            take(k).wait()
            hand_on(k).start()
        for k in order:
            leave(k).wait()
        for k in range(len(queries)):
            hand_on(k).wait()

    out_shapes = [shape((2, rows, width), bf16)] * peers
    if last:
        out_shapes += [shape((pencil, width), bf16)] * peers
    return call(
        kernel, "lay_out", me, 1, [projections, filter_taps],
        [pl.BlockSpec(memory_space=pltpu.HBM)] * 2,
        out_shapes,
        [pl.BlockSpec(memory_space=pltpu.HBM)] * len(out_shapes),
        [
            pltpu.VMEM((peers, 2, rows, width), bf16),
            pltpu.VMEM((peers, rows, width), f32),
            pltpu.VMEM((peers, 2, rows, width), bf16),
            pltpu.VMEM((peers, pencil, width), bf16),
            pltpu.SemaphoreType.DMA((peers, 3)),
            pltpu.SemaphoreType.DMA((peers,)),
            pltpu.SemaphoreType.DMA((peers, 2)),
        ],
        rows * peers * 0.015 * MICROSECOND,
    )


def by_track(me, head_weight, groups):
    channels, tracks = head_weight.shape
    half, own = channels // 2, tracks // groups
    padded = -(-own // LANES) * LANES
    rows = 2 * ROWS

    def kernel(me_ref, weight_ref, out_ref):
        for group in range(groups):
            out_ref[group, :, :own] = weight_ref[:, group * own : (group + 1) * own]
            if padded > own:
                out_ref[group, :, own:] = jnp.zeros((rows, padded - own), head_weight.dtype)

    out = shape((groups, half, padded), head_weight.dtype)
    steps = half // rows
    return call(
        kernel, "by_track", me, steps, [head_weight],
        [pl.BlockSpec((rows, tracks), lambda i, me: ((me[0] & 1) * steps + i, 0))],
        [out], [pl.BlockSpec((groups, rows, padded), lambda i, me: (0, i, 0))], [], 2 * MICROSECOND,
    )[0]


def weight_pair(weight_ref, seats, pencil, own):
    groups, _, padded = weight_ref.shape
    rows = weight_ref[...].reshape(groups, seats, pencil // (2 * ROWS), 2, ROWS, padded)
    count = groups * seats * pencil // 2
    left, right = rows[:, :, :, 0].reshape(count, padded), rows[:, :, :, 1].reshape(count, padded)
    return left[:, :own], right[:, :own]


def head_rates(me, got, mine, other, bias, counts):
    groups, peers, half_rows, _ = got.shape
    own = counts.shape[1]
    seats = peers // 2
    pencil = 2 * half_rows
    bins = LANES // 2
    f32 = jnp.float32

    def kernel(me_ref, got_ref, mine_ref, other_ref, bias_ref, counts_ref, logits_ref, sums_ref):
        odd = me_ref[0] & 1
        total = jnp.broadcast_to(bias_ref[...], (bins, own))
        for weight_ref, place in ((mine_ref, odd), (other_ref, 1 - odd)):
            block = got_ref[:, pl.ds(place * seats, seats)].reshape(groups * seats * half_rows, LANES)
            turned = block.astype(f32).T.astype(jnp.bfloat16)
            left, right = weight_pair(weight_ref, seats, pencil, own)
            total = total + dot(turned[:bins], left) + dot(turned[bins:], right)
        logits_ref[...] = total
        rates = jax.nn.softplus(total) + rate_floor
        observed = counts_ref[...].astype(f32)
        sums_ref[0:1, :] = jnp.sum(rates, axis=0, keepdims=True)
        sums_ref[1:2, :] = jnp.sum(observed, axis=0, keepdims=True)
        sums_ref[2:3, :] = jnp.sum(observed * jnp.log(rates), axis=0, keepdims=True)
        sums_ref[3:8, :] = jnp.zeros((5, own), f32)

    inputs = [got, mine, other, bias, counts]
    return call(
        kernel, "head_rates", me, 1, inputs, [whole(x) for x in inputs],
        [shape((bins, own), f32), shape((8, own), f32)],
        [pl.BlockSpec((bins, own), lambda i, me: (0, 0)), pl.BlockSpec((8, own), lambda i, me: (0, 0))],
        [], 2 * bins * groups * peers * pencil * own, near=range(7),
    )


def head_grads(me, logits, sums, mine, other, counts, peers):
    groups, half, _ = mine.shape
    own = counts.shape[1]
    seats = peers // 2
    pencil = half // seats
    bins = LANES // 2
    f32, bf16 = jnp.float32, jnp.bfloat16

    def kernel(me_ref, logits_ref, sums_ref, mine_ref, other_ref, counts_ref, out_ref, loss_ref):
        odd = me_ref[0] & 1
        totals = sums_ref[0]
        for seat in range(1, peers):
            totals = totals + sums_ref[seat]
        pred_total, obs_total, log_sum = totals[0:1], totals[1:2], totals[2:3]
        log_pred = jnp.log(pred_total)
        terms = total_weight * (pred_total - obs_total * log_pred) + obs_total * log_pred - log_sum
        loss_ref[...] = jnp.broadcast_to(jnp.sum(terms, axis=1, keepdims=True), loss_ref.shape)
        ratio = obs_total / pred_total
        logits_here = logits_ref[...]
        rates = jax.nn.softplus(logits_here) + rate_floor
        observed = counts_ref[...].astype(f32)
        grad_rates = total_weight * (1.0 - ratio) + ratio - observed / rates
        grads = (grad_rates * jax.nn.sigmoid(logits_here)).astype(bf16)
        none = jnp.zeros_like(grads)
        in_left = jnp.concatenate([grads, none], axis=0)
        in_right = jnp.concatenate([none, grads], axis=0)
        across = (((1,), (1,)), ((), ()))
        for weight_ref, place in ((mine_ref, odd), (other_ref, 1 - odd)):
            left, right = weight_pair(weight_ref, seats, pencil, own)
            part = lax.dot_general(left, in_left, across, preferred_element_type=f32)
            part = part + lax.dot_general(right, in_right, across, preferred_element_type=f32)
            out_ref[:, pl.ds(place * seats, seats)] = part.astype(bf16).reshape(groups, seats, pencil // 2, LANES)

    inputs = [logits, sums, mine, other, counts]
    out = shape((groups, peers, pencil // 2, LANES), bf16)
    return call(
        kernel, "head_grads", me, 1, inputs, [whole(x) for x in inputs],
        [out, shape((8, LANES), f32)],
        [pl.BlockSpec(out.shape, lambda i, me: (0, 0, 0, 0)), pl.BlockSpec((8, LANES), lambda i, me: (0, 0))],
        [], 4 * bins * groups * peers * pencil * own, near=(0, 1, 2, 3, 4, 6),
    )


def sum_grads(me, back):
    groups, peers, half_rows, _ = back.shape
    bins = LANES // 2
    f32 = jnp.float32

    def kernel(me_ref, back_ref, rows_ref, *refs):
        outs, total_ref = refs[:peers], refs[peers]
        for seat in range(peers):
            total = back_ref[0, seat].astype(f32)
            for group in range(1, groups):
                total = total + back_ref[group, seat].astype(f32)
            total_ref[seat] = total
            for i in range(half_rows // ROWS):
                pair = total[i * ROWS : (i + 1) * ROWS]
                lanes = slice(seat * bins, (seat + 1) * bins)
                rows_ref[2 * i * ROWS : (2 * i + 1) * ROWS, lanes] = pair[:, :bins]
                rows_ref[(2 * i + 1) * ROWS : (2 * i + 2) * ROWS, lanes] = pair[:, bins:]
        for k in range(peers):
            outs[k][...] = total_ref[me_ref[0] ^ k]

    packed = shape((half_rows, LANES), f32)
    out = call(
        kernel, "sum_grads", me, 1, [back], [whole(back)],
        [shape((2 * half_rows, peers * bins), f32)] + [packed] * peers,
        [pl.BlockSpec((2 * half_rows, peers * bins), lambda i, me: (0, 0))]
        + [pl.BlockSpec(packed.shape, lambda i, me: (0, 0))] * peers,
        [pltpu.VMEM((peers, half_rows, LANES), f32)], back.size, near=(0, 1),
    )
    return out[0], out[1:]


def finish(me, projections, mixed_home, grad_home, corr_home, spread, chunk, chunks, before):
    peers = len(mixed_home)
    _, channels, width = projections.shape
    pencil = channels // peers
    rows = pencil // chunks
    tiles = width // LANES
    each = LANES // POOL
    f32, bf16 = jnp.float32, jnp.bfloat16

    def kernel(me_ref, spread_ref, proj_ref, *refs):
        grad_refs, mixed_refs, corr_refs = refs[:peers], refs[peers : 2 * peers], refs[2 * peers : 3 * peers]
        out_ref, pair, far, done, lhs, sems, out_sems = refs[-7:]
        place = lax.broadcasted_iota(jnp.int32, (ROWS, LANES), 1) // each
        zero = jnp.zeros((ROWS, LANES), f32)

        def here(k):
            return pl.ds(pl.multiple_of((me_ref[0] ^ k) * pencil + chunk * rows, rows), rows)

        def fetch(k):
            return (
                pltpu.make_async_copy(mixed_refs[k].at[pl.ds(chunk * rows, rows)], far.at[k, 0], sems.at[k, 0]),
                pltpu.make_async_copy(corr_refs[k], far.at[k, 1], sems.at[k, 1]),
                pltpu.make_async_copy(proj_ref.at[1, here(k)], pair.at[k, 0], sems.at[k, 2]),
                pltpu.make_async_copy(proj_ref.at[2, here(k)], pair.at[k, 1], sems.at[k, 3]),
            )

        def leave(k, plane):
            return pltpu.make_async_copy(done.at[k, plane], out_ref.at[plane, here(k)], out_sems.at[k, plane])

        for k in range(peers):
            for copy in fetch(k):
                copy.start()
        for k in range(peers):
            mixed_copy, corr_copy, keyed_copy, valued_copy = fetch(k)
            corr_copy.wait()
            keyed_copy.wait()
            valued_copy.wait()
            corr = far[k, 1].astype(f32)
            done[k, 1] = corr * pair[k, 1].astype(f32)
            leave(k, 1).start()
            done[k, 2] = corr * pair[k, 0].astype(f32)
            leave(k, 2).start()
            mixed_copy.wait()
            for i in range(rows // ROWS):
                part = slice(i * ROWS, (i + 1) * ROWS)
                source = (chunk * rows + i * ROWS) // (2 * ROWS) * ROWS
                side = (chunk * rows // ROWS + i) % 2
                grads = grad_refs[k][source : source + ROWS, :]
                high = grads.astype(bf16).astype(f32)
                low = grads - high
                for t in range(tiles):
                    near = place == t + side * tiles
                    lhs[i, t * ROWS : (t + 1) * ROWS, :LANES] = jnp.where(near, high, zero).astype(bf16)
                    lhs[i, t * ROWS : (t + 1) * ROWS, LANES:] = jnp.where(near, low, zero).astype(bf16)
                grad = dot(lhs[i], spread_ref[...])
                for t in range(tiles):
                    lanes = slice(t * LANES, (t + 1) * LANES)
                    done[k, 0, part, lanes] = grad[t * ROWS : (t + 1) * ROWS] * far[k, 0, part, lanes].astype(f32)
            leave(k, 0).start()
        for k in range(peers):
            for plane in range(3):
                leave(k, plane).wait()

    inputs = [spread, projections, *grad_home, *mixed_home, *corr_home]
    in_specs = [whole(spread), pl.BlockSpec(memory_space=pltpu.HBM)]
    in_specs += [whole(x) for x in grad_home]
    in_specs += [pl.BlockSpec(memory_space=pl.ANY)] * (2 * peers)
    aliases = {}
    if before is not None:
        aliases = {1 + len(inputs): 0}
        inputs.append(before)
        in_specs.append(pl.BlockSpec(memory_space=pl.ANY))
    return call(
        kernel, "finish", me, 1, inputs, in_specs,
        [shape((3, channels, width), f32)], [pl.BlockSpec(memory_space=pltpu.HBM)],
        [
            pltpu.VMEM((peers, 2, rows, width), bf16),
            pltpu.VMEM((peers, 2, rows, width), bf16),
            pltpu.VMEM((peers, 3, rows, width), f32),
            pltpu.VMEM((rows // ROWS, tiles * ROWS, 2 * LANES), bf16),
            pltpu.SemaphoreType.DMA((peers, 4)),
            pltpu.SemaphoreType.DMA((peers, 3)),
        ],
        rows * peers * 0.03 * MICROSECOND, aliases, near=(0, *range(2, 2 + 3 * peers)),
    )[0]


def swap(value, k, count):
    if k == 0:
        return value
    return lax.ppermute(value, "seq", [(i, i ^ k) for i in range(count)])


def pad_rows(value, rows):
    short = rows - value.shape[-2]
    if short == 0:
        return value
    widths = [(0, 0)] * value.ndim
    widths[-2] = (0, short)
    return jnp.pad(value, widths)


def aligned(projections, filter_taps, skip_gain, head_weight, head_bias, counts):
    f32 = jnp.float32
    _, channels, width = projections.shape
    peers = lax.axis_size("seq")
    groups = lax.axis_size("chan")
    seat = lax.axis_index("seq")
    group = lax.axis_index("chan")
    bins = width // POOL
    length = width * peers
    tracks = head_weight.shape[1]
    own_tracks = tracks // groups
    pencil = channels // peers
    chunks = CHUNKS
    rows = pencil // chunks
    me = jnp.asarray(seat, jnp.int32).reshape(1)
    tables = transform_tables(length)
    gather, spread = pool_tables()

    laid, me_next = [], me
    for j in range(chunks):
        laid.append(lay_out(me_next, projections, filter_taps, peers, j, chunks))
        me_next, _ = lax.optimization_barrier((me, laid[j]))
    pieces = [[swap(laid[j][k], k, peers) for k in range(peers)] for j in range(chunks)]
    skip = lax.dynamic_index_in_dim(skip_gain.reshape(peers, pencil, 1), seat, axis=0, keepdims=False)

    mine = by_track(me_next, head_weight, groups)
    mine = lax.all_to_all(mine, "chan", split_axis=0, concat_axis=0, tiled=True)

    mixed, specs = None, []
    for j in range(chunks):
        mixed, spec = convolve(me, pieces[j], skip, tables, pencil, j * rows, mixed)
        specs.append(spec)
        if j == 0:
            queries, _ = lax.optimization_barrier((laid[-1][peers:], pieces[0]))
            queries = [swap(queries[k], k, peers) for k in range(peers)]
    mixed_out, sent = pool(me, queries, mixed, gather, groups)
    mixed_home = [swap(mixed_out[k], k, peers) for k in range(peers)]

    def exchange(blocks):
        flat = blocks.reshape(groups * peers, pencil // 2, LANES)
        flat = lax.all_to_all(flat, ("chan", "seq"), split_axis=0, concat_axis=0, tiled=True)
        return flat.reshape(blocks.shape)

    got = exchange(sent)
    mine, _ = lax.optimization_barrier((mine, sent))
    other = swap(mine, 1, peers)
    own_bias = lax.dynamic_slice_in_dim(head_bias, group * own_tracks, own_tracks).reshape(1, own_tracks)
    own_counts = lax.dynamic_slice_in_dim(counts, group * own_tracks, own_tracks, axis=1)
    logits, sums = head_rates(me, got, mine, other, own_bias, own_counts)
    all_sums = lax.all_gather(sums, "seq")
    part, loss = head_grads(me, logits, all_sums, mine, other, own_counts, peers)
    back = exchange(part)
    step = 1
    while step < groups:
        loss = loss + lax.ppermute(loss, "chan", [(i, i ^ step) for i in range(groups)])
        step *= 2
    mean_loss = loss[0, 0] / (bins * peers * tracks)

    grad_rows, grad_out = sum_grads(me, back)
    grad_home = [swap(grad_out[k], k, peers) for k in range(peers)]
    grads = None
    corr_home = []
    for j in range(chunks):
        corr = correlate(me, queries, grad_rows, specs[j], skip, tables, spread, j * rows)
        corr_home.append([swap(corr[k], k, peers) for k in range(peers)])
    for j in range(chunks):
        grads = finish(me, projections, mixed_home, grad_home, corr_home[j], spread, j, chunks, grads)
    return mean_loss, grads


def power_of_two(value):
    return value & (value - 1) == 0


def per_device(projections, filter_taps, skip_gain, head_weight, head_bias, counts):
    channels, width = projections.shape[1:]
    peers, groups = lax.axis_size("seq"), lax.axis_size("chan")
    pencil = channels // peers
    fits = (
        pencil % (2 * ROWS * CHUNKS) == 0
        and 2 * (width // POOL) == LANES
        and power_of_two(peers)
        and peers > 1
        and power_of_two(groups)
        and groups <= MOST_GROUPS
    )
    run = aligned if fits else general
    return run(projections, filter_taps, skip_gain, head_weight, head_bias, counts)


def general(projections, filter_taps, skip_gain, head_weight, head_bias, counts):
    f32, bf16 = jnp.float32, jnp.bfloat16
    _, channels, width = projections.shape
    peers = lax.axis_size("seq")
    groups = lax.axis_size("chan")
    seat = lax.axis_index("seq")
    group = lax.axis_index("chan")
    bins = width // POOL
    length = width * peers
    tracks = head_weight.shape[1]
    own_tracks = tracks // groups
    pencil = channels // peers
    rows = -(-pencil // ROWS) * ROWS
    me = jnp.asarray(seat, jnp.int32).reshape(1)
    tables = transform_tables(length)
    gather, spread = pool_tables()

    def block(array, k):
        return lax.dynamic_index_in_dim(array, seat ^ k, axis=-3, keepdims=False)

    query = projections[0]
    key_value = projections[1].astype(f32) * projections[2].astype(f32)
    stacked = jnp.stack([key_value.astype(bf16), filter_taps.astype(bf16)])
    stacked = stacked.reshape(2, peers, pencil, width)
    pieces = [pad_rows(swap(block(stacked, k), k, peers), rows) for k in range(peers)]
    query_blocks = query.reshape(peers, pencil, width)
    queries = [pad_rows(swap(block(query_blocks, k), k, peers), rows) for k in range(peers)]
    skip = pad_rows(block(skip_gain.reshape(peers, pencil, 1), 0), rows)

    half = channels // 2
    by_track = head_weight.reshape(2, half, groups, own_tracks).transpose(0, 2, 1, 3)
    mine = lax.dynamic_index_in_dim(by_track, seat & 1, axis=0, keepdims=False)
    mine = lax.all_to_all(mine, "chan", split_axis=0, concat_axis=0, tiled=True)
    other = swap(mine, 1, peers)
    mine = mine.reshape(groups * half, own_tracks)
    other = other.reshape(groups * half, own_tracks)

    mixed, spec = convolve(me, pieces, skip, tables, rows, 0, None)
    mixed_out, pooled = pool(me, queries, mixed, gather, 0)
    pooled = pooled[:pencil]
    mixed_home = [swap(mixed_out[k][:pencil], k, peers) for k in range(peers)]

    sent = pooled.reshape(pencil, peers, bins).transpose(1, 0, 2)
    sent = jnp.broadcast_to(sent[None], (groups, peers, pencil, bins))
    got = lax.all_to_all(
        sent.reshape(groups * peers, pencil, bins), ("chan", "seq"), split_axis=0, concat_axis=0, tiled=True
    )
    got = got.reshape(groups, 2, half, bins)
    low_half = got[:, 0].reshape(groups * half, bins)
    high_half = got[:, 1].reshape(groups * half, bins)
    odd = (seat & 1) == 1
    pooled_mine = jnp.where(odd, high_half, low_half)
    pooled_other = jnp.where(odd, low_half, high_half)

    def project(x, w):
        return lax.dot_general(x, w, (((0,), (0,)), ((), ())), preferred_element_type=f32)

    own_bias = lax.dynamic_slice_in_dim(head_bias, group * own_tracks, own_tracks)
    own_counts = lax.dynamic_slice_in_dim(counts, group * own_tracks, own_tracks, axis=1)
    logits = project(pooled_mine, mine) + project(pooled_other, other) + own_bias[None, :]
    rates = jax.nn.softplus(logits) + rate_floor
    observed = own_counts.astype(f32)
    partial_sums = jnp.stack(
        [jnp.sum(rates, axis=0), jnp.sum(observed, axis=0), jnp.sum(observed * jnp.log(rates), axis=0)]
    )
    pred_total, obs_total, log_sum = jnp.sum(lax.all_gather(partial_sums, "seq"), axis=0)
    log_pred = jnp.log(pred_total)
    loss_part = jnp.sum(
        total_weight * (pred_total - obs_total * log_pred) + obs_total * log_pred - log_sum
    )
    mean_loss = lax.psum(loss_part, "chan") / (bins * peers * tracks)
    ratio = obs_total / pred_total
    grad_rates = total_weight * (1.0 - ratio)[None, :] + ratio[None, :] - observed / rates
    grad_logits = (grad_rates * jax.nn.sigmoid(logits)).astype(bf16)

    def spread_back(w):
        return lax.dot_general(w, grad_logits, (((1,), (1,)), ((), ())), preferred_element_type=f32)

    part_mine = spread_back(mine).astype(bf16).reshape(groups, 1, half, bins)
    part_other = spread_back(other).astype(bf16).reshape(groups, 1, half, bins)
    part = jnp.concatenate(
        [jnp.where(odd, part_other, part_mine), jnp.where(odd, part_mine, part_other)], axis=1
    )
    back = lax.all_to_all(
        part.reshape(groups * peers, pencil, bins), ("chan", "seq"), split_axis=0, concat_axis=0, tiled=True
    )
    grad_pooled = jnp.sum(back.reshape(groups, peers, pencil, bins).astype(f32), axis=0)
    grad_home = [swap(block(grad_pooled, k), k, peers) for k in range(peers)]
    grad_rows = pad_rows(grad_pooled.transpose(1, 0, 2).reshape(pencil, peers * bins), rows)

    corr_out = correlate(me, queries, grad_rows, spec, skip, tables, spread, 0)
    corr_home = [swap(corr_out[k][:pencil], k, peers) for k in range(peers)]

    def assemble(parts):
        out = jnp.zeros((peers,) + parts[0].shape, parts[0].dtype)
        for k, part in enumerate(parts):
            out = lax.dynamic_update_index_in_dim(out, part, seat ^ k, axis=0)
        return out.reshape((channels,) + parts[0].shape[1:])

    grad_output = jnp.repeat(assemble(grad_home) / POOL, POOL, axis=1)
    grad_kv = assemble(corr_home).astype(f32)
    grad_query = grad_output * assemble(mixed_home).astype(f32)
    grads = jnp.stack(
        [grad_query, grad_kv * projections[2].astype(f32), grad_kv * projections[1].astype(f32)], axis=0
    )
    return mean_loss, grads


def solution(mesh):
    placed = (
        P(None, "chan", "seq"),
        P("chan", "seq"),
        P("chan"),
        P("chan", None),
        P(),
        P("seq", None),
    )
    return jax.shard_map(
        per_device,
        mesh=mesh,
        in_specs=placed,
        out_specs=(P(), P(None, "chan", "seq")),
        check_vma=False,
    )
```

```python
import math

import jax
import jax.numpy as jnp
import ml_dtypes
import numpy as np
from jax import lax
from jax.experimental import pallas as pl
from jax.experimental.pallas import tpu as pltpu
from jax.sharding import PartitionSpec as P

POOL = 32
LANES = 128
ROWS = 16
SHIFT = 0.25

total_weight = 0.2
rate_floor = 0.5

MICROSECOND = 1.0e9

VMEM_LIMIT = 20 * 1024 * 1024
CHUNKS = 2
SPECTRA = 4
MOST_GROUPS = 16


def split_bf16(table):
    high = table.astype(ml_dtypes.bfloat16)
    low = (table - high.astype(np.float64)).astype(ml_dtypes.bfloat16)
    return high, low


def radices(outer):
    first = 1
    while first * first < outer:
        first *= 2
    return first, outer // first


def transform_tables(length):
    outer = length // LANES
    idx = np.arange(LANES)
    angle = 2.0 * np.pi * (np.outer(idx, idx) % LANES) / LANES
    wr, wi = np.cos(angle), -np.sin(angle)
    forward = np.block([[wr, wi], [-wi, wr]])
    backward = np.block([[wr, -wi], [wi, wr]]) / length
    k1 = np.arange(outer)[:, None]
    twist = 2.0 * np.pi * (k1 - SHIFT) * idx[None, :] / length
    f_hi, f_lo = split_bf16(forward)
    b_hi, b_lo = split_bf16(backward)
    return dict(
        fwd=[f_hi, f_lo],
        bwd=[b_hi, b_lo],
        twist=np.stack([np.cos(twist), -np.sin(twist)]).astype(np.float32),
    )


def pool_tables():
    per = LANES // POOL
    lane = np.arange(LANES)
    hit = (lane[:, None] // POOL) == (lane[None, :] % per)
    gather = np.concatenate([hit, hit], axis=0) / POOL
    spread = np.concatenate([hit.T, hit.T], axis=0) / POOL
    return gather.astype(ml_dtypes.bfloat16), spread.astype(ml_dtypes.bfloat16)


def times(value, angle):
    re, im = value
    c, s = math.cos(angle), math.sin(angle)
    tiny = 1e-12
    if im is None:
        if abs(s) < tiny and c > 0:
            return (re, None)
        return (re * c, re * s)
    if abs(s) < tiny:
        return (re, im) if c > 0 else (-re, -im)
    if abs(c) < tiny:
        return (-im, re) if s > 0 else (im, -re)
    return (re * c - im * s, re * s + im * c)


def add(a, b):
    if a[1] is None and b[1] is None:
        return (a[0] + b[0], None)
    if a[1] is None:
        return (a[0] + b[0], b[1])
    if b[1] is None:
        return (a[0] + b[0], a[1])
    return (a[0] + b[0], a[1] + b[1])


def sub(a, b):
    if a[1] is None and b[1] is None:
        return (a[0] - b[0], None)
    if a[1] is None:
        return (a[0] - b[0], -b[1])
    if b[1] is None:
        return (a[0] - b[0], a[1])
    return (a[0] - b[0], a[1] - b[1])


def small_dft(values, sign):
    count = len(values)
    if count == 1:
        return values
    even = small_dft(values[0::2], sign)
    odd = small_dft(values[1::2], sign)
    out = [None] * count
    half = count // 2
    for k in range(half):
        turned = times(odd[k], sign * 2.0 * math.pi * k / count)
        out[k] = add(even[k], turned)
        out[k + half] = sub(even[k], turned)
    return out


def dot(a, b):
    return jnp.dot(a, b, preferred_element_type=jnp.float32)


def split(value):
    high = value.astype(jnp.bfloat16)
    return high, (value - high.astype(jnp.float32)).astype(jnp.bfloat16)


def put(re_parts, im_parts, lhs, start):
    for i, (re, im) in enumerate(zip(re_parts, im_parts)):
        rows = pl.ds(start + i * ROWS, ROWS)
        re_hi, re_lo = split(re)
        im_hi, im_lo = split(im)
        lhs[0, rows, :LANES] = re_hi
        lhs[0, rows, LANES:] = im_hi
        lhs[1, rows, :LANES] = re_lo
        lhs[1, rows, LANES:] = im_lo


def lane_transform(lhs, table_refs):
    high = lhs[0]
    table_high, table_low = table_refs[0][...], table_refs[1][...]
    return dot(high, table_high) + (dot(lhs[1], table_high) + dot(high, table_low))


def first_pass(load, store, outer):
    ra, rb = radices(outer)
    for b in range(rb):
        values = [times((load(rb * a + b), None), 2.0 * math.pi * a * SHIFT / ra) for a in range(ra)]
        out = small_dft(values, -1)
        for alpha in range(ra):
            re, im = times(out[alpha], -2.0 * math.pi * b * (alpha - SHIFT) / outer)
            store(b, alpha, re, im)


def second_pass(parts, alpha, outer, twist_ref):
    ra, rb = radices(outer)
    values = [(parts[0, b, alpha], parts[1, b, alpha]) for b in range(rb)]
    out = small_dft(values, -1)
    res, ims = [], []
    for beta in range(rb):
        k1 = alpha + ra * beta
        tr = twist_ref[0, k1 : k1 + 1, :]
        ti = twist_ref[1, k1 : k1 + 1, :]
        re, im = out[beta]
        res.append(re * tr - im * ti)
        ims.append(re * ti + im * tr)
    return res, ims


def back_second_pass(spectrum, alpha, outer, twist_ref, store):
    ra, rb = radices(outer)
    values = []
    for beta in range(rb):
        k1 = alpha + ra * beta
        tr = twist_ref[0, k1 : k1 + 1, :]
        ti = twist_ref[1, k1 : k1 + 1, :]
        re = spectrum[beta * ROWS : (beta + 1) * ROWS, :LANES]
        im = spectrum[beta * ROWS : (beta + 1) * ROWS, LANES:]
        values.append((re * tr + im * ti, im * tr - re * ti))
    out = small_dft(values, +1)
    for b in range(rb):
        re, im = times(out[b], 2.0 * math.pi * b * (alpha - SHIFT) / outer)
        store(b, alpha, re, im)


def back_first_pass(parts, outer, emit):
    ra, rb = radices(outer)
    for b in range(rb):
        values = [(parts[0, b, alpha], parts[1, b, alpha]) for alpha in range(ra)]
        out = small_dft(values, +1)
        for a in range(ra):
            angle = -2.0 * math.pi * a * SHIFT / ra
            re, im = out[a]
            c, s = math.cos(angle), math.sin(angle)
            emit(rb * a + b, re if a == 0 else re * c - im * s)


def put_product(re, im, lhs, start):
    rows = [slice(i, i + ROWS) for i in range(0, re.shape[0], ROWS)]
    put([re[r] for r in rows], [im[r] for r in rows], lhs, start)


def keep(parts):
    def store(b, alpha, re, im):
        parts[0, b, alpha] = re
        parts[1, b, alpha] = im

    return store


def conv_kernel(peers, outer, me_ref, *refs):
    pieces = refs[:peers]
    skip_ref, *tables, twist_ref = refs[peers : peers + 6]
    fwd_ref, bwd_ref = tables[:2], tables[2:]
    mixed_ref = refs[-6 - SPECTRA]
    spec_refs = refs[-5 - SPECTRA : -5]
    rows_in, parts_x, parts_h, parts_y, lhs = refs[-5:]
    me = me_ref[0]
    ra, rb = radices(outer)
    per = outer // peers
    for k in range(peers):
        rows_in[me ^ k] = pieces[k][...]

    def loader(which):
        def load(n1):
            lanes = slice((n1 % per) * LANES, (n1 % per + 1) * LANES)
            return rows_in[n1 // per, which, :, lanes].astype(jnp.float32)

        return load

    load_x = loader(0)
    first_pass(load_x, keep(parts_x), outer)
    first_pass(loader(1), keep(parts_h), outer)
    chunk = rb * ROWS
    for alpha in range(ra):
        put(*second_pass(parts_x, alpha, outer, twist_ref), lhs.at[alpha], 0)
        put(*second_pass(parts_h, alpha, outer, twist_ref), lhs.at[alpha], chunk)
    for alpha in range(ra):
        both = lane_transform(lhs.at[alpha], fwd_ref)
        x, h = both[:chunk], both[chunk:]
        each = ra // SPECTRA
        spec_refs[alpha // each][0, alpha % each * chunk : (alpha % each + 1) * chunk, :] = h
        xr, xi, hr, hi = x[:, :LANES], x[:, LANES:], h[:, :LANES], h[:, LANES:]
        put_product(xr * hr - xi * hi, xr * hi + xi * hr, lhs.at[ra + alpha // 2], alpha % 2 * chunk)
    for pair in range(ra // 2):
        y = lane_transform(lhs.at[ra + pair], bwd_ref)
        for i in range(2):
            back_second_pass(y[i * chunk : (i + 1) * chunk], 2 * pair + i, outer, twist_ref, keep(parts_y))
    skip = jnp.broadcast_to(skip_ref[...], (ROWS, LANES))

    def emit(n1, value):
        mixed_ref[:, n1 * LANES : (n1 + 1) * LANES] = value + skip * load_x(n1)

    back_first_pass(parts_y, outer, emit)


def pool_rows(rows_in, mixed_ref, rows_out, row, gather_ref, lhs, per, outer):
    for n1 in range(outer):
        lanes = slice((n1 % per) * LANES, (n1 % per + 1) * LANES)
        query = rows_in[n1 // per, row : row + ROWS, lanes].astype(jnp.float32)
        mixed = mixed_ref[row : row + ROWS, n1 * LANES : (n1 + 1) * LANES]
        rows_out[n1 // per, row : row + ROWS, lanes] = mixed.astype(jnp.bfloat16)
        high, low = split(query * mixed)
        lhs[n1 * ROWS : (n1 + 1) * ROWS, :LANES] = high
        lhs[n1 * ROWS : (n1 + 1) * ROWS, LANES:] = low
    sums = dot(lhs[...], gather_ref[...])
    each = LANES // POOL
    held = LANES // each
    place = lax.broadcasted_iota(jnp.int32, (ROWS, LANES), 1) // each
    tiles = []
    for tile in range(-(-outer // held)):
        total = jnp.zeros((ROWS, LANES), jnp.float32)
        for j in range(min(held, outer - tile * held)):
            n1 = tile * held + j
            total = jnp.where(place == j, sums[n1 * ROWS : (n1 + 1) * ROWS], total)
        tiles.append(total)
    return jnp.concatenate(tiles, axis=1)


def pool_kernel(peers, outer, me_ref, *refs):
    queries = refs[:peers]
    mixed_ref, gather_ref = refs[peers : peers + 2]
    outs = refs[peers + 2 : 2 * peers + 2]
    pooled_ref, rows_in, rows_out, lhs = refs[2 * peers + 2 :]
    me = me_ref[0]
    per = outer // peers
    for k in range(peers):
        rows_in[me ^ k] = queries[k][...]
    rows = mixed_ref.shape[0]
    bins = outer * LANES // POOL
    if rows == ROWS:
        pooled = pool_rows(rows_in, mixed_ref, rows_out, 0, gather_ref, lhs.at[0], per, outer)
        pooled_ref[...] = pooled[:, :bins].astype(jnp.bfloat16)
    else:
        left = pool_rows(rows_in, mixed_ref, rows_out, 0, gather_ref, lhs.at[0], per, outer)
        right = pool_rows(rows_in, mixed_ref, rows_out, ROWS, gather_ref, lhs.at[1], per, outer)
        each = bins // peers
        for seat in range(peers):
            mine = slice(seat * each, (seat + 1) * each)
            pair = jnp.concatenate([left[:, mine], right[:, mine]], axis=1).astype(jnp.bfloat16)
            for group in range(pooled_ref.shape[0]):
                pooled_ref[group, seat] = pair
    for k in range(peers):
        outs[k][...] = rows_out[me ^ k]


def corr_kernel(peers, outer, packed, me_ref, *refs):
    if packed:
        packed_ref, refs = refs[0], refs[1:]
    queries = refs[:peers]
    refs, spec_refs = refs[: peers] + refs[peers + SPECTRA :], refs[peers : peers + SPECTRA]
    grad_ref, skip_ref, *tables, twist_ref, spread_ref = refs[peers : peers + 8]
    fwd_ref, bwd_ref = tables[:2], tables[2:]
    outs = refs[peers + 8 : 2 * peers + 8]
    rows_in, lhs_g, gated, parts_g, parts_y, lhs, rows_out = refs[2 * peers + 8 :]
    me = me_ref[0]
    ra, rb = radices(outer)
    per = outer // peers
    for k in range(peers):
        rows_in[me ^ k] = queries[k][...]
    each = LANES // POOL
    held = LANES // each
    place = lax.broadcasted_iota(jnp.int32, (ROWS, LANES), 1) // each
    zero = jnp.zeros((ROWS, LANES), jnp.float32)
    for tile in range(-(-outer // held)):
        count = min(held, outer - tile * held)
        used = count * each
        part = grad_ref[:, tile * LANES : tile * LANES + used]
        if used < LANES:
            part = jnp.concatenate([part, jnp.zeros((ROWS, LANES - used), jnp.float32)], axis=1)
        high = part.astype(jnp.bfloat16).astype(jnp.float32)
        low = part - high
        for j in range(count):
            rows = pl.ds((tile * held + j) * ROWS, ROWS)
            lhs_g[rows, :LANES] = jnp.where(place == j, high, zero).astype(jnp.bfloat16)
            lhs_g[rows, LANES:] = jnp.where(place == j, low, zero).astype(jnp.bfloat16)
    gated[...] = dot(lhs_g[...], spread_ref[...])
    for n1 in range(outer):
        lanes = slice((n1 % per) * LANES, (n1 % per + 1) * LANES)
        rows = pl.ds(n1 * ROWS, ROWS)
        gated[rows, :] = gated[rows, :] * rows_in[n1 // per, :, lanes].astype(jnp.float32)

    def load_g(n1):
        return gated[n1 * ROWS : (n1 + 1) * ROWS, :]

    first_pass(load_g, keep(parts_g), outer)
    chunk = rb * ROWS
    for alpha in range(ra):
        put(*second_pass(parts_g, alpha, outer, twist_ref), lhs.at[alpha // 2], alpha % 2 * chunk)
    for pair in range(ra // 2):
        both = lane_transform(lhs.at[pair], fwd_ref)
        for i in range(2):
            alpha = 2 * pair + i
            g = both[i * chunk : (i + 1) * chunk]
            each = ra // SPECTRA
            h = spec_refs[alpha // each][0, alpha % each * chunk : (alpha % each + 1) * chunk, :]
            gr, gi, hr, hi = g[:, :LANES], g[:, LANES:], h[:, :LANES], h[:, LANES:]
            put_product(gr * hr + gi * hi, gi * hr - gr * hi, lhs.at[ra // 2 + pair], i * chunk)
    for pair in range(ra // 2):
        y = lane_transform(lhs.at[ra // 2 + pair], bwd_ref)
        for i in range(2):
            back_second_pass(y[i * chunk : (i + 1) * chunk], 2 * pair + i, outer, twist_ref, keep(parts_y))
    skip = jnp.broadcast_to(skip_ref[...], (ROWS, LANES))

    def emit(n1, value):
        lanes = slice((n1 % per) * LANES, (n1 % per + 1) * LANES)
        rows_out[n1 // per, :, lanes] = (value + skip * load_g(n1)).astype(jnp.bfloat16)

    back_first_pass(parts_y, outer, emit)
    step, steps = pl.program_id(0), pl.num_programs(0)
    for k in range(peers):
        outs[k][:, : per * LANES] = rows_out[me ^ k]
        if packed:
            half = steps // 2
            for chunk_at in range(packed_ref.shape[1] // (half * ROWS)):
                here = pl.ds((chunk_at * half + lax.rem(step, half)) * ROWS, ROWS)
                high, low = (part.astype(jnp.float32) for part in split(packed_ref[me ^ k, here, :]))
                lanes = slice((per + chunk_at) * LANES, (per + chunk_at + 1) * LANES)
                outs[k][:, lanes] = jnp.where(step < half, high, low).astype(jnp.bfloat16)


def whole(array):
    rank = len(array.shape)
    return pl.BlockSpec(array.shape, lambda i, me: (0,) * rank)


def by_rows(width, rows=ROWS, start=0):
    return pl.BlockSpec((rows, width), lambda i, me: (start + i, 0))


def call(kernel, name, me, steps, inputs, in_specs, out_shapes, out_specs, scratch, flops, aliases=None, near=(), vmem=()):
    moved = sum(x.size * x.dtype.itemsize for x in inputs)
    moved += sum(math.prod(o.shape) * o.dtype.itemsize for o in out_shapes)
    def space(i):
        return pltpu.VMEM if i in vmem else pltpu.HBM

    count = len(inputs)
    inputs = [x if i in near else pltpu.with_memory_space_constraint(x, space(i)) for i, x in enumerate(inputs)]
    out_shapes = [
        o if count + i in near else space(count + i)(o.shape, o.dtype) for i, o in enumerate(out_shapes)
    ]
    return pl.pallas_call(
        kernel,
        name=name,
        grid_spec=pltpu.PrefetchScalarGridSpec(
            num_scalar_prefetch=1,
            grid=(steps,),
            in_specs=in_specs,
            out_specs=out_specs,
            scratch_shapes=scratch,
        ),
        out_shape=out_shapes,
        input_output_aliases=aliases or {},
        compiler_params=pltpu.CompilerParams(
            dimension_semantics=("arbitrary",), vmem_limit_bytes=VMEM_LIMIT
        ),
        cost_estimate=pl.CostEstimate(flops=int(flops), bytes_accessed=moved, transcendentals=0),
    )(me, *inputs)


def shape(dims, dtype):
    return jax.ShapeDtypeStruct(dims, dtype)


def convolve(me, pieces, skip, tables, total_rows, start, before):
    peers = len(pieces)
    rows, width = pieces[0].shape[1:]
    length = width * peers
    outer = length // LANES
    ra, rb = radices(outer)
    chunk = rb * ROWS
    steps = rows // ROWS
    first = start // ROWS
    f32, bf16 = jnp.float32, jnp.bfloat16
    fwd, bwd, twist = tables["fwd"], tables["bwd"], tables["twist"]
    inputs = [*pieces, skip, *fwd, *bwd, twist]
    in_specs = [pl.BlockSpec((2, ROWS, width), lambda i, me: (0, i, 0))] * peers + [
        by_rows(1, start=first),
        *[whole(table) for table in (*fwd, *bwd, twist)],
    ]
    aliases = {}
    if before is not None:
        aliases = {1 + len(inputs): 0}
        inputs.append(before)
        in_specs.append(pl.BlockSpec(memory_space=pl.ANY))
    parts = pltpu.VMEM((2, rb, ra, ROWS, LANES), f32)

    def kernel(*refs):
        conv_kernel(peers, outer, *refs)

    part = (1, outer * ROWS // SPECTRA, 2 * LANES)
    out = call(
        kernel, "long_convolution", me, steps, inputs, in_specs,
        [shape((total_rows, length), f32)] + [shape((steps, *part[1:]), f32)] * SPECTRA,
        [by_rows(length, start=first)] + [pl.BlockSpec(part, lambda i, me: (i, 0, 0))] * SPECTRA,
        [
            pltpu.VMEM((peers, 2, ROWS, width), bf16),
            parts,
            parts,
            parts,
            pltpu.VMEM((ra + ra // 2, 2, 2 * chunk, 2 * LANES), bf16),
        ],
        rows * outer * 0.004 * MICROSECOND, aliases, (peers,), range(peers + 6, len(inputs) + 1),
    )
    return out[0], out[1:]


def pool(me, queries, mixed, gather, groups):
    peers = len(queries)
    rows, width = queries[0].shape
    length = width * peers
    outer = length // LANES
    bins = length // POOL
    bf16 = jnp.bfloat16
    if groups:
        step = 2 * ROWS
        pooled_shape = shape((groups, peers, rows // 2, LANES), bf16)
        pooled_spec = pl.BlockSpec((groups, peers, ROWS, LANES), lambda i, me: (0, 0, i, 0))
    else:
        step = ROWS
        pooled_shape = shape((rows, bins), bf16)
        pooled_spec = by_rows(bins)

    def kernel(*refs):
        pool_kernel(peers, outer, *refs)

    out = call(
        kernel, "pool_bins", me, rows // step, [*queries, mixed, gather],
        [by_rows(width, step)] * peers + [by_rows(length, step), whole(gather)],
        [shape((rows, width), bf16)] * peers + [pooled_shape],
        [by_rows(width, step)] * peers + [pooled_spec],
        [
            pltpu.VMEM((peers, step, width), bf16),
            pltpu.VMEM((peers, step, width), bf16),
            pltpu.VMEM((step // ROWS, outer * ROWS, 2 * LANES), bf16),
        ],
        rows * outer * 0.001 * MICROSECOND, vmem=(peers,),
    )
    return out[:peers], out[peers]


def correlate(me, queries, grad_pooled, spec, skip, tables, spread, start, packed):
    peers = len(queries)
    width = queries[0].shape[1]
    rows = spec[0].shape[0] * ROWS
    length = width * peers
    outer = length // LANES
    bins = length // POOL
    ra, rb = radices(outer)
    chunk = rb * ROWS
    first = start // ROWS
    f32, bf16 = jnp.float32, jnp.bfloat16
    fwd, bwd, twist = tables["fwd"], tables["bwd"], tables["twist"]
    in_specs = [by_rows(width, start=first)] * peers + [
        *[pl.BlockSpec((1, *part.shape[1:]), lambda i, me: (i, 0, 0)) for part in spec],
        by_rows(bins, start=first),
        by_rows(1, start=first),
        *[whole(table) for table in (*fwd, *bwd, twist, spread)],
    ]
    parts = pltpu.VMEM((2, rb, ra, ROWS, LANES), f32)
    scratch = [
        pltpu.VMEM((peers, ROWS, width), bf16),
        pltpu.VMEM((outer * ROWS, 2 * LANES), bf16),
        pltpu.VMEM((outer * ROWS, LANES), f32),
        parts,
        parts,
        pltpu.VMEM((ra, 2, 2 * chunk, 2 * LANES), bf16),
        pltpu.VMEM((peers, ROWS, width), bf16),
    ]

    def kernel(*refs):
        corr_kernel(peers, outer, packed is not None, *refs)

    inputs = [*queries, *spec, grad_pooled, skip, *fwd, *bwd, twist, spread]
    sent = width
    if packed is not None:
        sent = width + packed.shape[1] // (rows // 2) * LANES
        inputs = [packed, *inputs]
        in_specs = [whole(packed), *in_specs]
    near = len(inputs) - 8
    return call(
        kernel, "long_correlation", me, rows // ROWS, inputs, in_specs,
        [shape((rows, sent), bf16)] * peers, [by_rows(sent)] * peers,
        scratch, rows * outer * 0.004 * MICROSECOND, near=(0, near, near + 1) if packed is not None else (near, near + 1),
    )


def lay_out(me, projections, filter_taps, peers, chunk, chunks):
    last = chunk == chunks - 1
    _, channels, width = projections.shape
    pencil = channels // peers
    rows = pencil // chunks
    f32, bf16 = jnp.float32, jnp.bfloat16
    order = list(range(peers))[::-1]

    def kernel(me_ref, proj_ref, taps_ref, *refs):
        outs = refs[:peers]
        queries = refs[peers:-7]
        pair, taps, laid, passing, sems, out_sems, query_sems = refs[-7:]

        def take(k):
            block = pl.ds(pl.multiple_of((me_ref[0] ^ k) * pencil, pencil), pencil)
            return pltpu.make_async_copy(proj_ref.at[0, block], passing.at[k], query_sems.at[k, 0])

        def hand_on(k):
            return pltpu.make_async_copy(passing.at[k], queries[k], query_sems.at[k, 1])


        def fetch(k):
            here = pl.ds(pl.multiple_of((me_ref[0] ^ k) * pencil + chunk * rows, rows), rows)
            return (
                pltpu.make_async_copy(proj_ref.at[1, here], pair.at[k, 0], sems.at[k, 0]),
                pltpu.make_async_copy(proj_ref.at[2, here], pair.at[k, 1], sems.at[k, 1]),
                pltpu.make_async_copy(taps_ref.at[here], taps.at[k], sems.at[k, 2]),
            )

        def leave(k):
            return pltpu.make_async_copy(laid.at[k], outs[k], out_sems.at[k])

        for k in order:
            for copy in fetch(k):
                copy.start()
        for k in range(len(queries)):
            take(k).start()
        for k in order:
            keyed, valued, lags = fetch(k)
            keyed.wait()
            valued.wait()
            laid[k, 0] = (pair[k, 0].astype(f32) * pair[k, 1].astype(f32)).astype(bf16)
            lags.wait()
            laid[k, 1] = taps[k].astype(bf16)
            leave(k).start()
        for k in range(len(queries)):
            take(k).wait()
            hand_on(k).start()
        for k in order:
            leave(k).wait()
        for k in range(len(queries)):
            hand_on(k).wait()

    out_shapes = [shape((2, rows, width), bf16)] * peers
    if last:
        out_shapes += [shape((pencil, width), bf16)] * peers
    return call(
        kernel, "lay_out", me, 1, [projections, filter_taps],
        [pl.BlockSpec(memory_space=pltpu.HBM)] * 2,
        out_shapes,
        [pl.BlockSpec(memory_space=pltpu.HBM)] * len(out_shapes),
        [
            pltpu.VMEM((peers, 2, rows, width), bf16),
            pltpu.VMEM((peers, rows, width), f32),
            pltpu.VMEM((peers, 2, rows, width), bf16),
            pltpu.VMEM((peers, pencil, width), bf16),
            pltpu.SemaphoreType.DMA((peers, 3)),
            pltpu.SemaphoreType.DMA((peers,)),
            pltpu.SemaphoreType.DMA((peers, 2)),
        ],
        rows * peers * 0.015 * MICROSECOND,
    )


def by_track(me, head_weight, groups):
    channels, tracks = head_weight.shape
    half, own = channels // 2, tracks // groups
    padded = -(-own // LANES) * LANES
    dtype = head_weight.dtype
    steps = half // ROWS

    def kernel(me_ref, weight_ref, out_ref, rows_in, sems):
        first = pl.multiple_of((me_ref[0] & 1) * half, half)

        def fetch(i):
            return pltpu.make_async_copy(
                weight_ref.at[pl.ds(first + i * ROWS, ROWS)], rows_in.at[pl.ds(i * ROWS, ROWS)], sems.at[i]
            )

        for i in range(steps):
            fetch(i).start()
        for i in range(steps):
            fetch(i).wait()
        for group in range(groups):
            out_ref[group, :, :own] = rows_in[:, group * own : (group + 1) * own]
            if padded > own:
                out_ref[group, :, own:] = jnp.zeros((half, padded - own), dtype)

    out = shape((groups, half, padded), dtype)
    return call(
        kernel, "by_track", me, 1, [head_weight], [pl.BlockSpec(memory_space=pltpu.HBM)], [out], [whole(out)],
        [pltpu.VMEM((half, tracks), dtype), pltpu.SemaphoreType.DMA((steps,))], 2 * MICROSECOND, vmem=(1,),
    )[0]


def weight_pair(weight_ref, seats, pencil, own):
    groups, _, padded = weight_ref.shape
    rows = weight_ref[...].reshape(groups, seats, pencil // (2 * ROWS), 2, ROWS, padded)
    count = groups * seats * pencil // 2
    left, right = rows[:, :, :, 0].reshape(count, padded), rows[:, :, :, 1].reshape(count, padded)
    return left[:, :own], right[:, :own]


def head_rates(me, got, mine, other, bias, counts):
    groups, peers, half_rows, _ = got.shape
    own = counts.shape[1]
    seats = peers // 2
    pencil = 2 * half_rows
    bins = LANES // 2
    f32 = jnp.float32

    def kernel(me_ref, got_ref, mine_ref, other_ref, bias_ref, counts_ref, logits_ref, sums_ref):
        odd = me_ref[0] & 1
        total = jnp.broadcast_to(bias_ref[...], (bins, own))
        for weight_ref, place in ((mine_ref, odd), (other_ref, 1 - odd)):
            block = got_ref[:, pl.ds(place * seats, seats)].reshape(groups * seats * half_rows, LANES)
            turned = block.astype(f32).T.astype(jnp.bfloat16)
            left, right = weight_pair(weight_ref, seats, pencil, own)
            total = total + dot(turned[:bins], left) + dot(turned[bins:], right)
        logits_ref[...] = total
        rates = jax.nn.softplus(total) + rate_floor
        observed = counts_ref[...].astype(f32)
        sums_ref[0:1, :] = jnp.sum(rates, axis=0, keepdims=True)
        sums_ref[1:2, :] = jnp.sum(observed, axis=0, keepdims=True)
        sums_ref[2:3, :] = jnp.sum(observed * jnp.log(rates), axis=0, keepdims=True)
        sums_ref[3:8, :] = jnp.zeros((5, own), f32)

    inputs = [got, mine, other, bias, counts]
    return call(
        kernel, "head_rates", me, 1, inputs, [whole(x) for x in inputs],
        [shape((bins, own), f32), shape((8, own), f32)],
        [pl.BlockSpec((bins, own), lambda i, me: (0, 0)), pl.BlockSpec((8, own), lambda i, me: (0, 0))],
        [], 2 * bins * groups * peers * pencil * own, near=range(7),
    )


def head_grads(me, logits, sums, mine, other, counts, peers):
    groups, half, _ = mine.shape
    own = counts.shape[1]
    seats = peers // 2
    pencil = half // seats
    bins = LANES // 2
    f32, bf16 = jnp.float32, jnp.bfloat16

    def kernel(me_ref, logits_ref, sums_ref, mine_ref, other_ref, counts_ref, out_ref, loss_ref):
        odd = me_ref[0] & 1
        totals = sums_ref[0]
        for seat in range(1, peers):
            totals = totals + sums_ref[seat]
        pred_total, obs_total, log_sum = totals[0:1], totals[1:2], totals[2:3]
        log_pred = jnp.log(pred_total)
        terms = total_weight * (pred_total - obs_total * log_pred) + obs_total * log_pred - log_sum
        loss_ref[...] = jnp.broadcast_to(jnp.sum(terms, axis=1, keepdims=True), loss_ref.shape)
        ratio = obs_total / pred_total
        logits_here = logits_ref[...]
        rates = jax.nn.softplus(logits_here) + rate_floor
        observed = counts_ref[...].astype(f32)
        grad_rates = total_weight * (1.0 - ratio) + ratio - observed / rates
        grads = (grad_rates * jax.nn.sigmoid(logits_here)).astype(bf16)
        none = jnp.zeros_like(grads)
        in_left = jnp.concatenate([grads, none], axis=0)
        in_right = jnp.concatenate([none, grads], axis=0)
        across = (((1,), (1,)), ((), ()))
        for weight_ref, place in ((mine_ref, odd), (other_ref, 1 - odd)):
            left, right = weight_pair(weight_ref, seats, pencil, own)
            part = lax.dot_general(left, in_left, across, preferred_element_type=f32)
            part = part + lax.dot_general(right, in_right, across, preferred_element_type=f32)
            out_ref[:, pl.ds(place * seats, seats)] = part.astype(bf16).reshape(groups, seats, pencil // 2, LANES)

    inputs = [logits, sums, mine, other, counts]
    out = shape((groups, peers, pencil // 2, LANES), bf16)
    return call(
        kernel, "head_grads", me, 1, inputs, [whole(x) for x in inputs],
        [out, shape((8, LANES), f32)],
        [pl.BlockSpec(out.shape, lambda i, me: (0, 0, 0, 0)), pl.BlockSpec((8, LANES), lambda i, me: (0, 0))],
        [], 4 * bins * groups * peers * pencil * own, near=(0, 1, 2, 3, 4, 6),
    )


def sum_grads(me, back):
    groups, peers, half_rows, _ = back.shape
    bins = LANES // 2
    f32 = jnp.float32

    def kernel(me_ref, back_ref, rows_ref, packed_ref):
        for seat in range(peers):
            total = back_ref[0, seat].astype(f32)
            for group in range(1, groups):
                total = total + back_ref[group, seat].astype(f32)
            packed_ref[seat] = total
            for i in range(half_rows // ROWS):
                pair = total[i * ROWS : (i + 1) * ROWS]
                lanes = slice(seat * bins, (seat + 1) * bins)
                rows_ref[2 * i * ROWS : (2 * i + 1) * ROWS, lanes] = pair[:, :bins]
                rows_ref[(2 * i + 1) * ROWS : (2 * i + 2) * ROWS, lanes] = pair[:, bins:]

    rows, packed = shape((2 * half_rows, peers * bins), f32), shape((peers, half_rows, LANES), f32)
    return call(
        kernel, "sum_grads", me, 1, [back], [whole(back)], [rows, packed], [whole(rows), whole(packed)], [], back.size,
        near=(0, 1, 2),
    )


def finish(me, projections, mixed_home, corr_home, spread, chunk, chunks, before):
    peers = len(corr_home)
    _, channels, width = projections.shape
    pencil = channels // peers
    rows = pencil // chunks
    tiles = width // LANES
    each = LANES // POOL
    f32, bf16 = jnp.float32, jnp.bfloat16
    with_query = bool(mixed_home)
    payload = corr_home[0].shape[1]

    def kernel(me_ref, spread_ref, proj_ref, *refs):
        mixed_refs, corr_refs = refs[: len(mixed_home)], refs[len(mixed_home) : len(mixed_home) + peers]
        out_ref, pair, mixed_in, corr_in, done, query_done, lhs, sems, out_sems = refs[-9:]
        place = lax.broadcasted_iota(jnp.int32, (ROWS, LANES), 1) // each
        zero = jnp.zeros((ROWS, LANES), f32)

        def block(k, start, count):
            return pl.ds(pl.multiple_of((me_ref[0] ^ k) * pencil + start, ROWS), count)

        def here(k):
            return block(k, chunk * rows, rows)

        def fetch(k):
            return (
                pltpu.make_async_copy(corr_refs[k], corr_in.at[k], sems.at[k, 0]),
                pltpu.make_async_copy(proj_ref.at[1, here(k)], pair.at[k, 0], sems.at[k, 1]),
                pltpu.make_async_copy(proj_ref.at[2, here(k)], pair.at[k, 1], sems.at[k, 2]),
            )

        def fetch_mixed(k):
            return pltpu.make_async_copy(mixed_refs[k], mixed_in.at[k], sems.at[k, 3])

        def leave(k, plane):
            if plane == 0:
                return pltpu.make_async_copy(query_done.at[k], out_ref.at[0, block(k, 0, pencil)], out_sems.at[k, 0])
            return pltpu.make_async_copy(done.at[k, plane - 1], out_ref.at[plane, here(k)], out_sems.at[k, plane])

        for k in range(peers):
            for copy in fetch(k):
                copy.start()
            if with_query:
                fetch_mixed(k).start()
        for k in range(peers):
            for copy in fetch(k):
                copy.wait()
            corr = corr_in[k, :, :width].astype(f32)
            done[k, 0] = corr * pair[k, 1].astype(f32)
            leave(k, 1).start()
            done[k, 1] = corr * pair[k, 0].astype(f32)
            leave(k, 2).start()
            if not with_query:
                continue
            fetch_mixed(k).wait()
            for i in range(pencil // ROWS):
                part = slice(i * ROWS, (i + 1) * ROWS)
                inside = i % (rows // ROWS)
                source = inside // 2 * ROWS
                lanes = slice(width + i // (rows // ROWS) * LANES, width + (i // (rows // ROWS) + 1) * LANES)
                high = corr_in[k, source : source + ROWS, lanes].astype(f32)
                low = corr_in[k, rows // 2 + source : rows // 2 + source + ROWS, lanes].astype(f32)
                for t in range(tiles):
                    near = place == t + inside % 2 * tiles
                    lhs[i, t * ROWS : (t + 1) * ROWS, :LANES] = jnp.where(near, high, zero).astype(bf16)
                    lhs[i, t * ROWS : (t + 1) * ROWS, LANES:] = jnp.where(near, low, zero).astype(bf16)
                grad = dot(lhs[i], spread_ref[...])
                for t in range(tiles):
                    at = slice(t * LANES, (t + 1) * LANES)
                    query_done[k, part, at] = grad[t * ROWS : (t + 1) * ROWS] * mixed_in[k, part, at].astype(f32)
            leave(k, 0).start()
        for k in range(peers):
            for plane in range(0 if with_query else 1, 3):
                leave(k, plane).wait()

    inputs = [spread, projections, *mixed_home, *corr_home]
    in_specs = [whole(spread), pl.BlockSpec(memory_space=pltpu.HBM)]
    in_specs += [pl.BlockSpec(memory_space=pl.ANY)] * (len(inputs) - 2)
    near = (0, *range(2, len(inputs)))
    aliases = {}
    if before is not None:
        aliases = {1 + len(inputs): 0}
        inputs.append(before)
        in_specs.append(pl.BlockSpec(memory_space=pl.ANY))
    return call(
        kernel, "finish", me, 1, inputs, in_specs,
        [shape((3, channels, width), f32)], [pl.BlockSpec(memory_space=pltpu.HBM)],
        [
            pltpu.VMEM((peers, 2, rows, width), bf16),
            pltpu.VMEM((peers, pencil if with_query else ROWS, width), bf16),
            pltpu.VMEM((peers, rows, payload), bf16),
            pltpu.VMEM((peers, 2, rows, width), f32),
            pltpu.VMEM((peers, pencil if with_query else ROWS, width), f32),
            pltpu.VMEM((pencil // ROWS, tiles * ROWS, 2 * LANES), bf16),
            pltpu.SemaphoreType.DMA((peers, 4)),
            pltpu.SemaphoreType.DMA((peers, 3)),
        ],
        rows * peers * 0.03 * MICROSECOND, aliases, near=near,
    )[0]


def swap(value, k, count):
    if k == 0:
        return value
    return lax.ppermute(value, "seq", [(i, i ^ k) for i in range(count)])


def pad_rows(value, rows):
    short = rows - value.shape[-2]
    if short == 0:
        return value
    widths = [(0, 0)] * value.ndim
    widths[-2] = (0, short)
    return jnp.pad(value, widths)


def aligned(projections, filter_taps, skip_gain, head_weight, head_bias, counts):
    f32 = jnp.float32
    _, channels, width = projections.shape
    peers = lax.axis_size("seq")
    groups = lax.axis_size("chan")
    seat = lax.axis_index("seq")
    group = lax.axis_index("chan")
    bins = width // POOL
    length = width * peers
    tracks = head_weight.shape[1]
    own_tracks = tracks // groups
    pencil = channels // peers
    chunks = CHUNKS
    rows = pencil // chunks
    me = jnp.asarray(seat, jnp.int32).reshape(1)
    tables = transform_tables(length)
    gather, spread = pool_tables()

    laid, me_next = [], me
    for j in range(chunks):
        laid.append(lay_out(me_next, projections, filter_taps, peers, j, chunks))
        me_next, _ = lax.optimization_barrier((me, laid[j]))
    pieces = [[swap(laid[j][k], k, peers) for k in range(peers)] for j in range(chunks)]
    held_back, _ = lax.optimization_barrier((laid[-1][peers:], pieces[0]))
    queries = [swap(held_back[k], k, peers) for k in range(peers)]
    skip = lax.dynamic_index_in_dim(skip_gain.reshape(peers, pencil, 1), seat, axis=0, keepdims=False)

    mine = by_track(me_next, head_weight, groups)
    mine = lax.all_to_all(mine, "chan", split_axis=0, concat_axis=0, tiled=True)

    mixed, specs = None, []
    for j in range(chunks):
        mixed, spec = convolve(me, pieces[j], skip, tables, pencil, j * rows, mixed)
        specs.append(spec)
    mixed_out, sent = pool(me, queries, mixed, gather, groups)
    mixed_home = [swap(mixed_out[k], k, peers) for k in range(peers)]

    def exchange(blocks):
        flat = blocks.reshape(groups * peers, pencil // 2, LANES)
        flat = lax.all_to_all(flat, ("chan", "seq"), split_axis=0, concat_axis=0, tiled=True)
        return flat.reshape(blocks.shape)

    got = exchange(sent)
    mine, _ = lax.optimization_barrier((mine, sent))
    other = swap(mine, 1, peers)
    own_bias = lax.dynamic_slice_in_dim(head_bias, group * own_tracks, own_tracks).reshape(1, own_tracks)
    own_counts = lax.dynamic_slice_in_dim(counts, group * own_tracks, own_tracks, axis=1)
    logits, sums = head_rates(me, got, mine, other, own_bias, own_counts)
    all_sums = lax.all_gather(sums, "seq")
    part, loss = head_grads(me, logits, all_sums, mine, other, own_counts, peers)
    back = exchange(part)
    step = 1
    while step < groups:
        loss = loss + lax.ppermute(loss, "chan", [(i, i ^ step) for i in range(groups)])
        step *= 2
    mean_loss = loss[0, 0] / (bins * peers * tracks)

    grad_rows, packed = sum_grads(me, back)
    grads = None
    corr_home = []
    for j in range(chunks):
        corr = correlate(me, queries, grad_rows, specs[j], skip, tables, spread, j * rows, None if j else packed)
        corr_home.append([swap(corr[k], k, peers) for k in range(peers)])
    for j in range(chunks):
        grads = finish(me, projections, [] if j else mixed_home, corr_home[j], spread, j, chunks, grads)
    return mean_loss, grads


def power_of_two(value):
    return value & (value - 1) == 0


def per_device(projections, filter_taps, skip_gain, head_weight, head_bias, counts):
    channels, width = projections.shape[1:]
    peers, groups = lax.axis_size("seq"), lax.axis_size("chan")
    pencil = channels // peers
    fits = (
        pencil % (2 * ROWS * CHUNKS) == 0
        and 2 * (width // POOL) == LANES
        and power_of_two(peers)
        and peers > 1
        and power_of_two(groups)
        and groups <= MOST_GROUPS
    )
    run = aligned if fits else general
    return run(projections, filter_taps, skip_gain, head_weight, head_bias, counts)


def general(projections, filter_taps, skip_gain, head_weight, head_bias, counts):
    f32, bf16 = jnp.float32, jnp.bfloat16
    _, channels, width = projections.shape
    peers = lax.axis_size("seq")
    groups = lax.axis_size("chan")
    seat = lax.axis_index("seq")
    group = lax.axis_index("chan")
    bins = width // POOL
    length = width * peers
    tracks = head_weight.shape[1]
    own_tracks = tracks // groups
    pencil = channels // peers
    rows = -(-pencil // ROWS) * ROWS
    me = jnp.asarray(seat, jnp.int32).reshape(1)
    tables = transform_tables(length)
    gather, spread = pool_tables()

    def block(array, k):
        return lax.dynamic_index_in_dim(array, seat ^ k, axis=-3, keepdims=False)

    query = projections[0]
    key_value = projections[1].astype(f32) * projections[2].astype(f32)
    stacked = jnp.stack([key_value.astype(bf16), filter_taps.astype(bf16)])
    stacked = stacked.reshape(2, peers, pencil, width)
    pieces = [pad_rows(swap(block(stacked, k), k, peers), rows) for k in range(peers)]
    query_blocks = query.reshape(peers, pencil, width)
    queries = [pad_rows(swap(block(query_blocks, k), k, peers), rows) for k in range(peers)]
    skip = pad_rows(block(skip_gain.reshape(peers, pencil, 1), 0), rows)

    half = channels // 2
    by_track = head_weight.reshape(2, half, groups, own_tracks).transpose(0, 2, 1, 3)
    mine = lax.dynamic_index_in_dim(by_track, seat & 1, axis=0, keepdims=False)
    mine = lax.all_to_all(mine, "chan", split_axis=0, concat_axis=0, tiled=True)
    other = swap(mine, 1, peers)
    mine = mine.reshape(groups * half, own_tracks)
    other = other.reshape(groups * half, own_tracks)

    mixed, spec = convolve(me, pieces, skip, tables, rows, 0, None)
    mixed_out, pooled = pool(me, queries, mixed, gather, 0)
    pooled = pooled[:pencil]
    mixed_home = [swap(mixed_out[k][:pencil], k, peers) for k in range(peers)]

    sent = pooled.reshape(pencil, peers, bins).transpose(1, 0, 2)
    sent = jnp.broadcast_to(sent[None], (groups, peers, pencil, bins))
    got = lax.all_to_all(
        sent.reshape(groups * peers, pencil, bins), ("chan", "seq"), split_axis=0, concat_axis=0, tiled=True
    )
    got = got.reshape(groups, 2, half, bins)
    low_half = got[:, 0].reshape(groups * half, bins)
    high_half = got[:, 1].reshape(groups * half, bins)
    odd = (seat & 1) == 1
    pooled_mine = jnp.where(odd, high_half, low_half)
    pooled_other = jnp.where(odd, low_half, high_half)

    def project(x, w):
        return lax.dot_general(x, w, (((0,), (0,)), ((), ())), preferred_element_type=f32)

    own_bias = lax.dynamic_slice_in_dim(head_bias, group * own_tracks, own_tracks)
    own_counts = lax.dynamic_slice_in_dim(counts, group * own_tracks, own_tracks, axis=1)
    logits = project(pooled_mine, mine) + project(pooled_other, other) + own_bias[None, :]
    rates = jax.nn.softplus(logits) + rate_floor
    observed = own_counts.astype(f32)
    partial_sums = jnp.stack(
        [jnp.sum(rates, axis=0), jnp.sum(observed, axis=0), jnp.sum(observed * jnp.log(rates), axis=0)]
    )
    pred_total, obs_total, log_sum = jnp.sum(lax.all_gather(partial_sums, "seq"), axis=0)
    log_pred = jnp.log(pred_total)
    loss_part = jnp.sum(
        total_weight * (pred_total - obs_total * log_pred) + obs_total * log_pred - log_sum
    )
    mean_loss = lax.psum(loss_part, "chan") / (bins * peers * tracks)
    ratio = obs_total / pred_total
    grad_rates = total_weight * (1.0 - ratio)[None, :] + ratio[None, :] - observed / rates
    grad_logits = (grad_rates * jax.nn.sigmoid(logits)).astype(bf16)

    def spread_back(w):
        return lax.dot_general(w, grad_logits, (((1,), (1,)), ((), ())), preferred_element_type=f32)

    part_mine = spread_back(mine).astype(bf16).reshape(groups, 1, half, bins)
    part_other = spread_back(other).astype(bf16).reshape(groups, 1, half, bins)
    part = jnp.concatenate(
        [jnp.where(odd, part_other, part_mine), jnp.where(odd, part_mine, part_other)], axis=1
    )
    back = lax.all_to_all(
        part.reshape(groups * peers, pencil, bins), ("chan", "seq"), split_axis=0, concat_axis=0, tiled=True
    )
    grad_pooled = jnp.sum(back.reshape(groups, peers, pencil, bins).astype(f32), axis=0)
    grad_home = [swap(block(grad_pooled, k), k, peers) for k in range(peers)]
    grad_rows = pad_rows(grad_pooled.transpose(1, 0, 2).reshape(pencil, peers * bins), rows)

    corr_out = correlate(me, queries, grad_rows, spec, skip, tables, spread, 0, None)
    corr_home = [swap(corr_out[k][:pencil], k, peers) for k in range(peers)]

    def assemble(parts):
        out = jnp.zeros((peers,) + parts[0].shape, parts[0].dtype)
        for k, part in enumerate(parts):
            out = lax.dynamic_update_index_in_dim(out, part, seat ^ k, axis=0)
        return out.reshape((channels,) + parts[0].shape[1:])

    grad_output = jnp.repeat(assemble(grad_home) / POOL, POOL, axis=1)
    grad_kv = assemble(corr_home).astype(f32)
    grad_query = grad_output * assemble(mixed_home).astype(f32)
    grads = jnp.stack(
        [grad_query, grad_kv * projections[2].astype(f32), grad_kv * projections[1].astype(f32)], axis=0
    )
    return mean_loss, grads


def solution(mesh):
    placed = (
        P(None, "chan", "seq"),
        P("chan", "seq"),
        P("chan"),
        P("chan", None),
        P(),
        P("seq", None),
    )
    return jax.shard_map(
        per_device,
        mesh=mesh,
        in_specs=placed,
        out_specs=(P(), P(None, "chan", "seq")),
        check_vma=False,
    )
```

```python
import math

import jax
import jax.numpy as jnp
import ml_dtypes
import numpy as np
from jax import lax
from jax.experimental import pallas as pl
from jax.experimental.pallas import tpu as pltpu
from jax.sharding import PartitionSpec as P

POOL = 32
LANES = 128
ROWS = 16
SHIFT = 0.25

total_weight = 0.2
rate_floor = 0.5

MICROSECOND = 1.0e9

VMEM_LIMIT = 20 * 1024 * 1024
CHUNKS = 2
SPECTRA = 4
MOST_GROUPS = 16


def split_bf16(table):
    high = table.astype(ml_dtypes.bfloat16)
    low = (table - high.astype(np.float64)).astype(ml_dtypes.bfloat16)
    return high, low


def radices(outer):
    first = 1
    while first * first < outer:
        first *= 2
    return first, outer // first


def transform_tables(length):
    outer = length // LANES
    idx = np.arange(LANES)
    angle = 2.0 * np.pi * (np.outer(idx, idx) % LANES) / LANES
    wr, wi = np.cos(angle), -np.sin(angle)
    forward = np.block([[wr, wi], [-wi, wr]])
    backward = np.block([[wr, -wi], [wi, wr]]) / length
    k1 = np.arange(outer)[:, None]
    twist = 2.0 * np.pi * (k1 - SHIFT) * idx[None, :] / length
    f_hi, f_lo = split_bf16(forward)
    b_hi, b_lo = split_bf16(backward)
    return dict(
        fwd=[f_hi, f_lo],
        bwd=[b_hi, b_lo],
        twist=np.stack([np.cos(twist), -np.sin(twist)]).astype(np.float32),
    )


def pool_tables():
    per = LANES // POOL
    lane = np.arange(LANES)
    hit = (lane[:, None] // POOL) == (lane[None, :] % per)
    gather = np.concatenate([hit, hit], axis=0) / POOL
    spread = np.concatenate([hit.T, hit.T], axis=0) / POOL
    return gather.astype(ml_dtypes.bfloat16), spread.astype(ml_dtypes.bfloat16)


def times(value, angle):
    re, im = value
    c, s = math.cos(angle), math.sin(angle)
    tiny = 1e-12
    if im is None:
        if abs(s) < tiny and c > 0:
            return (re, None)
        return (re * c, re * s)
    if abs(s) < tiny:
        return (re, im) if c > 0 else (-re, -im)
    if abs(c) < tiny:
        return (-im, re) if s > 0 else (im, -re)
    return (re * c - im * s, re * s + im * c)


def add(a, b):
    if a[1] is None and b[1] is None:
        return (a[0] + b[0], None)
    if a[1] is None:
        return (a[0] + b[0], b[1])
    if b[1] is None:
        return (a[0] + b[0], a[1])
    return (a[0] + b[0], a[1] + b[1])


def sub(a, b):
    if a[1] is None and b[1] is None:
        return (a[0] - b[0], None)
    if a[1] is None:
        return (a[0] - b[0], -b[1])
    if b[1] is None:
        return (a[0] - b[0], a[1])
    return (a[0] - b[0], a[1] - b[1])


def small_dft(values, sign):
    count = len(values)
    if count == 1:
        return values
    even = small_dft(values[0::2], sign)
    odd = small_dft(values[1::2], sign)
    out = [None] * count
    half = count // 2
    for k in range(half):
        turned = times(odd[k], sign * 2.0 * math.pi * k / count)
        out[k] = add(even[k], turned)
        out[k + half] = sub(even[k], turned)
    return out


def dot(a, b):
    return jnp.dot(a, b, preferred_element_type=jnp.float32)


def split(value):
    high = value.astype(jnp.bfloat16)
    return high, (value - high.astype(jnp.float32)).astype(jnp.bfloat16)


def put(re_parts, im_parts, lhs, start):
    for i, (re, im) in enumerate(zip(re_parts, im_parts)):
        rows = pl.ds(start + i * ROWS, ROWS)
        re_hi, re_lo = split(re)
        im_hi, im_lo = split(im)
        lhs[0, rows, :LANES] = re_hi
        lhs[0, rows, LANES:] = im_hi
        lhs[1, rows, :LANES] = re_lo
        lhs[1, rows, LANES:] = im_lo


def lane_transform(lhs, table_refs):
    high = lhs[0]
    table_high, table_low = table_refs[0][...], table_refs[1][...]
    return dot(high, table_high) + (dot(lhs[1], table_high) + dot(high, table_low))


def first_pass(load, store, outer):
    ra, rb = radices(outer)
    for b in range(rb):
        values = [times((load(rb * a + b), None), 2.0 * math.pi * a * SHIFT / ra) for a in range(ra)]
        out = small_dft(values, -1)
        for alpha in range(ra):
            re, im = times(out[alpha], -2.0 * math.pi * b * (alpha - SHIFT) / outer)
            store(b, alpha, re, im)


def second_pass(parts, alpha, outer, twist_ref):
    ra, rb = radices(outer)
    values = [(parts[0, b, alpha], parts[1, b, alpha]) for b in range(rb)]
    out = small_dft(values, -1)
    res, ims = [], []
    for beta in range(rb):
        k1 = alpha + ra * beta
        tr = twist_ref[0, k1 : k1 + 1, :]
        ti = twist_ref[1, k1 : k1 + 1, :]
        re, im = out[beta]
        res.append(re * tr - im * ti)
        ims.append(re * ti + im * tr)
    return res, ims


def back_second_pass(spectrum, alpha, outer, twist_ref, store):
    ra, rb = radices(outer)
    values = []
    for beta in range(rb):
        k1 = alpha + ra * beta
        tr = twist_ref[0, k1 : k1 + 1, :]
        ti = twist_ref[1, k1 : k1 + 1, :]
        re = spectrum[beta * ROWS : (beta + 1) * ROWS, :LANES]
        im = spectrum[beta * ROWS : (beta + 1) * ROWS, LANES:]
        values.append((re * tr + im * ti, im * tr - re * ti))
    out = small_dft(values, +1)
    for b in range(rb):
        re, im = times(out[b], 2.0 * math.pi * b * (alpha - SHIFT) / outer)
        store(b, alpha, re, im)


def back_first_pass(parts, outer, emit):
    ra, rb = radices(outer)
    for b in range(rb):
        values = [(parts[0, b, alpha], parts[1, b, alpha]) for alpha in range(ra)]
        out = small_dft(values, +1)
        for a in range(ra):
            angle = -2.0 * math.pi * a * SHIFT / ra
            re, im = out[a]
            c, s = math.cos(angle), math.sin(angle)
            emit(rb * a + b, re if a == 0 else re * c - im * s)


def put_product(re, im, lhs, start):
    rows = [slice(i, i + ROWS) for i in range(0, re.shape[0], ROWS)]
    put([re[r] for r in rows], [im[r] for r in rows], lhs, start)


def keep(parts):
    def store(b, alpha, re, im):
        parts[0, b, alpha] = re
        parts[1, b, alpha] = im

    return store


def conv_kernel(peers, outer, me_ref, *refs):
    pieces = refs[:peers]
    skip_ref, *tables, twist_ref = refs[peers : peers + 6]
    fwd_ref, bwd_ref = tables[:2], tables[2:]
    mixed_ref = refs[-6 - SPECTRA]
    spec_refs = refs[-5 - SPECTRA : -5]
    rows_in, parts_x, parts_h, parts_y, lhs = refs[-5:]
    me = me_ref[0]
    ra, rb = radices(outer)
    per = outer // peers
    for k in range(peers):
        rows_in[me ^ k] = pieces[k][...]

    def loader(which):
        def load(n1):
            lanes = slice((n1 % per) * LANES, (n1 % per + 1) * LANES)
            return rows_in[n1 // per, which, :, lanes].astype(jnp.float32)

        return load

    load_x = loader(0)
    first_pass(load_x, keep(parts_x), outer)
    first_pass(loader(1), keep(parts_h), outer)
    chunk = rb * ROWS
    for alpha in range(ra):
        put(*second_pass(parts_x, alpha, outer, twist_ref), lhs.at[alpha], 0)
        put(*second_pass(parts_h, alpha, outer, twist_ref), lhs.at[alpha], chunk)
    for alpha in range(ra):
        both = lane_transform(lhs.at[alpha], fwd_ref)
        x, h = both[:chunk], both[chunk:]
        each = ra // SPECTRA
        spec_refs[alpha // each][0, alpha % each * chunk : (alpha % each + 1) * chunk, :] = h
        xr, xi, hr, hi = x[:, :LANES], x[:, LANES:], h[:, :LANES], h[:, LANES:]
        put_product(xr * hr - xi * hi, xr * hi + xi * hr, lhs.at[ra + alpha // 2], alpha % 2 * chunk)
    for pair in range(ra // 2):
        y = lane_transform(lhs.at[ra + pair], bwd_ref)
        for i in range(2):
            back_second_pass(y[i * chunk : (i + 1) * chunk], 2 * pair + i, outer, twist_ref, keep(parts_y))
    skip = jnp.broadcast_to(skip_ref[...], (ROWS, LANES))

    def emit(n1, value):
        mixed_ref[:, n1 * LANES : (n1 + 1) * LANES] = value + skip * load_x(n1)

    back_first_pass(parts_y, outer, emit)


def pool_rows(rows_in, mixed_ref, rows_out, row, gather_ref, lhs, per, outer):
    for n1 in range(outer):
        lanes = slice((n1 % per) * LANES, (n1 % per + 1) * LANES)
        query = rows_in[n1 // per, row : row + ROWS, lanes].astype(jnp.float32)
        mixed = mixed_ref[row : row + ROWS, n1 * LANES : (n1 + 1) * LANES]
        rows_out[n1 // per, row : row + ROWS, lanes] = mixed.astype(jnp.bfloat16)
        high, low = split(query * mixed)
        lhs[n1 * ROWS : (n1 + 1) * ROWS, :LANES] = high
        lhs[n1 * ROWS : (n1 + 1) * ROWS, LANES:] = low
    sums = dot(lhs[...], gather_ref[...])
    each = LANES // POOL
    held = LANES // each
    place = lax.broadcasted_iota(jnp.int32, (ROWS, LANES), 1) // each
    tiles = []
    for tile in range(-(-outer // held)):
        total = jnp.zeros((ROWS, LANES), jnp.float32)
        for j in range(min(held, outer - tile * held)):
            n1 = tile * held + j
            total = jnp.where(place == j, sums[n1 * ROWS : (n1 + 1) * ROWS], total)
        tiles.append(total)
    return jnp.concatenate(tiles, axis=1)


def pool_kernel(peers, outer, me_ref, *refs):
    queries = refs[:peers]
    mixed_ref, gather_ref = refs[peers : peers + 2]
    outs = refs[peers + 2 : 2 * peers + 2]
    pooled_ref, rows_in, rows_out, lhs = refs[2 * peers + 2 :]
    me = me_ref[0]
    per = outer // peers
    for k in range(peers):
        rows_in[me ^ k] = queries[k][...]
    rows = mixed_ref.shape[0]
    bins = outer * LANES // POOL
    if rows == ROWS:
        pooled = pool_rows(rows_in, mixed_ref, rows_out, 0, gather_ref, lhs.at[0], per, outer)
        pooled_ref[...] = pooled[:, :bins].astype(jnp.bfloat16)
    else:
        left = pool_rows(rows_in, mixed_ref, rows_out, 0, gather_ref, lhs.at[0], per, outer)
        right = pool_rows(rows_in, mixed_ref, rows_out, ROWS, gather_ref, lhs.at[1], per, outer)
        each = bins // peers
        for seat in range(peers):
            mine = slice(seat * each, (seat + 1) * each)
            pair = jnp.concatenate([left[:, mine], right[:, mine]], axis=1).astype(jnp.bfloat16)
            for group in range(pooled_ref.shape[0]):
                pooled_ref[group, seat] = pair
    for k in range(peers):
        outs[k][...] = rows_out[me ^ k]


def corr_kernel(peers, outer, packed, me_ref, *refs):
    if packed:
        packed_ref, refs = refs[0], refs[1:]
    queries = refs[:peers]
    refs, spec_refs = refs[: peers] + refs[peers + SPECTRA :], refs[peers : peers + SPECTRA]
    grad_ref, skip_ref, *tables, twist_ref, spread_ref = refs[peers : peers + 8]
    fwd_ref, bwd_ref = tables[:2], tables[2:]
    outs = refs[peers + 8 : 2 * peers + 8]
    rows_in, lhs_g, gated, parts_g, parts_y, lhs, rows_out = refs[2 * peers + 8 :]
    me = me_ref[0]
    ra, rb = radices(outer)
    per = outer // peers
    for k in range(peers):
        rows_in[me ^ k] = queries[k][...]
    each = LANES // POOL
    held = LANES // each
    place = lax.broadcasted_iota(jnp.int32, (ROWS, LANES), 1) // each
    zero = jnp.zeros((ROWS, LANES), jnp.float32)
    for tile in range(-(-outer // held)):
        count = min(held, outer - tile * held)
        used = count * each
        part = grad_ref[:, tile * LANES : tile * LANES + used]
        if used < LANES:
            part = jnp.concatenate([part, jnp.zeros((ROWS, LANES - used), jnp.float32)], axis=1)
        high = part.astype(jnp.bfloat16).astype(jnp.float32)
        low = part - high
        for j in range(count):
            rows = pl.ds((tile * held + j) * ROWS, ROWS)
            lhs_g[rows, :LANES] = jnp.where(place == j, high, zero).astype(jnp.bfloat16)
            lhs_g[rows, LANES:] = jnp.where(place == j, low, zero).astype(jnp.bfloat16)
    gated[...] = dot(lhs_g[...], spread_ref[...])
    for n1 in range(outer):
        lanes = slice((n1 % per) * LANES, (n1 % per + 1) * LANES)
        rows = pl.ds(n1 * ROWS, ROWS)
        gated[rows, :] = gated[rows, :] * rows_in[n1 // per, :, lanes].astype(jnp.float32)

    def load_g(n1):
        return gated[n1 * ROWS : (n1 + 1) * ROWS, :]

    first_pass(load_g, keep(parts_g), outer)
    chunk = rb * ROWS
    for alpha in range(ra):
        put(*second_pass(parts_g, alpha, outer, twist_ref), lhs.at[alpha // 2], alpha % 2 * chunk)
    for pair in range(ra // 2):
        both = lane_transform(lhs.at[pair], fwd_ref)
        for i in range(2):
            alpha = 2 * pair + i
            g = both[i * chunk : (i + 1) * chunk]
            each = ra // SPECTRA
            h = spec_refs[alpha // each][0, alpha % each * chunk : (alpha % each + 1) * chunk, :]
            gr, gi, hr, hi = g[:, :LANES], g[:, LANES:], h[:, :LANES], h[:, LANES:]
            put_product(gr * hr + gi * hi, gi * hr - gr * hi, lhs.at[ra // 2 + pair], i * chunk)
    for pair in range(ra // 2):
        y = lane_transform(lhs.at[ra // 2 + pair], bwd_ref)
        for i in range(2):
            back_second_pass(y[i * chunk : (i + 1) * chunk], 2 * pair + i, outer, twist_ref, keep(parts_y))
    skip = jnp.broadcast_to(skip_ref[...], (ROWS, LANES))

    def emit(n1, value):
        lanes = slice((n1 % per) * LANES, (n1 % per + 1) * LANES)
        rows_out[n1 // per, :, lanes] = (value + skip * load_g(n1)).astype(jnp.bfloat16)

    back_first_pass(parts_y, outer, emit)
    step, steps = pl.program_id(0), pl.num_programs(0)
    for k in range(peers):
        outs[k][:, : per * LANES] = rows_out[me ^ k]
        if packed:
            half = steps // 2
            for chunk_at in range(packed_ref.shape[1] // (half * ROWS)):
                here = pl.ds((chunk_at * half + lax.rem(step, half)) * ROWS, ROWS)
                high, low = (part.astype(jnp.float32) for part in split(packed_ref[me ^ k, here, :]))
                lanes = slice((per + chunk_at) * LANES, (per + chunk_at + 1) * LANES)
                outs[k][:, lanes] = jnp.where(step < half, high, low).astype(jnp.bfloat16)


def whole(array):
    rank = len(array.shape)
    return pl.BlockSpec(array.shape, lambda i, me: (0,) * rank)


def by_rows(width, rows=ROWS, start=0):
    return pl.BlockSpec((rows, width), lambda i, me: (start + i, 0))


def call(kernel, name, me, steps, inputs, in_specs, out_shapes, out_specs, scratch, flops, aliases=None, near=(), vmem=()):
    moved = sum(x.size * x.dtype.itemsize for x in inputs)
    moved += sum(math.prod(o.shape) * o.dtype.itemsize for o in out_shapes)
    def space(i):
        return pltpu.VMEM if i in vmem else pltpu.HBM

    count = len(inputs)
    inputs = [x if i in near else pltpu.with_memory_space_constraint(x, space(i)) for i, x in enumerate(inputs)]
    out_shapes = [
        o if count + i in near else space(count + i)(o.shape, o.dtype) for i, o in enumerate(out_shapes)
    ]
    return pl.pallas_call(
        kernel,
        name=name,
        grid_spec=pltpu.PrefetchScalarGridSpec(
            num_scalar_prefetch=1,
            grid=(steps,),
            in_specs=in_specs,
            out_specs=out_specs,
            scratch_shapes=scratch,
        ),
        out_shape=out_shapes,
        input_output_aliases=aliases or {},
        compiler_params=pltpu.CompilerParams(
            dimension_semantics=("arbitrary",), vmem_limit_bytes=VMEM_LIMIT
        ),
        cost_estimate=pl.CostEstimate(flops=int(flops), bytes_accessed=moved, transcendentals=0),
    )(me, *inputs)


def shape(dims, dtype):
    return jax.ShapeDtypeStruct(dims, dtype)


def convolve(me, pieces, skip, tables, total_rows, start, before):
    peers = len(pieces)
    rows, width = pieces[0].shape[1:]
    length = width * peers
    outer = length // LANES
    ra, rb = radices(outer)
    chunk = rb * ROWS
    steps = rows // ROWS
    first = start // ROWS
    f32, bf16 = jnp.float32, jnp.bfloat16
    fwd, bwd, twist = tables["fwd"], tables["bwd"], tables["twist"]
    inputs = [*pieces, skip, *fwd, *bwd, twist]
    in_specs = [pl.BlockSpec((2, ROWS, width), lambda i, me: (0, i, 0))] * peers + [
        by_rows(1, start=first),
        *[whole(table) for table in (*fwd, *bwd, twist)],
    ]
    aliases = {}
    if before is not None:
        aliases = {1 + len(inputs): 0}
        inputs.append(before)
        in_specs.append(pl.BlockSpec(memory_space=pl.ANY))
    parts = pltpu.VMEM((2, rb, ra, ROWS, LANES), f32)

    def kernel(*refs):
        conv_kernel(peers, outer, *refs)

    part = (1, outer * ROWS // SPECTRA, 2 * LANES)
    out = call(
        kernel, "long_convolution", me, steps, inputs, in_specs,
        [shape((total_rows, length), f32)] + [shape((steps, *part[1:]), f32)] * SPECTRA,
        [by_rows(length, start=first)] + [pl.BlockSpec(part, lambda i, me: (i, 0, 0))] * SPECTRA,
        [
            pltpu.VMEM((peers, 2, ROWS, width), bf16),
            parts,
            parts,
            parts,
            pltpu.VMEM((ra + ra // 2, 2, 2 * chunk, 2 * LANES), bf16),
        ],
        rows * outer * 0.004 * MICROSECOND, aliases, (peers,), range(peers + 6, len(inputs) + 1),
    )
    return out[0], out[1:]


def pool(me, queries, mixed, gather, groups):
    peers = len(queries)
    rows, width = queries[0].shape
    length = width * peers
    outer = length // LANES
    bins = length // POOL
    bf16 = jnp.bfloat16
    if groups:
        step = 2 * ROWS
        pooled_shape = shape((groups, peers, rows // 2, LANES), bf16)
        pooled_spec = pl.BlockSpec((groups, peers, ROWS, LANES), lambda i, me: (0, 0, i, 0))
    else:
        step = ROWS
        pooled_shape = shape((rows, bins), bf16)
        pooled_spec = by_rows(bins)

    def kernel(*refs):
        pool_kernel(peers, outer, *refs)

    out = call(
        kernel, "pool_bins", me, rows // step, [*queries, mixed, gather],
        [by_rows(width, step)] * peers + [by_rows(length, step), whole(gather)],
        [shape((rows, width), bf16)] * peers + [pooled_shape],
        [by_rows(width, step)] * peers + [pooled_spec],
        [
            pltpu.VMEM((peers, step, width), bf16),
            pltpu.VMEM((peers, step, width), bf16),
            pltpu.VMEM((step // ROWS, outer * ROWS, 2 * LANES), bf16),
        ],
        rows * outer * 0.001 * MICROSECOND, vmem=range(1, peers + 1),
    )
    return out[:peers], out[peers]


def correlate(me, queries, grad_pooled, spec, skip, tables, spread, start, packed):
    peers = len(queries)
    width = queries[0].shape[1]
    rows = spec[0].shape[0] * ROWS
    length = width * peers
    outer = length // LANES
    bins = length // POOL
    ra, rb = radices(outer)
    chunk = rb * ROWS
    first = start // ROWS
    f32, bf16 = jnp.float32, jnp.bfloat16
    fwd, bwd, twist = tables["fwd"], tables["bwd"], tables["twist"]
    in_specs = [by_rows(width, start=first)] * peers + [
        *[pl.BlockSpec((1, *part.shape[1:]), lambda i, me: (i, 0, 0)) for part in spec],
        by_rows(bins, start=first),
        by_rows(1, start=first),
        *[whole(table) for table in (*fwd, *bwd, twist, spread)],
    ]
    parts = pltpu.VMEM((2, rb, ra, ROWS, LANES), f32)
    scratch = [
        pltpu.VMEM((peers, ROWS, width), bf16),
        pltpu.VMEM((outer * ROWS, 2 * LANES), bf16),
        pltpu.VMEM((outer * ROWS, LANES), f32),
        parts,
        parts,
        pltpu.VMEM((ra, 2, 2 * chunk, 2 * LANES), bf16),
        pltpu.VMEM((peers, ROWS, width), bf16),
    ]

    def kernel(*refs):
        corr_kernel(peers, outer, packed is not None, *refs)

    inputs = [*queries, *spec, grad_pooled, skip, *fwd, *bwd, twist, spread]
    sent = width
    if packed is not None:
        sent = width + packed.shape[1] // (rows // 2) * LANES
        inputs = [packed, *inputs]
        in_specs = [whole(packed), *in_specs]
    near = len(inputs) - 8
    return call(
        kernel, "long_correlation", me, rows // ROWS, inputs, in_specs,
        [shape((rows, sent), bf16)] * peers, [by_rows(sent)] * peers,
        scratch, rows * outer * 0.004 * MICROSECOND, near=(0, near, near + 1) if packed is not None else (near, near + 1),
    )


def lay_out(me, projections, filter_taps, peers, chunk, chunks):
    last = chunk == chunks - 1
    _, channels, width = projections.shape
    pencil = channels // peers
    rows = pencil // chunks
    f32, bf16 = jnp.float32, jnp.bfloat16
    order = list(range(peers))[::-1]

    def kernel(me_ref, proj_ref, taps_ref, *refs):
        outs = refs[:peers]
        queries = refs[peers:-7]
        pair, taps, laid, passing, sems, out_sems, query_sems = refs[-7:]

        def take(k):
            block = pl.ds(pl.multiple_of((me_ref[0] ^ k) * pencil, pencil), pencil)
            return pltpu.make_async_copy(proj_ref.at[0, block], passing.at[k], query_sems.at[k, 0])

        def hand_on(k):
            return pltpu.make_async_copy(passing.at[k], queries[k], query_sems.at[k, 1])


        def fetch(k):
            here = pl.ds(pl.multiple_of((me_ref[0] ^ k) * pencil + chunk * rows, rows), rows)
            return (
                pltpu.make_async_copy(proj_ref.at[1, here], pair.at[k, 0], sems.at[k, 0]),
                pltpu.make_async_copy(proj_ref.at[2, here], pair.at[k, 1], sems.at[k, 1]),
                pltpu.make_async_copy(taps_ref.at[here], taps.at[k], sems.at[k, 2]),
            )

        def leave(k):
            return pltpu.make_async_copy(laid.at[k], outs[k], out_sems.at[k])

        for k in order:
            for copy in fetch(k):
                copy.start()
        for k in range(len(queries)):
            take(k).start()
        for k in order:
            keyed, valued, lags = fetch(k)
            keyed.wait()
            valued.wait()
            laid[k, 0] = (pair[k, 0].astype(f32) * pair[k, 1].astype(f32)).astype(bf16)
            lags.wait()
            laid[k, 1] = taps[k].astype(bf16)
            leave(k).start()
        for k in range(len(queries)):
            take(k).wait()
            hand_on(k).start()
        for k in order:
            leave(k).wait()
        for k in range(len(queries)):
            hand_on(k).wait()

    out_shapes = [shape((2, rows, width), bf16)] * peers
    if last:
        out_shapes += [shape((pencil, width), bf16)] * peers
    return call(
        kernel, "lay_out", me, 1, [projections, filter_taps],
        [pl.BlockSpec(memory_space=pltpu.HBM)] * 2,
        out_shapes,
        [pl.BlockSpec(memory_space=pltpu.HBM)] * len(out_shapes),
        [
            pltpu.VMEM((peers, 2, rows, width), bf16),
            pltpu.VMEM((peers, rows, width), f32),
            pltpu.VMEM((peers, 2, rows, width), bf16),
            pltpu.VMEM((peers, pencil, width), bf16),
            pltpu.SemaphoreType.DMA((peers, 3)),
            pltpu.SemaphoreType.DMA((peers,)),
            pltpu.SemaphoreType.DMA((peers, 2)),
        ],
        rows * peers * 0.015 * MICROSECOND,
    )


def by_track(me, head_weight, groups):
    channels, tracks = head_weight.shape
    half, own = channels // 2, tracks // groups
    padded = -(-own // LANES) * LANES
    dtype = head_weight.dtype
    steps = half // ROWS

    def kernel(me_ref, weight_ref, out_ref, rows_in, sems):
        first = pl.multiple_of((me_ref[0] & 1) * half, half)

        def fetch(i):
            return pltpu.make_async_copy(
                weight_ref.at[pl.ds(first + i * ROWS, ROWS)], rows_in.at[pl.ds(i * ROWS, ROWS)], sems.at[i]
            )

        for i in range(steps):
            fetch(i).start()
        for i in range(steps):
            fetch(i).wait()
        for group in range(groups):
            out_ref[group, :, :own] = rows_in[:, group * own : (group + 1) * own]
            if padded > own:
                out_ref[group, :, own:] = jnp.zeros((half, padded - own), dtype)

    out = shape((groups, half, padded), dtype)
    return call(
        kernel, "by_track", me, 1, [head_weight], [pl.BlockSpec(memory_space=pltpu.HBM)], [out], [whole(out)],
        [pltpu.VMEM((half, tracks), dtype), pltpu.SemaphoreType.DMA((steps,))], 2 * MICROSECOND, vmem=(1,),
    )[0]


def weight_pair(weight_ref, seats, pencil, own):
    groups, _, padded = weight_ref.shape
    rows = weight_ref[...].reshape(groups, seats, pencil // (2 * ROWS), 2, ROWS, padded)
    count = groups * seats * pencil // 2
    left, right = rows[:, :, :, 0].reshape(count, padded), rows[:, :, :, 1].reshape(count, padded)
    return left[:, :own], right[:, :own]


def head_rates(me, got, mine, other, bias, counts):
    groups, peers, half_rows, _ = got.shape
    own = counts.shape[1]
    seats = peers // 2
    pencil = 2 * half_rows
    bins = LANES // 2
    f32 = jnp.float32

    def kernel(me_ref, got_ref, mine_ref, other_ref, bias_ref, counts_ref, logits_ref, sums_ref):
        odd = me_ref[0] & 1
        total = jnp.broadcast_to(bias_ref[...], (bins, own))
        for weight_ref, place in ((mine_ref, odd), (other_ref, 1 - odd)):
            block = got_ref[:, pl.ds(place * seats, seats)].reshape(groups * seats * half_rows, LANES)
            turned = block.astype(f32).T.astype(jnp.bfloat16)
            left, right = weight_pair(weight_ref, seats, pencil, own)
            total = total + dot(turned[:bins], left) + dot(turned[bins:], right)
        logits_ref[...] = total
        rates = jax.nn.softplus(total) + rate_floor
        observed = counts_ref[...].astype(f32)
        sums_ref[0:1, :] = jnp.sum(rates, axis=0, keepdims=True)
        sums_ref[1:2, :] = jnp.sum(observed, axis=0, keepdims=True)
        sums_ref[2:3, :] = jnp.sum(observed * jnp.log(rates), axis=0, keepdims=True)
        sums_ref[3:8, :] = jnp.zeros((5, own), f32)

    inputs = [got, mine, other, bias, counts]
    return call(
        kernel, "head_rates", me, 1, inputs, [whole(x) for x in inputs],
        [shape((bins, own), f32), shape((8, own), f32)],
        [pl.BlockSpec((bins, own), lambda i, me: (0, 0)), pl.BlockSpec((8, own), lambda i, me: (0, 0))],
        [], 2 * bins * groups * peers * pencil * own, near=range(7),
    )


def head_grads(me, logits, sums, mine, other, counts):
    groups, half, _ = mine.shape
    own = counts.shape[1]
    peers = len(sums)
    seats = peers // 2
    pencil = half // seats
    bins = LANES // 2
    f32, bf16 = jnp.float32, jnp.bfloat16

    def kernel(me_ref, logits_ref, *refs):
        sums_refs = refs[:peers]
        mine_ref, other_ref, counts_ref, out_ref, loss_ref = refs[peers:]
        odd = me_ref[0] & 1
        totals = [ref[...] for ref in sums_refs]
        while len(totals) > 1:
            totals = [totals[i] + totals[i + 1] for i in range(0, len(totals), 2)]
        totals = totals[0]
        pred_total, obs_total, log_sum = totals[0:1], totals[1:2], totals[2:3]
        log_pred = jnp.log(pred_total)
        terms = total_weight * (pred_total - obs_total * log_pred) + obs_total * log_pred - log_sum
        mean = jnp.sum(terms, axis=1, keepdims=True) / (peers * bins * groups * own)
        loss_ref[...] = jnp.broadcast_to(mean, loss_ref.shape)
        ratio = obs_total / pred_total
        logits_here = logits_ref[...]
        rates = jax.nn.softplus(logits_here) + rate_floor
        observed = counts_ref[...].astype(f32)
        grad_rates = total_weight * (1.0 - ratio) + ratio - observed / rates
        grads = (grad_rates * jax.nn.sigmoid(logits_here)).astype(bf16)
        none = jnp.zeros_like(grads)
        in_left = jnp.concatenate([grads, none], axis=0)
        in_right = jnp.concatenate([none, grads], axis=0)
        across = (((1,), (1,)), ((), ()))
        for weight_ref, place in ((mine_ref, odd), (other_ref, 1 - odd)):
            left, right = weight_pair(weight_ref, seats, pencil, own)
            part = lax.dot_general(left, in_left, across, preferred_element_type=f32)
            part = part + lax.dot_general(right, in_right, across, preferred_element_type=f32)
            out_ref[:, pl.ds(place * seats, seats)] = part.astype(bf16).reshape(groups, seats, pencil // 2, LANES)

    inputs = [logits, *sums, mine, other, counts]
    out = shape((groups, peers, pencil // 2, LANES), bf16)
    return call(
        kernel, "head_grads", me, 1, inputs, [whole(x) for x in inputs],
        [out, shape((8, LANES), f32)],
        [whole(out), pl.BlockSpec((8, LANES), lambda i, me: (0, 0))],
        [], 4 * bins * groups * peers * pencil * own, near=(*range(peers + 4), peers + 5),
    )


def sum_grads(me, back):
    groups, peers, half_rows, _ = back.shape
    bins = LANES // 2
    f32 = jnp.float32

    def kernel(me_ref, back_ref, rows_ref, packed_ref):
        for seat in range(peers):
            total = back_ref[0, seat].astype(f32)
            for group in range(1, groups):
                total = total + back_ref[group, seat].astype(f32)
            packed_ref[seat] = total
            for i in range(half_rows // ROWS):
                pair = total[i * ROWS : (i + 1) * ROWS]
                lanes = slice(seat * bins, (seat + 1) * bins)
                rows_ref[2 * i * ROWS : (2 * i + 1) * ROWS, lanes] = pair[:, :bins]
                rows_ref[(2 * i + 1) * ROWS : (2 * i + 2) * ROWS, lanes] = pair[:, bins:]

    rows, packed = shape((2 * half_rows, peers * bins), f32), shape((peers, half_rows, LANES), f32)
    return call(
        kernel, "sum_grads", me, 1, [back], [whole(back)], [rows, packed], [whole(rows), whole(packed)], [], back.size,
        near=(0, 1, 2),
    )


def finish(me, projections, mixed_home, corr_home, spread, chunk, chunks, before, loss):
    peers = len(corr_home)
    _, channels, width = projections.shape
    pencil = channels // peers
    rows = pencil // chunks
    tiles = width // LANES
    each = LANES // POOL
    f32, bf16 = jnp.float32, jnp.bfloat16
    with_query = bool(mixed_home)
    payload = corr_home[0].shape[1]

    def kernel(me_ref, spread_ref, proj_ref, *refs):
        mixed_refs, corr_refs = refs[: len(mixed_home)], refs[len(mixed_home) : len(mixed_home) + peers]
        pair, mixed_in, corr_in, done, query_done, lhs, sems, out_sems = refs[-8:]
        if loss:
            loss_ref, mean_ref = refs[len(mixed_home) + peers], refs[-9]
            mean_ref[...] = loss_ref[0:1, 0:1]
        out_ref = refs[-9 - len(loss)]
        place = lax.broadcasted_iota(jnp.int32, (ROWS, LANES), 1) // each
        zero = jnp.zeros((ROWS, LANES), f32)

        def block(k, start, count):
            return pl.ds(pl.multiple_of((me_ref[0] ^ k) * pencil + start, ROWS), count)

        def here(k):
            return block(k, chunk * rows, rows)

        def fetch(k):
            return (
                pltpu.make_async_copy(corr_refs[k], corr_in.at[k], sems.at[k, 0]),
                pltpu.make_async_copy(proj_ref.at[1, here(k)], pair.at[k, 0], sems.at[k, 1]),
                pltpu.make_async_copy(proj_ref.at[2, here(k)], pair.at[k, 1], sems.at[k, 2]),
            )

        def fetch_mixed(k):
            return pltpu.make_async_copy(mixed_refs[k], mixed_in.at[k], sems.at[k, 3])

        def leave(k, plane):
            if plane == 0:
                return pltpu.make_async_copy(query_done.at[k], out_ref.at[0, block(k, 0, pencil)], out_sems.at[k, 0])
            return pltpu.make_async_copy(done.at[k, plane - 1], out_ref.at[plane, here(k)], out_sems.at[k, plane])

        for k in range(peers):
            for copy in fetch(k):
                copy.start()
            if with_query:
                fetch_mixed(k).start()
        for k in range(peers):
            for copy in fetch(k):
                copy.wait()
            corr = corr_in[k, :, :width].astype(f32)
            done[k, 0] = corr * pair[k, 1].astype(f32)
            leave(k, 1).start()
            done[k, 1] = corr * pair[k, 0].astype(f32)
            leave(k, 2).start()
            if not with_query:
                continue
            fetch_mixed(k).wait()
            for i in range(pencil // ROWS):
                part = slice(i * ROWS, (i + 1) * ROWS)
                inside = i % (rows // ROWS)
                source = inside // 2 * ROWS
                lanes = slice(width + i // (rows // ROWS) * LANES, width + (i // (rows // ROWS) + 1) * LANES)
                high = corr_in[k, source : source + ROWS, lanes].astype(f32)
                low = corr_in[k, rows // 2 + source : rows // 2 + source + ROWS, lanes].astype(f32)
                for t in range(tiles):
                    near = place == t + inside % 2 * tiles
                    lhs[i, t * ROWS : (t + 1) * ROWS, :LANES] = jnp.where(near, high, zero).astype(bf16)
                    lhs[i, t * ROWS : (t + 1) * ROWS, LANES:] = jnp.where(near, low, zero).astype(bf16)
                grad = dot(lhs[i], spread_ref[...])
                for t in range(tiles):
                    at = slice(t * LANES, (t + 1) * LANES)
                    query_done[k, part, at] = grad[t * ROWS : (t + 1) * ROWS] * mixed_in[k, part, at].astype(f32)
            leave(k, 0).start()
        for k in range(peers):
            for plane in range(0 if with_query else 1, 3):
                leave(k, plane).wait()

    inputs = [spread, projections, *mixed_home, *corr_home, *loss]
    in_specs = [whole(spread), pl.BlockSpec(memory_space=pltpu.HBM)]
    in_specs += [pl.BlockSpec(memory_space=pl.ANY)] * (len(mixed_home) + peers)
    in_specs += [whole(x) for x in loss]
    near = (0, *range(2, len(inputs)))
    aliases = {}
    if before is not None:
        aliases = {1 + len(inputs): 0}
        inputs.append(before)
        in_specs.append(pl.BlockSpec(memory_space=pl.ANY))
    return call(
        kernel, "finish", me, 1, inputs, in_specs,
        [shape((3, channels, width), f32)] + [shape((1, 1), f32)] * len(loss),
        [pl.BlockSpec(memory_space=pltpu.HBM)] + [pl.BlockSpec((1, 1), lambda i, me: (0, 0))] * len(loss),
        [
            pltpu.VMEM((peers, 2, rows, width), bf16),
            pltpu.VMEM((peers, pencil if with_query else ROWS, width), bf16),
            pltpu.VMEM((peers, rows, payload), bf16),
            pltpu.VMEM((peers, 2, rows, width), f32),
            pltpu.VMEM((peers, pencil if with_query else ROWS, width), f32),
            pltpu.VMEM((pencil // ROWS, tiles * ROWS, 2 * LANES), bf16),
            pltpu.SemaphoreType.DMA((peers, 4)),
            pltpu.SemaphoreType.DMA((peers, 3)),
        ],
        rows * peers * 0.03 * MICROSECOND, aliases, near=near,
    )


def swap(value, k, count):
    if k == 0:
        return value
    return lax.ppermute(value, "seq", [(i, i ^ k) for i in range(count)])


def pad_rows(value, rows):
    short = rows - value.shape[-2]
    if short == 0:
        return value
    widths = [(0, 0)] * value.ndim
    widths[-2] = (0, short)
    return jnp.pad(value, widths)


def aligned(projections, filter_taps, skip_gain, head_weight, head_bias, counts):
    f32 = jnp.float32
    _, channels, width = projections.shape
    peers = lax.axis_size("seq")
    groups = lax.axis_size("chan")
    seat = lax.axis_index("seq")
    group = lax.axis_index("chan")
    bins = width // POOL
    length = width * peers
    tracks = head_weight.shape[1]
    own_tracks = tracks // groups
    pencil = channels // peers
    chunks = CHUNKS
    rows = pencil // chunks
    me = jnp.asarray(seat, jnp.int32).reshape(1)
    tables = transform_tables(length)
    gather, spread = pool_tables()

    laid, me_next = [], me
    for j in range(chunks):
        laid.append(lay_out(me_next, projections, filter_taps, peers, j, chunks))
        me_next, _ = lax.optimization_barrier((me, laid[j]))
    pieces = [[swap(laid[j][k], k, peers) for k in range(peers)] for j in range(chunks)]
    held_back, _ = lax.optimization_barrier((laid[-1][peers:], pieces[0]))
    queries = [swap(held_back[k], k, peers) for k in range(peers)]
    skip = lax.dynamic_index_in_dim(skip_gain.reshape(peers, pencil, 1), seat, axis=0, keepdims=False)

    mine = by_track(me_next, head_weight, groups)
    mine = lax.all_to_all(mine, "chan", split_axis=0, concat_axis=0, tiled=True)

    mixed, specs = None, []
    for j in range(chunks):
        mixed, spec = convolve(me, pieces[j], skip, tables, pencil, j * rows, mixed)
        specs.append(spec)
    mixed_out, sent = pool(me, queries, mixed, gather, groups)
    mixed_home = [swap(mixed_out[k], k, peers) for k in range(peers)]

    def exchange(blocks):
        flat = blocks.reshape(groups * peers, pencil // 2, LANES)
        flat = lax.all_to_all(flat, ("chan", "seq"), split_axis=0, concat_axis=0, tiled=True)
        return flat.reshape(blocks.shape)

    got = exchange(sent)
    mine, _ = lax.optimization_barrier((mine, sent))
    other = swap(mine, 1, peers)
    own_bias = lax.dynamic_slice_in_dim(head_bias, group * own_tracks, own_tracks).reshape(1, own_tracks)
    own_counts = lax.dynamic_slice_in_dim(counts, group * own_tracks, own_tracks, axis=1)
    logits, sums = head_rates(me, got, mine, other, own_bias, own_counts)
    all_sums = [swap(sums, k, peers) for k in range(peers)]
    early, late = mixed_home[: peers - 1], mixed_home[peers - 1 :]
    logits, early = lax.optimization_barrier((logits, early))
    part, loss = head_grads(me, logits, all_sums, mine, other, own_counts)
    back = exchange(part)

    step = 1
    while step < groups:
        loss = loss + lax.ppermute(loss, "chan", [(i, i ^ step) for i in range(groups)])
        step *= 2

    back, loss, late = lax.optimization_barrier((back, loss, late))
    mixed_home = [*early, *late]
    grad_rows, packed = sum_grads(me, back)
    grads = None
    corr_home = []
    for j in range(chunks):
        corr = correlate(me, queries, grad_rows, specs[j], skip, tables, spread, j * rows, None if j else packed)
        grad_rows, _ = lax.optimization_barrier((grad_rows, corr))
        corr_home.append([swap(corr[k], k, peers) for k in range(peers)])
    for j in range(chunks):
        ours = [] if j else mixed_home
        grads, *rest = finish(me, projections, ours, corr_home[j], spread, j, chunks, grads, [] if j else [loss])
        if not j:
            mean_loss = rest[0].reshape(())
    return mean_loss, grads


def power_of_two(value):
    return value & (value - 1) == 0


def per_device(projections, filter_taps, skip_gain, head_weight, head_bias, counts):
    channels, width = projections.shape[1:]
    peers, groups = lax.axis_size("seq"), lax.axis_size("chan")
    pencil = channels // peers
    fits = (
        pencil % (2 * ROWS * CHUNKS) == 0
        and 2 * (width // POOL) == LANES
        and power_of_two(peers)
        and peers > 1
        and power_of_two(groups)
        and groups <= MOST_GROUPS
    )
    run = aligned if fits else general
    return run(projections, filter_taps, skip_gain, head_weight, head_bias, counts)


def general(projections, filter_taps, skip_gain, head_weight, head_bias, counts):
    f32, bf16 = jnp.float32, jnp.bfloat16
    _, channels, width = projections.shape
    peers = lax.axis_size("seq")
    groups = lax.axis_size("chan")
    seat = lax.axis_index("seq")
    group = lax.axis_index("chan")
    bins = width // POOL
    length = width * peers
    tracks = head_weight.shape[1]
    own_tracks = tracks // groups
    pencil = channels // peers
    rows = -(-pencil // ROWS) * ROWS
    me = jnp.asarray(seat, jnp.int32).reshape(1)
    tables = transform_tables(length)
    gather, spread = pool_tables()

    def block(array, k):
        return lax.dynamic_index_in_dim(array, seat ^ k, axis=-3, keepdims=False)

    query = projections[0]
    key_value = projections[1].astype(f32) * projections[2].astype(f32)
    stacked = jnp.stack([key_value.astype(bf16), filter_taps.astype(bf16)])
    stacked = stacked.reshape(2, peers, pencil, width)
    pieces = [pad_rows(swap(block(stacked, k), k, peers), rows) for k in range(peers)]
    query_blocks = query.reshape(peers, pencil, width)
    queries = [pad_rows(swap(block(query_blocks, k), k, peers), rows) for k in range(peers)]
    skip = pad_rows(block(skip_gain.reshape(peers, pencil, 1), 0), rows)

    half = channels // 2
    by_track = head_weight.reshape(2, half, groups, own_tracks).transpose(0, 2, 1, 3)
    mine = lax.dynamic_index_in_dim(by_track, seat & 1, axis=0, keepdims=False)
    mine = lax.all_to_all(mine, "chan", split_axis=0, concat_axis=0, tiled=True)
    other = swap(mine, 1, peers)
    mine = mine.reshape(groups * half, own_tracks)
    other = other.reshape(groups * half, own_tracks)

    mixed, spec = convolve(me, pieces, skip, tables, rows, 0, None)
    mixed_out, pooled = pool(me, queries, mixed, gather, 0)
    pooled = pooled[:pencil]
    mixed_home = [swap(mixed_out[k][:pencil], k, peers) for k in range(peers)]

    sent = pooled.reshape(pencil, peers, bins).transpose(1, 0, 2)
    sent = jnp.broadcast_to(sent[None], (groups, peers, pencil, bins))
    got = lax.all_to_all(
        sent.reshape(groups * peers, pencil, bins), ("chan", "seq"), split_axis=0, concat_axis=0, tiled=True
    )
    got = got.reshape(groups, 2, half, bins)
    low_half = got[:, 0].reshape(groups * half, bins)
    high_half = got[:, 1].reshape(groups * half, bins)
    odd = (seat & 1) == 1
    pooled_mine = jnp.where(odd, high_half, low_half)
    pooled_other = jnp.where(odd, low_half, high_half)

    def project(x, w):
        return lax.dot_general(x, w, (((0,), (0,)), ((), ())), preferred_element_type=f32)

    own_bias = lax.dynamic_slice_in_dim(head_bias, group * own_tracks, own_tracks)
    own_counts = lax.dynamic_slice_in_dim(counts, group * own_tracks, own_tracks, axis=1)
    logits = project(pooled_mine, mine) + project(pooled_other, other) + own_bias[None, :]
    rates = jax.nn.softplus(logits) + rate_floor
    observed = own_counts.astype(f32)
    partial_sums = jnp.stack(
        [jnp.sum(rates, axis=0), jnp.sum(observed, axis=0), jnp.sum(observed * jnp.log(rates), axis=0)]
    )
    pred_total, obs_total, log_sum = jnp.sum(lax.all_gather(partial_sums, "seq"), axis=0)
    log_pred = jnp.log(pred_total)
    loss_part = jnp.sum(
        total_weight * (pred_total - obs_total * log_pred) + obs_total * log_pred - log_sum
    )
    mean_loss = lax.psum(loss_part, "chan") / (bins * peers * tracks)
    ratio = obs_total / pred_total
    grad_rates = total_weight * (1.0 - ratio)[None, :] + ratio[None, :] - observed / rates
    grad_logits = (grad_rates * jax.nn.sigmoid(logits)).astype(bf16)

    def spread_back(w):
        return lax.dot_general(w, grad_logits, (((1,), (1,)), ((), ())), preferred_element_type=f32)

    part_mine = spread_back(mine).astype(bf16).reshape(groups, 1, half, bins)
    part_other = spread_back(other).astype(bf16).reshape(groups, 1, half, bins)
    part = jnp.concatenate(
        [jnp.where(odd, part_other, part_mine), jnp.where(odd, part_mine, part_other)], axis=1
    )
    back = lax.all_to_all(
        part.reshape(groups * peers, pencil, bins), ("chan", "seq"), split_axis=0, concat_axis=0, tiled=True
    )
    grad_pooled = jnp.sum(back.reshape(groups, peers, pencil, bins).astype(f32), axis=0)
    grad_home = [swap(block(grad_pooled, k), k, peers) for k in range(peers)]
    grad_rows = pad_rows(grad_pooled.transpose(1, 0, 2).reshape(pencil, peers * bins), rows)

    corr_out = correlate(me, queries, grad_rows, spec, skip, tables, spread, 0, None)
    corr_home = [swap(corr_out[k][:pencil], k, peers) for k in range(peers)]

    def assemble(parts):
        out = jnp.zeros((peers,) + parts[0].shape, parts[0].dtype)
        for k, part in enumerate(parts):
            out = lax.dynamic_update_index_in_dim(out, part, seat ^ k, axis=0)
        return out.reshape((channels,) + parts[0].shape[1:])

    grad_output = jnp.repeat(assemble(grad_home) / POOL, POOL, axis=1)
    grad_kv = assemble(corr_home).astype(f32)
    grad_query = grad_output * assemble(mixed_home).astype(f32)
    grads = jnp.stack(
        [grad_query, grad_kv * projections[2].astype(f32), grad_kv * projections[1].astype(f32)], axis=0
    )
    return mean_loss, grads


def solution(mesh):
    placed = (
        P(None, "chan", "seq"),
        P("chan", "seq"),
        P("chan"),
        P("chan", None),
        P(),
        P("seq", None),
    )
    return jax.shard_map(
        per_device,
        mesh=mesh,
        in_specs=placed,
        out_specs=(P(), P(None, "chan", "seq")),
        check_vma=False,
    )
```

```python
import math

import jax
import jax.numpy as jnp
import ml_dtypes
import numpy as np
from jax import lax
from jax.experimental import pallas as pl
from jax.experimental.pallas import tpu as pltpu
from jax.sharding import PartitionSpec as P

POOL = 32
LANES = 128
ROWS = 16
SHIFT = 0.25

total_weight = 0.2
rate_floor = 0.5

MICROSECOND = 1.0e9

VMEM_LIMIT = 20 * 1024 * 1024
CHUNKS = 2
SPECTRA = 4
MOST_GROUPS = 16


def split_bf16(table):
    high = table.astype(ml_dtypes.bfloat16)
    low = (table - high.astype(np.float64)).astype(ml_dtypes.bfloat16)
    return high, low


def kind_scale(table):
    values = np.unique(np.abs(table))
    factors = np.linspace(1.0, 2.0, 4001)

    def lost(factor):
        scaled = table[: LANES // 2] * factor
        return np.sum((scaled - split_bf16(scaled)[0].astype(np.float64)) ** 2) / factor**2

    rough = [np.sum((values * f - split_bf16(values * f)[0].astype(np.float64)) ** 2) / f**2 for f in factors]
    best = np.argsort(rough, kind="stable")[:8]
    return float(min((factors[i] for i in best), key=lost))


def radices(outer):
    first = 1
    while first * first < outer:
        first *= 2
    return first, outer // first


def transform_tables(length):
    outer = length // LANES
    idx = np.arange(LANES)
    angle = 2.0 * np.pi * (np.outer(idx, idx) % LANES) / LANES
    wr, wi = np.cos(angle), -np.sin(angle)
    forward = np.block([[wr, wi], [-wi, wr]])
    backward = np.block([[wr, -wi], [wi, wr]]) / length
    k1 = np.arange(outer)[:, None]
    twist = 2.0 * np.pi * (k1 - SHIFT) * idx[None, :] / length
    scale = kind_scale(forward)
    f_hi, f_lo = split_bf16(forward)
    b_hi, b_lo = split_bf16(backward)
    return dict(
        fwd=[f_hi, f_lo],
        bwd=[b_hi, b_lo],
        scale=scale,
        fwd_scaled=[split_bf16(forward * scale)[0]],
        bwd_scaled=[split_bf16(backward * scale)[0]],
        twist=np.stack([np.cos(twist), -np.sin(twist)]).astype(np.float32),
    )


def pool_tables():
    per = LANES // POOL
    lane = np.arange(LANES)
    hit = (lane[:, None] // POOL) == (lane[None, :] % per)
    gather = np.concatenate([hit, hit], axis=0) / POOL
    spread = np.concatenate([hit.T, hit.T], axis=0) / POOL
    return gather.astype(ml_dtypes.bfloat16), spread.astype(ml_dtypes.bfloat16)


def times(value, angle):
    re, im = value
    c, s = math.cos(angle), math.sin(angle)
    tiny = 1e-12
    if im is None:
        if abs(s) < tiny and c > 0:
            return (re, None)
        return (re * c, re * s)
    if abs(s) < tiny:
        return (re, im) if c > 0 else (-re, -im)
    if abs(c) < tiny:
        return (-im, re) if s > 0 else (im, -re)
    return (re * c - im * s, re * s + im * c)


def add(a, b):
    if a[1] is None and b[1] is None:
        return (a[0] + b[0], None)
    if a[1] is None:
        return (a[0] + b[0], b[1])
    if b[1] is None:
        return (a[0] + b[0], a[1])
    return (a[0] + b[0], a[1] + b[1])


def sub(a, b):
    if a[1] is None and b[1] is None:
        return (a[0] - b[0], None)
    if a[1] is None:
        return (a[0] - b[0], -b[1])
    if b[1] is None:
        return (a[0] - b[0], a[1])
    return (a[0] - b[0], a[1] - b[1])


def small_dft(values, sign):
    count = len(values)
    if count == 1:
        return values
    even = small_dft(values[0::2], sign)
    odd = small_dft(values[1::2], sign)
    out = [None] * count
    half = count // 2
    for k in range(half):
        turned = times(odd[k], sign * 2.0 * math.pi * k / count)
        out[k] = add(even[k], turned)
        out[k + half] = sub(even[k], turned)
    return out


def dot(a, b):
    return jnp.dot(a, b, preferred_element_type=jnp.float32)


def split(value):
    high = value.astype(jnp.bfloat16)
    return high, (value - high.astype(jnp.float32)).astype(jnp.bfloat16)


def put(re_parts, im_parts, lhs, start):
    for i, (re, im) in enumerate(zip(re_parts, im_parts)):
        rows = pl.ds(start + i * ROWS, ROWS)
        re_hi, re_lo = split(re)
        im_hi, im_lo = split(im)
        lhs[0, rows, :LANES] = re_hi
        lhs[0, rows, LANES:] = im_hi
        lhs[1, rows, :LANES] = re_lo
        lhs[1, rows, LANES:] = im_lo


def lane_transform(lhs, table_refs):
    high = lhs[0]
    if len(table_refs) == 1:
        table = table_refs[0][...]
        return dot(high, table) + dot(lhs[1], table)
    table_high, table_low = table_refs[0][...], table_refs[1][...]
    return dot(high, table_high) + (dot(lhs[1], table_high) + dot(high, table_low))


def first_pass(load, store, outer):
    ra, rb = radices(outer)
    for b in range(rb):
        values = [times((load(rb * a + b), None), 2.0 * math.pi * a * SHIFT / ra) for a in range(ra)]
        out = small_dft(values, -1)
        for alpha in range(ra):
            re, im = times(out[alpha], -2.0 * math.pi * b * (alpha - SHIFT) / outer)
            store(b, alpha, re, im)


def second_pass(parts, alpha, outer, twist_ref):
    ra, rb = radices(outer)
    values = [(parts[0, b, alpha], parts[1, b, alpha]) for b in range(rb)]
    out = small_dft(values, -1)
    res, ims = [], []
    for beta in range(rb):
        k1 = alpha + ra * beta
        tr = twist_ref[0, k1 : k1 + 1, :]
        ti = twist_ref[1, k1 : k1 + 1, :]
        re, im = out[beta]
        res.append(re * tr - im * ti)
        ims.append(re * ti + im * tr)
    return res, ims


def back_second_pass(spectrum, alpha, outer, twist_ref, store):
    ra, rb = radices(outer)
    values = []
    for beta in range(rb):
        k1 = alpha + ra * beta
        tr = twist_ref[0, k1 : k1 + 1, :]
        ti = twist_ref[1, k1 : k1 + 1, :]
        re = spectrum[beta * ROWS : (beta + 1) * ROWS, :LANES]
        im = spectrum[beta * ROWS : (beta + 1) * ROWS, LANES:]
        values.append((re * tr + im * ti, im * tr - re * ti))
    out = small_dft(values, +1)
    for b in range(rb):
        re, im = times(out[b], 2.0 * math.pi * b * (alpha - SHIFT) / outer)
        store(b, alpha, re, im)


def back_first_pass(parts, outer, emit, scale=1.0):
    ra, rb = radices(outer)
    for b in range(rb):
        values = [(parts[0, b, alpha], parts[1, b, alpha]) for alpha in range(ra)]
        out = small_dft(values, +1)
        for a in range(ra):
            angle = -2.0 * math.pi * a * SHIFT / ra
            re, im = out[a]
            c, s = math.cos(angle) * scale, math.sin(angle) * scale
            if a == 0:
                emit(rb * a + b, re if scale == 1.0 else re * scale)
            else:
                emit(rb * a + b, re * c - im * s)


def put_product(re, im, lhs, start):
    rows = [slice(i, i + ROWS) for i in range(0, re.shape[0], ROWS)]
    put([re[r] for r in rows], [im[r] for r in rows], lhs, start)


def keep(parts):
    def store(b, alpha, re, im):
        parts[0, b, alpha] = re
        parts[1, b, alpha] = im

    return store


def conv_kernel(peers, outer, me_ref, *refs):
    pieces = refs[:peers]
    skip_ref, *tables, twist_ref = refs[peers : peers + 6]
    fwd_ref, bwd_ref = tables[:2], tables[2:]
    mixed_ref = refs[-6 - SPECTRA]
    spec_refs = refs[-5 - SPECTRA : -5]
    rows_in, parts_x, parts_h, parts_y, lhs = refs[-5:]
    me = me_ref[0]
    ra, rb = radices(outer)
    per = outer // peers
    for k in range(peers):
        rows_in[me ^ k] = pieces[k][...]

    def loader(which):
        def load(n1):
            lanes = slice((n1 % per) * LANES, (n1 % per + 1) * LANES)
            return rows_in[n1 // per, which, :, lanes].astype(jnp.float32)

        return load

    load_x = loader(0)
    first_pass(load_x, keep(parts_x), outer)
    first_pass(loader(1), keep(parts_h), outer)
    chunk = rb * ROWS
    for alpha in range(ra):
        put(*second_pass(parts_x, alpha, outer, twist_ref), lhs.at[alpha], 0)
        put(*second_pass(parts_h, alpha, outer, twist_ref), lhs.at[alpha], chunk)
    for alpha in range(ra):
        both = lane_transform(lhs.at[alpha], fwd_ref)
        x, h = both[:chunk], both[chunk:]
        each = ra // SPECTRA
        spec_refs[alpha // each][0, alpha % each * chunk : (alpha % each + 1) * chunk, :] = h
        xr, xi, hr, hi = x[:, :LANES], x[:, LANES:], h[:, :LANES], h[:, LANES:]
        put_product(xr * hr - xi * hi, xr * hi + xi * hr, lhs.at[ra + alpha // 2], alpha % 2 * chunk)
    for pair in range(ra // 2):
        y = lane_transform(lhs.at[ra + pair], bwd_ref)
        for i in range(2):
            back_second_pass(y[i * chunk : (i + 1) * chunk], 2 * pair + i, outer, twist_ref, keep(parts_y))
    skip = jnp.broadcast_to(skip_ref[...], (ROWS, LANES))

    def emit(n1, value):
        mixed_ref[:, n1 * LANES : (n1 + 1) * LANES] = value + skip * load_x(n1)

    back_first_pass(parts_y, outer, emit)


def pool_rows(rows_in, mixed_ref, rows_out, row, gather_ref, lhs, per, outer):
    for n1 in range(outer):
        lanes = slice((n1 % per) * LANES, (n1 % per + 1) * LANES)
        query = rows_in[n1 // per, row : row + ROWS, lanes].astype(jnp.float32)
        mixed = mixed_ref[row : row + ROWS, n1 * LANES : (n1 + 1) * LANES]
        rows_out[n1 // per, row : row + ROWS, lanes] = mixed.astype(jnp.bfloat16)
        high, low = split(query * mixed)
        lhs[n1 * ROWS : (n1 + 1) * ROWS, :LANES] = high
        lhs[n1 * ROWS : (n1 + 1) * ROWS, LANES:] = low
    sums = dot(lhs[...], gather_ref[...])
    each = LANES // POOL
    held = LANES // each
    place = lax.broadcasted_iota(jnp.int32, (ROWS, LANES), 1) // each
    tiles = []
    for tile in range(-(-outer // held)):
        total = jnp.zeros((ROWS, LANES), jnp.float32)
        for j in range(min(held, outer - tile * held)):
            n1 = tile * held + j
            total = jnp.where(place == j, sums[n1 * ROWS : (n1 + 1) * ROWS], total)
        tiles.append(total)
    return jnp.concatenate(tiles, axis=1)


def pool_kernel(peers, outer, me_ref, *refs):
    queries = refs[:peers]
    mixed_ref, gather_ref = refs[peers : peers + 2]
    outs = refs[peers + 2 : 2 * peers + 2]
    pooled_ref, rows_in, rows_out, lhs = refs[2 * peers + 2 :]
    me = me_ref[0]
    per = outer // peers
    for k in range(peers):
        rows_in[me ^ k] = queries[k][...]
    rows = mixed_ref.shape[0]
    bins = outer * LANES // POOL
    if rows == ROWS:
        pooled = pool_rows(rows_in, mixed_ref, rows_out, 0, gather_ref, lhs.at[0], per, outer)
        pooled_ref[...] = pooled[:, :bins].astype(jnp.bfloat16)
    else:
        left = pool_rows(rows_in, mixed_ref, rows_out, 0, gather_ref, lhs.at[0], per, outer)
        right = pool_rows(rows_in, mixed_ref, rows_out, ROWS, gather_ref, lhs.at[1], per, outer)
        each = bins // peers
        for seat in range(peers):
            mine = slice(seat * each, (seat + 1) * each)
            pair = jnp.concatenate([left[:, mine], right[:, mine]], axis=1).astype(jnp.bfloat16)
            for group in range(pooled_ref.shape[0]):
                pooled_ref[group, seat] = pair
    for k in range(peers):
        outs[k][...] = rows_out[me ^ k]


def corr_kernel(peers, outer, packed, scale, me_ref, *refs):
    if packed:
        packed_ref, refs = refs[0], refs[1:]
    queries = refs[:peers]
    refs, spec_refs = refs[: peers] + refs[peers + SPECTRA :], refs[peers : peers + SPECTRA]
    grad_ref, skip_ref, *tables, twist_ref, spread_ref = refs[peers : peers + 6]
    fwd_ref, bwd_ref = tables[:1], tables[1:]
    outs = refs[peers + 6 : 2 * peers + 6]
    rows_in, lhs_g, gated, parts_g, parts_y, lhs, rows_out = refs[2 * peers + 6 :]
    me = me_ref[0]
    ra, rb = radices(outer)
    per = outer // peers
    for k in range(peers):
        rows_in[me ^ k] = queries[k][...]
    each = LANES // POOL
    held = LANES // each
    place = lax.broadcasted_iota(jnp.int32, (ROWS, LANES), 1) // each
    zero = jnp.zeros((ROWS, LANES), jnp.float32)
    for tile in range(-(-outer // held)):
        count = min(held, outer - tile * held)
        used = count * each
        part = grad_ref[:, tile * LANES : tile * LANES + used]
        if used < LANES:
            part = jnp.concatenate([part, jnp.zeros((ROWS, LANES - used), jnp.float32)], axis=1)
        high = part.astype(jnp.bfloat16).astype(jnp.float32)
        low = part - high
        for j in range(count):
            rows = pl.ds((tile * held + j) * ROWS, ROWS)
            lhs_g[rows, :LANES] = jnp.where(place == j, high, zero).astype(jnp.bfloat16)
            lhs_g[rows, LANES:] = jnp.where(place == j, low, zero).astype(jnp.bfloat16)
    gated[...] = dot(lhs_g[...], spread_ref[...])
    for n1 in range(outer):
        lanes = slice((n1 % per) * LANES, (n1 % per + 1) * LANES)
        rows = pl.ds(n1 * ROWS, ROWS)
        gated[rows, :] = gated[rows, :] * rows_in[n1 // per, :, lanes].astype(jnp.float32)

    def load_g(n1):
        return gated[n1 * ROWS : (n1 + 1) * ROWS, :]

    first_pass(load_g, keep(parts_g), outer)
    chunk = rb * ROWS
    for alpha in range(ra):
        put(*second_pass(parts_g, alpha, outer, twist_ref), lhs.at[alpha // 2], alpha % 2 * chunk)
    for pair in range(ra // 2):
        both = lane_transform(lhs.at[pair], fwd_ref)
        for i in range(2):
            alpha = 2 * pair + i
            g = both[i * chunk : (i + 1) * chunk]
            each = ra // SPECTRA
            h = spec_refs[alpha // each][0, alpha % each * chunk : (alpha % each + 1) * chunk, :]
            gr, gi, hr, hi = g[:, :LANES], g[:, LANES:], h[:, :LANES], h[:, LANES:]
            put_product(gr * hr + gi * hi, gi * hr - gr * hi, lhs.at[ra // 2 + pair], i * chunk)
    for pair in range(ra // 2):
        y = lane_transform(lhs.at[ra // 2 + pair], bwd_ref)
        for i in range(2):
            back_second_pass(y[i * chunk : (i + 1) * chunk], 2 * pair + i, outer, twist_ref, keep(parts_y))
    skip = jnp.broadcast_to(skip_ref[...], (ROWS, LANES))

    def emit(n1, value):
        lanes = slice((n1 % per) * LANES, (n1 % per + 1) * LANES)
        rows_out[n1 // per, :, lanes] = (value + skip * load_g(n1)).astype(jnp.bfloat16)

    back_first_pass(parts_y, outer, emit, scale)
    step, steps = pl.program_id(0), pl.num_programs(0)
    for k in range(peers):
        outs[k][:, : per * LANES] = rows_out[me ^ k]
        if packed:
            half = steps // 2
            for chunk_at in range(packed_ref.shape[1] // (half * ROWS)):
                here = pl.ds((chunk_at * half + lax.rem(step, half)) * ROWS, ROWS)
                high, low = (part.astype(jnp.float32) for part in split(packed_ref[me ^ k, here, :]))
                lanes = slice((per + chunk_at) * LANES, (per + chunk_at + 1) * LANES)
                outs[k][:, lanes] = jnp.where(step < half, high, low).astype(jnp.bfloat16)


def whole(array):
    rank = len(array.shape)
    return pl.BlockSpec(array.shape, lambda i, me: (0,) * rank)


def by_rows(width, rows=ROWS, start=0):
    return pl.BlockSpec((rows, width), lambda i, me: (start + i, 0))


def call(kernel, name, me, steps, inputs, in_specs, out_shapes, out_specs, scratch, flops, aliases=None, near=(), vmem=()):
    moved = sum(x.size * x.dtype.itemsize for x in inputs)
    moved += sum(math.prod(o.shape) * o.dtype.itemsize for o in out_shapes)
    def space(i):
        return pltpu.VMEM if i in vmem else pltpu.HBM

    count = len(inputs)
    inputs = [x if i in near else pltpu.with_memory_space_constraint(x, space(i)) for i, x in enumerate(inputs)]
    out_shapes = [
        o if count + i in near else space(count + i)(o.shape, o.dtype) for i, o in enumerate(out_shapes)
    ]
    return pl.pallas_call(
        kernel,
        name=name,
        grid_spec=pltpu.PrefetchScalarGridSpec(
            num_scalar_prefetch=1,
            grid=(steps,),
            in_specs=in_specs,
            out_specs=out_specs,
            scratch_shapes=scratch,
        ),
        out_shape=out_shapes,
        input_output_aliases=aliases or {},
        compiler_params=pltpu.CompilerParams(
            dimension_semantics=("arbitrary",), vmem_limit_bytes=VMEM_LIMIT
        ),
        cost_estimate=pl.CostEstimate(flops=int(flops), bytes_accessed=moved, transcendentals=0),
    )(me, *inputs)


def shape(dims, dtype):
    return jax.ShapeDtypeStruct(dims, dtype)


def convolve(me, pieces, skip, tables, total_rows, start, before):
    peers = len(pieces)
    rows, width = pieces[0].shape[1:]
    length = width * peers
    outer = length // LANES
    ra, rb = radices(outer)
    chunk = rb * ROWS
    steps = rows // ROWS
    first = start // ROWS
    f32, bf16 = jnp.float32, jnp.bfloat16
    fwd, bwd, twist = tables["fwd"], tables["bwd"], tables["twist"]
    inputs = [*pieces, skip, *fwd, *bwd, twist]
    in_specs = [pl.BlockSpec((2, ROWS, width), lambda i, me: (0, i, 0))] * peers + [
        by_rows(1, start=first),
        *[whole(table) for table in (*fwd, *bwd, twist)],
    ]
    aliases = {}
    if before is not None:
        aliases = {1 + len(inputs): 0}
        inputs.append(before)
        in_specs.append(pl.BlockSpec(memory_space=pl.ANY))
    parts = pltpu.VMEM((2, rb, ra, ROWS, LANES), f32)

    def kernel(*refs):
        conv_kernel(peers, outer, *refs)

    part = (1, outer * ROWS // SPECTRA, 2 * LANES)
    out = call(
        kernel, "long_convolution", me, steps, inputs, in_specs,
        [shape((total_rows, length), f32)] + [shape((steps, *part[1:]), f32)] * SPECTRA,
        [by_rows(length, start=first)] + [pl.BlockSpec(part, lambda i, me: (i, 0, 0))] * SPECTRA,
        [
            pltpu.VMEM((peers, 2, ROWS, width), bf16),
            parts,
            parts,
            parts,
            pltpu.VMEM((ra + ra // 2, 2, 2 * chunk, 2 * LANES), bf16),
        ],
        rows * outer * 0.004 * MICROSECOND, aliases, (peers,), range(peers + 6, len(inputs) + 1),
    )
    return out[0], out[1:]


def pool(me, queries, mixed, gather, groups):
    peers = len(queries)
    rows, width = queries[0].shape
    length = width * peers
    outer = length // LANES
    bins = length // POOL
    bf16 = jnp.bfloat16
    if groups:
        step = 2 * ROWS
        pooled_shape = shape((groups, peers, rows // 2, LANES), bf16)
        pooled_spec = pl.BlockSpec((groups, peers, ROWS, LANES), lambda i, me: (0, 0, i, 0))
    else:
        step = ROWS
        pooled_shape = shape((rows, bins), bf16)
        pooled_spec = by_rows(bins)

    def kernel(*refs):
        pool_kernel(peers, outer, *refs)

    out = call(
        kernel, "pool_bins", me, rows // step, [*queries, mixed, gather],
        [by_rows(width, step)] * peers + [by_rows(length, step), whole(gather)],
        [shape((rows, width), bf16)] * peers + [pooled_shape],
        [by_rows(width, step)] * peers + [pooled_spec],
        [
            pltpu.VMEM((peers, step, width), bf16),
            pltpu.VMEM((peers, step, width), bf16),
            pltpu.VMEM((step // ROWS, outer * ROWS, 2 * LANES), bf16),
        ],
        rows * outer * 0.001 * MICROSECOND, vmem=range(1, peers + 1),
    )
    return out[:peers], out[peers]


def correlate(me, queries, grad_pooled, spec, skip, tables, spread, start, packed):
    peers = len(queries)
    width = queries[0].shape[1]
    rows = spec[0].shape[0] * ROWS
    length = width * peers
    outer = length // LANES
    bins = length // POOL
    ra, rb = radices(outer)
    chunk = rb * ROWS
    first = start // ROWS
    f32, bf16 = jnp.float32, jnp.bfloat16
    fwd, bwd, twist = tables["fwd_scaled"], tables["bwd_scaled"], tables["twist"]
    in_specs = [by_rows(width, start=first)] * peers + [
        *[pl.BlockSpec((1, *part.shape[1:]), lambda i, me: (i, 0, 0)) for part in spec],
        by_rows(bins, start=first),
        by_rows(1, start=first),
        *[whole(table) for table in (*fwd, *bwd, twist, spread)],
    ]
    parts = pltpu.VMEM((2, rb, ra, ROWS, LANES), f32)
    scratch = [
        pltpu.VMEM((peers, ROWS, width), bf16),
        pltpu.VMEM((outer * ROWS, 2 * LANES), bf16),
        pltpu.VMEM((outer * ROWS, LANES), f32),
        parts,
        parts,
        pltpu.VMEM((ra, 2, 2 * chunk, 2 * LANES), bf16),
        pltpu.VMEM((peers, ROWS, width), bf16),
    ]

    def kernel(*refs):
        corr_kernel(peers, outer, packed is not None, 1.0 / tables["scale"] ** 2, *refs)

    inputs = [*queries, *spec, grad_pooled, skip, *fwd, *bwd, twist, spread]
    sent = width
    if packed is not None:
        sent = width + packed.shape[1] // (rows // 2) * LANES
        inputs = [packed, *inputs]
        in_specs = [whole(packed), *in_specs]
    near = len(inputs) - 6
    return call(
        kernel, "long_correlation", me, rows // ROWS, inputs, in_specs,
        [shape((rows, sent), bf16)] * peers, [by_rows(sent)] * peers,
        scratch, rows * outer * 0.004 * MICROSECOND, near=((0,) if packed is not None else ()) + (near, near + 1, *range(len(inputs), len(inputs) + peers)),
    )


def lay_out(me, projections, filter_taps, peers, chunk, chunks):
    last = chunk == chunks - 1
    _, channels, width = projections.shape
    pencil = channels // peers
    rows = pencil // chunks
    f32, bf16 = jnp.float32, jnp.bfloat16
    order = list(range(peers))[::-1]

    def kernel(me_ref, proj_ref, taps_ref, *refs):
        outs = refs[:peers]
        queries = refs[peers:-7]
        pair, taps, laid, passing, sems, out_sems, query_sems = refs[-7:]

        def take(k):
            block = pl.ds(pl.multiple_of((me_ref[0] ^ k) * pencil, pencil), pencil)
            return pltpu.make_async_copy(proj_ref.at[0, block], passing.at[k], query_sems.at[k, 0])

        def hand_on(k):
            return pltpu.make_async_copy(passing.at[k], queries[k], query_sems.at[k, 1])


        def fetch(k):
            here = pl.ds(pl.multiple_of((me_ref[0] ^ k) * pencil + chunk * rows, rows), rows)
            return (
                pltpu.make_async_copy(proj_ref.at[1, here], pair.at[k, 0], sems.at[k, 0]),
                pltpu.make_async_copy(proj_ref.at[2, here], pair.at[k, 1], sems.at[k, 1]),
                pltpu.make_async_copy(taps_ref.at[here], taps.at[k], sems.at[k, 2]),
            )

        def leave(k):
            return pltpu.make_async_copy(laid.at[k], outs[k], out_sems.at[k])

        for k in order:
            for copy in fetch(k):
                copy.start()
        for k in range(len(queries)):
            take(k).start()
        for k in order:
            keyed, valued, lags = fetch(k)
            keyed.wait()
            valued.wait()
            laid[k, 0] = (pair[k, 0].astype(f32) * pair[k, 1].astype(f32)).astype(bf16)
            lags.wait()
            laid[k, 1] = taps[k].astype(bf16)
            leave(k).start()
        for k in range(len(queries)):
            take(k).wait()
            hand_on(k).start()
        for k in order:
            leave(k).wait()
        for k in range(len(queries)):
            hand_on(k).wait()

    out_shapes = [shape((2, rows, width), bf16)] * peers
    if last:
        out_shapes += [shape((pencil, width), bf16)] * peers
    return call(
        kernel, "lay_out", me, 1, [projections, filter_taps],
        [pl.BlockSpec(memory_space=pltpu.HBM)] * 2,
        out_shapes,
        [pl.BlockSpec(memory_space=pltpu.HBM)] * len(out_shapes),
        [
            pltpu.VMEM((peers, 2, rows, width), bf16),
            pltpu.VMEM((peers, rows, width), f32),
            pltpu.VMEM((peers, 2, rows, width), bf16),
            pltpu.VMEM((peers, pencil, width), bf16),
            pltpu.SemaphoreType.DMA((peers, 3)),
            pltpu.SemaphoreType.DMA((peers,)),
            pltpu.SemaphoreType.DMA((peers, 2)),
        ],
        rows * peers * 0.015 * MICROSECOND,
    )


def by_track(me, head_weight, groups):
    channels, tracks = head_weight.shape
    half, own = channels // 2, tracks // groups
    padded = -(-own // LANES) * LANES
    dtype = head_weight.dtype
    steps = half // ROWS

    def kernel(me_ref, weight_ref, out_ref, rows_in, sems):
        first = pl.multiple_of((me_ref[0] & 1) * half, half)

        def fetch(i):
            return pltpu.make_async_copy(
                weight_ref.at[pl.ds(first + i * ROWS, ROWS)], rows_in.at[pl.ds(i * ROWS, ROWS)], sems.at[i]
            )

        for i in range(steps):
            fetch(i).start()
        for i in range(steps):
            fetch(i).wait()
        for group in range(groups):
            out_ref[group, :, :own] = rows_in[:, group * own : (group + 1) * own]
            if padded > own:
                out_ref[group, :, own:] = jnp.zeros((half, padded - own), dtype)

    out = shape((groups, half, padded), dtype)
    return call(
        kernel, "by_track", me, 1, [head_weight], [pl.BlockSpec(memory_space=pltpu.HBM)], [out], [whole(out)],
        [pltpu.VMEM((half, tracks), dtype), pltpu.SemaphoreType.DMA((steps,))], 2 * MICROSECOND, vmem=(1,),
    )[0]


def weight_pair(weight_ref, seats, pencil, own):
    groups, _, padded = weight_ref.shape
    rows = weight_ref[...].reshape(groups, seats, pencil // (2 * ROWS), 2, ROWS, padded)
    count = groups * seats * pencil // 2
    left, right = rows[:, :, :, 0].reshape(count, padded), rows[:, :, :, 1].reshape(count, padded)
    return left[:, :own], right[:, :own]


def head_rates(me, got, mine, other, bias, counts):
    groups, peers, half_rows, _ = got.shape
    own = counts.shape[1]
    seats = peers // 2
    pencil = 2 * half_rows
    bins = LANES // 2
    f32 = jnp.float32

    def kernel(me_ref, got_ref, mine_ref, other_ref, bias_ref, counts_ref, logits_ref, sums_ref):
        odd = me_ref[0] & 1
        total = jnp.broadcast_to(bias_ref[...], (bins, own))
        for weight_ref, place in ((mine_ref, odd), (other_ref, 1 - odd)):
            block = got_ref[:, pl.ds(place * seats, seats)].reshape(groups * seats * half_rows, LANES)
            turned = block.astype(f32).T.astype(jnp.bfloat16)
            left, right = weight_pair(weight_ref, seats, pencil, own)
            total = total + dot(turned[:bins], left) + dot(turned[bins:], right)
        logits_ref[...] = total
        rates = jax.nn.softplus(total) + rate_floor
        observed = counts_ref[...].astype(f32)
        sums_ref[0:1, :] = jnp.sum(rates, axis=0, keepdims=True)
        sums_ref[1:2, :] = jnp.sum(observed, axis=0, keepdims=True)
        sums_ref[2:3, :] = jnp.sum(observed * jnp.log(rates), axis=0, keepdims=True)
        sums_ref[3:8, :] = jnp.zeros((5, own), f32)

    inputs = [got, mine, other, bias, counts]
    return call(
        kernel, "head_rates", me, 1, inputs, [whole(x) for x in inputs],
        [shape((bins, own), f32), shape((8, own), f32)],
        [pl.BlockSpec((bins, own), lambda i, me: (0, 0)), pl.BlockSpec((8, own), lambda i, me: (0, 0))],
        [], 2 * bins * groups * peers * pencil * own, near=range(7),
    )


def head_grads(me, logits, sums, mine, other, counts):
    groups, half, _ = mine.shape
    own = counts.shape[1]
    peers = len(sums)
    seats = peers // 2
    pencil = half // seats
    bins = LANES // 2
    f32, bf16 = jnp.float32, jnp.bfloat16

    def kernel(me_ref, logits_ref, *refs):
        sums_refs = refs[:peers]
        mine_ref, other_ref, counts_ref, out_ref, loss_ref = refs[peers:]
        odd = me_ref[0] & 1
        totals = [ref[...] for ref in sums_refs]
        while len(totals) > 1:
            totals = [totals[i] + totals[i + 1] for i in range(0, len(totals), 2)]
        totals = totals[0]
        pred_total, obs_total, log_sum = totals[0:1], totals[1:2], totals[2:3]
        log_pred = jnp.log(pred_total)
        terms = total_weight * (pred_total - obs_total * log_pred) + obs_total * log_pred - log_sum
        mean = jnp.sum(terms, axis=1, keepdims=True) / (peers * bins * groups * own)
        loss_ref[...] = jnp.broadcast_to(mean, loss_ref.shape)
        ratio = obs_total / pred_total
        logits_here = logits_ref[...]
        rates = jax.nn.softplus(logits_here) + rate_floor
        observed = counts_ref[...].astype(f32)
        grad_rates = total_weight * (1.0 - ratio) + ratio - observed / rates
        grads = (grad_rates * jax.nn.sigmoid(logits_here)).astype(bf16)
        none = jnp.zeros_like(grads)
        in_left = jnp.concatenate([grads, none], axis=0)
        in_right = jnp.concatenate([none, grads], axis=0)
        across = (((1,), (1,)), ((), ()))
        for weight_ref, place in ((mine_ref, odd), (other_ref, 1 - odd)):
            left, right = weight_pair(weight_ref, seats, pencil, own)
            part = lax.dot_general(left, in_left, across, preferred_element_type=f32)
            part = part + lax.dot_general(right, in_right, across, preferred_element_type=f32)
            out_ref[:, pl.ds(place * seats, seats)] = part.astype(bf16).reshape(groups, seats, pencil // 2, LANES)

    inputs = [logits, *sums, mine, other, counts]
    out = shape((groups, peers, pencil // 2, LANES), bf16)
    return call(
        kernel, "head_grads", me, 1, inputs, [whole(x) for x in inputs],
        [out, shape((8, LANES), f32)],
        [whole(out), pl.BlockSpec((8, LANES), lambda i, me: (0, 0))],
        [], 4 * bins * groups * peers * pencil * own, near=(*range(peers + 4), peers + 5),
    )


def sum_grads(me, back):
    groups, peers, half_rows, _ = back.shape
    bins = LANES // 2
    f32 = jnp.float32

    def kernel(me_ref, back_ref, rows_ref, packed_ref):
        for seat in range(peers):
            total = back_ref[0, seat].astype(f32)
            for group in range(1, groups):
                total = total + back_ref[group, seat].astype(f32)
            packed_ref[seat] = total
            for i in range(half_rows // ROWS):
                pair = total[i * ROWS : (i + 1) * ROWS]
                lanes = slice(seat * bins, (seat + 1) * bins)
                rows_ref[2 * i * ROWS : (2 * i + 1) * ROWS, lanes] = pair[:, :bins]
                rows_ref[(2 * i + 1) * ROWS : (2 * i + 2) * ROWS, lanes] = pair[:, bins:]

    rows, packed = shape((2 * half_rows, peers * bins), f32), shape((peers, half_rows, LANES), f32)
    return call(
        kernel, "sum_grads", me, 1, [back], [whole(back)], [rows, packed], [whole(rows), whole(packed)], [], back.size,
        near=(0, 1, 2),
    )


def finish(me, projections, mixed_home, corr_home, spread, chunk, chunks, before, loss):
    peers = len(corr_home)
    _, channels, width = projections.shape
    pencil = channels // peers
    rows = pencil // chunks
    tiles = width // LANES
    each = LANES // POOL
    f32, bf16 = jnp.float32, jnp.bfloat16
    with_query = bool(mixed_home)
    payload = corr_home[0].shape[1]

    def kernel(me_ref, spread_ref, proj_ref, *refs):
        mixed_refs, corr_refs = refs[: len(mixed_home)], refs[len(mixed_home) : len(mixed_home) + peers]
        pair, mixed_in, corr_in, done, query_done, lhs, sems, out_sems = refs[-8:]
        if loss:
            loss_ref, mean_ref = refs[len(mixed_home) + peers], refs[-9]
            mean_ref[...] = loss_ref[0:1, 0:1]
        out_ref = refs[-9 - len(loss)]
        place = lax.broadcasted_iota(jnp.int32, (ROWS, LANES), 1) // each
        zero = jnp.zeros((ROWS, LANES), f32)

        def block(k, start, count):
            return pl.ds(pl.multiple_of((me_ref[0] ^ k) * pencil + start, ROWS), count)

        def here(k):
            return block(k, chunk * rows, rows)

        def fetch(k):
            return (
                pltpu.make_async_copy(corr_refs[k], corr_in.at[k], sems.at[k, 0]),
                pltpu.make_async_copy(proj_ref.at[1, here(k)], pair.at[k, 0], sems.at[k, 1]),
                pltpu.make_async_copy(proj_ref.at[2, here(k)], pair.at[k, 1], sems.at[k, 2]),
            )

        def fetch_mixed(k):
            return pltpu.make_async_copy(mixed_refs[k], mixed_in.at[k], sems.at[k, 3])

        def leave(k, plane):
            if plane == 0:
                return pltpu.make_async_copy(query_done.at[k], out_ref.at[0, block(k, 0, pencil)], out_sems.at[k, 0])
            return pltpu.make_async_copy(done.at[k, plane - 1], out_ref.at[plane, here(k)], out_sems.at[k, plane])

        for k in range(peers):
            for copy in fetch(k):
                copy.start()
            if with_query:
                fetch_mixed(k).start()
        for k in range(peers):
            for copy in fetch(k):
                copy.wait()
            corr = corr_in[k, :, :width].astype(f32)
            done[k, 0] = corr * pair[k, 1].astype(f32)
            leave(k, 1).start()
            done[k, 1] = corr * pair[k, 0].astype(f32)
            leave(k, 2).start()
            if not with_query:
                continue
            fetch_mixed(k).wait()
            for i in range(pencil // ROWS):
                part = slice(i * ROWS, (i + 1) * ROWS)
                inside = i % (rows // ROWS)
                source = inside // 2 * ROWS
                lanes = slice(width + i // (rows // ROWS) * LANES, width + (i // (rows // ROWS) + 1) * LANES)
                high = corr_in[k, source : source + ROWS, lanes].astype(f32)
                low = corr_in[k, rows // 2 + source : rows // 2 + source + ROWS, lanes].astype(f32)
                for t in range(tiles):
                    near = place == t + inside % 2 * tiles
                    lhs[i, t * ROWS : (t + 1) * ROWS, :LANES] = jnp.where(near, high, zero).astype(bf16)
                    lhs[i, t * ROWS : (t + 1) * ROWS, LANES:] = jnp.where(near, low, zero).astype(bf16)
                grad = dot(lhs[i], spread_ref[...])
                for t in range(tiles):
                    at = slice(t * LANES, (t + 1) * LANES)
                    query_done[k, part, at] = grad[t * ROWS : (t + 1) * ROWS] * mixed_in[k, part, at].astype(f32)
            leave(k, 0).start()
        for k in range(peers):
            for plane in range(0 if with_query else 1, 3):
                leave(k, plane).wait()

    inputs = [spread, projections, *mixed_home, *corr_home, *loss]
    in_specs = [whole(spread), pl.BlockSpec(memory_space=pltpu.HBM)]
    in_specs += [pl.BlockSpec(memory_space=pl.ANY)] * (len(mixed_home) + peers)
    in_specs += [whole(x) for x in loss]
    near = (0, *range(2, len(inputs)))
    aliases = {}
    if before is not None:
        aliases = {1 + len(inputs): 0}
        inputs.append(before)
        in_specs.append(pl.BlockSpec(memory_space=pl.ANY))
    return call(
        kernel, "finish", me, 1, inputs, in_specs,
        [shape((3, channels, width), f32)] + [shape((1, 1), f32)] * len(loss),
        [pl.BlockSpec(memory_space=pltpu.HBM)] + [pl.BlockSpec((1, 1), lambda i, me: (0, 0))] * len(loss),
        [
            pltpu.VMEM((peers, 2, rows, width), bf16),
            pltpu.VMEM((peers, pencil if with_query else ROWS, width), bf16),
            pltpu.VMEM((peers, rows, payload), bf16),
            pltpu.VMEM((peers, 2, rows, width), f32),
            pltpu.VMEM((peers, pencil if with_query else ROWS, width), f32),
            pltpu.VMEM((pencil // ROWS, tiles * ROWS, 2 * LANES), bf16),
            pltpu.SemaphoreType.DMA((peers, 4)),
            pltpu.SemaphoreType.DMA((peers, 3)),
        ],
        rows * peers * 0.03 * MICROSECOND, aliases, near=near,
    )


def swap(value, k, count):
    if k == 0:
        return value
    return lax.ppermute(value, "seq", [(i, i ^ k) for i in range(count)])


def pad_rows(value, rows):
    short = rows - value.shape[-2]
    if short == 0:
        return value
    widths = [(0, 0)] * value.ndim
    widths[-2] = (0, short)
    return jnp.pad(value, widths)


def aligned(projections, filter_taps, skip_gain, head_weight, head_bias, counts):
    f32 = jnp.float32
    _, channels, width = projections.shape
    peers = lax.axis_size("seq")
    groups = lax.axis_size("chan")
    seat = lax.axis_index("seq")
    group = lax.axis_index("chan")
    bins = width // POOL
    length = width * peers
    tracks = head_weight.shape[1]
    own_tracks = tracks // groups
    pencil = channels // peers
    chunks = CHUNKS
    rows = pencil // chunks
    me = jnp.asarray(seat, jnp.int32).reshape(1)
    tables = transform_tables(length)
    gather, spread = pool_tables()

    laid, me_next = [], me
    for j in range(chunks):
        laid.append(lay_out(me_next, projections, filter_taps, peers, j, chunks))
        me_next, _ = lax.optimization_barrier((me, laid[j]))
    pieces = [[swap(laid[j][k], k, peers) for k in range(peers)] for j in range(chunks)]
    held_back, _ = lax.optimization_barrier((laid[-1][peers:], pieces[0]))
    queries = [swap(held_back[k], k, peers) for k in range(peers)]
    skip = lax.dynamic_index_in_dim(skip_gain.reshape(peers, pencil, 1), seat, axis=0, keepdims=False)

    mine = by_track(me_next, head_weight, groups)
    mine = lax.all_to_all(mine, "chan", split_axis=0, concat_axis=0, tiled=True)

    mixed, specs = None, []
    for j in range(chunks):
        mixed, spec = convolve(me, pieces[j], skip, tables, pencil, j * rows, mixed)
        specs.append(spec)
    mixed_out, sent = pool(me, queries, mixed, gather, groups)
    mixed_home = [swap(mixed_out[k], k, peers) for k in range(peers)]

    def exchange(blocks):
        flat = blocks.reshape(groups * peers, pencil // 2, LANES)
        flat = lax.all_to_all(flat, ("chan", "seq"), split_axis=0, concat_axis=0, tiled=True)
        return flat.reshape(blocks.shape)

    got = exchange(sent)
    mine, _ = lax.optimization_barrier((mine, sent))
    other = swap(mine, 1, peers)
    own_bias = lax.dynamic_slice_in_dim(head_bias, group * own_tracks, own_tracks).reshape(1, own_tracks)
    own_counts = lax.dynamic_slice_in_dim(counts, group * own_tracks, own_tracks, axis=1)
    logits, sums = head_rates(me, got, mine, other, own_bias, own_counts)
    all_sums = [swap(sums, k, peers) for k in range(peers)]
    early, late = mixed_home[: peers - 1], mixed_home[peers - 1 :]
    logits, early = lax.optimization_barrier((logits, early))
    part, loss = head_grads(me, logits, all_sums, mine, other, own_counts)
    back = exchange(part)

    step = 1
    while step < groups:
        loss = loss + lax.ppermute(loss, "chan", [(i, i ^ step) for i in range(groups)])
        step *= 2

    back, loss, late = lax.optimization_barrier((back, loss, late))
    mixed_home = [*early, *late]
    grad_rows, packed = sum_grads(me, back)
    grads = None
    corr_home = []
    for j in range(chunks):
        corr = correlate(me, queries, grad_rows, specs[j], skip, tables, spread, j * rows, None if j else packed)
        grad_rows, _ = lax.optimization_barrier((grad_rows, corr))
        corr_home.append([swap(corr[k], k, peers) for k in range(peers)])
    for j in range(chunks):
        ours = [] if j else mixed_home
        grads, *rest = finish(me, projections, ours, corr_home[j], spread, j, chunks, grads, [] if j else [loss])
        if not j:
            mean_loss = rest[0].reshape(())
    return mean_loss, grads


def power_of_two(value):
    return value & (value - 1) == 0


def per_device(projections, filter_taps, skip_gain, head_weight, head_bias, counts):
    channels, width = projections.shape[1:]
    peers, groups = lax.axis_size("seq"), lax.axis_size("chan")
    pencil = channels // peers
    fits = (
        pencil % (2 * ROWS * CHUNKS) == 0
        and 2 * (width // POOL) == LANES
        and power_of_two(peers)
        and peers > 1
        and power_of_two(groups)
        and groups <= MOST_GROUPS
    )
    run = aligned if fits else general
    return run(projections, filter_taps, skip_gain, head_weight, head_bias, counts)


def general(projections, filter_taps, skip_gain, head_weight, head_bias, counts):
    f32, bf16 = jnp.float32, jnp.bfloat16
    _, channels, width = projections.shape
    peers = lax.axis_size("seq")
    groups = lax.axis_size("chan")
    seat = lax.axis_index("seq")
    group = lax.axis_index("chan")
    bins = width // POOL
    length = width * peers
    tracks = head_weight.shape[1]
    own_tracks = tracks // groups
    pencil = channels // peers
    rows = -(-pencil // ROWS) * ROWS
    me = jnp.asarray(seat, jnp.int32).reshape(1)
    tables = transform_tables(length)
    gather, spread = pool_tables()

    def block(array, k):
        return lax.dynamic_index_in_dim(array, seat ^ k, axis=-3, keepdims=False)

    query = projections[0]
    key_value = projections[1].astype(f32) * projections[2].astype(f32)
    stacked = jnp.stack([key_value.astype(bf16), filter_taps.astype(bf16)])
    stacked = stacked.reshape(2, peers, pencil, width)
    pieces = [pad_rows(swap(block(stacked, k), k, peers), rows) for k in range(peers)]
    query_blocks = query.reshape(peers, pencil, width)
    queries = [pad_rows(swap(block(query_blocks, k), k, peers), rows) for k in range(peers)]
    skip = pad_rows(block(skip_gain.reshape(peers, pencil, 1), 0), rows)

    half = channels // 2
    by_track = head_weight.reshape(2, half, groups, own_tracks).transpose(0, 2, 1, 3)
    mine = lax.dynamic_index_in_dim(by_track, seat & 1, axis=0, keepdims=False)
    mine = lax.all_to_all(mine, "chan", split_axis=0, concat_axis=0, tiled=True)
    other = swap(mine, 1, peers)
    mine = mine.reshape(groups * half, own_tracks)
    other = other.reshape(groups * half, own_tracks)

    mixed, spec = convolve(me, pieces, skip, tables, rows, 0, None)
    mixed_out, pooled = pool(me, queries, mixed, gather, 0)
    pooled = pooled[:pencil]
    mixed_home = [swap(mixed_out[k][:pencil], k, peers) for k in range(peers)]

    sent = pooled.reshape(pencil, peers, bins).transpose(1, 0, 2)
    sent = jnp.broadcast_to(sent[None], (groups, peers, pencil, bins))
    got = lax.all_to_all(
        sent.reshape(groups * peers, pencil, bins), ("chan", "seq"), split_axis=0, concat_axis=0, tiled=True
    )
    got = got.reshape(groups, 2, half, bins)
    low_half = got[:, 0].reshape(groups * half, bins)
    high_half = got[:, 1].reshape(groups * half, bins)
    odd = (seat & 1) == 1
    pooled_mine = jnp.where(odd, high_half, low_half)
    pooled_other = jnp.where(odd, low_half, high_half)

    def project(x, w):
        return lax.dot_general(x, w, (((0,), (0,)), ((), ())), preferred_element_type=f32)

    own_bias = lax.dynamic_slice_in_dim(head_bias, group * own_tracks, own_tracks)
    own_counts = lax.dynamic_slice_in_dim(counts, group * own_tracks, own_tracks, axis=1)
    logits = project(pooled_mine, mine) + project(pooled_other, other) + own_bias[None, :]
    rates = jax.nn.softplus(logits) + rate_floor
    observed = own_counts.astype(f32)
    partial_sums = jnp.stack(
        [jnp.sum(rates, axis=0), jnp.sum(observed, axis=0), jnp.sum(observed * jnp.log(rates), axis=0)]
    )
    pred_total, obs_total, log_sum = jnp.sum(lax.all_gather(partial_sums, "seq"), axis=0)
    log_pred = jnp.log(pred_total)
    loss_part = jnp.sum(
        total_weight * (pred_total - obs_total * log_pred) + obs_total * log_pred - log_sum
    )
    mean_loss = lax.psum(loss_part, "chan") / (bins * peers * tracks)
    ratio = obs_total / pred_total
    grad_rates = total_weight * (1.0 - ratio)[None, :] + ratio[None, :] - observed / rates
    grad_logits = (grad_rates * jax.nn.sigmoid(logits)).astype(bf16)

    def spread_back(w):
        return lax.dot_general(w, grad_logits, (((1,), (1,)), ((), ())), preferred_element_type=f32)

    part_mine = spread_back(mine).astype(bf16).reshape(groups, 1, half, bins)
    part_other = spread_back(other).astype(bf16).reshape(groups, 1, half, bins)
    part = jnp.concatenate(
        [jnp.where(odd, part_other, part_mine), jnp.where(odd, part_mine, part_other)], axis=1
    )
    back = lax.all_to_all(
        part.reshape(groups * peers, pencil, bins), ("chan", "seq"), split_axis=0, concat_axis=0, tiled=True
    )
    grad_pooled = jnp.sum(back.reshape(groups, peers, pencil, bins).astype(f32), axis=0)
    grad_home = [swap(block(grad_pooled, k), k, peers) for k in range(peers)]
    grad_rows = pad_rows(grad_pooled.transpose(1, 0, 2).reshape(pencil, peers * bins), rows)

    corr_out = correlate(me, queries, grad_rows, spec, skip, tables, spread, 0, None)
    corr_home = [swap(corr_out[k][:pencil], k, peers) for k in range(peers)]

    def assemble(parts):
        out = jnp.zeros((peers,) + parts[0].shape, parts[0].dtype)
        for k, part in enumerate(parts):
            out = lax.dynamic_update_index_in_dim(out, part, seat ^ k, axis=0)
        return out.reshape((channels,) + parts[0].shape[1:])

    grad_output = jnp.repeat(assemble(grad_home) / POOL, POOL, axis=1)
    grad_kv = assemble(corr_home).astype(f32)
    grad_query = grad_output * assemble(mixed_home).astype(f32)
    grads = jnp.stack(
        [grad_query, grad_kv * projections[2].astype(f32), grad_kv * projections[1].astype(f32)], axis=0
    )
    return mean_loss, grads


def solution(mesh):
    placed = (
        P(None, "chan", "seq"),
        P("chan", "seq"),
        P("chan"),
        P("chan", None),
        P(),
        P("seq", None),
    )
    return jax.shard_map(
        per_device,
        mesh=mesh,
        in_specs=placed,
        out_specs=(P(), P(None, "chan", "seq")),
        check_vma=False,
    )
```

```python
import math

import jax
import jax.numpy as jnp
import ml_dtypes
import numpy as np
from jax import lax
from jax.experimental import pallas as pl
from jax.experimental.pallas import tpu as pltpu
from jax.sharding import PartitionSpec as P

POOL = 32
LANES = 128
ROWS = 16
SHIFT = 0.25

total_weight = 0.2
rate_floor = 0.5

MICROSECOND = 1.0e9

VMEM_LIMIT = 20 * 1024 * 1024
CHUNKS = 2
SPECTRA = 4
MOST_GROUPS = 16


def split_bf16(table):
    high = table.astype(ml_dtypes.bfloat16)
    low = (table - high.astype(np.float64)).astype(ml_dtypes.bfloat16)
    return high, low


def kind_scale(table):
    values = np.unique(np.abs(table))
    factors = np.linspace(1.0, 2.0, 4001)

    def lost(factor):
        scaled = table[: LANES // 2] * factor
        return np.sum((scaled - split_bf16(scaled)[0].astype(np.float64)) ** 2) / factor**2

    rough = [np.sum((values * f - split_bf16(values * f)[0].astype(np.float64)) ** 2) / f**2 for f in factors]
    best = np.argsort(rough, kind="stable")[:8]
    return float(min((factors[i] for i in best), key=lost))


def radices(outer):
    first = 1
    while first * first < outer:
        first *= 2
    return first, outer // first


def transform_tables(length):
    outer = length // LANES
    idx = np.arange(LANES)
    angle = 2.0 * np.pi * (np.outer(idx, idx) % LANES) / LANES
    wr, wi = np.cos(angle), -np.sin(angle)
    forward = np.block([[wr, wi], [-wi, wr]])
    backward = np.block([[wr, -wi], [wi, wr]]) / length
    k1 = np.arange(outer)[:, None]
    twist = 2.0 * np.pi * (k1 - SHIFT) * idx[None, :] / length
    scale = kind_scale(forward)
    f_hi, f_lo = split_bf16(forward)
    b_hi, b_lo = split_bf16(backward)
    return dict(
        fwd=[f_hi, f_lo],
        bwd=[b_hi, b_lo],
        scale=scale,
        fwd_scaled=[split_bf16(forward * scale)[0]],
        bwd_scaled=[split_bf16(backward * scale)[0]],
        twist=np.stack([np.cos(twist), -np.sin(twist)]).astype(np.float32),
    )


def pool_tables():
    per = LANES // POOL
    lane = np.arange(LANES)
    hit = (lane[:, None] // POOL) == (lane[None, :] % per)
    gather = np.concatenate([hit, hit], axis=0) / POOL
    spread = np.concatenate([hit.T, hit.T], axis=0) / POOL
    return gather.astype(ml_dtypes.bfloat16), spread.astype(ml_dtypes.bfloat16)


def times(value, angle):
    re, im = value
    c, s = math.cos(angle), math.sin(angle)
    tiny = 1e-12
    if im is None:
        if abs(s) < tiny and c > 0:
            return (re, None)
        return (re * c, re * s)
    if abs(s) < tiny:
        return (re, im) if c > 0 else (-re, -im)
    if abs(c) < tiny:
        return (-im, re) if s > 0 else (im, -re)
    return (re * c - im * s, re * s + im * c)


def add(a, b):
    if a[1] is None and b[1] is None:
        return (a[0] + b[0], None)
    if a[1] is None:
        return (a[0] + b[0], b[1])
    if b[1] is None:
        return (a[0] + b[0], a[1])
    return (a[0] + b[0], a[1] + b[1])


def sub(a, b):
    if a[1] is None and b[1] is None:
        return (a[0] - b[0], None)
    if a[1] is None:
        return (a[0] - b[0], -b[1])
    if b[1] is None:
        return (a[0] - b[0], a[1])
    return (a[0] - b[0], a[1] - b[1])


def small_dft(values, sign):
    count = len(values)
    if count == 1:
        return values
    even = small_dft(values[0::2], sign)
    odd = small_dft(values[1::2], sign)
    out = [None] * count
    half = count // 2
    for k in range(half):
        turned = times(odd[k], sign * 2.0 * math.pi * k / count)
        out[k] = add(even[k], turned)
        out[k + half] = sub(even[k], turned)
    return out


def dot(a, b):
    return jnp.dot(a, b, preferred_element_type=jnp.float32)


def split(value):
    high = value.astype(jnp.bfloat16)
    return high, (value - high.astype(jnp.float32)).astype(jnp.bfloat16)


def put(re_parts, im_parts, lhs, start):
    for i, (re, im) in enumerate(zip(re_parts, im_parts)):
        rows = pl.ds(start + i * ROWS, ROWS)
        re_hi, re_lo = split(re)
        im_hi, im_lo = split(im)
        lhs[0, rows, :LANES] = re_hi
        lhs[0, rows, LANES:] = im_hi
        lhs[1, rows, :LANES] = re_lo
        lhs[1, rows, LANES:] = im_lo


def lane_transform(lhs, table_refs):
    high = lhs[0]
    if len(table_refs) == 1:
        table = table_refs[0][...]
        return dot(high, table) + dot(lhs[1], table)
    table_high, table_low = table_refs[0][...], table_refs[1][...]
    return dot(high, table_high) + (dot(lhs[1], table_high) + dot(high, table_low))


def first_pass(load, store, outer):
    ra, rb = radices(outer)
    for b in range(rb):
        values = [times((load(rb * a + b), None), 2.0 * math.pi * a * SHIFT / ra) for a in range(ra)]
        out = small_dft(values, -1)
        for alpha in range(ra):
            re, im = times(out[alpha], -2.0 * math.pi * b * (alpha - SHIFT) / outer)
            store(b, alpha, re, im)


def second_pass(parts, alpha, outer, twist_ref):
    ra, rb = radices(outer)
    values = [(parts[0, b, alpha], parts[1, b, alpha]) for b in range(rb)]
    out = small_dft(values, -1)
    res, ims = [], []
    for beta in range(rb):
        k1 = alpha + ra * beta
        tr = twist_ref[0, k1 : k1 + 1, :]
        ti = twist_ref[1, k1 : k1 + 1, :]
        re, im = out[beta]
        res.append(re * tr - im * ti)
        ims.append(re * ti + im * tr)
    return res, ims


def back_second_pass(spectrum, alpha, outer, twist_ref, store):
    ra, rb = radices(outer)
    values = []
    for beta in range(rb):
        k1 = alpha + ra * beta
        tr = twist_ref[0, k1 : k1 + 1, :]
        ti = twist_ref[1, k1 : k1 + 1, :]
        re = spectrum[beta * ROWS : (beta + 1) * ROWS, :LANES]
        im = spectrum[beta * ROWS : (beta + 1) * ROWS, LANES:]
        values.append((re * tr + im * ti, im * tr - re * ti))
    out = small_dft(values, +1)
    for b in range(rb):
        re, im = times(out[b], 2.0 * math.pi * b * (alpha - SHIFT) / outer)
        store(b, alpha, re, im)


def back_first_pass(parts, outer, emit, scale=1.0):
    ra, rb = radices(outer)
    for b in range(rb):
        values = [(parts[0, b, alpha], parts[1, b, alpha]) for alpha in range(ra)]
        out = small_dft(values, +1)
        for a in range(ra):
            angle = -2.0 * math.pi * a * SHIFT / ra
            re, im = out[a]
            c, s = math.cos(angle) * scale, math.sin(angle) * scale
            if a == 0:
                emit(rb * a + b, re if scale == 1.0 else re * scale)
            else:
                emit(rb * a + b, re * c - im * s)


def put_product(re, im, lhs, start):
    rows = [slice(i, i + ROWS) for i in range(0, re.shape[0], ROWS)]
    put([re[r] for r in rows], [im[r] for r in rows], lhs, start)


def keep(parts):
    def store(b, alpha, re, im):
        parts[0, b, alpha] = re
        parts[1, b, alpha] = im

    return store


def conv_kernel(peers, outer, me_ref, *refs):
    pieces = refs[:peers]
    skip_ref, *tables, twist_ref = refs[peers : peers + 6]
    fwd_ref, bwd_ref = tables[:2], tables[2:]
    mixed_ref = refs[-6 - SPECTRA]
    spec_refs = refs[-5 - SPECTRA : -5]
    rows_in, parts_x, parts_h, parts_y, lhs = refs[-5:]
    me = me_ref[0]
    ra, rb = radices(outer)
    per = outer // peers
    for k in range(peers):
        rows_in[me ^ k] = pieces[k][...]

    def loader(which):
        def load(n1):
            lanes = slice((n1 % per) * LANES, (n1 % per + 1) * LANES)
            return rows_in[n1 // per, which, :, lanes].astype(jnp.float32)

        return load

    load_x = loader(0)
    first_pass(load_x, keep(parts_x), outer)
    first_pass(loader(1), keep(parts_h), outer)
    chunk = rb * ROWS
    for alpha in range(ra):
        put(*second_pass(parts_x, alpha, outer, twist_ref), lhs.at[alpha], 0)
        put(*second_pass(parts_h, alpha, outer, twist_ref), lhs.at[alpha], chunk)
    for alpha in range(ra):
        both = lane_transform(lhs.at[alpha], fwd_ref)
        x, h = both[:chunk], both[chunk:]
        each = ra // SPECTRA
        spec_refs[alpha // each][0, alpha % each * chunk : (alpha % each + 1) * chunk, :] = h
        xr, xi, hr, hi = x[:, :LANES], x[:, LANES:], h[:, :LANES], h[:, LANES:]
        put_product(xr * hr - xi * hi, xr * hi + xi * hr, lhs.at[ra + alpha // 2], alpha % 2 * chunk)
    for pair in range(ra // 2):
        y = lane_transform(lhs.at[ra + pair], bwd_ref)
        for i in range(2):
            back_second_pass(y[i * chunk : (i + 1) * chunk], 2 * pair + i, outer, twist_ref, keep(parts_y))
    skip = jnp.broadcast_to(skip_ref[...], (ROWS, LANES))

    def emit(n1, value):
        mixed_ref[:, n1 * LANES : (n1 + 1) * LANES] = value + skip * load_x(n1)

    back_first_pass(parts_y, outer, emit)


def pool_rows(rows_in, mixed_ref, rows_out, row, gather_ref, lhs, per, outer):
    for n1 in range(outer):
        lanes = slice((n1 % per) * LANES, (n1 % per + 1) * LANES)
        query = rows_in[n1 // per, row : row + ROWS, lanes].astype(jnp.float32)
        mixed = mixed_ref[row : row + ROWS, n1 * LANES : (n1 + 1) * LANES]
        rows_out[n1 // per, row : row + ROWS, lanes] = mixed.astype(jnp.bfloat16)
        high, low = split(query * mixed)
        lhs[n1 * ROWS : (n1 + 1) * ROWS, :LANES] = high
        lhs[n1 * ROWS : (n1 + 1) * ROWS, LANES:] = low
    sums = dot(lhs[...], gather_ref[...])
    each = LANES // POOL
    held = LANES // each
    place = lax.broadcasted_iota(jnp.int32, (ROWS, LANES), 1) // each
    tiles = []
    for tile in range(-(-outer // held)):
        total = jnp.zeros((ROWS, LANES), jnp.float32)
        for j in range(min(held, outer - tile * held)):
            n1 = tile * held + j
            total = jnp.where(place == j, sums[n1 * ROWS : (n1 + 1) * ROWS], total)
        tiles.append(total)
    return jnp.concatenate(tiles, axis=1)


def pool_kernel(peers, outer, me_ref, *refs):
    queries = refs[:peers]
    mixed_ref, gather_ref = refs[peers : peers + 2]
    outs = refs[peers + 2 : 2 * peers + 2]
    pooled_ref, rows_in, rows_out, lhs = refs[2 * peers + 2 :]
    me = me_ref[0]
    per = outer // peers
    for k in range(peers):
        rows_in[me ^ k] = queries[k][...]
    rows = mixed_ref.shape[0]
    bins = outer * LANES // POOL
    if rows == ROWS:
        pooled = pool_rows(rows_in, mixed_ref, rows_out, 0, gather_ref, lhs.at[0], per, outer)
        pooled_ref[...] = pooled[:, :bins].astype(jnp.bfloat16)
    else:
        left = pool_rows(rows_in, mixed_ref, rows_out, 0, gather_ref, lhs.at[0], per, outer)
        right = pool_rows(rows_in, mixed_ref, rows_out, ROWS, gather_ref, lhs.at[1], per, outer)
        each = bins // peers
        for seat in range(peers):
            mine = slice(seat * each, (seat + 1) * each)
            pair = jnp.concatenate([left[:, mine], right[:, mine]], axis=1).astype(jnp.bfloat16)
            for group in range(pooled_ref.shape[0]):
                pooled_ref[group, seat] = pair
    for k in range(peers):
        outs[k][...] = rows_out[me ^ k]


def corr_kernel(peers, outer, packed, scale, me_ref, *refs):
    if packed:
        packed_ref, refs = refs[0], refs[1:]
    queries = refs[:peers]
    refs, spec_refs = refs[: peers] + refs[peers + SPECTRA :], refs[peers : peers + SPECTRA]
    grad_ref, skip_ref, *tables, twist_ref, spread_ref = refs[peers : peers + 6]
    fwd_ref, bwd_ref = tables[:1], tables[1:]
    outs = refs[peers + 6 : 2 * peers + 6]
    rows_in, lhs_g, gated, parts_g, parts_y, lhs, rows_out = refs[2 * peers + 6 :]
    me = me_ref[0]
    ra, rb = radices(outer)
    per = outer // peers
    for k in range(peers):
        rows_in[me ^ k] = queries[k][...]
    each = LANES // POOL
    held = LANES // each
    place = lax.broadcasted_iota(jnp.int32, (ROWS, LANES), 1) // each
    zero = jnp.zeros((ROWS, LANES), jnp.float32)
    for tile in range(-(-outer // held)):
        count = min(held, outer - tile * held)
        used = count * each
        part = grad_ref[:, tile * LANES : tile * LANES + used]
        if used < LANES:
            part = jnp.concatenate([part, jnp.zeros((ROWS, LANES - used), jnp.float32)], axis=1)
        high = part.astype(jnp.bfloat16).astype(jnp.float32)
        low = part - high
        for j in range(count):
            rows = pl.ds((tile * held + j) * ROWS, ROWS)
            lhs_g[rows, :LANES] = jnp.where(place == j, high, zero).astype(jnp.bfloat16)
            lhs_g[rows, LANES:] = jnp.where(place == j, low, zero).astype(jnp.bfloat16)
    gated[...] = dot(lhs_g[...], spread_ref[...])
    for n1 in range(outer):
        lanes = slice((n1 % per) * LANES, (n1 % per + 1) * LANES)
        rows = pl.ds(n1 * ROWS, ROWS)
        gated[rows, :] = gated[rows, :] * rows_in[n1 // per, :, lanes].astype(jnp.float32)

    def load_g(n1):
        return gated[n1 * ROWS : (n1 + 1) * ROWS, :]

    first_pass(load_g, keep(parts_g), outer)
    chunk = rb * ROWS
    for alpha in range(ra):
        put(*second_pass(parts_g, alpha, outer, twist_ref), lhs.at[alpha // 2], alpha % 2 * chunk)
    for pair in range(ra // 2):
        both = lane_transform(lhs.at[pair], fwd_ref)
        for i in range(2):
            alpha = 2 * pair + i
            g = both[i * chunk : (i + 1) * chunk]
            each = ra // SPECTRA
            h = spec_refs[alpha // each][0, alpha % each * chunk : (alpha % each + 1) * chunk, :]
            gr, gi, hr, hi = g[:, :LANES], g[:, LANES:], h[:, :LANES], h[:, LANES:]
            put_product(gr * hr + gi * hi, gi * hr - gr * hi, lhs.at[ra // 2 + pair], i * chunk)
    for pair in range(ra // 2):
        y = lane_transform(lhs.at[ra // 2 + pair], bwd_ref)
        for i in range(2):
            back_second_pass(y[i * chunk : (i + 1) * chunk], 2 * pair + i, outer, twist_ref, keep(parts_y))
    skip = jnp.broadcast_to(skip_ref[...], (ROWS, LANES))

    def emit(n1, value):
        lanes = slice((n1 % per) * LANES, (n1 % per + 1) * LANES)
        rows_out[n1 // per, :, lanes] = (value + skip * load_g(n1)).astype(jnp.bfloat16)

    back_first_pass(parts_y, outer, emit, scale)
    step, steps = pl.program_id(0), pl.num_programs(0)
    for k in range(peers):
        outs[k][:, : per * LANES] = rows_out[me ^ k]
        if packed:
            half = steps // 2
            for chunk_at in range(packed_ref.shape[1] // (half * ROWS)):
                here = pl.ds((chunk_at * half + lax.rem(step, half)) * ROWS, ROWS)
                high, low = (part.astype(jnp.float32) for part in split(packed_ref[me ^ k, here, :]))
                lanes = slice((per + chunk_at) * LANES, (per + chunk_at + 1) * LANES)
                outs[k][:, lanes] = jnp.where(step < half, high, low).astype(jnp.bfloat16)


def whole(array):
    rank = len(array.shape)
    return pl.BlockSpec(array.shape, lambda i, me: (0,) * rank)


def by_rows(width, rows=ROWS, start=0):
    return pl.BlockSpec((rows, width), lambda i, me: (start + i, 0))


def call(kernel, name, me, steps, inputs, in_specs, out_shapes, out_specs, scratch, flops, aliases=None, near=(), vmem=()):
    moved = sum(x.size * x.dtype.itemsize for x in inputs)
    moved += sum(math.prod(o.shape) * o.dtype.itemsize for o in out_shapes)
    def space(i):
        return pltpu.VMEM if i in vmem else pltpu.HBM

    count = len(inputs)
    inputs = [x if i in near else pltpu.with_memory_space_constraint(x, space(i)) for i, x in enumerate(inputs)]
    out_shapes = [
        o if count + i in near else space(count + i)(o.shape, o.dtype) for i, o in enumerate(out_shapes)
    ]
    return pl.pallas_call(
        kernel,
        name=name,
        grid_spec=pltpu.PrefetchScalarGridSpec(
            num_scalar_prefetch=1,
            grid=(steps,),
            in_specs=in_specs,
            out_specs=out_specs,
            scratch_shapes=scratch,
        ),
        out_shape=out_shapes,
        input_output_aliases=aliases or {},
        compiler_params=pltpu.CompilerParams(
            dimension_semantics=("arbitrary",), vmem_limit_bytes=VMEM_LIMIT
        ),
        cost_estimate=pl.CostEstimate(flops=int(flops), bytes_accessed=moved, transcendentals=0),
    )(me, *inputs)


def shape(dims, dtype):
    return jax.ShapeDtypeStruct(dims, dtype)


def convolve(me, pieces, skip, tables, total_rows, start, before):
    peers = len(pieces)
    rows, width = pieces[0].shape[1:]
    length = width * peers
    outer = length // LANES
    ra, rb = radices(outer)
    chunk = rb * ROWS
    steps = rows // ROWS
    first = start // ROWS
    f32, bf16 = jnp.float32, jnp.bfloat16
    fwd, bwd, twist = tables["fwd"], tables["bwd"], tables["twist"]
    inputs = [*pieces, skip, *fwd, *bwd, twist]
    in_specs = [pl.BlockSpec((2, ROWS, width), lambda i, me: (0, i, 0))] * peers + [
        by_rows(1, start=first),
        *[whole(table) for table in (*fwd, *bwd, twist)],
    ]
    aliases = {}
    if before is not None:
        aliases = {1 + len(inputs): 0}
        inputs.append(before)
        in_specs.append(pl.BlockSpec(memory_space=pl.ANY))
    parts = pltpu.VMEM((2, rb, ra, ROWS, LANES), f32)

    def kernel(*refs):
        conv_kernel(peers, outer, *refs)

    part = (1, outer * ROWS // SPECTRA, 2 * LANES)
    out = call(
        kernel, "long_convolution", me, steps, inputs, in_specs,
        [shape((total_rows, length), f32)] + [shape((steps, *part[1:]), f32)] * SPECTRA,
        [by_rows(length, start=first)] + [pl.BlockSpec(part, lambda i, me: (i, 0, 0))] * SPECTRA,
        [
            pltpu.VMEM((peers, 2, ROWS, width), bf16),
            parts,
            parts,
            parts,
            pltpu.VMEM((ra + ra // 2, 2, 2 * chunk, 2 * LANES), bf16),
        ],
        rows * outer * 0.004 * MICROSECOND, aliases, (peers,), range(peers + 6, len(inputs) + 1),
    )
    return out[0], out[1:]


def pool(me, queries, mixed, gather, groups):
    peers = len(queries)
    rows, width = queries[0].shape
    length = width * peers
    outer = length // LANES
    bins = length // POOL
    bf16 = jnp.bfloat16
    if groups:
        step = 2 * ROWS
        pooled_shape = shape((groups, peers, rows // 2, LANES), bf16)
        pooled_spec = pl.BlockSpec((groups, peers, ROWS, LANES), lambda i, me: (0, 0, i, 0))
    else:
        step = ROWS
        pooled_shape = shape((rows, bins), bf16)
        pooled_spec = by_rows(bins)

    def kernel(*refs):
        pool_kernel(peers, outer, *refs)

    out = call(
        kernel, "pool_bins", me, rows // step, [*queries, mixed, gather],
        [by_rows(width, step)] * peers + [by_rows(length, step), whole(gather)],
        [shape((rows, width), bf16)] * peers + [pooled_shape],
        [by_rows(width, step)] * peers + [pooled_spec],
        [
            pltpu.VMEM((peers, step, width), bf16),
            pltpu.VMEM((peers, step, width), bf16),
            pltpu.VMEM((step // ROWS, outer * ROWS, 2 * LANES), bf16),
        ],
        rows * outer * 0.001 * MICROSECOND, vmem=range(1, peers + 1),
    )
    return out[:peers], out[peers]


def correlate(me, queries, grad_pooled, spec, skip, tables, spread, start, packed):
    peers = len(queries)
    width = queries[0].shape[1]
    rows = spec[0].shape[0] * ROWS
    length = width * peers
    outer = length // LANES
    bins = length // POOL
    ra, rb = radices(outer)
    chunk = rb * ROWS
    first = start // ROWS
    f32, bf16 = jnp.float32, jnp.bfloat16
    fwd, bwd, twist = tables["fwd_scaled"], tables["bwd_scaled"], tables["twist"]
    in_specs = [by_rows(width, start=first)] * peers + [
        *[pl.BlockSpec((1, *part.shape[1:]), lambda i, me: (i, 0, 0)) for part in spec],
        by_rows(bins, start=first),
        by_rows(1, start=first),
        *[whole(table) for table in (*fwd, *bwd, twist, spread)],
    ]
    parts = pltpu.VMEM((2, rb, ra, ROWS, LANES), f32)
    scratch = [
        pltpu.VMEM((peers, ROWS, width), bf16),
        pltpu.VMEM((outer * ROWS, 2 * LANES), bf16),
        pltpu.VMEM((outer * ROWS, LANES), f32),
        parts,
        parts,
        pltpu.VMEM((ra, 2, 2 * chunk, 2 * LANES), bf16),
        pltpu.VMEM((peers, ROWS, width), bf16),
    ]

    def kernel(*refs):
        corr_kernel(peers, outer, packed is not None, 1.0 / tables["scale"] ** 2, *refs)

    inputs = [*queries, *spec, grad_pooled, skip, *fwd, *bwd, twist, spread]
    sent = width
    if packed is not None:
        sent = width + packed.shape[1] // (rows // 2) * LANES
        inputs = [packed, *inputs]
        in_specs = [whole(packed), *in_specs]
    near = len(inputs) - 6
    return call(
        kernel, "long_correlation", me, rows // ROWS, inputs, in_specs,
        [shape((rows, sent), bf16)] * peers, [by_rows(sent)] * peers,
        scratch, rows * outer * 0.004 * MICROSECOND, near=((0,) if packed is not None else ()) + (near, near + 1, *range(len(inputs), len(inputs) + peers)),
    )


def lay_out(me, projections, filter_taps, peers, chunks, jobs, with_query):
    _, channels, width = projections.shape
    pencil = channels // peers
    rows = pencil // chunks
    f32, bf16 = jnp.float32, jnp.bfloat16
    count = len(jobs)
    query_count = peers if with_query else 0

    def kernel(me_ref, proj_ref, taps_ref, *refs):
        outs, queries = refs[:count], refs[count:-7]
        pair, taps, laid, passing, sems, out_sems, query_sems = refs[-7:]

        def fetch(i):
            chunk, k = jobs[i]
            here = pl.ds(pl.multiple_of((me_ref[0] ^ k) * pencil + chunk * rows, rows), rows)
            return (
                pltpu.make_async_copy(proj_ref.at[1, here], pair.at[i, 0], sems.at[i, 0]),
                pltpu.make_async_copy(proj_ref.at[2, here], pair.at[i, 1], sems.at[i, 1]),
                pltpu.make_async_copy(taps_ref.at[here], taps.at[i], sems.at[i, 2]),
            )

        def leave(i):
            return pltpu.make_async_copy(laid.at[i], outs[i], out_sems.at[i])

        def take(k):
            block = pl.ds(pl.multiple_of((me_ref[0] ^ k) * pencil, pencil), pencil)
            return pltpu.make_async_copy(proj_ref.at[0, block], passing.at[k], query_sems.at[k, 0])

        def hand_on(k):
            return pltpu.make_async_copy(passing.at[k], queries[k], query_sems.at[k, 1])

        for i in range(count):
            for copy in fetch(i):
                copy.start()
        for k in range(query_count):
            take(k).start()
        for i in range(count):
            keyed, valued, lags = fetch(i)
            keyed.wait()
            valued.wait()
            laid[i, 0] = (pair[i, 0].astype(f32) * pair[i, 1].astype(f32)).astype(bf16)
            lags.wait()
            laid[i, 1] = taps[i].astype(bf16)
            leave(i).start()
        for k in range(query_count):
            take(k).wait()
            hand_on(k).start()
        for i in range(count):
            leave(i).wait()
        for k in range(query_count):
            hand_on(k).wait()

    out_shapes = [shape((2, rows, width), bf16)] * count + [shape((pencil, width), bf16)] * query_count
    return call(
        kernel, "lay_out", me, 1, [projections, filter_taps],
        [pl.BlockSpec(memory_space=pltpu.HBM)] * 2,
        out_shapes,
        [pl.BlockSpec(memory_space=pltpu.HBM)] * len(out_shapes),
        [
            pltpu.VMEM((count, 2, rows, width), bf16),
            pltpu.VMEM((count, rows, width), f32),
            pltpu.VMEM((count, 2, rows, width), bf16),
            pltpu.VMEM((max(query_count, 1), pencil, width), bf16),
            pltpu.SemaphoreType.DMA((count, 3)),
            pltpu.SemaphoreType.DMA((count,)),
            pltpu.SemaphoreType.DMA((max(query_count, 1), 2)),
        ],
        rows * count * 0.015 * MICROSECOND,
    )


def by_track(me, head_weight, groups):
    channels, tracks = head_weight.shape
    half, own = channels // 2, tracks // groups
    padded = -(-own // LANES) * LANES
    dtype = head_weight.dtype
    steps = half // ROWS

    def kernel(me_ref, weight_ref, out_ref, rows_in, sems):
        first = pl.multiple_of((me_ref[0] & 1) * half, half)

        def fetch(i):
            return pltpu.make_async_copy(
                weight_ref.at[pl.ds(first + i * ROWS, ROWS)], rows_in.at[pl.ds(i * ROWS, ROWS)], sems.at[i]
            )

        for i in range(steps):
            fetch(i).start()
        for i in range(steps):
            fetch(i).wait()
        for group in range(groups):
            out_ref[group, :, :own] = rows_in[:, group * own : (group + 1) * own]
            if padded > own:
                out_ref[group, :, own:] = jnp.zeros((half, padded - own), dtype)

    out = shape((groups, half, padded), dtype)
    return call(
        kernel, "by_track", me, 1, [head_weight], [pl.BlockSpec(memory_space=pltpu.HBM)], [out], [whole(out)],
        [pltpu.VMEM((half, tracks), dtype), pltpu.SemaphoreType.DMA((steps,))], 2 * MICROSECOND, vmem=(1,),
    )[0]


def weight_pair(weight_ref, seats, pencil, own):
    groups, _, padded = weight_ref.shape
    rows = weight_ref[...].reshape(groups, seats, pencil // (2 * ROWS), 2, ROWS, padded)
    count = groups * seats * pencil // 2
    left, right = rows[:, :, :, 0].reshape(count, padded), rows[:, :, :, 1].reshape(count, padded)
    return left[:, :own], right[:, :own]


def head_rates(me, got, mine, other, bias, counts):
    groups, peers, half_rows, _ = got.shape
    own = counts.shape[1]
    seats = peers // 2
    pencil = 2 * half_rows
    bins = LANES // 2
    f32 = jnp.float32

    def kernel(me_ref, got_ref, mine_ref, other_ref, bias_ref, counts_ref, logits_ref, sums_ref):
        odd = me_ref[0] & 1
        total = jnp.broadcast_to(bias_ref[...], (bins, own))
        for weight_ref, place in ((mine_ref, odd), (other_ref, 1 - odd)):
            block = got_ref[:, pl.ds(place * seats, seats)].reshape(groups * seats * half_rows, LANES)
            turned = block.astype(f32).T.astype(jnp.bfloat16)
            left, right = weight_pair(weight_ref, seats, pencil, own)
            total = total + dot(turned[:bins], left) + dot(turned[bins:], right)
        logits_ref[...] = total
        rates = jax.nn.softplus(total) + rate_floor
        observed = counts_ref[...].astype(f32)
        sums_ref[0:1, :] = jnp.sum(rates, axis=0, keepdims=True)
        sums_ref[1:2, :] = jnp.sum(observed, axis=0, keepdims=True)
        sums_ref[2:3, :] = jnp.sum(observed * jnp.log(rates), axis=0, keepdims=True)
        sums_ref[3:8, :] = jnp.zeros((5, own), f32)

    inputs = [got, mine, other, bias, counts]
    return call(
        kernel, "head_rates", me, 1, inputs, [whole(x) for x in inputs],
        [shape((bins, own), f32), shape((8, own), f32)],
        [pl.BlockSpec((bins, own), lambda i, me: (0, 0)), pl.BlockSpec((8, own), lambda i, me: (0, 0))],
        [], 2 * bins * groups * peers * pencil * own, near=range(7),
    )


def head_grads(me, logits, sums, mine, other, counts):
    groups, half, _ = mine.shape
    own = counts.shape[1]
    peers = len(sums)
    seats = peers // 2
    pencil = half // seats
    bins = LANES // 2
    f32, bf16 = jnp.float32, jnp.bfloat16

    def kernel(me_ref, logits_ref, *refs):
        sums_refs = refs[:peers]
        mine_ref, other_ref, counts_ref, out_ref, loss_ref = refs[peers:]
        odd = me_ref[0] & 1
        totals = [ref[...] for ref in sums_refs]
        while len(totals) > 1:
            totals = [totals[i] + totals[i + 1] for i in range(0, len(totals), 2)]
        totals = totals[0]
        pred_total, obs_total, log_sum = totals[0:1], totals[1:2], totals[2:3]
        log_pred = jnp.log(pred_total)
        terms = total_weight * (pred_total - obs_total * log_pred) + obs_total * log_pred - log_sum
        mean = jnp.sum(terms, axis=1, keepdims=True) / (peers * bins * groups * own)
        loss_ref[...] = jnp.broadcast_to(mean, loss_ref.shape)
        ratio = obs_total / pred_total
        logits_here = logits_ref[...]
        rates = jax.nn.softplus(logits_here) + rate_floor
        observed = counts_ref[...].astype(f32)
        grad_rates = total_weight * (1.0 - ratio) + ratio - observed / rates
        grads = (grad_rates * jax.nn.sigmoid(logits_here)).astype(bf16)
        none = jnp.zeros_like(grads)
        in_left = jnp.concatenate([grads, none], axis=0)
        in_right = jnp.concatenate([none, grads], axis=0)
        across = (((1,), (1,)), ((), ()))
        for weight_ref, place in ((mine_ref, odd), (other_ref, 1 - odd)):
            left, right = weight_pair(weight_ref, seats, pencil, own)
            part = lax.dot_general(left, in_left, across, preferred_element_type=f32)
            part = part + lax.dot_general(right, in_right, across, preferred_element_type=f32)
            out_ref[:, pl.ds(place * seats, seats)] = part.astype(bf16).reshape(groups, seats, pencil // 2, LANES)

    inputs = [logits, *sums, mine, other, counts]
    out = shape((groups, peers, pencil // 2, LANES), bf16)
    return call(
        kernel, "head_grads", me, 1, inputs, [whole(x) for x in inputs],
        [out, shape((8, LANES), f32)],
        [whole(out), pl.BlockSpec((8, LANES), lambda i, me: (0, 0))],
        [], 4 * bins * groups * peers * pencil * own, near=(*range(peers + 4), peers + 5),
    )


def sum_grads(me, back):
    groups, peers, half_rows, _ = back.shape
    bins = LANES // 2
    f32 = jnp.float32

    def kernel(me_ref, back_ref, rows_ref, packed_ref):
        for seat in range(peers):
            total = back_ref[0, seat].astype(f32)
            for group in range(1, groups):
                total = total + back_ref[group, seat].astype(f32)
            packed_ref[seat] = total
            for i in range(half_rows // ROWS):
                pair = total[i * ROWS : (i + 1) * ROWS]
                lanes = slice(seat * bins, (seat + 1) * bins)
                rows_ref[2 * i * ROWS : (2 * i + 1) * ROWS, lanes] = pair[:, :bins]
                rows_ref[(2 * i + 1) * ROWS : (2 * i + 2) * ROWS, lanes] = pair[:, bins:]

    rows, packed = shape((2 * half_rows, peers * bins), f32), shape((peers, half_rows, LANES), f32)
    return call(
        kernel, "sum_grads", me, 1, [back], [whole(back)], [rows, packed], [whole(rows), whole(packed)], [], back.size,
        near=(0, 1, 2),
    )


def finish(me, projections, mixed_home, corr_home, spread, chunk, chunks, before, loss):
    peers = len(corr_home)
    _, channels, width = projections.shape
    pencil = channels // peers
    rows = pencil // chunks
    tiles = width // LANES
    each = LANES // POOL
    f32, bf16 = jnp.float32, jnp.bfloat16
    with_query = bool(mixed_home)
    payload = corr_home[0].shape[1]

    def kernel(me_ref, spread_ref, proj_ref, *refs):
        mixed_refs, corr_refs = refs[: len(mixed_home)], refs[len(mixed_home) : len(mixed_home) + peers]
        pair, mixed_in, corr_in, done, query_done, lhs, sems, out_sems = refs[-8:]
        if loss:
            loss_ref, mean_ref = refs[len(mixed_home) + peers], refs[-9]
            mean_ref[...] = loss_ref[0:1, 0:1]
        out_ref = refs[-9 - len(loss)]
        place = lax.broadcasted_iota(jnp.int32, (ROWS, LANES), 1) // each
        zero = jnp.zeros((ROWS, LANES), f32)

        def block(k, start, count):
            return pl.ds(pl.multiple_of((me_ref[0] ^ k) * pencil + start, ROWS), count)

        def here(k):
            return block(k, chunk * rows, rows)

        def fetch(k):
            return (
                pltpu.make_async_copy(corr_refs[k], corr_in.at[k], sems.at[k, 0]),
                pltpu.make_async_copy(proj_ref.at[1, here(k)], pair.at[k, 0], sems.at[k, 1]),
                pltpu.make_async_copy(proj_ref.at[2, here(k)], pair.at[k, 1], sems.at[k, 2]),
            )

        def fetch_mixed(k):
            return pltpu.make_async_copy(mixed_refs[k], mixed_in.at[k], sems.at[k, 3])

        def leave(k, plane):
            if plane == 0:
                return pltpu.make_async_copy(query_done.at[k], out_ref.at[0, block(k, 0, pencil)], out_sems.at[k, 0])
            return pltpu.make_async_copy(done.at[k, plane - 1], out_ref.at[plane, here(k)], out_sems.at[k, plane])

        for k in range(peers):
            for copy in fetch(k):
                copy.start()
            if with_query:
                fetch_mixed(k).start()
        for k in range(peers):
            for copy in fetch(k):
                copy.wait()
            corr = corr_in[k, :, :width].astype(f32)
            done[k, 0] = corr * pair[k, 1].astype(f32)
            leave(k, 1).start()
            done[k, 1] = corr * pair[k, 0].astype(f32)
            leave(k, 2).start()
            if not with_query:
                continue
            fetch_mixed(k).wait()
            for i in range(pencil // ROWS):
                part = slice(i * ROWS, (i + 1) * ROWS)
                inside = i % (rows // ROWS)
                source = inside // 2 * ROWS
                lanes = slice(width + i // (rows // ROWS) * LANES, width + (i // (rows // ROWS) + 1) * LANES)
                high = corr_in[k, source : source + ROWS, lanes].astype(f32)
                low = corr_in[k, rows // 2 + source : rows // 2 + source + ROWS, lanes].astype(f32)
                for t in range(tiles):
                    near = place == t + inside % 2 * tiles
                    lhs[i, t * ROWS : (t + 1) * ROWS, :LANES] = jnp.where(near, high, zero).astype(bf16)
                    lhs[i, t * ROWS : (t + 1) * ROWS, LANES:] = jnp.where(near, low, zero).astype(bf16)
                grad = dot(lhs[i], spread_ref[...])
                for t in range(tiles):
                    at = slice(t * LANES, (t + 1) * LANES)
                    query_done[k, part, at] = grad[t * ROWS : (t + 1) * ROWS] * mixed_in[k, part, at].astype(f32)
            leave(k, 0).start()
        for k in range(peers):
            for plane in range(0 if with_query else 1, 3):
                leave(k, plane).wait()

    inputs = [spread, projections, *mixed_home, *corr_home, *loss]
    in_specs = [whole(spread), pl.BlockSpec(memory_space=pltpu.HBM)]
    in_specs += [pl.BlockSpec(memory_space=pl.ANY)] * (len(mixed_home) + peers)
    in_specs += [whole(x) for x in loss]
    near = (0, *range(2, len(inputs)))
    aliases = {}
    if before is not None:
        aliases = {1 + len(inputs): 0}
        inputs.append(before)
        in_specs.append(pl.BlockSpec(memory_space=pl.ANY))
    return call(
        kernel, "finish", me, 1, inputs, in_specs,
        [shape((3, channels, width), f32)] + [shape((1, 1), f32)] * len(loss),
        [pl.BlockSpec(memory_space=pltpu.HBM)] + [pl.BlockSpec((1, 1), lambda i, me: (0, 0))] * len(loss),
        [
            pltpu.VMEM((peers, 2, rows, width), bf16),
            pltpu.VMEM((peers, pencil if with_query else ROWS, width), bf16),
            pltpu.VMEM((peers, rows, payload), bf16),
            pltpu.VMEM((peers, 2, rows, width), f32),
            pltpu.VMEM((peers, pencil if with_query else ROWS, width), f32),
            pltpu.VMEM((pencil // ROWS, tiles * ROWS, 2 * LANES), bf16),
            pltpu.SemaphoreType.DMA((peers, 4)),
            pltpu.SemaphoreType.DMA((peers, 3)),
        ],
        rows * peers * 0.03 * MICROSECOND, aliases, near=near,
    )


def swap(value, k, count):
    if k == 0:
        return value
    return lax.ppermute(value, "seq", [(i, i ^ k) for i in range(count)])


def pad_rows(value, rows):
    short = rows - value.shape[-2]
    if short == 0:
        return value
    widths = [(0, 0)] * value.ndim
    widths[-2] = (0, short)
    return jnp.pad(value, widths)


def aligned(projections, filter_taps, skip_gain, head_weight, head_bias, counts):
    f32 = jnp.float32
    _, channels, width = projections.shape
    peers = lax.axis_size("seq")
    groups = lax.axis_size("chan")
    seat = lax.axis_index("seq")
    group = lax.axis_index("chan")
    bins = width // POOL
    length = width * peers
    tracks = head_weight.shape[1]
    own_tracks = tracks // groups
    pencil = channels // peers
    chunks = CHUNKS
    rows = pencil // chunks
    me = jnp.asarray(seat, jnp.int32).reshape(1)
    tables = transform_tables(length)
    gather, spread = pool_tables()

    first = [(0, k) for k in range(peers // 2, peers)]
    others = [(0, k) for k in range(peers // 2)] + [(j, k) for j in range(1, chunks) for k in range(peers)]
    far = lay_out(me, projections, filter_taps, peers, chunks, first, False)
    me_next, _ = lax.optimization_barrier((me, far))
    rest = lay_out(me_next, projections, filter_taps, peers, chunks, others, True)
    me_next, _ = lax.optimization_barrier((me, rest))
    laid = dict(zip(first + others, [*far, *rest]))
    pieces = [[swap(laid[j, k], k, peers) for k in range(peers)] for j in range(chunks)]
    held_back, _ = lax.optimization_barrier((rest[len(others) :], pieces[0]))
    queries = [swap(held_back[k], k, peers) for k in range(peers)]
    skip = lax.dynamic_index_in_dim(skip_gain.reshape(peers, pencil, 1), seat, axis=0, keepdims=False)

    mine = by_track(me_next, head_weight, groups)
    mine = lax.all_to_all(mine, "chan", split_axis=0, concat_axis=0, tiled=True)

    mixed, specs = None, []
    for j in range(chunks):
        mixed, spec = convolve(me, pieces[j], skip, tables, pencil, j * rows, mixed)
        specs.append(spec)
    mixed_out, sent = pool(me, queries, mixed, gather, groups)
    mixed_home = [swap(mixed_out[k], k, peers) for k in range(peers)]

    def exchange(blocks):
        flat = blocks.reshape(groups * peers, pencil // 2, LANES)
        flat = lax.all_to_all(flat, ("chan", "seq"), split_axis=0, concat_axis=0, tiled=True)
        return flat.reshape(blocks.shape)

    got = exchange(sent)
    mine, _ = lax.optimization_barrier((mine, sent))
    other = swap(mine, 1, peers)
    own_bias = lax.dynamic_slice_in_dim(head_bias, group * own_tracks, own_tracks).reshape(1, own_tracks)
    own_counts = lax.dynamic_slice_in_dim(counts, group * own_tracks, own_tracks, axis=1)
    logits, sums = head_rates(me, got, mine, other, own_bias, own_counts)
    all_sums = [swap(sums, k, peers) for k in range(peers)]
    early, late = mixed_home[: peers - 1], mixed_home[peers - 1 :]
    logits, early = lax.optimization_barrier((logits, early))
    part, loss = head_grads(me, logits, all_sums, mine, other, own_counts)
    back = exchange(part)

    step = 1
    while step < groups:
        loss = loss + lax.ppermute(loss, "chan", [(i, i ^ step) for i in range(groups)])
        step *= 2

    back, loss, late = lax.optimization_barrier((back, loss, late))
    mixed_home = [*early, *late]
    grad_rows, packed = sum_grads(me, back)
    grads = None
    corr_home = []
    for j in range(chunks):
        corr = correlate(me, queries, grad_rows, specs[j], skip, tables, spread, j * rows, None if j else packed)
        grad_rows, _ = lax.optimization_barrier((grad_rows, corr))
        corr_home.append([swap(corr[k], k, peers) for k in range(peers)])
    for j in range(chunks):
        ours = [] if j else mixed_home
        grads, *rest = finish(me, projections, ours, corr_home[j], spread, j, chunks, grads, [] if j else [loss])
        if not j:
            mean_loss = rest[0].reshape(())
    return mean_loss, grads


def power_of_two(value):
    return value & (value - 1) == 0


def per_device(projections, filter_taps, skip_gain, head_weight, head_bias, counts):
    channels, width = projections.shape[1:]
    peers, groups = lax.axis_size("seq"), lax.axis_size("chan")
    pencil = channels // peers
    fits = (
        pencil % (2 * ROWS * CHUNKS) == 0
        and 2 * (width // POOL) == LANES
        and power_of_two(peers)
        and peers > 1
        and power_of_two(groups)
        and groups <= MOST_GROUPS
    )
    run = aligned if fits else general
    return run(projections, filter_taps, skip_gain, head_weight, head_bias, counts)


def general(projections, filter_taps, skip_gain, head_weight, head_bias, counts):
    f32, bf16 = jnp.float32, jnp.bfloat16
    _, channels, width = projections.shape
    peers = lax.axis_size("seq")
    groups = lax.axis_size("chan")
    seat = lax.axis_index("seq")
    group = lax.axis_index("chan")
    bins = width // POOL
    length = width * peers
    tracks = head_weight.shape[1]
    own_tracks = tracks // groups
    pencil = channels // peers
    rows = -(-pencil // ROWS) * ROWS
    me = jnp.asarray(seat, jnp.int32).reshape(1)
    tables = transform_tables(length)
    gather, spread = pool_tables()

    def block(array, k):
        return lax.dynamic_index_in_dim(array, seat ^ k, axis=-3, keepdims=False)

    query = projections[0]
    key_value = projections[1].astype(f32) * projections[2].astype(f32)
    stacked = jnp.stack([key_value.astype(bf16), filter_taps.astype(bf16)])
    stacked = stacked.reshape(2, peers, pencil, width)
    pieces = [pad_rows(swap(block(stacked, k), k, peers), rows) for k in range(peers)]
    query_blocks = query.reshape(peers, pencil, width)
    queries = [pad_rows(swap(block(query_blocks, k), k, peers), rows) for k in range(peers)]
    skip = pad_rows(block(skip_gain.reshape(peers, pencil, 1), 0), rows)

    half = channels // 2
    by_track = head_weight.reshape(2, half, groups, own_tracks).transpose(0, 2, 1, 3)
    mine = lax.dynamic_index_in_dim(by_track, seat & 1, axis=0, keepdims=False)
    mine = lax.all_to_all(mine, "chan", split_axis=0, concat_axis=0, tiled=True)
    other = swap(mine, 1, peers)
    mine = mine.reshape(groups * half, own_tracks)
    other = other.reshape(groups * half, own_tracks)

    mixed, spec = convolve(me, pieces, skip, tables, rows, 0, None)
    mixed_out, pooled = pool(me, queries, mixed, gather, 0)
    pooled = pooled[:pencil]
    mixed_home = [swap(mixed_out[k][:pencil], k, peers) for k in range(peers)]

    sent = pooled.reshape(pencil, peers, bins).transpose(1, 0, 2)
    sent = jnp.broadcast_to(sent[None], (groups, peers, pencil, bins))
    got = lax.all_to_all(
        sent.reshape(groups * peers, pencil, bins), ("chan", "seq"), split_axis=0, concat_axis=0, tiled=True
    )
    got = got.reshape(groups, 2, half, bins)
    low_half = got[:, 0].reshape(groups * half, bins)
    high_half = got[:, 1].reshape(groups * half, bins)
    odd = (seat & 1) == 1
    pooled_mine = jnp.where(odd, high_half, low_half)
    pooled_other = jnp.where(odd, low_half, high_half)

    def project(x, w):
        return lax.dot_general(x, w, (((0,), (0,)), ((), ())), preferred_element_type=f32)

    own_bias = lax.dynamic_slice_in_dim(head_bias, group * own_tracks, own_tracks)
    own_counts = lax.dynamic_slice_in_dim(counts, group * own_tracks, own_tracks, axis=1)
    logits = project(pooled_mine, mine) + project(pooled_other, other) + own_bias[None, :]
    rates = jax.nn.softplus(logits) + rate_floor
    observed = own_counts.astype(f32)
    partial_sums = jnp.stack(
        [jnp.sum(rates, axis=0), jnp.sum(observed, axis=0), jnp.sum(observed * jnp.log(rates), axis=0)]
    )
    pred_total, obs_total, log_sum = jnp.sum(lax.all_gather(partial_sums, "seq"), axis=0)
    log_pred = jnp.log(pred_total)
    loss_part = jnp.sum(
        total_weight * (pred_total - obs_total * log_pred) + obs_total * log_pred - log_sum
    )
    mean_loss = lax.psum(loss_part, "chan") / (bins * peers * tracks)
    ratio = obs_total / pred_total
    grad_rates = total_weight * (1.0 - ratio)[None, :] + ratio[None, :] - observed / rates
    grad_logits = (grad_rates * jax.nn.sigmoid(logits)).astype(bf16)

    def spread_back(w):
        return lax.dot_general(w, grad_logits, (((1,), (1,)), ((), ())), preferred_element_type=f32)

    part_mine = spread_back(mine).astype(bf16).reshape(groups, 1, half, bins)
    part_other = spread_back(other).astype(bf16).reshape(groups, 1, half, bins)
    part = jnp.concatenate(
        [jnp.where(odd, part_other, part_mine), jnp.where(odd, part_mine, part_other)], axis=1
    )
    back = lax.all_to_all(
        part.reshape(groups * peers, pencil, bins), ("chan", "seq"), split_axis=0, concat_axis=0, tiled=True
    )
    grad_pooled = jnp.sum(back.reshape(groups, peers, pencil, bins).astype(f32), axis=0)
    grad_home = [swap(block(grad_pooled, k), k, peers) for k in range(peers)]
    grad_rows = pad_rows(grad_pooled.transpose(1, 0, 2).reshape(pencil, peers * bins), rows)

    corr_out = correlate(me, queries, grad_rows, spec, skip, tables, spread, 0, None)
    corr_home = [swap(corr_out[k][:pencil], k, peers) for k in range(peers)]

    def assemble(parts):
        out = jnp.zeros((peers,) + parts[0].shape, parts[0].dtype)
        for k, part in enumerate(parts):
            out = lax.dynamic_update_index_in_dim(out, part, seat ^ k, axis=0)
        return out.reshape((channels,) + parts[0].shape[1:])

    grad_output = jnp.repeat(assemble(grad_home) / POOL, POOL, axis=1)
    grad_kv = assemble(corr_home).astype(f32)
    grad_query = grad_output * assemble(mixed_home).astype(f32)
    grads = jnp.stack(
        [grad_query, grad_kv * projections[2].astype(f32), grad_kv * projections[1].astype(f32)], axis=0
    )
    return mean_loss, grads


def solution(mesh):
    placed = (
        P(None, "chan", "seq"),
        P("chan", "seq"),
        P("chan"),
        P("chan", None),
        P(),
        P("seq", None),
    )
    return jax.shard_map(
        per_device,
        mesh=mesh,
        in_specs=placed,
        out_specs=(P(), P(None, "chan", "seq")),
        check_vma=False,
    )
```

```python
import math

import jax
import jax.numpy as jnp
import ml_dtypes
import numpy as np
from jax import lax
from jax.experimental import pallas as pl
from jax.experimental.pallas import tpu as pltpu
from jax.sharding import PartitionSpec as P

POOL = 32
LANES = 128
ROWS = 16
SHIFT = 0.25

total_weight = 0.2
rate_floor = 0.5

MICROSECOND = 1.0e9

VMEM_LIMIT = 20 * 1024 * 1024
CHUNKS = 2
SPECTRA = 4
MOST_GROUPS = 16


def split_bf16(table):
    high = table.astype(ml_dtypes.bfloat16)
    low = (table - high.astype(np.float64)).astype(ml_dtypes.bfloat16)
    return high, low


def kind_scale(table):
    values = np.unique(np.abs(table))
    factors = np.linspace(1.0, 2.0, 4001)

    def lost(factor):
        scaled = table[: LANES // 2] * factor
        return np.sum((scaled - split_bf16(scaled)[0].astype(np.float64)) ** 2) / factor**2

    rough = [np.sum((values * f - split_bf16(values * f)[0].astype(np.float64)) ** 2) / f**2 for f in factors]
    best = np.argsort(rough, kind="stable")[:8]
    return float(min((factors[i] for i in best), key=lost))


def radices(outer):
    first = 1
    while first * first < outer:
        first *= 2
    return first, outer // first


def transform_tables(length):
    outer = length // LANES
    idx = np.arange(LANES)
    angle = 2.0 * np.pi * (np.outer(idx, idx) % LANES) / LANES
    wr, wi = np.cos(angle), -np.sin(angle)
    forward = np.block([[wr, wi], [-wi, wr]])
    backward = np.block([[wr, -wi], [wi, wr]]) / length
    k1 = np.arange(outer)[:, None]
    twist = 2.0 * np.pi * (k1 - SHIFT) * idx[None, :] / length
    scale = kind_scale(forward)
    f_hi, f_lo = split_bf16(forward)
    b_hi, b_lo = split_bf16(backward)
    return dict(
        fwd=[f_hi, f_lo],
        bwd=[b_hi, b_lo],
        scale=scale,
        fwd_scaled=[split_bf16(forward * scale)[0]],
        bwd_scaled=[split_bf16(backward * scale)[0]],
        twist=np.stack([np.cos(twist), -np.sin(twist)]).astype(np.float32),
    )


def pool_tables():
    per = LANES // POOL
    lane = np.arange(LANES)
    hit = (lane[:, None] // POOL) == (lane[None, :] % per)
    gather = np.concatenate([hit, hit], axis=0) / POOL
    spread = np.concatenate([hit.T, hit.T], axis=0) / POOL
    return gather.astype(ml_dtypes.bfloat16), spread.astype(ml_dtypes.bfloat16)


def times(value, angle):
    re, im = value
    c, s = math.cos(angle), math.sin(angle)
    tiny = 1e-12
    if im is None:
        if abs(s) < tiny and c > 0:
            return (re, None)
        return (re * c, re * s)
    if abs(s) < tiny:
        return (re, im) if c > 0 else (-re, -im)
    if abs(c) < tiny:
        return (-im, re) if s > 0 else (im, -re)
    return (re * c - im * s, re * s + im * c)


def add(a, b):
    if a[1] is None and b[1] is None:
        return (a[0] + b[0], None)
    if a[1] is None:
        return (a[0] + b[0], b[1])
    if b[1] is None:
        return (a[0] + b[0], a[1])
    return (a[0] + b[0], a[1] + b[1])


def sub(a, b):
    if a[1] is None and b[1] is None:
        return (a[0] - b[0], None)
    if a[1] is None:
        return (a[0] - b[0], -b[1])
    if b[1] is None:
        return (a[0] - b[0], a[1])
    return (a[0] - b[0], a[1] - b[1])


def small_dft(values, sign):
    count = len(values)
    if count == 1:
        return values
    even = small_dft(values[0::2], sign)
    odd = small_dft(values[1::2], sign)
    out = [None] * count
    half = count // 2
    for k in range(half):
        turned = times(odd[k], sign * 2.0 * math.pi * k / count)
        out[k] = add(even[k], turned)
        out[k + half] = sub(even[k], turned)
    return out


def dot(a, b):
    return jnp.dot(a, b, preferred_element_type=jnp.float32)


def split(value):
    high = value.astype(jnp.bfloat16)
    return high, (value - high.astype(jnp.float32)).astype(jnp.bfloat16)


def put(re_parts, im_parts, lhs, start):
    for i, (re, im) in enumerate(zip(re_parts, im_parts)):
        rows = pl.ds(start + i * ROWS, ROWS)
        re_hi, re_lo = split(re)
        im_hi, im_lo = split(im)
        lhs[0, rows, :LANES] = re_hi
        lhs[0, rows, LANES:] = im_hi
        lhs[1, rows, :LANES] = re_lo
        lhs[1, rows, LANES:] = im_lo


def lane_transform(lhs, table_refs):
    high = lhs[0]
    if len(table_refs) == 1:
        table = table_refs[0][...]
        return dot(high, table) + dot(lhs[1], table)
    table_high, table_low = table_refs[0][...], table_refs[1][...]
    return dot(high, table_high) + (dot(lhs[1], table_high) + dot(high, table_low))


def first_pass(load, store, outer):
    ra, rb = radices(outer)
    for b in range(rb):
        values = [times((load(rb * a + b), None), 2.0 * math.pi * a * SHIFT / ra) for a in range(ra)]
        out = small_dft(values, -1)
        for alpha in range(ra):
            re, im = times(out[alpha], -2.0 * math.pi * b * (alpha - SHIFT) / outer)
            store(b, alpha, re, im)


def second_pass(parts, alpha, outer, twist_ref):
    ra, rb = radices(outer)
    values = [(parts[0, b, alpha], parts[1, b, alpha]) for b in range(rb)]
    out = small_dft(values, -1)
    res, ims = [], []
    for beta in range(rb):
        k1 = alpha + ra * beta
        tr = twist_ref[0, k1 : k1 + 1, :]
        ti = twist_ref[1, k1 : k1 + 1, :]
        re, im = out[beta]
        res.append(re * tr - im * ti)
        ims.append(re * ti + im * tr)
    return res, ims


def back_second_pass(spectrum, alpha, outer, twist_ref, store):
    ra, rb = radices(outer)
    values = []
    for beta in range(rb):
        k1 = alpha + ra * beta
        tr = twist_ref[0, k1 : k1 + 1, :]
        ti = twist_ref[1, k1 : k1 + 1, :]
        re = spectrum[beta * ROWS : (beta + 1) * ROWS, :LANES]
        im = spectrum[beta * ROWS : (beta + 1) * ROWS, LANES:]
        values.append((re * tr + im * ti, im * tr - re * ti))
    out = small_dft(values, +1)
    for b in range(rb):
        re, im = times(out[b], 2.0 * math.pi * b * (alpha - SHIFT) / outer)
        store(b, alpha, re, im)


def back_first_pass(parts, outer, emit, scale=1.0):
    ra, rb = radices(outer)
    for b in range(rb):
        values = [(parts[0, b, alpha], parts[1, b, alpha]) for alpha in range(ra)]
        out = small_dft(values, +1)
        for a in range(ra):
            angle = -2.0 * math.pi * a * SHIFT / ra
            re, im = out[a]
            c, s = math.cos(angle) * scale, math.sin(angle) * scale
            if a == 0:
                emit(rb * a + b, re if scale == 1.0 else re * scale)
            else:
                emit(rb * a + b, re * c - im * s)


def put_product(re, im, lhs, start):
    rows = [slice(i, i + ROWS) for i in range(0, re.shape[0], ROWS)]
    put([re[r] for r in rows], [im[r] for r in rows], lhs, start)


def keep(parts):
    def store(b, alpha, re, im):
        parts[0, b, alpha] = re
        parts[1, b, alpha] = im

    return store


def conv_kernel(peers, outer, me_ref, *refs):
    pieces = refs[:peers]
    skip_ref, *tables, twist_ref = refs[peers : peers + 6]
    fwd_ref, bwd_ref = tables[:2], tables[2:]
    mixed_ref = refs[-6 - SPECTRA]
    spec_refs = refs[-5 - SPECTRA : -5]
    rows_in, parts_x, parts_h, parts_y, lhs = refs[-5:]
    me = me_ref[0]
    ra, rb = radices(outer)
    per = outer // peers
    for k in range(peers):
        rows_in[me ^ k] = pieces[k][...]

    def loader(which):
        def load(n1):
            lanes = slice((n1 % per) * LANES, (n1 % per + 1) * LANES)
            return rows_in[n1 // per, which, :, lanes].astype(jnp.float32)

        return load

    load_x = loader(0)
    first_pass(load_x, keep(parts_x), outer)
    first_pass(loader(1), keep(parts_h), outer)
    chunk = rb * ROWS
    for alpha in range(ra):
        put(*second_pass(parts_x, alpha, outer, twist_ref), lhs.at[alpha], 0)
        put(*second_pass(parts_h, alpha, outer, twist_ref), lhs.at[alpha], chunk)
    for alpha in range(ra):
        both = lane_transform(lhs.at[alpha], fwd_ref)
        x, h = both[:chunk], both[chunk:]
        each = ra // SPECTRA
        spec_refs[alpha // each][0, alpha % each * chunk : (alpha % each + 1) * chunk, :] = h
        xr, xi, hr, hi = x[:, :LANES], x[:, LANES:], h[:, :LANES], h[:, LANES:]
        put_product(xr * hr - xi * hi, xr * hi + xi * hr, lhs.at[ra + alpha // 2], alpha % 2 * chunk)
    for pair in range(ra // 2):
        y = lane_transform(lhs.at[ra + pair], bwd_ref)
        for i in range(2):
            back_second_pass(y[i * chunk : (i + 1) * chunk], 2 * pair + i, outer, twist_ref, keep(parts_y))
    skip = jnp.broadcast_to(skip_ref[...], (ROWS, LANES))

    def emit(n1, value):
        mixed_ref[:, n1 * LANES : (n1 + 1) * LANES] = value + skip * load_x(n1)

    back_first_pass(parts_y, outer, emit)


def pool_rows(rows_in, mixed_ref, rows_out, row, gather_ref, lhs, per, outer):
    for n1 in range(outer):
        lanes = slice((n1 % per) * LANES, (n1 % per + 1) * LANES)
        query = rows_in[n1 // per, row : row + ROWS, lanes].astype(jnp.float32)
        mixed = mixed_ref[row : row + ROWS, n1 * LANES : (n1 + 1) * LANES]
        rows_out[n1 // per, row : row + ROWS, lanes] = mixed.astype(jnp.bfloat16)
        high, low = split(query * mixed)
        lhs[n1 * ROWS : (n1 + 1) * ROWS, :LANES] = high
        lhs[n1 * ROWS : (n1 + 1) * ROWS, LANES:] = low
    sums = dot(lhs[...], gather_ref[...])
    each = LANES // POOL
    held = LANES // each
    place = lax.broadcasted_iota(jnp.int32, (ROWS, LANES), 1) // each
    tiles = []
    for tile in range(-(-outer // held)):
        total = jnp.zeros((ROWS, LANES), jnp.float32)
        for j in range(min(held, outer - tile * held)):
            n1 = tile * held + j
            total = jnp.where(place == j, sums[n1 * ROWS : (n1 + 1) * ROWS], total)
        tiles.append(total)
    return jnp.concatenate(tiles, axis=1)


def pool_kernel(peers, outer, me_ref, *refs):
    queries = refs[:peers]
    mixed_ref, gather_ref = refs[peers : peers + 2]
    outs = refs[peers + 2 : 2 * peers + 2]
    pooled_ref, rows_in, rows_out, lhs = refs[2 * peers + 2 :]
    me = me_ref[0]
    per = outer // peers
    for k in range(peers):
        rows_in[me ^ k] = queries[k][...]
    rows = mixed_ref.shape[0]
    bins = outer * LANES // POOL
    if rows == ROWS:
        pooled = pool_rows(rows_in, mixed_ref, rows_out, 0, gather_ref, lhs.at[0], per, outer)
        pooled_ref[...] = pooled[:, :bins].astype(jnp.bfloat16)
    else:
        left = pool_rows(rows_in, mixed_ref, rows_out, 0, gather_ref, lhs.at[0], per, outer)
        right = pool_rows(rows_in, mixed_ref, rows_out, ROWS, gather_ref, lhs.at[1], per, outer)
        each = bins // peers
        for seat in range(peers):
            mine = slice(seat * each, (seat + 1) * each)
            pair = jnp.concatenate([left[:, mine], right[:, mine]], axis=1).astype(jnp.bfloat16)
            for group in range(pooled_ref.shape[0]):
                pooled_ref[group, seat] = pair
    for k in range(peers):
        outs[k][...] = rows_out[me ^ k]


def corr_kernel(peers, outer, packed, scale, me_ref, *refs):
    if packed:
        packed_ref, refs = refs[0], refs[1:]
    queries = refs[:peers]
    refs, spec_refs = refs[: peers] + refs[peers + SPECTRA :], refs[peers : peers + SPECTRA]
    grad_ref, skip_ref, *tables, twist_ref, spread_ref = refs[peers : peers + 6]
    fwd_ref, bwd_ref = tables[:1], tables[1:]
    outs = refs[peers + 6 : 2 * peers + 6]
    rows_in, lhs_g, gated, parts_g, parts_y, lhs, rows_out = refs[2 * peers + 6 :]
    me = me_ref[0]
    ra, rb = radices(outer)
    per = outer // peers
    for k in range(peers):
        rows_in[me ^ k] = queries[k][...]
    each = LANES // POOL
    held = LANES // each
    place = lax.broadcasted_iota(jnp.int32, (ROWS, LANES), 1) // each
    zero = jnp.zeros((ROWS, LANES), jnp.float32)
    for tile in range(-(-outer // held)):
        count = min(held, outer - tile * held)
        used = count * each
        part = grad_ref[:, tile * LANES : tile * LANES + used]
        if used < LANES:
            part = jnp.concatenate([part, jnp.zeros((ROWS, LANES - used), jnp.float32)], axis=1)
        high = part.astype(jnp.bfloat16).astype(jnp.float32)
        low = part - high
        for j in range(count):
            rows = pl.ds((tile * held + j) * ROWS, ROWS)
            lhs_g[rows, :LANES] = jnp.where(place == j, high, zero).astype(jnp.bfloat16)
            lhs_g[rows, LANES:] = jnp.where(place == j, low, zero).astype(jnp.bfloat16)
    gated[...] = dot(lhs_g[...], spread_ref[...])
    for n1 in range(outer):
        lanes = slice((n1 % per) * LANES, (n1 % per + 1) * LANES)
        rows = pl.ds(n1 * ROWS, ROWS)
        gated[rows, :] = gated[rows, :] * rows_in[n1 // per, :, lanes].astype(jnp.float32)

    def load_g(n1):
        return gated[n1 * ROWS : (n1 + 1) * ROWS, :]

    first_pass(load_g, keep(parts_g), outer)
    chunk = rb * ROWS
    for alpha in range(ra):
        put(*second_pass(parts_g, alpha, outer, twist_ref), lhs.at[alpha // 2], alpha % 2 * chunk)
    for pair in range(ra // 2):
        both = lane_transform(lhs.at[pair], fwd_ref)
        for i in range(2):
            alpha = 2 * pair + i
            g = both[i * chunk : (i + 1) * chunk]
            each = ra // SPECTRA
            h = spec_refs[alpha // each][0, alpha % each * chunk : (alpha % each + 1) * chunk, :]
            gr, gi, hr, hi = g[:, :LANES], g[:, LANES:], h[:, :LANES], h[:, LANES:]
            put_product(gr * hr + gi * hi, gi * hr - gr * hi, lhs.at[ra // 2 + pair], i * chunk)
    for pair in range(ra // 2):
        y = lane_transform(lhs.at[ra // 2 + pair], bwd_ref)
        for i in range(2):
            back_second_pass(y[i * chunk : (i + 1) * chunk], 2 * pair + i, outer, twist_ref, keep(parts_y))
    skip = jnp.broadcast_to(skip_ref[...], (ROWS, LANES))

    def emit(n1, value):
        lanes = slice((n1 % per) * LANES, (n1 % per + 1) * LANES)
        rows_out[n1 // per, :, lanes] = (value + skip * load_g(n1)).astype(jnp.bfloat16)

    back_first_pass(parts_y, outer, emit, scale)
    step, steps = pl.program_id(0), pl.num_programs(0)
    for k in range(peers):
        outs[k][:, : per * LANES] = rows_out[me ^ k]
        if packed:
            half = steps // 2
            for chunk_at in range(packed_ref.shape[1] // (half * ROWS)):
                here = pl.ds((chunk_at * half + lax.rem(step, half)) * ROWS, ROWS)
                high, low = (part.astype(jnp.float32) for part in split(packed_ref[me ^ k, here, :]))
                lanes = slice((per + chunk_at) * LANES, (per + chunk_at + 1) * LANES)
                outs[k][:, lanes] = jnp.where(step < half, high, low).astype(jnp.bfloat16)


def whole(array):
    rank = len(array.shape)
    return pl.BlockSpec(array.shape, lambda i, me: (0,) * rank)


def by_rows(width, rows=ROWS, start=0):
    return pl.BlockSpec((rows, width), lambda i, me: (start + i, 0))


def call(kernel, name, me, steps, inputs, in_specs, out_shapes, out_specs, scratch, flops, aliases=None, near=(), vmem=()):
    moved = sum(x.size * x.dtype.itemsize for x in inputs)
    moved += sum(math.prod(o.shape) * o.dtype.itemsize for o in out_shapes)
    def space(i):
        return pltpu.VMEM if i in vmem else pltpu.HBM

    count = len(inputs)
    inputs = [x if i in near else pltpu.with_memory_space_constraint(x, space(i)) for i, x in enumerate(inputs)]
    out_shapes = [
        o if count + i in near else space(count + i)(o.shape, o.dtype) for i, o in enumerate(out_shapes)
    ]
    return pl.pallas_call(
        kernel,
        name=name,
        grid_spec=pltpu.PrefetchScalarGridSpec(
            num_scalar_prefetch=1,
            grid=(steps,),
            in_specs=in_specs,
            out_specs=out_specs,
            scratch_shapes=scratch,
        ),
        out_shape=out_shapes,
        input_output_aliases=aliases or {},
        compiler_params=pltpu.CompilerParams(
            dimension_semantics=("arbitrary",), vmem_limit_bytes=VMEM_LIMIT
        ),
        cost_estimate=pl.CostEstimate(flops=int(flops), bytes_accessed=moved, transcendentals=0),
    )(me, *inputs)


def shape(dims, dtype):
    return jax.ShapeDtypeStruct(dims, dtype)


def convolve(me, pieces, skip, tables, total_rows, start, before):
    peers = len(pieces)
    rows, width = pieces[0].shape[1:]
    length = width * peers
    outer = length // LANES
    ra, rb = radices(outer)
    chunk = rb * ROWS
    steps = rows // ROWS
    first = start // ROWS
    f32, bf16 = jnp.float32, jnp.bfloat16
    fwd, bwd, twist = tables["fwd"], tables["bwd"], tables["twist"]
    inputs = [*pieces, skip, *fwd, *bwd, twist]
    in_specs = [pl.BlockSpec((2, ROWS, width), lambda i, me: (0, i, 0))] * peers + [
        by_rows(1, start=first),
        *[whole(table) for table in (*fwd, *bwd, twist)],
    ]
    aliases = {}
    if before is not None:
        aliases = {1 + len(inputs): 0}
        inputs.append(before)
        in_specs.append(pl.BlockSpec(memory_space=pl.ANY))
    parts = pltpu.VMEM((2, rb, ra, ROWS, LANES), f32)

    def kernel(*refs):
        conv_kernel(peers, outer, *refs)

    part = (1, outer * ROWS // SPECTRA, 2 * LANES)
    out = call(
        kernel, "long_convolution", me, steps, inputs, in_specs,
        [shape((total_rows, length), f32)] + [shape((steps, *part[1:]), f32)] * SPECTRA,
        [by_rows(length, start=first)] + [pl.BlockSpec(part, lambda i, me: (i, 0, 0))] * SPECTRA,
        [
            pltpu.VMEM((peers, 2, ROWS, width), bf16),
            parts,
            parts,
            parts,
            pltpu.VMEM((ra + ra // 2, 2, 2 * chunk, 2 * LANES), bf16),
        ],
        rows * outer * 0.004 * MICROSECOND, aliases, (peers,), range(peers + 6, len(inputs) + 1),
    )
    return out[0], out[1:]


def pool(me, queries, mixed, gather, groups):
    peers = len(queries)
    rows, width = queries[0].shape
    length = width * peers
    outer = length // LANES
    bins = length // POOL
    bf16 = jnp.bfloat16
    if groups:
        step = 2 * ROWS
        pooled_shape = shape((groups, peers, rows // 2, LANES), bf16)
        pooled_spec = pl.BlockSpec((groups, peers, ROWS, LANES), lambda i, me: (0, 0, i, 0))
    else:
        step = ROWS
        pooled_shape = shape((rows, bins), bf16)
        pooled_spec = by_rows(bins)

    def kernel(*refs):
        pool_kernel(peers, outer, *refs)

    out = call(
        kernel, "pool_bins", me, rows // step, [*queries, mixed, gather],
        [by_rows(width, step)] * peers + [by_rows(length, step), whole(gather)],
        [shape((rows, width), bf16)] * peers + [pooled_shape],
        [by_rows(width, step)] * peers + [pooled_spec],
        [
            pltpu.VMEM((peers, step, width), bf16),
            pltpu.VMEM((peers, step, width), bf16),
            pltpu.VMEM((step // ROWS, outer * ROWS, 2 * LANES), bf16),
        ],
        rows * outer * 0.001 * MICROSECOND, vmem=range(1, peers + 1),
    )
    return out[:peers], out[peers]


def correlate(me, queries, grad_pooled, spec, skip, tables, spread, start, packed):
    peers = len(queries)
    width = queries[0].shape[1]
    rows = spec[0].shape[0] * ROWS
    length = width * peers
    outer = length // LANES
    bins = length // POOL
    ra, rb = radices(outer)
    chunk = rb * ROWS
    first = start // ROWS
    f32, bf16 = jnp.float32, jnp.bfloat16
    fwd, bwd, twist = tables["fwd_scaled"], tables["bwd_scaled"], tables["twist"]
    in_specs = [by_rows(width, start=first)] * peers + [
        *[pl.BlockSpec((1, *part.shape[1:]), lambda i, me: (i, 0, 0)) for part in spec],
        by_rows(bins, start=first),
        by_rows(1, start=first),
        *[whole(table) for table in (*fwd, *bwd, twist, spread)],
    ]
    parts = pltpu.VMEM((2, rb, ra, ROWS, LANES), f32)
    scratch = [
        pltpu.VMEM((peers, ROWS, width), bf16),
        pltpu.VMEM((outer * ROWS, 2 * LANES), bf16),
        pltpu.VMEM((outer * ROWS, LANES), f32),
        parts,
        parts,
        pltpu.VMEM((ra, 2, 2 * chunk, 2 * LANES), bf16),
        pltpu.VMEM((peers, ROWS, width), bf16),
    ]

    def kernel(*refs):
        corr_kernel(peers, outer, packed is not None, 1.0 / tables["scale"] ** 2, *refs)

    inputs = [*queries, *spec, grad_pooled, skip, *fwd, *bwd, twist, spread]
    sent = width
    if packed is not None:
        sent = width + packed.shape[1] // (rows // 2) * LANES
        inputs = [packed, *inputs]
        in_specs = [whole(packed), *in_specs]
    near = len(inputs) - 6
    return call(
        kernel, "long_correlation", me, rows // ROWS, inputs, in_specs,
        [shape((rows, sent), bf16)] * peers, [by_rows(sent)] * peers,
        scratch, rows * outer * 0.004 * MICROSECOND, near=((0,) if packed is not None else ()) + (near, near + 1, *range(len(inputs), len(inputs) + peers)),
    )


def lay_out(me, projections, filter_taps, peers, chunks, jobs, with_query):
    _, channels, width = projections.shape
    pencil = channels // peers
    rows = pencil // chunks
    f32, bf16 = jnp.float32, jnp.bfloat16
    count = len(jobs)
    query_count = peers if with_query else 0

    def kernel(me_ref, proj_ref, taps_ref, *refs):
        outs, queries = refs[:count], refs[count:-7]
        pair, taps, laid, passing, sems, out_sems, query_sems = refs[-7:]

        def fetch(i):
            chunk, k = jobs[i]
            here = pl.ds(pl.multiple_of((me_ref[0] ^ k) * pencil + chunk * rows, rows), rows)
            return (
                pltpu.make_async_copy(proj_ref.at[1, here], pair.at[i, 0], sems.at[i, 0]),
                pltpu.make_async_copy(proj_ref.at[2, here], pair.at[i, 1], sems.at[i, 1]),
                pltpu.make_async_copy(taps_ref.at[here], taps.at[i], sems.at[i, 2]),
            )

        def leave(i):
            return pltpu.make_async_copy(laid.at[i], outs[i], out_sems.at[i])

        def take(k):
            block = pl.ds(pl.multiple_of((me_ref[0] ^ k) * pencil, pencil), pencil)
            return pltpu.make_async_copy(proj_ref.at[0, block], passing.at[k], query_sems.at[k, 0])

        def hand_on(k):
            return pltpu.make_async_copy(passing.at[k], queries[k], query_sems.at[k, 1])

        for i in range(count):
            for copy in fetch(i):
                copy.start()
        for k in range(query_count):
            take(k).start()
        for i in range(count):
            keyed, valued, lags = fetch(i)
            keyed.wait()
            valued.wait()
            laid[i, 0] = (pair[i, 0].astype(f32) * pair[i, 1].astype(f32)).astype(bf16)
            lags.wait()
            laid[i, 1] = taps[i].astype(bf16)
            leave(i).start()
        for k in range(query_count):
            take(k).wait()
            hand_on(k).start()
        for i in range(count):
            leave(i).wait()
        for k in range(query_count):
            hand_on(k).wait()

    out_shapes = [shape((2, rows, width), bf16)] * count + [shape((pencil, width), bf16)] * query_count
    return call(
        kernel, "lay_out", me, 1, [projections, filter_taps],
        [pl.BlockSpec(memory_space=pltpu.HBM)] * 2,
        out_shapes,
        [pl.BlockSpec(memory_space=pltpu.HBM)] * len(out_shapes),
        [
            pltpu.VMEM((max(count, 1), 2, rows, width), bf16),
            pltpu.VMEM((max(count, 1), rows, width), f32),
            pltpu.VMEM((max(count, 1), 2, rows, width), bf16),
            pltpu.VMEM((max(query_count, 1), pencil, width), bf16),
            pltpu.SemaphoreType.DMA((max(count, 1), 3)),
            pltpu.SemaphoreType.DMA((max(count, 1),)),
            pltpu.SemaphoreType.DMA((max(query_count, 1), 2)),
        ],
        max(rows * count * 0.015, 2.0) * MICROSECOND,
    )


def by_track(me, head_weight, groups):
    channels, tracks = head_weight.shape
    half, own = channels // 2, tracks // groups
    padded = -(-own // LANES) * LANES
    dtype = head_weight.dtype
    steps = half // ROWS

    def kernel(me_ref, weight_ref, out_ref, rows_in, sems):
        first = pl.multiple_of((me_ref[0] & 1) * half, half)

        def fetch(i):
            return pltpu.make_async_copy(
                weight_ref.at[pl.ds(first + i * ROWS, ROWS)], rows_in.at[pl.ds(i * ROWS, ROWS)], sems.at[i]
            )

        for i in range(steps):
            fetch(i).start()
        for i in range(steps):
            fetch(i).wait()
        for group in range(groups):
            out_ref[group, :, :own] = rows_in[:, group * own : (group + 1) * own]
            if padded > own:
                out_ref[group, :, own:] = jnp.zeros((half, padded - own), dtype)

    out = shape((groups, half, padded), dtype)
    return call(
        kernel, "by_track", me, 1, [head_weight], [pl.BlockSpec(memory_space=pltpu.HBM)], [out], [whole(out)],
        [pltpu.VMEM((half, tracks), dtype), pltpu.SemaphoreType.DMA((steps,))], 2 * MICROSECOND, vmem=(1,),
    )[0]


def weight_pair(weight_ref, seats, pencil, own):
    groups, _, padded = weight_ref.shape
    rows = weight_ref[...].reshape(groups, seats, pencil // (2 * ROWS), 2, ROWS, padded)
    count = groups * seats * pencil // 2
    left, right = rows[:, :, :, 0].reshape(count, padded), rows[:, :, :, 1].reshape(count, padded)
    return left[:, :own], right[:, :own]


def head_rates(me, got, mine, other, bias, counts):
    groups, peers, half_rows, _ = got.shape
    own = counts.shape[1]
    seats = peers // 2
    pencil = 2 * half_rows
    bins = LANES // 2
    f32 = jnp.float32

    def kernel(me_ref, got_ref, mine_ref, other_ref, bias_ref, counts_ref, logits_ref, sums_ref):
        odd = me_ref[0] & 1
        total = jnp.broadcast_to(bias_ref[...], (bins, own))
        for weight_ref, place in ((mine_ref, odd), (other_ref, 1 - odd)):
            block = got_ref[:, pl.ds(place * seats, seats)].reshape(groups * seats * half_rows, LANES)
            turned = block.astype(f32).T.astype(jnp.bfloat16)
            left, right = weight_pair(weight_ref, seats, pencil, own)
            total = total + dot(turned[:bins], left) + dot(turned[bins:], right)
        logits_ref[...] = total
        rates = jax.nn.softplus(total) + rate_floor
        observed = counts_ref[...].astype(f32)
        sums_ref[0:1, :] = jnp.sum(rates, axis=0, keepdims=True)
        sums_ref[1:2, :] = jnp.sum(observed, axis=0, keepdims=True)
        sums_ref[2:3, :] = jnp.sum(observed * jnp.log(rates), axis=0, keepdims=True)
        sums_ref[3:8, :] = jnp.zeros((5, own), f32)

    inputs = [got, mine, other, bias, counts]
    return call(
        kernel, "head_rates", me, 1, inputs, [whole(x) for x in inputs],
        [shape((bins, own), f32), shape((8, own), f32)],
        [pl.BlockSpec((bins, own), lambda i, me: (0, 0)), pl.BlockSpec((8, own), lambda i, me: (0, 0))],
        [], 2 * bins * groups * peers * pencil * own, near=range(7),
    )


def head_grads(me, logits, sums, mine, other, counts):
    groups, half, _ = mine.shape
    own = counts.shape[1]
    peers = len(sums)
    seats = peers // 2
    pencil = half // seats
    bins = LANES // 2
    f32, bf16 = jnp.float32, jnp.bfloat16

    def kernel(me_ref, logits_ref, *refs):
        sums_refs = refs[:peers]
        mine_ref, other_ref, counts_ref, out_ref, loss_ref = refs[peers:]
        odd = me_ref[0] & 1
        totals = [ref[...] for ref in sums_refs]
        while len(totals) > 1:
            totals = [totals[i] + totals[i + 1] for i in range(0, len(totals), 2)]
        totals = totals[0]
        pred_total, obs_total, log_sum = totals[0:1], totals[1:2], totals[2:3]
        log_pred = jnp.log(pred_total)
        terms = total_weight * (pred_total - obs_total * log_pred) + obs_total * log_pred - log_sum
        mean = jnp.sum(terms, axis=1, keepdims=True) / (peers * bins * groups * own)
        loss_ref[...] = jnp.broadcast_to(mean, loss_ref.shape)
        ratio = obs_total / pred_total
        logits_here = logits_ref[...]
        rates = jax.nn.softplus(logits_here) + rate_floor
        observed = counts_ref[...].astype(f32)
        grad_rates = total_weight * (1.0 - ratio) + ratio - observed / rates
        grads = (grad_rates * jax.nn.sigmoid(logits_here)).astype(bf16)
        none = jnp.zeros_like(grads)
        in_left = jnp.concatenate([grads, none], axis=0)
        in_right = jnp.concatenate([none, grads], axis=0)
        across = (((1,), (1,)), ((), ()))
        for weight_ref, place in ((mine_ref, odd), (other_ref, 1 - odd)):
            left, right = weight_pair(weight_ref, seats, pencil, own)
            part = lax.dot_general(left, in_left, across, preferred_element_type=f32)
            part = part + lax.dot_general(right, in_right, across, preferred_element_type=f32)
            out_ref[:, pl.ds(place * seats, seats)] = part.astype(bf16).reshape(groups, seats, pencil // 2, LANES)

    inputs = [logits, *sums, mine, other, counts]
    out = shape((groups, peers, pencil // 2, LANES), bf16)
    return call(
        kernel, "head_grads", me, 1, inputs, [whole(x) for x in inputs],
        [out, shape((8, LANES), f32)],
        [whole(out), pl.BlockSpec((8, LANES), lambda i, me: (0, 0))],
        [], 4 * bins * groups * peers * pencil * own, near=(*range(peers + 4), peers + 5),
    )


def sum_grads(me, back):
    groups, peers, half_rows, _ = back.shape
    bins = LANES // 2
    f32 = jnp.float32

    def kernel(me_ref, back_ref, rows_ref, packed_ref):
        for seat in range(peers):
            total = back_ref[0, seat].astype(f32)
            for group in range(1, groups):
                total = total + back_ref[group, seat].astype(f32)
            packed_ref[seat] = total
            for i in range(half_rows // ROWS):
                pair = total[i * ROWS : (i + 1) * ROWS]
                lanes = slice(seat * bins, (seat + 1) * bins)
                rows_ref[2 * i * ROWS : (2 * i + 1) * ROWS, lanes] = pair[:, :bins]
                rows_ref[(2 * i + 1) * ROWS : (2 * i + 2) * ROWS, lanes] = pair[:, bins:]

    rows, packed = shape((2 * half_rows, peers * bins), f32), shape((peers, half_rows, LANES), f32)
    return call(
        kernel, "sum_grads", me, 1, [back], [whole(back)], [rows, packed], [whole(rows), whole(packed)], [], back.size,
        near=(0, 1, 2),
    )


def finish(me, projections, mixed_home, corr_home, spread, chunk, chunks, before, loss):
    peers = len(corr_home)
    _, channels, width = projections.shape
    pencil = channels // peers
    rows = pencil // chunks
    tiles = width // LANES
    each = LANES // POOL
    f32, bf16 = jnp.float32, jnp.bfloat16
    with_query = bool(mixed_home)
    payload = corr_home[0].shape[1]

    def kernel(me_ref, spread_ref, proj_ref, *refs):
        mixed_refs, corr_refs = refs[: len(mixed_home)], refs[len(mixed_home) : len(mixed_home) + peers]
        pair, mixed_in, corr_in, done, query_done, lhs, sems, out_sems = refs[-8:]
        if loss:
            loss_ref, mean_ref = refs[len(mixed_home) + peers], refs[-9]
            mean_ref[...] = loss_ref[0:1, 0:1]
        out_ref = refs[-9 - len(loss)]
        place = lax.broadcasted_iota(jnp.int32, (ROWS, LANES), 1) // each
        zero = jnp.zeros((ROWS, LANES), f32)

        def block(k, start, count):
            return pl.ds(pl.multiple_of((me_ref[0] ^ k) * pencil + start, ROWS), count)

        def here(k):
            return block(k, chunk * rows, rows)

        def fetch(k):
            return (
                pltpu.make_async_copy(corr_refs[k], corr_in.at[k], sems.at[k, 0]),
                pltpu.make_async_copy(proj_ref.at[1, here(k)], pair.at[k, 0], sems.at[k, 1]),
                pltpu.make_async_copy(proj_ref.at[2, here(k)], pair.at[k, 1], sems.at[k, 2]),
            )

        def fetch_mixed(k):
            return pltpu.make_async_copy(mixed_refs[k], mixed_in.at[k], sems.at[k, 3])

        def leave(k, plane):
            if plane == 0:
                return pltpu.make_async_copy(query_done.at[k], out_ref.at[0, block(k, 0, pencil)], out_sems.at[k, 0])
            return pltpu.make_async_copy(done.at[k, plane - 1], out_ref.at[plane, here(k)], out_sems.at[k, plane])

        for k in range(peers):
            for copy in fetch(k):
                copy.start()
            if with_query:
                fetch_mixed(k).start()
        for k in range(peers):
            for copy in fetch(k):
                copy.wait()
            corr = corr_in[k, :, :width].astype(f32)
            done[k, 0] = corr * pair[k, 1].astype(f32)
            leave(k, 1).start()
            done[k, 1] = corr * pair[k, 0].astype(f32)
            leave(k, 2).start()
            if not with_query:
                continue
            fetch_mixed(k).wait()
            for i in range(pencil // ROWS):
                part = slice(i * ROWS, (i + 1) * ROWS)
                inside = i % (rows // ROWS)
                source = inside // 2 * ROWS
                lanes = slice(width + i // (rows // ROWS) * LANES, width + (i // (rows // ROWS) + 1) * LANES)
                high = corr_in[k, source : source + ROWS, lanes].astype(f32)
                low = corr_in[k, rows // 2 + source : rows // 2 + source + ROWS, lanes].astype(f32)
                for t in range(tiles):
                    near = place == t + inside % 2 * tiles
                    lhs[i, t * ROWS : (t + 1) * ROWS, :LANES] = jnp.where(near, high, zero).astype(bf16)
                    lhs[i, t * ROWS : (t + 1) * ROWS, LANES:] = jnp.where(near, low, zero).astype(bf16)
                grad = dot(lhs[i], spread_ref[...])
                for t in range(tiles):
                    at = slice(t * LANES, (t + 1) * LANES)
                    query_done[k, part, at] = grad[t * ROWS : (t + 1) * ROWS] * mixed_in[k, part, at].astype(f32)
            leave(k, 0).start()
        for k in range(peers):
            for plane in range(0 if with_query else 1, 3):
                leave(k, plane).wait()

    inputs = [spread, projections, *mixed_home, *corr_home, *loss]
    in_specs = [whole(spread), pl.BlockSpec(memory_space=pltpu.HBM)]
    in_specs += [pl.BlockSpec(memory_space=pl.ANY)] * (len(mixed_home) + peers)
    in_specs += [whole(x) for x in loss]
    near = (0, *range(2, len(inputs)))
    aliases = {}
    if before is not None:
        aliases = {1 + len(inputs): 0}
        inputs.append(before)
        in_specs.append(pl.BlockSpec(memory_space=pl.ANY))
    return call(
        kernel, "finish", me, 1, inputs, in_specs,
        [shape((3, channels, width), f32)] + [shape((1, 1), f32)] * len(loss),
        [pl.BlockSpec(memory_space=pltpu.HBM)] + [pl.BlockSpec((1, 1), lambda i, me: (0, 0))] * len(loss),
        [
            pltpu.VMEM((peers, 2, rows, width), bf16),
            pltpu.VMEM((peers, pencil if with_query else ROWS, width), bf16),
            pltpu.VMEM((peers, rows, payload), bf16),
            pltpu.VMEM((peers, 2, rows, width), f32),
            pltpu.VMEM((peers, pencil if with_query else ROWS, width), f32),
            pltpu.VMEM((pencil // ROWS, tiles * ROWS, 2 * LANES), bf16),
            pltpu.SemaphoreType.DMA((peers, 4)),
            pltpu.SemaphoreType.DMA((peers, 3)),
        ],
        rows * peers * 0.03 * MICROSECOND, aliases, near=near,
    )


def swap(value, k, count):
    if k == 0:
        return value
    return lax.ppermute(value, "seq", [(i, i ^ k) for i in range(count)])


def pad_rows(value, rows):
    short = rows - value.shape[-2]
    if short == 0:
        return value
    widths = [(0, 0)] * value.ndim
    widths[-2] = (0, short)
    return jnp.pad(value, widths)


def aligned(projections, filter_taps, skip_gain, head_weight, head_bias, counts):
    f32 = jnp.float32
    _, channels, width = projections.shape
    peers = lax.axis_size("seq")
    groups = lax.axis_size("chan")
    seat = lax.axis_index("seq")
    group = lax.axis_index("chan")
    bins = width // POOL
    length = width * peers
    tracks = head_weight.shape[1]
    own_tracks = tracks // groups
    pencil = channels // peers
    chunks = CHUNKS
    rows = pencil // chunks
    me = jnp.asarray(seat, jnp.int32).reshape(1)
    tables = transform_tables(length)
    gather, spread = pool_tables()

    first = [(0, k) for k in range(peers // 2, peers)]
    others = [(0, k) for k in range(peers // 2)] + [(j, k) for j in range(1, chunks) for k in range(peers)]
    far = lay_out(me, projections, filter_taps, peers, chunks, first, False)
    me_next, _ = lax.optimization_barrier((me, far))
    rest = lay_out(me_next, projections, filter_taps, peers, chunks, others, False)
    me_next, _ = lax.optimization_barrier((me, rest))
    laid = dict(zip(first + others, [*far, *rest]))
    pieces = [[swap(laid[j, k], k, peers) for k in range(peers)] for j in range(chunks)]
    me_query, _ = lax.optimization_barrier((me, pieces[0]))
    held_back = lay_out(me_query, projections, filter_taps, peers, chunks, [], True)
    queries = [swap(held_back[k], k, peers) for k in range(peers)]
    skip = lax.dynamic_index_in_dim(skip_gain.reshape(peers, pencil, 1), seat, axis=0, keepdims=False)

    mine = by_track(me_next, head_weight, groups)
    mine = lax.all_to_all(mine, "chan", split_axis=0, concat_axis=0, tiled=True)

    mixed, specs = None, []
    for j in range(chunks):
        mixed, spec = convolve(me, pieces[j], skip, tables, pencil, j * rows, mixed)
        specs.append(spec)
    mixed_out, sent = pool(me, queries, mixed, gather, groups)
    mixed_home = [swap(mixed_out[k], k, peers) for k in range(peers)]

    def exchange(blocks):
        flat = blocks.reshape(groups * peers, pencil // 2, LANES)
        flat = lax.all_to_all(flat, ("chan", "seq"), split_axis=0, concat_axis=0, tiled=True)
        return flat.reshape(blocks.shape)

    got = exchange(sent)
    mine, _ = lax.optimization_barrier((mine, sent))
    other = swap(mine, 1, peers)
    own_bias = lax.dynamic_slice_in_dim(head_bias, group * own_tracks, own_tracks).reshape(1, own_tracks)
    own_counts = lax.dynamic_slice_in_dim(counts, group * own_tracks, own_tracks, axis=1)
    logits, sums = head_rates(me, got, mine, other, own_bias, own_counts)
    all_sums = [swap(sums, k, peers) for k in range(peers)]
    early, late = mixed_home[: peers - 1], mixed_home[peers - 1 :]
    logits, early = lax.optimization_barrier((logits, early))
    part, loss = head_grads(me, logits, all_sums, mine, other, own_counts)
    back = exchange(part)

    step = 1
    while step < groups:
        loss = loss + lax.ppermute(loss, "chan", [(i, i ^ step) for i in range(groups)])
        step *= 2

    back, loss, late = lax.optimization_barrier((back, loss, late))
    mixed_home = [*early, *late]
    grad_rows, packed = sum_grads(me, back)
    grads = None
    corr_home = []
    for j in range(chunks):
        corr = correlate(me, queries, grad_rows, specs[j], skip, tables, spread, j * rows, None if j else packed)
        grad_rows, _ = lax.optimization_barrier((grad_rows, corr))
        corr_home.append([swap(corr[k], k, peers) for k in range(peers)])
    for j in range(chunks):
        ours = [] if j else mixed_home
        grads, *rest = finish(me, projections, ours, corr_home[j], spread, j, chunks, grads, [] if j else [loss])
        if not j:
            mean_loss = rest[0].reshape(())
    return mean_loss, grads


def power_of_two(value):
    return value & (value - 1) == 0


def per_device(projections, filter_taps, skip_gain, head_weight, head_bias, counts):
    channels, width = projections.shape[1:]
    peers, groups = lax.axis_size("seq"), lax.axis_size("chan")
    pencil = channels // peers
    fits = (
        pencil % (2 * ROWS * CHUNKS) == 0
        and 2 * (width // POOL) == LANES
        and power_of_two(peers)
        and peers > 1
        and power_of_two(groups)
        and groups <= MOST_GROUPS
    )
    run = aligned if fits else general
    return run(projections, filter_taps, skip_gain, head_weight, head_bias, counts)


def general(projections, filter_taps, skip_gain, head_weight, head_bias, counts):
    f32, bf16 = jnp.float32, jnp.bfloat16
    _, channels, width = projections.shape
    peers = lax.axis_size("seq")
    groups = lax.axis_size("chan")
    seat = lax.axis_index("seq")
    group = lax.axis_index("chan")
    bins = width // POOL
    length = width * peers
    tracks = head_weight.shape[1]
    own_tracks = tracks // groups
    pencil = channels // peers
    rows = -(-pencil // ROWS) * ROWS
    me = jnp.asarray(seat, jnp.int32).reshape(1)
    tables = transform_tables(length)
    gather, spread = pool_tables()

    def block(array, k):
        return lax.dynamic_index_in_dim(array, seat ^ k, axis=-3, keepdims=False)

    query = projections[0]
    key_value = projections[1].astype(f32) * projections[2].astype(f32)
    stacked = jnp.stack([key_value.astype(bf16), filter_taps.astype(bf16)])
    stacked = stacked.reshape(2, peers, pencil, width)
    pieces = [pad_rows(swap(block(stacked, k), k, peers), rows) for k in range(peers)]
    query_blocks = query.reshape(peers, pencil, width)
    queries = [pad_rows(swap(block(query_blocks, k), k, peers), rows) for k in range(peers)]
    skip = pad_rows(block(skip_gain.reshape(peers, pencil, 1), 0), rows)

    half = channels // 2
    by_track = head_weight.reshape(2, half, groups, own_tracks).transpose(0, 2, 1, 3)
    mine = lax.dynamic_index_in_dim(by_track, seat & 1, axis=0, keepdims=False)
    mine = lax.all_to_all(mine, "chan", split_axis=0, concat_axis=0, tiled=True)
    other = swap(mine, 1, peers)
    mine = mine.reshape(groups * half, own_tracks)
    other = other.reshape(groups * half, own_tracks)

    mixed, spec = convolve(me, pieces, skip, tables, rows, 0, None)
    mixed_out, pooled = pool(me, queries, mixed, gather, 0)
    pooled = pooled[:pencil]
    mixed_home = [swap(mixed_out[k][:pencil], k, peers) for k in range(peers)]

    sent = pooled.reshape(pencil, peers, bins).transpose(1, 0, 2)
    sent = jnp.broadcast_to(sent[None], (groups, peers, pencil, bins))
    got = lax.all_to_all(
        sent.reshape(groups * peers, pencil, bins), ("chan", "seq"), split_axis=0, concat_axis=0, tiled=True
    )
    got = got.reshape(groups, 2, half, bins)
    low_half = got[:, 0].reshape(groups * half, bins)
    high_half = got[:, 1].reshape(groups * half, bins)
    odd = (seat & 1) == 1
    pooled_mine = jnp.where(odd, high_half, low_half)
    pooled_other = jnp.where(odd, low_half, high_half)

    def project(x, w):
        return lax.dot_general(x, w, (((0,), (0,)), ((), ())), preferred_element_type=f32)

    own_bias = lax.dynamic_slice_in_dim(head_bias, group * own_tracks, own_tracks)
    own_counts = lax.dynamic_slice_in_dim(counts, group * own_tracks, own_tracks, axis=1)
    logits = project(pooled_mine, mine) + project(pooled_other, other) + own_bias[None, :]
    rates = jax.nn.softplus(logits) + rate_floor
    observed = own_counts.astype(f32)
    partial_sums = jnp.stack(
        [jnp.sum(rates, axis=0), jnp.sum(observed, axis=0), jnp.sum(observed * jnp.log(rates), axis=0)]
    )
    pred_total, obs_total, log_sum = jnp.sum(lax.all_gather(partial_sums, "seq"), axis=0)
    log_pred = jnp.log(pred_total)
    loss_part = jnp.sum(
        total_weight * (pred_total - obs_total * log_pred) + obs_total * log_pred - log_sum
    )
    mean_loss = lax.psum(loss_part, "chan") / (bins * peers * tracks)
    ratio = obs_total / pred_total
    grad_rates = total_weight * (1.0 - ratio)[None, :] + ratio[None, :] - observed / rates
    grad_logits = (grad_rates * jax.nn.sigmoid(logits)).astype(bf16)

    def spread_back(w):
        return lax.dot_general(w, grad_logits, (((1,), (1,)), ((), ())), preferred_element_type=f32)

    part_mine = spread_back(mine).astype(bf16).reshape(groups, 1, half, bins)
    part_other = spread_back(other).astype(bf16).reshape(groups, 1, half, bins)
    part = jnp.concatenate(
        [jnp.where(odd, part_other, part_mine), jnp.where(odd, part_mine, part_other)], axis=1
    )
    back = lax.all_to_all(
        part.reshape(groups * peers, pencil, bins), ("chan", "seq"), split_axis=0, concat_axis=0, tiled=True
    )
    grad_pooled = jnp.sum(back.reshape(groups, peers, pencil, bins).astype(f32), axis=0)
    grad_home = [swap(block(grad_pooled, k), k, peers) for k in range(peers)]
    grad_rows = pad_rows(grad_pooled.transpose(1, 0, 2).reshape(pencil, peers * bins), rows)

    corr_out = correlate(me, queries, grad_rows, spec, skip, tables, spread, 0, None)
    corr_home = [swap(corr_out[k][:pencil], k, peers) for k in range(peers)]

    def assemble(parts):
        out = jnp.zeros((peers,) + parts[0].shape, parts[0].dtype)
        for k, part in enumerate(parts):
            out = lax.dynamic_update_index_in_dim(out, part, seat ^ k, axis=0)
        return out.reshape((channels,) + parts[0].shape[1:])

    grad_output = jnp.repeat(assemble(grad_home) / POOL, POOL, axis=1)
    grad_kv = assemble(corr_home).astype(f32)
    grad_query = grad_output * assemble(mixed_home).astype(f32)
    grads = jnp.stack(
        [grad_query, grad_kv * projections[2].astype(f32), grad_kv * projections[1].astype(f32)], axis=0
    )
    return mean_loss, grads


def solution(mesh):
    placed = (
        P(None, "chan", "seq"),
        P("chan", "seq"),
        P("chan"),
        P("chan", None),
        P(),
        P("seq", None),
    )
    return jax.shard_map(
        per_device,
        mesh=mesh,
        in_specs=placed,
        out_specs=(P(), P(None, "chan", "seq")),
        check_vma=False,
    )
```

```python
import math

import jax
import jax.numpy as jnp
import ml_dtypes
import numpy as np
from jax import lax
from jax.experimental import pallas as pl
from jax.experimental.pallas import tpu as pltpu
from jax.sharding import PartitionSpec as P

POOL = 32
LANES = 128
ROWS = 16
SHIFT = 0.25

total_weight = 0.2
rate_floor = 0.5

MICROSECOND = 1.0e9

VMEM_LIMIT = 20 * 1024 * 1024
CHUNKS = 2
SPECTRA = 1
MOST_GROUPS = 16


def split_bf16(table):
    high = table.astype(ml_dtypes.bfloat16)
    low = (table - high.astype(np.float64)).astype(ml_dtypes.bfloat16)
    return high, low


def kind_scale(table):
    values = np.unique(np.abs(table))
    factors = np.linspace(1.0, 2.0, 4001)

    def lost(factor):
        scaled = table[: LANES // 2] * factor
        return np.sum((scaled - split_bf16(scaled)[0].astype(np.float64)) ** 2) / factor**2

    rough = [np.sum((values * f - split_bf16(values * f)[0].astype(np.float64)) ** 2) / f**2 for f in factors]
    best = np.argsort(rough, kind="stable")[:8]
    return float(min((factors[i] for i in best), key=lost))


def radices(outer):
    first = 1
    while first * first < outer:
        first *= 2
    return first, outer // first


def transform_tables(length):
    outer = length // LANES
    idx = np.arange(LANES)
    angle = 2.0 * np.pi * (np.outer(idx, idx) % LANES) / LANES
    wr, wi = np.cos(angle), -np.sin(angle)
    forward = np.block([[wr, wi], [-wi, wr]])
    backward = np.block([[wr, -wi], [wi, wr]]) / length
    k1 = np.arange(outer)[:, None]
    twist = 2.0 * np.pi * (k1 - SHIFT) * idx[None, :] / length
    scale = kind_scale(forward)
    f_hi, f_lo = split_bf16(forward)
    b_hi, b_lo = split_bf16(backward)
    return dict(
        fwd=[f_hi, f_lo],
        bwd=[b_hi, b_lo],
        scale=scale,
        fwd_scaled=[split_bf16(forward * scale)[0]],
        bwd_scaled=[split_bf16(backward * scale)[0]],
        twist=np.stack([np.cos(twist), -np.sin(twist)]).astype(np.float32),
    )


def pool_tables():
    per = LANES // POOL
    lane = np.arange(LANES)
    hit = (lane[:, None] // POOL) == (lane[None, :] % per)
    gather = np.concatenate([hit, hit], axis=0) / POOL
    spread = np.concatenate([hit.T, hit.T], axis=0) / POOL
    return gather.astype(ml_dtypes.bfloat16), spread.astype(ml_dtypes.bfloat16)


def times(value, angle):
    re, im = value
    c, s = math.cos(angle), math.sin(angle)
    tiny = 1e-12
    if im is None:
        if abs(s) < tiny and c > 0:
            return (re, None)
        return (re * c, re * s)
    if abs(s) < tiny:
        return (re, im) if c > 0 else (-re, -im)
    if abs(c) < tiny:
        return (-im, re) if s > 0 else (im, -re)
    return (re * c - im * s, re * s + im * c)


def add(a, b):
    if a[1] is None and b[1] is None:
        return (a[0] + b[0], None)
    if a[1] is None:
        return (a[0] + b[0], b[1])
    if b[1] is None:
        return (a[0] + b[0], a[1])
    return (a[0] + b[0], a[1] + b[1])


def sub(a, b):
    if a[1] is None and b[1] is None:
        return (a[0] - b[0], None)
    if a[1] is None:
        return (a[0] - b[0], -b[1])
    if b[1] is None:
        return (a[0] - b[0], a[1])
    return (a[0] - b[0], a[1] - b[1])


def small_dft(values, sign):
    count = len(values)
    if count == 1:
        return values
    even = small_dft(values[0::2], sign)
    odd = small_dft(values[1::2], sign)
    out = [None] * count
    half = count // 2
    for k in range(half):
        turned = times(odd[k], sign * 2.0 * math.pi * k / count)
        out[k] = add(even[k], turned)
        out[k + half] = sub(even[k], turned)
    return out


def dot(a, b):
    return jnp.dot(a, b, preferred_element_type=jnp.float32)


def split(value):
    high = value.astype(jnp.bfloat16)
    return high, (value - high.astype(jnp.float32)).astype(jnp.bfloat16)


def put(re_parts, im_parts, lhs, start):
    for i, (re, im) in enumerate(zip(re_parts, im_parts)):
        rows = pl.ds(start + i * ROWS, ROWS)
        re_hi, re_lo = split(re)
        im_hi, im_lo = split(im)
        lhs[0, rows, :LANES] = re_hi
        lhs[0, rows, LANES:] = im_hi
        lhs[1, rows, :LANES] = re_lo
        lhs[1, rows, LANES:] = im_lo


def lane_transform(lhs, table_refs):
    high = lhs[0]
    if len(table_refs) == 1:
        table = table_refs[0][...]
        return dot(high, table) + dot(lhs[1], table)
    table_high, table_low = table_refs[0][...], table_refs[1][...]
    return dot(high, table_high) + (dot(lhs[1], table_high) + dot(high, table_low))


def first_pass(load, store, outer):
    ra, rb = radices(outer)
    for b in range(rb):
        values = [times((load(rb * a + b), None), 2.0 * math.pi * a * SHIFT / ra) for a in range(ra)]
        out = small_dft(values, -1)
        for alpha in range(ra):
            re, im = times(out[alpha], -2.0 * math.pi * b * (alpha - SHIFT) / outer)
            store(b, alpha, re, im)


def second_pass(parts, alpha, outer, twist_ref):
    ra, rb = radices(outer)
    values = [(parts[0, b, alpha], parts[1, b, alpha]) for b in range(rb)]
    out = small_dft(values, -1)
    res, ims = [], []
    for beta in range(rb):
        k1 = alpha + ra * beta
        tr = twist_ref[0, k1 : k1 + 1, :]
        ti = twist_ref[1, k1 : k1 + 1, :]
        re, im = out[beta]
        res.append(re * tr - im * ti)
        ims.append(re * ti + im * tr)
    return res, ims


def back_second_pass(spectrum, alpha, outer, twist_ref, store):
    ra, rb = radices(outer)
    values = []
    for beta in range(rb):
        k1 = alpha + ra * beta
        tr = twist_ref[0, k1 : k1 + 1, :]
        ti = twist_ref[1, k1 : k1 + 1, :]
        re = spectrum[beta * ROWS : (beta + 1) * ROWS, :LANES]
        im = spectrum[beta * ROWS : (beta + 1) * ROWS, LANES:]
        values.append((re * tr + im * ti, im * tr - re * ti))
    out = small_dft(values, +1)
    for b in range(rb):
        re, im = times(out[b], 2.0 * math.pi * b * (alpha - SHIFT) / outer)
        store(b, alpha, re, im)


def back_first_pass(parts, outer, emit, scale=1.0):
    ra, rb = radices(outer)
    for b in range(rb):
        values = [(parts[0, b, alpha], parts[1, b, alpha]) for alpha in range(ra)]
        out = small_dft(values, +1)
        for a in range(ra):
            angle = -2.0 * math.pi * a * SHIFT / ra
            re, im = out[a]
            c, s = math.cos(angle) * scale, math.sin(angle) * scale
            if a == 0:
                emit(rb * a + b, re if scale == 1.0 else re * scale)
            else:
                emit(rb * a + b, re * c - im * s)


def put_product(re, im, lhs, start):
    rows = [slice(i, i + ROWS) for i in range(0, re.shape[0], ROWS)]
    put([re[r] for r in rows], [im[r] for r in rows], lhs, start)


def keep(parts):
    def store(b, alpha, re, im):
        parts[0, b, alpha] = re
        parts[1, b, alpha] = im

    return store


def conv_kernel(peers, outer, me_ref, *refs):
    pieces = refs[:peers]
    skip_ref, *tables, twist_ref = refs[peers : peers + 6]
    fwd_ref, bwd_ref = tables[:2], tables[2:]
    mixed_ref = refs[-6 - SPECTRA]
    spec_refs = refs[-5 - SPECTRA : -5]
    rows_in, parts_x, parts_h, parts_y, lhs = refs[-5:]
    me = me_ref[0]
    ra, rb = radices(outer)
    per = outer // peers
    for k in range(peers):
        rows_in[me ^ k] = pieces[k][...]

    def loader(which):
        def load(n1):
            lanes = slice((n1 % per) * LANES, (n1 % per + 1) * LANES)
            return rows_in[n1 // per, which, :, lanes].astype(jnp.float32)

        return load

    load_x = loader(0)
    first_pass(load_x, keep(parts_x), outer)
    first_pass(loader(1), keep(parts_h), outer)
    chunk = rb * ROWS
    for alpha in range(ra):
        put(*second_pass(parts_x, alpha, outer, twist_ref), lhs.at[alpha], 0)
        put(*second_pass(parts_h, alpha, outer, twist_ref), lhs.at[alpha], chunk)
    for alpha in range(ra):
        both = lane_transform(lhs.at[alpha], fwd_ref)
        x, h = both[:chunk], both[chunk:]
        each = ra // SPECTRA
        spec_refs[alpha // each][0, alpha % each * chunk : (alpha % each + 1) * chunk, :] = h
        xr, xi, hr, hi = x[:, :LANES], x[:, LANES:], h[:, :LANES], h[:, LANES:]
        put_product(xr * hr - xi * hi, xr * hi + xi * hr, lhs.at[ra + alpha // 2], alpha % 2 * chunk)
    for pair in range(ra // 2):
        y = lane_transform(lhs.at[ra + pair], bwd_ref)
        for i in range(2):
            back_second_pass(y[i * chunk : (i + 1) * chunk], 2 * pair + i, outer, twist_ref, keep(parts_y))
    skip = jnp.broadcast_to(skip_ref[...], (ROWS, LANES))

    def emit(n1, value):
        mixed_ref[:, n1 * LANES : (n1 + 1) * LANES] = value + skip * load_x(n1)

    back_first_pass(parts_y, outer, emit)


def pool_rows(rows_in, mixed_ref, rows_out, row, gather_ref, lhs, per, outer):
    for n1 in range(outer):
        lanes = slice((n1 % per) * LANES, (n1 % per + 1) * LANES)
        query = rows_in[n1 // per, row : row + ROWS, lanes].astype(jnp.float32)
        mixed = mixed_ref[row : row + ROWS, n1 * LANES : (n1 + 1) * LANES]
        rows_out[n1 // per, row : row + ROWS, lanes] = mixed.astype(jnp.bfloat16)
        high, low = split(query * mixed)
        lhs[n1 * ROWS : (n1 + 1) * ROWS, :LANES] = high
        lhs[n1 * ROWS : (n1 + 1) * ROWS, LANES:] = low
    sums = dot(lhs[...], gather_ref[...])
    each = LANES // POOL
    held = LANES // each
    place = lax.broadcasted_iota(jnp.int32, (ROWS, LANES), 1) // each
    tiles = []
    for tile in range(-(-outer // held)):
        total = jnp.zeros((ROWS, LANES), jnp.float32)
        for j in range(min(held, outer - tile * held)):
            n1 = tile * held + j
            total = jnp.where(place == j, sums[n1 * ROWS : (n1 + 1) * ROWS], total)
        tiles.append(total)
    return jnp.concatenate(tiles, axis=1)


def pool_kernel(peers, outer, me_ref, *refs):
    queries = refs[:peers]
    mixed_ref, gather_ref = refs[peers : peers + 2]
    outs = refs[peers + 2 : 2 * peers + 2]
    pooled_ref, rows_in, rows_out, lhs = refs[2 * peers + 2 :]
    me = me_ref[0]
    per = outer // peers
    for k in range(peers):
        rows_in[me ^ k] = queries[k][...]
    rows = mixed_ref.shape[0]
    bins = outer * LANES // POOL
    if rows == ROWS:
        pooled = pool_rows(rows_in, mixed_ref, rows_out, 0, gather_ref, lhs.at[0], per, outer)
        pooled_ref[...] = pooled[:, :bins].astype(jnp.bfloat16)
    else:
        left = pool_rows(rows_in, mixed_ref, rows_out, 0, gather_ref, lhs.at[0], per, outer)
        right = pool_rows(rows_in, mixed_ref, rows_out, ROWS, gather_ref, lhs.at[1], per, outer)
        each = bins // peers
        for seat in range(peers):
            mine = slice(seat * each, (seat + 1) * each)
            pair = jnp.concatenate([left[:, mine], right[:, mine]], axis=1).astype(jnp.bfloat16)
            for group in range(pooled_ref.shape[0]):
                pooled_ref[group, seat] = pair
    for k in range(peers):
        outs[k][...] = rows_out[me ^ k]


def corr_kernel(peers, outer, packed, scale, me_ref, *refs):
    if packed:
        packed_ref, refs = refs[0], refs[1:]
    queries = refs[:peers]
    refs, spec_refs = refs[: peers] + refs[peers + SPECTRA :], refs[peers : peers + SPECTRA]
    grad_ref, skip_ref, *tables, twist_ref, spread_ref = refs[peers : peers + 6]
    fwd_ref, bwd_ref = tables[:1], tables[1:]
    outs = refs[peers + 6 : 2 * peers + 6]
    rows_in, lhs_g, gated, parts_g, parts_y, lhs, rows_out = refs[2 * peers + 6 :]
    me = me_ref[0]
    ra, rb = radices(outer)
    per = outer // peers
    for k in range(peers):
        rows_in[me ^ k] = queries[k][...]
    each = LANES // POOL
    held = LANES // each
    place = lax.broadcasted_iota(jnp.int32, (ROWS, LANES), 1) // each
    zero = jnp.zeros((ROWS, LANES), jnp.float32)
    for tile in range(-(-outer // held)):
        count = min(held, outer - tile * held)
        used = count * each
        part = grad_ref[:, tile * LANES : tile * LANES + used]
        if used < LANES:
            part = jnp.concatenate([part, jnp.zeros((ROWS, LANES - used), jnp.float32)], axis=1)
        high = part.astype(jnp.bfloat16).astype(jnp.float32)
        low = part - high
        for j in range(count):
            rows = pl.ds((tile * held + j) * ROWS, ROWS)
            lhs_g[rows, :LANES] = jnp.where(place == j, high, zero).astype(jnp.bfloat16)
            lhs_g[rows, LANES:] = jnp.where(place == j, low, zero).astype(jnp.bfloat16)
    gated[...] = dot(lhs_g[...], spread_ref[...])
    for n1 in range(outer):
        lanes = slice((n1 % per) * LANES, (n1 % per + 1) * LANES)
        rows = pl.ds(n1 * ROWS, ROWS)
        gated[rows, :] = gated[rows, :] * rows_in[n1 // per, :, lanes].astype(jnp.float32)

    def load_g(n1):
        return gated[n1 * ROWS : (n1 + 1) * ROWS, :]

    first_pass(load_g, keep(parts_g), outer)
    chunk = rb * ROWS
    for alpha in range(ra):
        put(*second_pass(parts_g, alpha, outer, twist_ref), lhs.at[alpha // 2], alpha % 2 * chunk)
    for pair in range(ra // 2):
        both = lane_transform(lhs.at[pair], fwd_ref)
        for i in range(2):
            alpha = 2 * pair + i
            g = both[i * chunk : (i + 1) * chunk]
            each = ra // SPECTRA
            h = spec_refs[alpha // each][0, alpha % each * chunk : (alpha % each + 1) * chunk, :]
            gr, gi, hr, hi = g[:, :LANES], g[:, LANES:], h[:, :LANES], h[:, LANES:]
            put_product(gr * hr + gi * hi, gi * hr - gr * hi, lhs.at[ra // 2 + pair], i * chunk)
    for pair in range(ra // 2):
        y = lane_transform(lhs.at[ra // 2 + pair], bwd_ref)
        for i in range(2):
            back_second_pass(y[i * chunk : (i + 1) * chunk], 2 * pair + i, outer, twist_ref, keep(parts_y))
    skip = jnp.broadcast_to(skip_ref[...], (ROWS, LANES))

    def emit(n1, value):
        lanes = slice((n1 % per) * LANES, (n1 % per + 1) * LANES)
        rows_out[n1 // per, :, lanes] = (value + skip * load_g(n1)).astype(jnp.bfloat16)

    back_first_pass(parts_y, outer, emit, scale)
    step, steps = pl.program_id(0), pl.num_programs(0)
    for k in range(peers):
        outs[k][:, : per * LANES] = rows_out[me ^ k]
        if packed:
            half = steps // 2
            for chunk_at in range(packed_ref.shape[1] // (half * ROWS)):
                here = pl.ds((chunk_at * half + lax.rem(step, half)) * ROWS, ROWS)
                high, low = (part.astype(jnp.float32) for part in split(packed_ref[me ^ k, here, :]))
                lanes = slice((per + chunk_at) * LANES, (per + chunk_at + 1) * LANES)
                outs[k][:, lanes] = jnp.where(step < half, high, low).astype(jnp.bfloat16)


def whole(array):
    rank = len(array.shape)
    return pl.BlockSpec(array.shape, lambda i, me: (0,) * rank)


def by_rows(width, rows=ROWS, start=0):
    return pl.BlockSpec((rows, width), lambda i, me: (start + i, 0))


def call(kernel, name, me, steps, inputs, in_specs, out_shapes, out_specs, scratch, flops, aliases=None, near=(), vmem=()):
    moved = sum(x.size * x.dtype.itemsize for x in inputs)
    moved += sum(math.prod(o.shape) * o.dtype.itemsize for o in out_shapes)
    def space(i):
        return pltpu.VMEM if i in vmem else pltpu.HBM

    count = len(inputs)
    inputs = [x if i in near else pltpu.with_memory_space_constraint(x, space(i)) for i, x in enumerate(inputs)]
    out_shapes = [
        o if count + i in near else space(count + i)(o.shape, o.dtype) for i, o in enumerate(out_shapes)
    ]
    return pl.pallas_call(
        kernel,
        name=name,
        grid_spec=pltpu.PrefetchScalarGridSpec(
            num_scalar_prefetch=1,
            grid=(steps,),
            in_specs=in_specs,
            out_specs=out_specs,
            scratch_shapes=scratch,
        ),
        out_shape=out_shapes,
        input_output_aliases=aliases or {},
        compiler_params=pltpu.CompilerParams(
            dimension_semantics=("arbitrary",), vmem_limit_bytes=VMEM_LIMIT
        ),
        cost_estimate=pl.CostEstimate(flops=int(flops), bytes_accessed=moved, transcendentals=0),
    )(me, *inputs)


def shape(dims, dtype):
    return jax.ShapeDtypeStruct(dims, dtype)


def convolve(me, pieces, skip, tables, total_rows, start, before):
    peers = len(pieces)
    rows, width = pieces[0].shape[1:]
    length = width * peers
    outer = length // LANES
    ra, rb = radices(outer)
    chunk = rb * ROWS
    steps = rows // ROWS
    first = start // ROWS
    f32, bf16 = jnp.float32, jnp.bfloat16
    fwd, bwd, twist = tables["fwd"], tables["bwd"], tables["twist"]
    inputs = [*pieces, skip, *fwd, *bwd, twist]
    in_specs = [pl.BlockSpec((2, ROWS, width), lambda i, me: (0, i, 0))] * peers + [
        by_rows(1, start=first),
        *[whole(table) for table in (*fwd, *bwd, twist)],
    ]
    aliases = {}
    if before is not None:
        aliases = {1 + len(inputs): 0}
        inputs.append(before)
        in_specs.append(pl.BlockSpec(memory_space=pl.ANY))
    parts = pltpu.VMEM((2, rb, ra, ROWS, LANES), f32)

    def kernel(*refs):
        conv_kernel(peers, outer, *refs)

    part = (1, outer * ROWS // SPECTRA, 2 * LANES)
    out = call(
        kernel, "long_convolution", me, steps, inputs, in_specs,
        [shape((total_rows, length), f32)] + [shape((steps, *part[1:]), f32)] * SPECTRA,
        [by_rows(length, start=first)] + [pl.BlockSpec(part, lambda i, me: (i, 0, 0))] * SPECTRA,
        [
            pltpu.VMEM((peers, 2, ROWS, width), bf16),
            parts,
            parts,
            parts,
            pltpu.VMEM((ra + ra // 2, 2, 2 * chunk, 2 * LANES), bf16),
        ],
        rows * outer * 0.004 * MICROSECOND, aliases, (peers,), range(peers + 6, len(inputs) + 1),
    )
    return out[0], out[1:]


def pool(me, queries, mixed, gather, groups):
    peers = len(queries)
    rows, width = queries[0].shape
    length = width * peers
    outer = length // LANES
    bins = length // POOL
    bf16 = jnp.bfloat16
    if groups:
        step = 2 * ROWS
        pooled_shape = shape((groups, peers, rows // 2, LANES), bf16)
        pooled_spec = pl.BlockSpec((groups, peers, ROWS, LANES), lambda i, me: (0, 0, i, 0))
    else:
        step = ROWS
        pooled_shape = shape((rows, bins), bf16)
        pooled_spec = by_rows(bins)

    def kernel(*refs):
        pool_kernel(peers, outer, *refs)

    out = call(
        kernel, "pool_bins", me, rows // step, [*queries, mixed, gather],
        [by_rows(width, step)] * peers + [by_rows(length, step), whole(gather)],
        [shape((rows, width), bf16)] * peers + [pooled_shape],
        [by_rows(width, step)] * peers + [pooled_spec],
        [
            pltpu.VMEM((peers, step, width), bf16),
            pltpu.VMEM((peers, step, width), bf16),
            pltpu.VMEM((step // ROWS, outer * ROWS, 2 * LANES), bf16),
        ],
        rows * outer * 0.001 * MICROSECOND, vmem=range(1, peers + 1),
    )
    return out[:peers], out[peers]


def correlate(me, queries, grad_pooled, spec, skip, tables, spread, start, packed):
    peers = len(queries)
    width = queries[0].shape[1]
    rows = spec[0].shape[0] * ROWS
    length = width * peers
    outer = length // LANES
    bins = length // POOL
    ra, rb = radices(outer)
    chunk = rb * ROWS
    first = start // ROWS
    f32, bf16 = jnp.float32, jnp.bfloat16
    fwd, bwd, twist = tables["fwd_scaled"], tables["bwd_scaled"], tables["twist"]
    in_specs = [by_rows(width, start=first)] * peers + [
        *[pl.BlockSpec((1, *part.shape[1:]), lambda i, me: (i, 0, 0)) for part in spec],
        by_rows(bins, start=first),
        by_rows(1, start=first),
        *[whole(table) for table in (*fwd, *bwd, twist, spread)],
    ]
    parts = pltpu.VMEM((2, rb, ra, ROWS, LANES), f32)
    scratch = [
        pltpu.VMEM((peers, ROWS, width), bf16),
        pltpu.VMEM((outer * ROWS, 2 * LANES), bf16),
        pltpu.VMEM((outer * ROWS, LANES), f32),
        parts,
        parts,
        pltpu.VMEM((ra, 2, 2 * chunk, 2 * LANES), bf16),
        pltpu.VMEM((peers, ROWS, width), bf16),
    ]

    def kernel(*refs):
        corr_kernel(peers, outer, packed is not None, 1.0 / tables["scale"] ** 2, *refs)

    inputs = [*queries, *spec, grad_pooled, skip, *fwd, *bwd, twist, spread]
    sent = width
    if packed is not None:
        sent = width + packed.shape[1] // (rows // 2) * LANES
        inputs = [packed, *inputs]
        in_specs = [whole(packed), *in_specs]
    near = len(inputs) - 6
    return call(
        kernel, "long_correlation", me, rows // ROWS, inputs, in_specs,
        [shape((rows, sent), bf16)] * peers, [by_rows(sent)] * peers,
        scratch, rows * outer * 0.004 * MICROSECOND, near=((0,) if packed is not None else ()) + (near, near + 1, *range(len(inputs), len(inputs) + peers)),
    )


def lay_out(me, projections, filter_taps, peers, chunks, jobs, with_query):
    _, channels, width = projections.shape
    pencil = channels // peers
    rows = pencil // chunks
    f32, bf16 = jnp.float32, jnp.bfloat16
    count = len(jobs)
    query_count = peers if with_query else 0

    def kernel(me_ref, proj_ref, taps_ref, *refs):
        outs, queries = refs[:count], refs[count:-7]
        pair, taps, laid, passing, sems, out_sems, query_sems = refs[-7:]

        def fetch(i):
            chunk, k = jobs[i]
            here = pl.ds(pl.multiple_of((me_ref[0] ^ k) * pencil + chunk * rows, rows), rows)
            return (
                pltpu.make_async_copy(proj_ref.at[1, here], pair.at[i, 0], sems.at[i, 0]),
                pltpu.make_async_copy(proj_ref.at[2, here], pair.at[i, 1], sems.at[i, 1]),
                pltpu.make_async_copy(taps_ref.at[here], taps.at[i], sems.at[i, 2]),
            )

        def leave(i):
            return pltpu.make_async_copy(laid.at[i], outs[i], out_sems.at[i])

        def take(k):
            block = pl.ds(pl.multiple_of((me_ref[0] ^ k) * pencil, pencil), pencil)
            return pltpu.make_async_copy(proj_ref.at[0, block], passing.at[k], query_sems.at[k, 0])

        def hand_on(k):
            return pltpu.make_async_copy(passing.at[k], queries[k], query_sems.at[k, 1])

        for i in range(count):
            for copy in fetch(i):
                copy.start()
        for k in range(query_count):
            take(k).start()
        for i in range(count):
            keyed, valued, lags = fetch(i)
            keyed.wait()
            valued.wait()
            laid[i, 0] = (pair[i, 0].astype(f32) * pair[i, 1].astype(f32)).astype(bf16)
            lags.wait()
            laid[i, 1] = taps[i].astype(bf16)
            leave(i).start()
        for k in range(query_count):
            take(k).wait()
            hand_on(k).start()
        for i in range(count):
            leave(i).wait()
        for k in range(query_count):
            hand_on(k).wait()

    out_shapes = [shape((2, rows, width), bf16)] * count + [shape((pencil, width), bf16)] * query_count
    return call(
        kernel, "lay_out", me, 1, [projections, filter_taps],
        [pl.BlockSpec(memory_space=pltpu.HBM)] * 2,
        out_shapes,
        [pl.BlockSpec(memory_space=pltpu.HBM)] * len(out_shapes),
        [
            pltpu.VMEM((count, 2, rows, width), bf16),
            pltpu.VMEM((count, rows, width), f32),
            pltpu.VMEM((count, 2, rows, width), bf16),
            pltpu.VMEM((max(query_count, 1), pencil, width), bf16),
            pltpu.SemaphoreType.DMA((count, 3)),
            pltpu.SemaphoreType.DMA((count,)),
            pltpu.SemaphoreType.DMA((max(query_count, 1), 2)),
        ],
        rows * count * 0.015 * MICROSECOND,
    )


def by_track(me, head_weight, groups):
    channels, tracks = head_weight.shape
    half, own = channels // 2, tracks // groups
    padded = -(-own // LANES) * LANES
    dtype = head_weight.dtype
    steps = half // ROWS

    def kernel(me_ref, weight_ref, out_ref, rows_in, sems):
        first = pl.multiple_of((me_ref[0] & 1) * half, half)

        def fetch(i):
            return pltpu.make_async_copy(
                weight_ref.at[pl.ds(first + i * ROWS, ROWS)], rows_in.at[pl.ds(i * ROWS, ROWS)], sems.at[i]
            )

        for i in range(steps):
            fetch(i).start()
        for i in range(steps):
            fetch(i).wait()
        for group in range(groups):
            out_ref[group, :, :own] = rows_in[:, group * own : (group + 1) * own]
            if padded > own:
                out_ref[group, :, own:] = jnp.zeros((half, padded - own), dtype)

    out = shape((groups, half, padded), dtype)
    return call(
        kernel, "by_track", me, 1, [head_weight], [pl.BlockSpec(memory_space=pltpu.HBM)], [out], [whole(out)],
        [pltpu.VMEM((half, tracks), dtype), pltpu.SemaphoreType.DMA((steps,))], 2 * MICROSECOND, vmem=(1,),
    )[0]


def weight_pair(weight_ref, seats, pencil, own):
    groups, _, padded = weight_ref.shape
    rows = weight_ref[...].reshape(groups, seats, pencil // (2 * ROWS), 2, ROWS, padded)
    count = groups * seats * pencil // 2
    left, right = rows[:, :, :, 0].reshape(count, padded), rows[:, :, :, 1].reshape(count, padded)
    return left[:, :own], right[:, :own]


def head_rates(me, got, mine, other, bias, counts):
    groups, peers, half_rows, _ = got.shape
    own = counts.shape[1]
    seats = peers // 2
    pencil = 2 * half_rows
    bins = LANES // 2
    f32 = jnp.float32

    def kernel(me_ref, got_ref, mine_ref, other_ref, bias_ref, counts_ref, logits_ref, sums_ref):
        odd = me_ref[0] & 1
        total = jnp.broadcast_to(bias_ref[...], (bins, own))
        for weight_ref, place in ((mine_ref, odd), (other_ref, 1 - odd)):
            block = got_ref[:, pl.ds(place * seats, seats)].reshape(groups * seats * half_rows, LANES)
            turned = block.astype(f32).T.astype(jnp.bfloat16)
            left, right = weight_pair(weight_ref, seats, pencil, own)
            total = total + dot(turned[:bins], left) + dot(turned[bins:], right)
        logits_ref[...] = total
        rates = jax.nn.softplus(total) + rate_floor
        observed = counts_ref[...].astype(f32)
        sums_ref[0:1, :] = jnp.sum(rates, axis=0, keepdims=True)
        sums_ref[1:2, :] = jnp.sum(observed, axis=0, keepdims=True)
        sums_ref[2:3, :] = jnp.sum(observed * jnp.log(rates), axis=0, keepdims=True)
        sums_ref[3:8, :] = jnp.zeros((5, own), f32)

    inputs = [got, mine, other, bias, counts]
    return call(
        kernel, "head_rates", me, 1, inputs, [whole(x) for x in inputs],
        [shape((bins, own), f32), shape((8, own), f32)],
        [pl.BlockSpec((bins, own), lambda i, me: (0, 0)), pl.BlockSpec((8, own), lambda i, me: (0, 0))],
        [], 2 * bins * groups * peers * pencil * own, near=range(7),
    )


def head_grads(me, logits, sums, mine, other, counts):
    groups, half, _ = mine.shape
    own = counts.shape[1]
    peers = len(sums)
    seats = peers // 2
    pencil = half // seats
    bins = LANES // 2
    f32, bf16 = jnp.float32, jnp.bfloat16

    def kernel(me_ref, logits_ref, *refs):
        sums_refs = refs[:peers]
        mine_ref, other_ref, counts_ref, out_ref, loss_ref = refs[peers:]
        odd = me_ref[0] & 1
        totals = [ref[...] for ref in sums_refs]
        while len(totals) > 1:
            totals = [totals[i] + totals[i + 1] for i in range(0, len(totals), 2)]
        totals = totals[0]
        pred_total, obs_total, log_sum = totals[0:1], totals[1:2], totals[2:3]
        log_pred = jnp.log(pred_total)
        terms = total_weight * (pred_total - obs_total * log_pred) + obs_total * log_pred - log_sum
        mean = jnp.sum(terms, axis=1, keepdims=True) / (peers * bins * groups * own)
        loss_ref[...] = jnp.broadcast_to(mean, loss_ref.shape)
        ratio = obs_total / pred_total
        logits_here = logits_ref[...]
        rates = jax.nn.softplus(logits_here) + rate_floor
        observed = counts_ref[...].astype(f32)
        grad_rates = total_weight * (1.0 - ratio) + ratio - observed / rates
        grads = (grad_rates * jax.nn.sigmoid(logits_here)).astype(bf16)
        none = jnp.zeros_like(grads)
        in_left = jnp.concatenate([grads, none], axis=0)
        in_right = jnp.concatenate([none, grads], axis=0)
        across = (((1,), (1,)), ((), ()))
        for weight_ref, place in ((mine_ref, odd), (other_ref, 1 - odd)):
            left, right = weight_pair(weight_ref, seats, pencil, own)
            part = lax.dot_general(left, in_left, across, preferred_element_type=f32)
            part = part + lax.dot_general(right, in_right, across, preferred_element_type=f32)
            out_ref[:, pl.ds(place * seats, seats)] = part.astype(bf16).reshape(groups, seats, pencil // 2, LANES)

    inputs = [logits, *sums, mine, other, counts]
    out = shape((groups, peers, pencil // 2, LANES), bf16)
    return call(
        kernel, "head_grads", me, 1, inputs, [whole(x) for x in inputs],
        [out, shape((8, LANES), f32)],
        [whole(out), pl.BlockSpec((8, LANES), lambda i, me: (0, 0))],
        [], 4 * bins * groups * peers * pencil * own, near=(*range(peers + 4), peers + 5),
    )


def sum_grads(me, back):
    groups, peers, half_rows, _ = back.shape
    bins = LANES // 2
    f32 = jnp.float32

    def kernel(me_ref, back_ref, rows_ref, packed_ref):
        for seat in range(peers):
            total = back_ref[0, seat].astype(f32)
            for group in range(1, groups):
                total = total + back_ref[group, seat].astype(f32)
            packed_ref[seat] = total
            for i in range(half_rows // ROWS):
                pair = total[i * ROWS : (i + 1) * ROWS]
                lanes = slice(seat * bins, (seat + 1) * bins)
                rows_ref[2 * i * ROWS : (2 * i + 1) * ROWS, lanes] = pair[:, :bins]
                rows_ref[(2 * i + 1) * ROWS : (2 * i + 2) * ROWS, lanes] = pair[:, bins:]

    rows, packed = shape((2 * half_rows, peers * bins), f32), shape((peers, half_rows, LANES), f32)
    return call(
        kernel, "sum_grads", me, 1, [back], [whole(back)], [rows, packed], [whole(rows), whole(packed)], [], back.size,
        near=(0, 1, 2),
    )


def finish(me, projections, mixed_home, corr_home, spread, chunk, chunks, before, loss):
    peers = len(corr_home)
    _, channels, width = projections.shape
    pencil = channels // peers
    rows = pencil // chunks
    tiles = width // LANES
    each = LANES // POOL
    f32, bf16 = jnp.float32, jnp.bfloat16
    with_query = bool(mixed_home)
    payload = corr_home[0].shape[1]

    def kernel(me_ref, spread_ref, proj_ref, *refs):
        mixed_refs, corr_refs = refs[: len(mixed_home)], refs[len(mixed_home) : len(mixed_home) + peers]
        pair, mixed_in, corr_in, done, query_done, lhs, sems, out_sems = refs[-8:]
        if loss:
            loss_ref, mean_ref = refs[len(mixed_home) + peers], refs[-9]
            mean_ref[...] = loss_ref[0:1, 0:1]
        out_ref = refs[-9 - len(loss)]
        place = lax.broadcasted_iota(jnp.int32, (ROWS, LANES), 1) // each
        zero = jnp.zeros((ROWS, LANES), f32)

        def block(k, start, count):
            return pl.ds(pl.multiple_of((me_ref[0] ^ k) * pencil + start, ROWS), count)

        def here(k):
            return block(k, chunk * rows, rows)

        def fetch(k):
            return (
                pltpu.make_async_copy(corr_refs[k], corr_in.at[k], sems.at[k, 0]),
                pltpu.make_async_copy(proj_ref.at[1, here(k)], pair.at[k, 0], sems.at[k, 1]),
                pltpu.make_async_copy(proj_ref.at[2, here(k)], pair.at[k, 1], sems.at[k, 2]),
            )

        def fetch_mixed(k):
            return pltpu.make_async_copy(mixed_refs[k], mixed_in.at[k], sems.at[k, 3])

        def leave(k, plane):
            if plane == 0:
                return pltpu.make_async_copy(query_done.at[k], out_ref.at[0, block(k, 0, pencil)], out_sems.at[k, 0])
            return pltpu.make_async_copy(done.at[k, plane - 1], out_ref.at[plane, here(k)], out_sems.at[k, plane])

        for k in range(peers):
            for copy in fetch(k):
                copy.start()
            if with_query:
                fetch_mixed(k).start()
        for k in range(peers):
            for copy in fetch(k):
                copy.wait()
            corr = corr_in[k, :, :width].astype(f32)
            done[k, 0] = corr * pair[k, 1].astype(f32)
            leave(k, 1).start()
            done[k, 1] = corr * pair[k, 0].astype(f32)
            leave(k, 2).start()
            if not with_query:
                continue
            fetch_mixed(k).wait()
            for i in range(pencil // ROWS):
                part = slice(i * ROWS, (i + 1) * ROWS)
                inside = i % (rows // ROWS)
                source = inside // 2 * ROWS
                lanes = slice(width + i // (rows // ROWS) * LANES, width + (i // (rows // ROWS) + 1) * LANES)
                high = corr_in[k, source : source + ROWS, lanes].astype(f32)
                low = corr_in[k, rows // 2 + source : rows // 2 + source + ROWS, lanes].astype(f32)
                for t in range(tiles):
                    near = place == t + inside % 2 * tiles
                    lhs[i, t * ROWS : (t + 1) * ROWS, :LANES] = jnp.where(near, high, zero).astype(bf16)
                    lhs[i, t * ROWS : (t + 1) * ROWS, LANES:] = jnp.where(near, low, zero).astype(bf16)
                grad = dot(lhs[i], spread_ref[...])
                for t in range(tiles):
                    at = slice(t * LANES, (t + 1) * LANES)
                    query_done[k, part, at] = grad[t * ROWS : (t + 1) * ROWS] * mixed_in[k, part, at].astype(f32)
            leave(k, 0).start()
        for k in range(peers):
            for plane in range(0 if with_query else 1, 3):
                leave(k, plane).wait()

    inputs = [spread, projections, *mixed_home, *corr_home, *loss]
    in_specs = [whole(spread), pl.BlockSpec(memory_space=pltpu.HBM)]
    in_specs += [pl.BlockSpec(memory_space=pl.ANY)] * (len(mixed_home) + peers)
    in_specs += [whole(x) for x in loss]
    near = (0, *range(2, len(inputs)))
    aliases = {}
    if before is not None:
        aliases = {1 + len(inputs): 0}
        inputs.append(before)
        in_specs.append(pl.BlockSpec(memory_space=pl.ANY))
    return call(
        kernel, "finish", me, 1, inputs, in_specs,
        [shape((3, channels, width), f32)] + [shape((1, 1), f32)] * len(loss),
        [pl.BlockSpec(memory_space=pltpu.HBM)] + [pl.BlockSpec((1, 1), lambda i, me: (0, 0))] * len(loss),
        [
            pltpu.VMEM((peers, 2, rows, width), bf16),
            pltpu.VMEM((peers, pencil if with_query else ROWS, width), bf16),
            pltpu.VMEM((peers, rows, payload), bf16),
            pltpu.VMEM((peers, 2, rows, width), f32),
            pltpu.VMEM((peers, pencil if with_query else ROWS, width), f32),
            pltpu.VMEM((pencil // ROWS, tiles * ROWS, 2 * LANES), bf16),
            pltpu.SemaphoreType.DMA((peers, 4)),
            pltpu.SemaphoreType.DMA((peers, 3)),
        ],
        rows * peers * 0.03 * MICROSECOND, aliases, near=near,
    )


def swap(value, k, count):
    if k == 0:
        return value
    return lax.ppermute(value, "seq", [(i, i ^ k) for i in range(count)])


def pad_rows(value, rows):
    short = rows - value.shape[-2]
    if short == 0:
        return value
    widths = [(0, 0)] * value.ndim
    widths[-2] = (0, short)
    return jnp.pad(value, widths)


def aligned(projections, filter_taps, skip_gain, head_weight, head_bias, counts):
    f32 = jnp.float32
    _, channels, width = projections.shape
    peers = lax.axis_size("seq")
    groups = lax.axis_size("chan")
    seat = lax.axis_index("seq")
    group = lax.axis_index("chan")
    bins = width // POOL
    length = width * peers
    tracks = head_weight.shape[1]
    own_tracks = tracks // groups
    pencil = channels // peers
    chunks = CHUNKS
    rows = pencil // chunks
    me = jnp.asarray(seat, jnp.int32).reshape(1)
    tables = transform_tables(length)
    gather, spread = pool_tables()

    first = [(0, k) for k in range(peers // 2, peers)]
    others = [(0, k) for k in range(peers // 2)] + [(j, k) for j in range(1, chunks) for k in range(peers)]
    far = lay_out(me, projections, filter_taps, peers, chunks, first, False)
    me_next, _ = lax.optimization_barrier((me, far))
    rest = lay_out(me_next, projections, filter_taps, peers, chunks, others, True)
    me_next, _ = lax.optimization_barrier((me, rest))
    laid = dict(zip(first + others, [*far, *rest]))
    pieces = [[swap(laid[j, k], k, peers) for k in range(peers)] for j in range(chunks)]
    held_back, _ = lax.optimization_barrier((rest[len(others) :], pieces[0]))
    queries = [swap(held_back[k], k, peers) for k in range(peers)]
    skip = lax.dynamic_index_in_dim(skip_gain.reshape(peers, pencil, 1), seat, axis=0, keepdims=False)

    mine = by_track(me_next, head_weight, groups)
    mine = lax.all_to_all(mine, "chan", split_axis=0, concat_axis=0, tiled=True)

    mixed, specs = None, []
    for j in range(chunks):
        mixed, spec = convolve(me, pieces[j], skip, tables, pencil, j * rows, mixed)
        specs.append(spec)
    mixed_out, sent = pool(me, queries, mixed, gather, groups)
    mixed_home = [swap(mixed_out[k], k, peers) for k in range(peers)]

    def exchange(blocks):
        flat = blocks.reshape(groups * peers, pencil // 2, LANES)
        flat = lax.all_to_all(flat, ("chan", "seq"), split_axis=0, concat_axis=0, tiled=True)
        return flat.reshape(blocks.shape)

    got = exchange(sent)
    mine, _ = lax.optimization_barrier((mine, sent))
    other = swap(mine, 1, peers)
    own_bias = lax.dynamic_slice_in_dim(head_bias, group * own_tracks, own_tracks).reshape(1, own_tracks)
    own_counts = lax.dynamic_slice_in_dim(counts, group * own_tracks, own_tracks, axis=1)
    logits, sums = head_rates(me, got, mine, other, own_bias, own_counts)
    all_sums = [swap(sums, k, peers) for k in range(peers)]
    early, late = mixed_home[: peers - 1], mixed_home[peers - 1 :]
    logits, early = lax.optimization_barrier((logits, early))
    part, loss = head_grads(me, logits, all_sums, mine, other, own_counts)
    back = exchange(part)

    step = 1
    while step < groups:
        loss = loss + lax.ppermute(loss, "chan", [(i, i ^ step) for i in range(groups)])
        step *= 2

    back, loss, late = lax.optimization_barrier((back, loss, late))
    mixed_home = [*early, *late]
    grad_rows, packed = sum_grads(me, back)
    grads = None
    corr_home = []
    for j in range(chunks):
        corr = correlate(me, queries, grad_rows, specs[j], skip, tables, spread, j * rows, None if j else packed)
        grad_rows, _ = lax.optimization_barrier((grad_rows, corr))
        corr_home.append([swap(corr[k], k, peers) for k in range(peers)])
    for j in range(chunks):
        ours = [] if j else mixed_home
        grads, *rest = finish(me, projections, ours, corr_home[j], spread, j, chunks, grads, [] if j else [loss])
        if not j:
            mean_loss = rest[0].reshape(())
    return mean_loss, grads


def power_of_two(value):
    return value & (value - 1) == 0


def per_device(projections, filter_taps, skip_gain, head_weight, head_bias, counts):
    channels, width = projections.shape[1:]
    peers, groups = lax.axis_size("seq"), lax.axis_size("chan")
    pencil = channels // peers
    fits = (
        pencil % (2 * ROWS * CHUNKS) == 0
        and 2 * (width // POOL) == LANES
        and power_of_two(peers)
        and peers > 1
        and power_of_two(groups)
        and groups <= MOST_GROUPS
    )
    run = aligned if fits else general
    return run(projections, filter_taps, skip_gain, head_weight, head_bias, counts)


def general(projections, filter_taps, skip_gain, head_weight, head_bias, counts):
    f32, bf16 = jnp.float32, jnp.bfloat16
    _, channels, width = projections.shape
    peers = lax.axis_size("seq")
    groups = lax.axis_size("chan")
    seat = lax.axis_index("seq")
    group = lax.axis_index("chan")
    bins = width // POOL
    length = width * peers
    tracks = head_weight.shape[1]
    own_tracks = tracks // groups
    pencil = channels // peers
    rows = -(-pencil // ROWS) * ROWS
    me = jnp.asarray(seat, jnp.int32).reshape(1)
    tables = transform_tables(length)
    gather, spread = pool_tables()

    def block(array, k):
        return lax.dynamic_index_in_dim(array, seat ^ k, axis=-3, keepdims=False)

    query = projections[0]
    key_value = projections[1].astype(f32) * projections[2].astype(f32)
    stacked = jnp.stack([key_value.astype(bf16), filter_taps.astype(bf16)])
    stacked = stacked.reshape(2, peers, pencil, width)
    pieces = [pad_rows(swap(block(stacked, k), k, peers), rows) for k in range(peers)]
    query_blocks = query.reshape(peers, pencil, width)
    queries = [pad_rows(swap(block(query_blocks, k), k, peers), rows) for k in range(peers)]
    skip = pad_rows(block(skip_gain.reshape(peers, pencil, 1), 0), rows)

    half = channels // 2
    by_track = head_weight.reshape(2, half, groups, own_tracks).transpose(0, 2, 1, 3)
    mine = lax.dynamic_index_in_dim(by_track, seat & 1, axis=0, keepdims=False)
    mine = lax.all_to_all(mine, "chan", split_axis=0, concat_axis=0, tiled=True)
    other = swap(mine, 1, peers)
    mine = mine.reshape(groups * half, own_tracks)
    other = other.reshape(groups * half, own_tracks)

    mixed, spec = convolve(me, pieces, skip, tables, rows, 0, None)
    mixed_out, pooled = pool(me, queries, mixed, gather, 0)
    pooled = pooled[:pencil]
    mixed_home = [swap(mixed_out[k][:pencil], k, peers) for k in range(peers)]

    sent = pooled.reshape(pencil, peers, bins).transpose(1, 0, 2)
    sent = jnp.broadcast_to(sent[None], (groups, peers, pencil, bins))
    got = lax.all_to_all(
        sent.reshape(groups * peers, pencil, bins), ("chan", "seq"), split_axis=0, concat_axis=0, tiled=True
    )
    got = got.reshape(groups, 2, half, bins)
    low_half = got[:, 0].reshape(groups * half, bins)
    high_half = got[:, 1].reshape(groups * half, bins)
    odd = (seat & 1) == 1
    pooled_mine = jnp.where(odd, high_half, low_half)
    pooled_other = jnp.where(odd, low_half, high_half)

    def project(x, w):
        return lax.dot_general(x, w, (((0,), (0,)), ((), ())), preferred_element_type=f32)

    own_bias = lax.dynamic_slice_in_dim(head_bias, group * own_tracks, own_tracks)
    own_counts = lax.dynamic_slice_in_dim(counts, group * own_tracks, own_tracks, axis=1)
    logits = project(pooled_mine, mine) + project(pooled_other, other) + own_bias[None, :]
    rates = jax.nn.softplus(logits) + rate_floor
    observed = own_counts.astype(f32)
    partial_sums = jnp.stack(
        [jnp.sum(rates, axis=0), jnp.sum(observed, axis=0), jnp.sum(observed * jnp.log(rates), axis=0)]
    )
    pred_total, obs_total, log_sum = jnp.sum(lax.all_gather(partial_sums, "seq"), axis=0)
    log_pred = jnp.log(pred_total)
    loss_part = jnp.sum(
        total_weight * (pred_total - obs_total * log_pred) + obs_total * log_pred - log_sum
    )
    mean_loss = lax.psum(loss_part, "chan") / (bins * peers * tracks)
    ratio = obs_total / pred_total
    grad_rates = total_weight * (1.0 - ratio)[None, :] + ratio[None, :] - observed / rates
    grad_logits = (grad_rates * jax.nn.sigmoid(logits)).astype(bf16)

    def spread_back(w):
        return lax.dot_general(w, grad_logits, (((1,), (1,)), ((), ())), preferred_element_type=f32)

    part_mine = spread_back(mine).astype(bf16).reshape(groups, 1, half, bins)
    part_other = spread_back(other).astype(bf16).reshape(groups, 1, half, bins)
    part = jnp.concatenate(
        [jnp.where(odd, part_other, part_mine), jnp.where(odd, part_mine, part_other)], axis=1
    )
    back = lax.all_to_all(
        part.reshape(groups * peers, pencil, bins), ("chan", "seq"), split_axis=0, concat_axis=0, tiled=True
    )
    grad_pooled = jnp.sum(back.reshape(groups, peers, pencil, bins).astype(f32), axis=0)
    grad_home = [swap(block(grad_pooled, k), k, peers) for k in range(peers)]
    grad_rows = pad_rows(grad_pooled.transpose(1, 0, 2).reshape(pencil, peers * bins), rows)

    corr_out = correlate(me, queries, grad_rows, spec, skip, tables, spread, 0, None)
    corr_home = [swap(corr_out[k][:pencil], k, peers) for k in range(peers)]

    def assemble(parts):
        out = jnp.zeros((peers,) + parts[0].shape, parts[0].dtype)
        for k, part in enumerate(parts):
            out = lax.dynamic_update_index_in_dim(out, part, seat ^ k, axis=0)
        return out.reshape((channels,) + parts[0].shape[1:])

    grad_output = jnp.repeat(assemble(grad_home) / POOL, POOL, axis=1)
    grad_kv = assemble(corr_home).astype(f32)
    grad_query = grad_output * assemble(mixed_home).astype(f32)
    grads = jnp.stack(
        [grad_query, grad_kv * projections[2].astype(f32), grad_kv * projections[1].astype(f32)], axis=0
    )
    return mean_loss, grads


def solution(mesh):
    placed = (
        P(None, "chan", "seq"),
        P("chan", "seq"),
        P("chan"),
        P("chan", None),
        P(),
        P("seq", None),
    )
    return jax.shard_map(
        per_device,
        mesh=mesh,
        in_specs=placed,
        out_specs=(P(), P(None, "chan", "seq")),
        check_vma=False,
    )
```
